32 devices in a mesh: dp: 4 (over y, x), fsdp: 8 (over z, core).
Axes of the slice: x: 2, y: 2, z: 4, core: 2. Of those that a mesh axis runs over, the one named last changes fastest.
Arguments:
- hidden_in: bfloat16 [16384, 768], P(('dp', 'fsdp')), may hold values from -6 to 6
- teacher_hidden: bfloat16 [16384, 768], P(('dp', 'fsdp')), may hold values from -6 to 6
- teacher_scores: bfloat16 [16384, 12, 256], P(('dp', 'fsdp')), may hold values from -8 to 8
- seq_lengths: int32 [32, 4], P(('dp', 'fsdp')), may hold values from 16 to 256, as said below
- live_counts: int32 [32, 3], P(('dp', 'fsdp')), may hold values from 0 to 2, as said below
- triple_latent: float32 [2, 768, 2304], P(None, 'fsdp'), may hold values from -1.5 to 1.5
- mixing_latent: float32 [2, 768, 768], P(None, 'fsdp'), may hold values from -1.5 to 1.5
- widen_latent: float32 [2, 768, 3072], P(None, 'fsdp'), may hold values from -1.5 to 1.5
- narrow_latent: float32 [2, 3072, 768], P(None, 'fsdp'), may hold values from -1.5 to 1.5
- triple_bias: float32 [3, 768], P(None, 'fsdp'), may hold values from -1.2 to 1.2
- mixing_bias: float32 [768], P('fsdp'), may hold values from -1.2 to 1.2
- widen_bias: float32 [3072], P('fsdp'), may hold values from -1.2 to 1.2
- narrow_bias: float32 [768], P('fsdp'), may hold values from -1.2 to 1.2
- norm_gain: float32 [2, 768], P(None, 'fsdp'), may hold values from 0.5 to 1.5
- norm_shift: float32 [2, 768], P(None, 'fsdp'), may hold values from -1.2 to 1.2
- clip_level: float32 [4], replicated, may hold values from 0.8 to 3
Outputs:
- layer_out: bfloat16 [16384, 768], P(('dp', 'fsdp'))
- loss: float32 [], replicated
- input_grad: float32 [16384, 768], P(('dp', 'fsdp'))
- triple_latent_grad: float32 [2, 768, 2304], P(None, 'fsdp')
- mixing_latent_grad: float32 [2, 768, 768], P(None, 'fsdp')
- widen_latent_grad: float32 [2, 768, 3072], P(None, 'fsdp')
- narrow_latent_grad: float32 [2, 3072, 768], P(None, 'fsdp')
- triple_bias_grad: float32 [3, 768], P(None, 'fsdp')
- mixing_bias_grad: float32 [768], P('fsdp')
- widen_bias_grad: float32 [3072], P('fsdp')
- narrow_bias_grad: float32 [768], P('fsdp')
- norm_gain_grad: float32 [2, 768], P(None, 'fsdp')
- norm_shift_grad: float32 [2, 768], P(None, 'fsdp')
- clip_level_grad: float32 [4], replicated
The draws below stay inside these ranges and needn't reach their ends.
Inputs may be any that keep to these rules, and one draw needn't show every extreme that they name: `seq_lengths`: slot j of every device has at most its bucket's number of rows (256, 128 or 64) and at least a quarter of it; every slot column is full on some device. `live_counts`: columns are the long, middle and short bucket; each entry is at most that bucket's number of slots, the live slots are the first ones, and some device has all its slots live.
All inputs are finite; a program needn't handle non-finite values.
Results may differ from the reference program's by a relative error of at most 0.0074.
Values sent between devices are 32-bit elements; how exact they have to be, the bound alone decides.
A program may use at most 256 MiB of HBM per device.

```python
import math
import jax
import jax.numpy as jnp
from jax import lax

D = 768
HEADS = 12
HEAD_DIM = 64
FF = 3072
LONG_LEN = 256
MID_LEN = 128
SHORT_LEN = 64
LONG_SLOTS = 1
MID_SLOTS = 1
SHORT_SLOTS = 2
SLOTS = 4
ROWS_DEV = 512
TOKENS = 16384
DEVICES = 32


def slot_caps():
    return jnp.concatenate([jnp.full((LONG_SLOTS,), LONG_LEN, jnp.int32), jnp.full((MID_SLOTS,), MID_LEN, jnp.int32), jnp.full((SHORT_SLOTS,), SHORT_LEN, jnp.int32)])


def draw_seq_lengths(key, part):
    caps = slot_caps()
    floors = jnp.maximum(caps // 4, 1)
    length_key = jax.random.fold_in(key, 11)
    full_key = jax.random.fold_in(key, 12)
    fraction = jax.random.randint(length_key, (DEVICES, SLOTS), 0, 1 << 20, dtype=jnp.int32)
    lengths = floors[None, :] + jnp.right_shift(fraction * (caps - floors + 1)[None, :], 20)
    chosen = jax.random.randint(full_key, (SLOTS,), 0, DEVICES, dtype=jnp.int32)
    full_mark = jnp.arange(DEVICES, dtype=jnp.int32)[:, None] == chosen[None, :]
    return jnp.where(full_mark, caps[None, :], lengths).astype(jnp.int32)


def draw_live_counts(key, part):
    limits = jnp.array([LONG_SLOTS, MID_SLOTS, SHORT_SLOTS], jnp.int32)
    flag_key = jax.random.fold_in(key, 21)
    drop_key = jax.random.fold_in(key, 22)
    full_key = jax.random.fold_in(key, 23)
    short_flag = jax.random.randint(flag_key, (DEVICES, 3), 0, 4, dtype=jnp.int32) == 0
    fraction = jax.random.randint(drop_key, (DEVICES, 3), 0, 1 << 20, dtype=jnp.int32)
    dropped = 1 + jnp.right_shift(fraction * limits[None, :], 20)
    counts = jnp.where(short_flag, limits[None, :] - dropped, limits[None, :])
    chosen = jax.random.randint(full_key, (), 0, DEVICES, dtype=jnp.int32)
    full_mark = jnp.arange(DEVICES, dtype=jnp.int32)[:, None] == chosen
    return jnp.where(full_mark, limits[None, :], counts).astype(jnp.int32)


def level_of(key, dims, shards, low, high):
    def one(dim, blocks):
        heights = jax.random.uniform(jax.random.fold_in(jax.random.fold_in(key, 6), dim), (blocks,), jnp.float32, low / len(shards), high / len(shards))
        return jnp.repeat(jnp.exp(heights), dims[dim] // blocks).reshape((-1,) + (1,) * (len(dims) - dim - 1))

    loudness = one(*shards[0])
    for cut in shards[1:]:
        loudness = loudness * one(*cut)
    return loudness


def normal_values(stream_key, shape, spread, reach, split=(), held_as=jnp.bfloat16):
    values = spread * jax.random.normal(stream_key, shape, jnp.float32)
    if split:
        values = values * level_of(stream_key, shape, split, -0.22, 0.18)
    return jnp.clip(values, -reach, reach).astype(held_as)


def setup_inputs(seed: int = 0) -> dict:
    key_of = jax.random.split(jax.random.key(seed), 17)
    hidden_in = normal_values(key_of[0], (TOKENS, D), 1.0, 6.0, ((0, 32),))
    teacher_hidden = normal_values(key_of[1], (TOKENS, D), 1.0, 6.0, ((0, 32),))
    teacher_scores = normal_values(key_of[2], (TOKENS, HEADS, LONG_LEN), 1.5, 8.0, ((0, 32),))
    seq_lengths = draw_seq_lengths(jax.random.fold_in(key_of[16], 71), 0)
    live_counts = draw_live_counts(jax.random.fold_in(key_of[16], 71), 0)
    triple_latent = jnp.clip(jax.random.uniform(key_of[5], (2, D, 3 * D), jnp.float32, -1.5, 1.5) * level_of(key_of[5], (2, D, 3 * D), ((1, 8),), -0.4, 0.0), -1.5, 1.5)
    mixing_latent = jnp.clip(jax.random.uniform(key_of[6], (2, D, D), jnp.float32, -1.5, 1.5) * level_of(key_of[6], (2, D, D), ((1, 8),), -0.4, 0.0), -1.5, 1.5)
    widen_latent = jnp.clip(jax.random.uniform(key_of[7], (2, D, FF), jnp.float32, -1.5, 1.5) * level_of(key_of[7], (2, D, FF), ((1, 8),), -0.4, 0.0), -1.5, 1.5)
    narrow_latent = jnp.clip(jax.random.uniform(key_of[8], (2, FF, D), jnp.float32, -1.5, 1.5) * level_of(key_of[8], (2, FF, D), ((1, 8),), -0.4, 0.0), -1.5, 1.5)
    triple_bias = normal_values(key_of[9], (3, D), 0.2, 1.2, ((1, 8),), jnp.float32)
    mixing_bias = normal_values(key_of[10], (D,), 0.2, 1.2, ((0, 8),), jnp.float32)
    widen_bias = normal_values(key_of[11], (FF,), 0.2, 1.2, ((0, 8),), jnp.float32)
    narrow_bias = normal_values(key_of[12], (D,), 0.2, 1.2, ((0, 8),), jnp.float32)
    norm_gain = jnp.clip(1.0 + 0.1 * jax.random.normal(key_of[13], (2, D), jnp.float32), 0.5, 1.5)
    norm_shift = normal_values(key_of[14], (2, D), 0.2, 1.2, ((1, 8),), jnp.float32)
    clip_level = jnp.clip(jnp.exp(jax.random.uniform(key_of[15], (4,), jnp.float32, math.log(0.8), math.log(3.0))), 0.8, 3.0)
    return dict(hidden_in=hidden_in, teacher_hidden=teacher_hidden, teacher_scores=teacher_scores, seq_lengths=seq_lengths, live_counts=live_counts, triple_latent=triple_latent, mixing_latent=mixing_latent, widen_latent=widen_latent, narrow_latent=narrow_latent, triple_bias=triple_bias, mixing_bias=mixing_bias, widen_bias=widen_bias, narrow_bias=narrow_bias, norm_gain=norm_gain, norm_shift=norm_shift, clip_level=clip_level)


@jax.custom_vjp
def low(v):
    return lax.optimization_barrier(v.astype(jnp.bfloat16)).astype(jnp.float32)

@jax.custom_vjp
def low_back(v):
    return v

def low_keep(v):
    return (low(v), None)

def low_pass(kept, grad):
    return (grad,)

def back_keep(v):
    return (v, None)

def back_low(kept, grad):
    return (low(grad),)
low.defvjp(low_keep, low_pass)
low_back.defvjp(back_keep, back_low)
norm_epsilon = 1e-12
masked_fill = -1e+30
highest = lax.Precision.HIGHEST

def soft_clip(values, clip_at):
    return clip_at * jnp.tanh(values / clip_at)

def layer_norm(values, gain_row, shift_row):
    center = values - lax.optimization_barrier(jnp.mean(values, axis=-1, keepdims=True))
    variance = lax.optimization_barrier(jnp.mean(center * center, axis=-1, keepdims=True))
    return center * lax.rsqrt(variance + norm_epsilon) * gain_row + shift_row

def gelu_exact(values):
    return 0.5 * values * (1.0 + lax.erf(values * (1.0 / math.sqrt(2.0))))

def product(left, right):
    return jnp.dot(left, right, precision=highest, preferred_element_type=jnp.float32)

def binarized(latent, fan_in):
    scales = lax.optimization_barrier(jnp.mean(jnp.abs(latent), axis=-1, keepdims=True)) / math.sqrt(fan_in)
    sign_values = jnp.where(latent > 0, 1.0, -1.0)
    return scales[0] * sign_values[0] + scales[1] * sign_values[1]

def clipped_sum(latent, fan_in):
    return lax.optimization_barrier(jnp.sum(jnp.clip(latent, -1.0, 1.0), axis=0)) / math.sqrt(fan_in)

def bucket_shapes():
    return ((LONG_SLOTS, LONG_LEN), (MID_SLOTS, MID_LEN), (SHORT_SLOTS, SHORT_LEN))

def bucket_attention(qkv_rows, teacher_rows, lengths, live_count, slot_count, bucket_len):
    queries = qkv_rows[:, :D].reshape(slot_count, bucket_len, HEADS, HEAD_DIM)
    keys_part = qkv_rows[:, D:2 * D].reshape(slot_count, bucket_len, HEADS, HEAD_DIM)
    values_part = qkv_rows[:, 2 * D:].reshape(slot_count, bucket_len, HEADS, HEAD_DIM)
    scores = jnp.einsum('sqhd,skhd->shqk', queries, keys_part, precision=highest) * HEAD_DIM ** (-0.5)
    scores = low_back(scores)
    places = jnp.arange(bucket_len, dtype=jnp.int32)
    key_ok = places[None, :] < lengths[:, None]
    query_ok = jnp.logical_and(key_ok, jnp.arange(slot_count, dtype=jnp.int32)[:, None] < live_count)
    masked = jnp.where(key_ok[:, None, None, :], scores, masked_fill)
    row_top = lax.optimization_barrier(jnp.max(masked, axis=-1, keepdims=True))
    exponent = jnp.exp(masked - row_top)
    attention = exponent / lax.optimization_barrier(jnp.sum(exponent, axis=-1, keepdims=True))
    context = jnp.einsum('shqk,skhd->sqhd', low(attention), values_part, precision=highest)
    teacher = jnp.transpose(teacher_rows.reshape(slot_count, bucket_len, HEADS, LONG_LEN)[..., :bucket_len], (0, 2, 1, 3))
    pair_ok = jnp.logical_and(query_ok[:, None, :, None], key_ok[:, None, None, :])
    score_gap = jnp.where(pair_ok, scores - teacher, 0.0)
    distill = 0.5 / LONG_LEN * jnp.sum(score_gap * score_gap)
    return (context.reshape(slot_count * bucket_len, D), query_ok.reshape(slot_count * bucket_len), distill)

def device_block(params, piece):
    weights, biases, norm_gain, norm_shift, clip_level = params
    inputs, teacher_hidden, teacher_scores, lengths, counts = piece
    teacher_hidden = teacher_hidden.astype(jnp.float32)
    teacher_scores = teacher_scores.astype(jnp.float32)
    inputs_low = low(soft_clip(inputs, clip_level[0]))
    qkv_all = low(low_back(product(inputs_low, weights[0]) + biases[0].reshape(3 * D)))
    contexts = []
    oks = []
    distill_sum = jnp.zeros((), jnp.float32)
    row_start = 0
    slot_start = 0
    for bucket, shape_pair in enumerate(bucket_shapes()):
        slot_count, bucket_len = shape_pair
        row_end = row_start + slot_count * bucket_len
        context, query_ok, distill = bucket_attention(qkv_all[row_start:row_end], teacher_scores[row_start:row_end], lengths[slot_start:slot_start + slot_count], counts[bucket], slot_count, bucket_len)
        contexts.append(context)
        oks.append(query_ok)
        distill_sum = distill_sum + distill
        row_start = row_end
        slot_start = slot_start + slot_count
    context = low_back(jnp.concatenate(contexts, axis=0))
    context_low = low(soft_clip(context, clip_level[1]))
    mixed = low_back(product(context_low, weights[1]) + biases[1])
    first_sum = inputs + mixed
    first_norm = layer_norm(first_sum, norm_gain[0], norm_shift[0])
    widen_low = low(soft_clip(first_norm, clip_level[2]))
    widened = low_back(product(widen_low, weights[2]) + biases[2])
    activated_low = low(soft_clip(gelu_exact(widened), clip_level[3]))
    narrowed = low_back(product(activated_low, weights[3]) + biases[3])
    second_sum = first_norm + narrowed
    layer_out = layer_norm(second_sum, norm_gain[1], norm_shift[1])
    token_ok = jnp.concatenate(oks)
    out_gap = jnp.where(token_ok[:, None], layer_out - teacher_hidden, 0.0)
    return (layer_out, 0.5 * jnp.sum(out_gap * out_gap) + distill_sum)

def reference(hidden_in, teacher_hidden, teacher_scores, seq_lengths, live_counts, triple_latent, mixing_latent, widen_latent, narrow_latent, triple_bias, mixing_bias, widen_bias, narrow_bias, norm_gain, norm_shift, clip_level):
    latents = (triple_latent, mixing_latent, widen_latent, narrow_latent)
    biases = (triple_bias, mixing_bias, widen_bias, narrow_bias)
    fan_ins = (D, D, D, FF)
    rounded = tuple((low(binarized(latent, fan_in)) for latent, fan_in in zip(latents, fan_ins)))
    anchors = tuple((clipped_sum(latent, fan_in) for latent, fan_in in zip(latents, fan_ins)))

    def forward(hidden, latent_set, bias_set, gains, shifts, clips):
        weights = tuple((rounded_part + (clipped_sum(latent, fan_in) - anchor) for rounded_part, latent, fan_in, anchor in zip(rounded, latent_set, fan_ins, anchors)))
        params = (weights, bias_set, gains, shifts, clips)
        block_call = jax.checkpoint(device_block)

        def step(carry, piece):
            out_block, loss_block = block_call(params, piece)
            return (carry + loss_block, out_block)
        pieces = (hidden.reshape(DEVICES, ROWS_DEV, D), teacher_hidden.reshape(DEVICES, ROWS_DEV, D), teacher_scores.reshape(DEVICES, ROWS_DEV, HEADS, LONG_LEN), seq_lengths, live_counts)
        loss_total, out_blocks = lax.scan(step, jnp.zeros((), jnp.float32), pieces)
        return (out_blocks.reshape(TOKENS, D), loss_total)
    hidden = hidden_in.astype(jnp.float32)
    outputs, back_call = jax.vjp(forward, hidden, latents, biases, norm_gain, norm_shift, clip_level)
    grads = back_call((jnp.zeros((TOKENS, D), jnp.float32), jnp.ones((), jnp.float32)))
    hidden_grad, latent_grads, bias_grads, gain_grad, shift_grad, clip_grad = grads
    layer_out, loss_total = outputs
    return (layer_out.astype(jnp.bfloat16), loss_total / (TOKENS * D), hidden_grad, latent_grads[0], latent_grads[1], latent_grads[2], latent_grads[3], bias_grads[0], bias_grads[1], bias_grads[2], bias_grads[3], gain_grad, shift_grad, clip_grad)
```

```python
import math

import jax
import jax.numpy as jnp
from jax import lax
from jax.experimental import pallas as pl
from jax.experimental.pallas import tpu as pltpu
from jax.sharding import PartitionSpec as P

D = 768
HEADS = 12
HEAD_DIM = 64
FF = 3072
LONG_LEN = 256
MID_LEN = 128
SHORT_LEN = 64
LONG_SLOTS = 1
MID_SLOTS = 1
SHORT_SLOTS = 2


bit_count = 32
norm_epsilon = 1e-12
masked_fill = -1e30


def soft_clip(values, clip_at):
    return clip_at * jnp.tanh(values / clip_at)


def layer_norm(values, gain_row, shift_row):
    center = values - jnp.mean(values, axis=-1, keepdims=True)
    variance = jnp.mean(center * center, axis=-1, keepdims=True)
    return center * lax.rsqrt(variance + norm_epsilon) * gain_row + shift_row


def gelu_exact(values):
    return 0.5 * values * (1.0 + lax.erf(values * (1.0 / math.sqrt(2.0))))


def pack_signs(latent):
    halves, row_count, columns = latent.shape
    sign_bits = (
        (latent > 0).astype(jnp.int32).reshape(halves, row_count, columns // bit_count, bit_count)
    )
    places = jnp.arange(bit_count, dtype=jnp.int32)
    return jnp.sum(jnp.left_shift(sign_bits, places), axis=-1, dtype=jnp.int32)


def unpack_weight(sign_words, scales):
    halves, row_count, word_count = sign_words.shape
    places = jnp.arange(bit_count, dtype=jnp.int32)
    sign_bits = jnp.bitwise_and(jnp.right_shift(sign_words[..., None], places), 1)
    sign_values = (
        (2 * sign_bits - 1).astype(jnp.float32).reshape(halves, row_count, word_count * bit_count)
    )
    return (scales[0][:, None] * sign_values[0] + scales[1][:, None] * sign_values[1]).astype(
        jnp.bfloat16
    )


def bucket_shapes():
    return ((LONG_SLOTS, LONG_LEN), (MID_SLOTS, MID_LEN), (SHORT_SLOTS, SHORT_LEN))


def bucket_masks(lengths, live_count, slot_count, bucket_len):
    places = jnp.arange(bucket_len, dtype=jnp.int32)
    key_ok = places[None, :] < lengths[:, None]
    query_ok = jnp.logical_and(
        key_ok, jnp.arange(slot_count, dtype=jnp.int32)[:, None] < live_count
    )
    return (key_ok, query_ok)


def split_heads(block, slot_count, bucket_len):
    return block.reshape(slot_count, bucket_len, HEADS, HEAD_DIM)


def bucket_scores(qkv_rows, teacher_rows, key_ok, query_ok, slot_count, bucket_len):
    queries = split_heads(qkv_rows[:, :D], slot_count, bucket_len)
    keys_part = split_heads(qkv_rows[:, D : 2 * D], slot_count, bucket_len)
    scores = jnp.einsum(
        "sqhd,skhd->shqk", queries, keys_part, preferred_element_type=jnp.float32
    ) * HEAD_DIM ** (-0.5)
    masked = jnp.where(key_ok[:, None, None, :], scores, masked_fill)
    teacher = jnp.transpose(
        teacher_rows.reshape(slot_count, bucket_len, HEADS, LONG_LEN)[..., :bucket_len],
        (0, 2, 1, 3),
    ).astype(jnp.float32)
    pair_ok = jnp.logical_and(query_ok[:, None, :, None], key_ok[:, None, None, :])
    score_gap = jnp.where(pair_ok, scores - teacher, 0.0)
    return (queries, keys_part, masked, score_gap)


def attend(qkv_rows, teacher_rows, key_ok, query_ok, slot_count, bucket_len):
    queries, keys_part, masked, score_gap = bucket_scores(
        qkv_rows, teacher_rows, key_ok, query_ok, slot_count, bucket_len
    )
    values_part = split_heads(qkv_rows[:, 2 * D :], slot_count, bucket_len)
    row_top = jnp.max(masked, axis=-1, keepdims=True)
    exponent = jnp.exp(masked - row_top)
    exp_total = jnp.sum(exponent, axis=-1, keepdims=True)
    attention = exponent / exp_total
    context = jnp.einsum(
        "shqk,skhd->sqhd",
        attention.astype(jnp.bfloat16),
        values_part,
        preferred_element_type=jnp.float32,
    )
    distill = 0.5 / LONG_LEN * jnp.sum(score_gap * score_gap)
    return (context.reshape(slot_count * bucket_len, D), row_top + jnp.log(exp_total), distill)


def attend_back(
    qkv_rows, teacher_rows, key_ok, query_ok, slot_count, bucket_len, log_total, context_grad
):
    queries, keys_part, masked, score_gap = bucket_scores(
        qkv_rows, teacher_rows, key_ok, query_ok, slot_count, bucket_len
    )
    values_part = split_heads(qkv_rows[:, 2 * D :], slot_count, bucket_len)
    attention = jnp.exp(masked - log_total)
    grad_heads = split_heads(context_grad, slot_count, bucket_len)
    values_grad = jnp.einsum(
        "shqk,sqhd->skhd",
        attention.astype(jnp.bfloat16),
        grad_heads,
        preferred_element_type=jnp.float32,
    )
    weight_grad = jnp.einsum(
        "sqhd,skhd->shqk", grad_heads, values_part, preferred_element_type=jnp.float32
    )
    score_grad = attention * (
        weight_grad - jnp.sum(weight_grad * attention, axis=-1, keepdims=True)
    ) + score_gap * (1.0 / LONG_LEN)
    score_low = score_grad.astype(jnp.bfloat16)
    score_scale = HEAD_DIM ** (-0.5)
    queries_grad = (
        jnp.einsum("shqk,skhd->sqhd", score_low, keys_part, preferred_element_type=jnp.float32)
        * score_scale
    )
    keys_grad = (
        jnp.einsum("shqk,sqhd->skhd", score_low, queries, preferred_element_type=jnp.float32)
        * score_scale
    )
    row_count = slot_count * bucket_len
    return jnp.concatenate(
        [
            queries_grad.reshape(row_count, D),
            keys_grad.reshape(row_count, D),
            values_grad.reshape(row_count, D),
        ],
        axis=-1,
    )


def on_device(
    hidden_in,
    teacher_hidden,
    teacher_scores,
    seq_lengths,
    live_counts,
    triple_latent,
    mixing_latent,
    widen_latent,
    narrow_latent,
    triple_bias,
    mixing_bias,
    widen_bias,
    narrow_bias,
    norm_gain,
    norm_shift,
    clip_level,
):
    latents = (triple_latent, mixing_latent, widen_latent, narrow_latent)
    fan_ins = (D, D, D, FF)
    own_scales = tuple(
        (
            jnp.mean(jnp.abs(latent), axis=-1) / math.sqrt(fan_in)
            for latent, fan_in in zip(latents, fan_ins)
        )
    )
    packed = tuple((pack_signs(latent) for latent in latents))
    gathered = (
        lax.all_gather(packed[0], "fsdp", axis=1, tiled=True),
        lax.all_gather(packed[1], "fsdp", axis=1, tiled=True),
        lax.all_gather(packed[2], "fsdp", axis=1, tiled=True),
        lax.all_gather(packed[3], "fsdp", axis=1, tiled=True),
    )
    factors = (
        lax.all_gather(own_scales[0], "fsdp", axis=1, tiled=True),
        lax.all_gather(own_scales[1], "fsdp", axis=1, tiled=True),
        lax.all_gather(own_scales[2], "fsdp", axis=1, tiled=True),
        lax.all_gather(own_scales[3], "fsdp", axis=1, tiled=True),
        lax.all_gather(triple_bias, "fsdp", axis=1, tiled=True),
        lax.all_gather(mixing_bias, "fsdp", axis=0, tiled=True),
        lax.all_gather(widen_bias, "fsdp", axis=0, tiled=True),
        lax.all_gather(narrow_bias, "fsdp", axis=0, tiled=True),
        lax.all_gather(norm_gain, "fsdp", axis=1, tiled=True),
        lax.all_gather(norm_shift, "fsdp", axis=1, tiled=True),
    )
    scales = factors[:4]
    triple_rows, full_mixing_bias, full_widen_bias, full_narrow_bias, gains, shifts = factors[4:]
    full_triple_bias = triple_rows.reshape(3 * D)
    weights = tuple(
        (unpack_weight(words_part, scale_part) for words_part, scale_part in zip(gathered, scales))
    )
    inputs = hidden_in.astype(jnp.float32)
    inputs_low = soft_clip(inputs, clip_level[0]).astype(jnp.bfloat16)
    qkv_all = (
        jnp.dot(inputs_low, weights[0], preferred_element_type=jnp.float32) + full_triple_bias
    ).astype(jnp.bfloat16)
    lengths = seq_lengths[0]
    counts = live_counts[0]
    plans = []
    row_start = 0
    slot_start = 0
    for bucket, shape_pair in enumerate(bucket_shapes()):
        slot_count, bucket_len = shape_pair
        key_ok, query_ok = bucket_masks(
            lengths[slot_start : slot_start + slot_count], counts[bucket], slot_count, bucket_len
        )
        plans.append(
            (
                row_start,
                row_start + slot_count * bucket_len,
                slot_count,
                bucket_len,
                key_ok,
                query_ok,
            )
        )
        row_start = row_start + slot_count * bucket_len
        slot_start = slot_start + slot_count
    contexts = []
    log_totals = []
    distill_sum = 0.0
    for plan in plans:
        row_begin, row_end, slot_count, bucket_len, key_ok, query_ok = plan
        context, log_total, distill = attend(
            qkv_all[row_begin:row_end],
            teacher_scores[row_begin:row_end],
            key_ok,
            query_ok,
            slot_count,
            bucket_len,
        )
        contexts.append(context)
        log_totals.append(log_total)
        distill_sum = distill_sum + distill
    context = jnp.concatenate(contexts, axis=0)
    token_ok = jnp.concatenate([plan[5].reshape(-1) for plan in plans])
    context_low = soft_clip(context, clip_level[1]).astype(jnp.bfloat16)
    mixed = jnp.dot(context_low, weights[1], preferred_element_type=jnp.float32) + full_mixing_bias
    first_sum = inputs + mixed
    first_norm = layer_norm(first_sum, gains[0], shifts[0])
    widen_low = soft_clip(first_norm, clip_level[2]).astype(jnp.bfloat16)
    widened = jnp.dot(widen_low, weights[2], preferred_element_type=jnp.float32) + full_widen_bias
    activated = gelu_exact(widened)
    activated_low = soft_clip(activated, clip_level[3]).astype(jnp.bfloat16)
    narrowed = (
        jnp.dot(activated_low, weights[3], preferred_element_type=jnp.float32) + full_narrow_bias
    )
    second_sum = first_norm + narrowed
    out_full = layer_norm(second_sum, gains[1], shifts[1])
    out_gap = jnp.where(token_ok[:, None], out_full - teacher_hidden.astype(jnp.float32), 0.0)
    loss_local = 0.5 * jnp.sum(out_gap * out_gap) + distill_sum
    regathered = (
        lax.all_gather(packed[0], "fsdp", axis=1, tiled=True),
        lax.all_gather(packed[1], "fsdp", axis=1, tiled=True),
        lax.all_gather(packed[2], "fsdp", axis=1, tiled=True),
        lax.all_gather(packed[3], "fsdp", axis=1, tiled=True),
    )
    back_weights = tuple(
        (
            unpack_weight(words_part, scale_part)
            for words_part, scale_part in zip(regathered, scales)
        )
    )
    _, second_back = jax.vjp(layer_norm, second_sum, gains[1], shifts[1])
    second_grad, gain_two, shift_two = second_back(out_gap)
    narrow_low = second_grad.astype(jnp.bfloat16)
    narrow_weight_grad = jnp.einsum(
        "rf,rd->fd", activated_low, narrow_low, preferred_element_type=jnp.float32
    )
    act_low_grad = jnp.einsum(
        "rd,fd->rf", narrow_low, back_weights[3], preferred_element_type=jnp.float32
    )
    _, clip_three_back = jax.vjp(soft_clip, activated, clip_level[3])
    act_grad, clip_three = clip_three_back(act_low_grad)
    _, gelu_back = jax.vjp(gelu_exact, widened)
    (widened_grad,) = gelu_back(act_grad)
    widen_grad_low = widened_grad.astype(jnp.bfloat16)
    widen_weight_grad = jnp.einsum(
        "rd,rf->df", widen_low, widen_grad_low, preferred_element_type=jnp.float32
    )
    norm_low_grad = jnp.einsum(
        "rf,df->rd", widen_grad_low, back_weights[2], preferred_element_type=jnp.float32
    )
    _, clip_two_back = jax.vjp(soft_clip, first_norm, clip_level[2])
    norm_grad, clip_two = clip_two_back(norm_low_grad)
    norm_grad = norm_grad + second_grad
    _, first_back = jax.vjp(layer_norm, first_sum, gains[0], shifts[0])
    first_grad, gain_one, shift_one = first_back(norm_grad)
    mixed_low = first_grad.astype(jnp.bfloat16)
    mixing_weight_grad = jnp.einsum(
        "rc,rd->cd", context_low, mixed_low, preferred_element_type=jnp.float32
    )
    context_low_grad = jnp.einsum(
        "rd,cd->rc", mixed_low, back_weights[1], preferred_element_type=jnp.float32
    )
    _, clip_one_back = jax.vjp(soft_clip, context, clip_level[1])
    context_grad, clip_one = clip_one_back(context_low_grad)
    context_grad_low = context_grad.astype(jnp.bfloat16)
    qkv_grads = []
    for plan, log_total in zip(plans, log_totals):
        row_begin, row_end, slot_count, bucket_len, key_ok, query_ok = plan
        qkv_grads.append(
            attend_back(
                qkv_all[row_begin:row_end],
                teacher_scores[row_begin:row_end],
                key_ok,
                query_ok,
                slot_count,
                bucket_len,
                log_total,
                context_grad_low[row_begin:row_end],
            )
        )
    qkv_grad_low = jnp.concatenate(qkv_grads, axis=0).astype(jnp.bfloat16)
    triple_weight_grad = jnp.einsum(
        "rd,re->de", inputs_low, qkv_grad_low, preferred_element_type=jnp.float32
    )
    input_low_grad = jnp.einsum(
        "re,de->rd", qkv_grad_low, back_weights[0], preferred_element_type=jnp.float32
    )
    _, clip_zero_back = jax.vjp(soft_clip, inputs, clip_level[0])
    input_side, clip_zero = clip_zero_back(input_low_grad)
    input_grad = input_side + first_grad
    bias_sums = (
        jnp.sum(qkv_grad_low, axis=0, dtype=jnp.float32).reshape(3, D),
        jnp.sum(mixed_low, axis=0, dtype=jnp.float32),
        jnp.sum(widen_grad_low, axis=0, dtype=jnp.float32),
        jnp.sum(narrow_low, axis=0, dtype=jnp.float32),
    )
    row_shares = (
        lax.psum_scatter(triple_weight_grad, "fsdp", scatter_dimension=0, tiled=True),
        lax.psum_scatter(mixing_weight_grad, "fsdp", scatter_dimension=0, tiled=True),
        lax.psum_scatter(widen_weight_grad, "fsdp", scatter_dimension=0, tiled=True),
        lax.psum_scatter(narrow_weight_grad, "fsdp", scatter_dimension=0, tiled=True),
    )
    totals = lax.psum((row_shares[0], row_shares[1], row_shares[2], row_shares[3]), "dp")
    small_sums = lax.psum(
        (
            bias_sums[0],
            bias_sums[1],
            bias_sums[2],
            bias_sums[3],
            jnp.stack([gain_one, gain_two]),
            jnp.stack([shift_one, shift_two]),
            jnp.stack([clip_zero, clip_one, clip_two, clip_three]),
            loss_local,
        ),
        ("dp", "fsdp"),
    )
    shard_index = lax.axis_index("fsdp")
    shard_parts = lax.axis_size("fsdp")

    def own_part(vector, along):
        share_width = vector.shape[along] // shard_parts
        return lax.dynamic_slice_in_dim(vector, shard_index * share_width, share_width, along)

    latent_grads = tuple(
        (
            jnp.where(jnp.abs(latent) <= 1.0, (total / math.sqrt(fan_in))[None], 0.0)
            for latent, total, fan_in in zip(latents, totals, fan_ins)
        )
    )
    loss = small_sums[7] / (hidden_in.shape[0] * D * lax.axis_size("dp") * shard_parts)
    return (
        out_full.astype(jnp.bfloat16),
        loss,
        input_grad,
        latent_grads[0],
        latent_grads[1],
        latent_grads[2],
        latent_grads[3],
        own_part(small_sums[0], 1),
        own_part(small_sums[1], 0),
        own_part(small_sums[2], 0),
        own_part(small_sums[3], 0),
        own_part(small_sums[4], 1),
        own_part(small_sums[5], 1),
        small_sums[6],
    )


bf16 = jnp.bfloat16
f32 = jnp.float32
MESH = pl.DeviceIdType.MESH
VMEM_CAP = 60 * 1024 * 1024
ROWS = LONG_SLOTS * LONG_LEN + MID_SLOTS * MID_LEN + SHORT_SLOTS * SHORT_LEN
BLOCK = 96
CHUNK = 512
CHUNKS = 18
SLOTS = 4


def dot_nn(a, b):
    return lax.dot_general(a, b, (((1,), (0,)), ((), ())), preferred_element_type=f32)


def dot_nt(a, b):
    return lax.dot_general(a, b, (((1,), (1,)), ((), ())), preferred_element_type=f32)


def dot_tn(a, b):
    return lax.dot_general(a, b, (((0,), (0,)), ((), ())), preferred_element_type=f32)


def loop(count, step, body):
    def run(i, carry):
        body(pl.multiple_of(i * step, step))
        return carry

    lax.fori_loop(0, count, run, 0)


def latent_piece(refs, block, half, group):
    triple, mixing, widen, narrow = refs
    rows = pl.ds(group * 8, 8)
    if block < 3:
        return triple[half, rows, block * D : (block + 1) * D]
    if block == 3:
        return mixing[half, rows, :]
    if block < 8:
        return widen[half, rows, (block - 4) * D : (block - 3) * D]
    return narrow[half, pl.ds((block - 8) * BLOCK + group * 8, 8), :]


def plane_of(block, half, group):
    place = block * 24 + half * 12 + group
    bit = place % 32
    return place // 32, (1 << bit) if bit < 31 else -(1 << 31)


def gather_kernel(
    triple, mixing, widen, narrow, tb, mb, wb, nb, gain, shift,
    words, small, spread, wsend, wrecv, ssend, srecv, cwsend, cwrecv, cssend, csrecv,
):
    dp = lax.axis_index("dp")
    me = lax.axis_index("fsdp")
    z = lax.div(me, 2)
    core = lax.rem(me, 2)
    refs = (triple, mixing, widen, narrow)
    masks = [[] for _ in range(9)]
    for block in range(12):
        for half in range(2):
            for group in range(12):
                word, bit = plane_of(block, half, group)
                masks[word].append((block, half, group, bit))
    for word in range(9):
        total = jnp.zeros((8, D), jnp.int32)
        for block, half, group, bit in masks[word]:
            piece = latent_piece(refs, block, half, group)
            total = total | jnp.where(piece > 0, jnp.int32(bit), jnp.int32(0))
        words[me, word * 8 : (word + 1) * 8, :] = total
    lane = lax.broadcasted_iota(jnp.int32, (8, 128), 1)

    def scale_rows(group, carry):
        tile = jnp.zeros((8, 128), f32)
        rows = pl.ds(pl.multiple_of(group * 8, 8), 8)
        for half in range(2):
            for index in range(7):
                if index == 0:
                    part = triple[half, rows, :]
                elif index == 1:
                    part = mixing[half, rows, :]
                elif index == 2:
                    part = widen[half, rows, :]
                else:
                    part = narrow[
                        half, pl.ds(pl.multiple_of((index - 3) * BLOCK + group * 8, 8), 8), :
                    ]
                fan = FF if index >= 3 else D
                mean = jnp.sum(jnp.abs(part), axis=1, keepdims=True) * (1.0 / part.shape[1])
                tile = jnp.where(lane == index * 2 + half, mean / math.sqrt(fan), tile)
        small[me, rows, :] = tile
        return carry

    lax.fori_loop(0, 12, scale_rows, 0)
    spread[...] = jnp.zeros_like(spread)
    spread[0:3, 0:BLOCK] = tb[...]
    spread[3:4, 0:BLOCK] = mb[...]
    spread[4:5, 0:BLOCK] = nb[...]
    spread[5:7, 0:BLOCK] = gain[...]
    spread[7:9, 0:BLOCK] = shift[...]
    spread[16:17, 0 : 4 * BLOCK] = wb[...]
    placed = pltpu.roll(spread[0:16, :], me * BLOCK, 1)
    wide = pltpu.roll(spread[16:24, :], core * (4 * BLOCK), 1)
    row = lax.broadcasted_iota(jnp.int32, (16, D), 0)
    wide_rows = jnp.broadcast_to(wide[0:1, :], (16, D))
    placed = placed + jnp.where(row == 9 + z, wide_rows, 0.0)
    for part in range(6):
        small[me, 96 + part * 16 : 112 + part * 16, :] = placed[:, part * 128 : (part + 1) * 128]

    def over_z(hop, ref, send, recv):
        peer = lax.rem(z + hop, 4) * 2 + core
        return pltpu.make_async_remote_copy(
            src_ref=ref.at[me], dst_ref=ref.at[me], send_sem=send.at[hop - 1],
            recv_sem=recv.at[hop - 1], device_id=(dp, peer), device_id_type=MESH,
        )

    def over_core(hop, ref, send, recv):
        owner = lax.rem(z + 4 - hop, 4) * 2 + core
        return pltpu.make_async_remote_copy(
            src_ref=ref.at[owner], dst_ref=ref.at[owner], send_sem=send.at[hop],
            recv_sem=recv.at[hop], device_id=(dp, z * 2 + 1 - core), device_id_type=MESH,
        )

    for hop in (1, 2, 3):
        over_z(hop, small, ssend, srecv).start()
    for hop in (1, 2, 3):
        over_z(hop, words, wsend, wrecv).start()
    over_core(0, small, cssend, csrecv).start()
    over_core(0, words, cwsend, cwrecv).start()
    for hop in (1, 2, 3):
        over_z(hop, small, ssend, srecv).wait()
        over_core(hop, small, cssend, csrecv).start()
    for hop in (1, 2, 3):
        over_z(hop, words, wsend, wrecv).wait()
        over_core(hop, words, cwsend, cwrecv).start()
    for hop in range(4):
        over_core(hop, small, cssend, csrecv).wait()
        over_core(hop, words, cwsend, cwrecv).wait()


def gather(triple, mixing, widen, narrow, tb, mb, wb, nb, gain, shift):
    vm = pl.BlockSpec(memory_space=pltpu.VMEM)
    return pl.pallas_call(
        gather_kernel,
        out_shape=(
            jax.ShapeDtypeStruct((8, 72, D), jnp.int32),
            jax.ShapeDtypeStruct((8, 192, 128), f32),
        ),
        in_specs=[vm] * 10,
        out_specs=(vm, vm),
        scratch_shapes=[pltpu.VMEM((24, D), f32)]
        + [pltpu.SemaphoreType.DMA((3,))] * 4
        + [pltpu.SemaphoreType.DMA((4,))] * 4,
        compiler_params=pltpu.CompilerParams(has_side_effects=True, vmem_limit_bytes=VMEM_CAP),
        name="gather_weights",
    )(triple, mixing, widen, narrow, tb, mb, wb, nb, gain, shift)


def unpack_block(words, small, block, dst):
    index = 0 if block < 3 else 1 if block == 3 else 2 if block < 8 else block - 5

    def one(owner, carry):
        for pair in range(6):
            parts = []
            for group in (2 * pair, 2 * pair + 1):
                total = None
                for half in range(2):
                    word, bit = plane_of(block, half, group)
                    bits = words[owner, word * 8 : (word + 1) * 8, :] & jnp.int32(bit)
                    column = index * 2 + half
                    scale = jnp.broadcast_to(
                        small[owner, group * 8 : (group + 1) * 8, column : column + 1], (8, D)
                    )
                    value = jnp.where(bits != 0, scale, -scale)
                    total = value if total is None else total + value
                parts.append(total)
            tile = jnp.concatenate(parts, axis=0).astype(bf16)
            if block < 8:
                start = owner * BLOCK + pair * 16
            else:
                start = owner * (4 * BLOCK) + (block - 8) * BLOCK + pair * 16
            rows = pl.ds(pl.multiple_of(start, 16), 16)
            if block < 3:
                dst[rows, block * D : (block + 1) * D] = tile
            elif block < 8 and block > 3:
                dst[rows, (block - 4) * D : (block - 3) * D] = tile
            else:
                dst[rows, :] = tile
        return carry

    lax.fori_loop(0, 8, one, 0)


def clip_back(grad, value, level, inverse):
    u = value * inverse
    t = jnp.tanh(u)
    slope = 1.0 - t * t
    return grad * slope, jnp.sum(grad * (t - u * slope), axis=0, keepdims=True)


def norm_rows(v):
    center = v - jnp.mean(v, axis=1, keepdims=True)
    variance = jnp.mean(center * center, axis=1, keepdims=True)
    rstd = lax.rsqrt(variance + norm_epsilon)
    return center * rstd, rstd


def norm_rows_back(grad, hat, rstd, gain_row):
    g = grad * gain_row
    return rstd * (
        g - jnp.mean(g, axis=1, keepdims=True) - hat * jnp.mean(g * hat, axis=1, keepdims=True)
    )


def colsum(v):
    return jnp.sum(v, axis=0, keepdims=True)


HALF_ROOT = 1.0 / math.sqrt(2.0)
DENSITY = 1.0 / math.sqrt(2.0 * math.pi)


def layer_kernel(
    seq, live, level, words, small, hid, teach, teach_scores,
    out, input_grad, xlT, clT, wlT, nlT, act, wg, mlow, qg, sums,
    wt, wm, ww, wn, prm, bias, wbias, qkv, low, ctx, hat1, rstd1, widened, acc, gacc, sgrad,
    cgrad, valid, pair,
):
    c0, c1, c2, c3 = level[0], level[1], level[2], level[3]
    i0, i1, i2, i3 = 1.0 / c0, 1.0 / c1, 1.0 / c2, 1.0 / c3
    for part in range(6):
        total = small[0, 96 + part * 16 : 112 + part * 16, :]
        for owner in range(1, 8):
            total = total + small[owner, 96 + part * 16 : 112 + part * 16, :]
        prm[:, part * 128 : (part + 1) * 128] = total
    for part in range(3):
        bias[0:1, part * D : (part + 1) * D] = prm[part : part + 1, :]
    for part in range(4):
        wbias[0:1, part * D : (part + 1) * D] = prm[9 + part : 10 + part, :]
    sums[...] = jnp.zeros_like(sums)
    row = lax.broadcasted_iota(jnp.int32, (256, 256), 0)
    col = lax.broadcasted_iota(jnp.int32, (256, 256), 1)
    key_ok = col < seq[0, 0]
    query_ok = row < seq[0, 0] * live[0, 0]
    valid[0] = jnp.where(key_ok, 1.0, 0.0)
    pair[0] = jnp.where(key_ok & query_ok, 1.0, 0.0)

    def in_slots(at):
        mid = (at < 128) & (at < seq[0, 1])
        one = (at >= 128) & (at < 192) & (at - 128 < seq[0, 2])
        two = (at >= 192) & (at - 192 < seq[0, 3])
        return mid, one, two

    km, ko, kt = in_slots(col)
    qm, qo, qt = in_slots(row)
    key_ok = (km & (row < 128)) | (ko & (row >= 128) & (row < 192)) | (kt & (row >= 192))
    live_mid = row * 0 + live[0, 1] > 0
    live_one = row * 0 + live[0, 2] > 0
    live_two = row * 0 + live[0, 2] > 1
    query_ok = (qm & live_mid) | (qo & live_one) | (qt & live_two)
    valid[1] = jnp.where(key_ok, 1.0, 0.0)
    pair[1] = jnp.where(key_ok & query_ok, 1.0, 0.0)
    ones = jnp.where(query_ok, 1.0, 0.0)

    for block in range(12):
        unpack_block(
            words, small, block, wt if block < 3 else wm if block == 3 else ww if block < 8 else wn
        )

    def clip_in(r):
        x = hid[pl.ds(r, 128), :].astype(f32)
        lo = (c0 * jnp.tanh(x * i0)).astype(bf16)
        low[pl.ds(r, 128), :] = lo
        xlT[:, pl.ds(r, 128)] = lo.T

    loop(4, 128, clip_in)

    def qkv_cols(c):
        cs = pl.ds(c, 256)
        qkv[:, cs] = (dot_nn(low[...], wt[:, cs]) + bias[0:1, cs]).astype(bf16)

    loop(9, 256, qkv_cols)
    lane = lax.broadcasted_iota(jnp.int32, (256, 128), 1)
    first = lane < 64

    def pick(v, j):
        return jnp.where(first, v, jnp.zeros_like(v)) if j == 0 else jnp.where(first, jnp.zeros_like(v), v)

    def softmax(q, k, ok, j):
        s = dot_nt(pick(q, j), k) * (HEAD_DIM**-0.5)
        masked = jnp.where(ok, s, masked_fill)
        e = jnp.exp(masked - jnp.max(masked, axis=1, keepdims=True))
        return s, e / jnp.sum(e, axis=1, keepdims=True)

    def attend_pair(u, carry):
        g = lax.div(u, 6)
        hp = lax.rem(u, 6)
        rs = pl.ds(pl.multiple_of(g * 256, 256), 256)
        qs = pl.multiple_of(hp * 128, 128)
        q = qkv[rs, pl.ds(qs, 128)]
        k = qkv[rs, pl.ds(pl.multiple_of(D + qs, 128), 128)]
        v = qkv[rs, pl.ds(pl.multiple_of(2 * D + qs, 128), 128)]
        ok = valid[g] > 0.5
        parts = []
        for j in range(2):
            s, p = softmax(q, k, ok, j)
            parts.append(dot_nn(p.astype(bf16), v))
        ctx[rs, pl.ds(qs, 128)] = jnp.where(first, parts[0], parts[1])
        return carry

    lax.fori_loop(0, 12, attend_pair, 0)

    def clip_ctx(r):
        lo = (c1 * jnp.tanh(ctx[pl.ds(r, 128), :] * i1)).astype(bf16)
        low[pl.ds(r, 128), :] = lo
        clT[:, pl.ds(r, 128)] = lo.T

    loop(4, 128, clip_ctx)

    def mix_cols(c):
        cs = pl.ds(c, 256)
        acc[:, cs] = dot_nn(low[...], wm[:, cs]) + prm[3:4, cs] + hid[:, cs].astype(f32)

    loop(3, 256, mix_cols)

    def norm_one(r):
        rs = pl.ds(r, 128)
        hat, rstd = norm_rows(acc[rs, :])
        hat1[rs, :] = hat
        rstd1[rs, :] = jnp.broadcast_to(rstd, (128, 128))
        normed = hat * prm[5:6, :] + prm[7:8, :]
        lo = (c2 * jnp.tanh(normed * i2)).astype(bf16)
        low[rs, :] = lo
        wlT[:, rs] = lo.T
        acc[rs, :] = normed + prm[4:5, :]

    loop(4, 128, norm_one)

    def feed(c):
        cs = pl.ds(c, 512)
        w = dot_nn(low[...], ww[:, cs]) + wbias[0:1, cs]
        widened[:, cs] = w
        a = 0.5 * w * (1.0 + lax.erf(w * HALF_ROOT))
        lo = (c3 * jnp.tanh(a * i3)).astype(bf16)
        act[:, cs] = lo
        acc[...] += dot_nn(lo, wn[cs, :])

    loop(6, 512, feed)

    def norm_two(r):
        rs = pl.ds(r, 128)
        hat, rstd = norm_rows(acc[rs, :])
        full = hat * prm[6:7, :] + prm[8:9, :]
        out[rs, :] = full.astype(bf16)
        at = lax.broadcasted_iota(jnp.int32, (128, D), 0) + r
        l0, l1, l2, l3 = seq[0, 0] * live[0, 0], seq[0, 1], seq[0, 2], seq[0, 3]
        l1 = jnp.where(live[0, 1] > 0, l1, 0)
        l2 = jnp.where(live[0, 2] > 0, l2, 0)
        l3 = jnp.where(live[0, 2] > 1, l3, 0)
        ok = (at < l0) | ((at >= 256) & (at < 256 + l1)) | ((at >= 384) & (at < 384 + l2))
        ok = ok | ((at >= 448) & (at < 448 + l3))
        gap = jnp.where(ok, full - teach[rs, :].astype(f32), 0.0)
        sums[15:16, :] += colsum(gap * gap) * 0.5
        sums[6:7, :] += colsum(gap * hat)
        sums[8:9, :] += colsum(gap)
        grad = norm_rows_back(gap, hat, rstd, prm[6:7, :])
        sgrad[rs, :] = grad
        lo = grad.astype(bf16)
        low[rs, :] = lo
        nlT[:, rs] = lo.T
        sums[4:5, :] += colsum(lo.astype(f32))

    loop(4, 128, norm_two)
    gacc[...] = sgrad[...] * 0.0

    def feed_back(t, carry):
        cs = pl.ds(pl.multiple_of(t * 512, 512), 512)
        g = dot_nt(low[...], wn[cs, :])
        w = widened[:, cs]
        e = 0.5 * (1.0 + lax.erf(w * HALF_ROOT))
        a = w * e
        u = a * i3
        th = jnp.tanh(u)
        slope = 1.0 - th * th
        clip_sum = colsum(g * (th - u * slope))
        sums[14:15, 0:512] += clip_sum
        back = g * slope * (e + w * (DENSITY * jnp.exp(-0.5 * w * w)))
        lo = back.astype(bf16)
        wg[:, cs] = lo
        wbias[1:2, cs] = colsum(lo.astype(f32))
        gacc[...] += dot_nt(lo, ww[:, cs])
        return carry

    lax.fori_loop(0, 6, feed_back, 0)
    for part in range(4):
        sums[9 + part : 10 + part, :] = wbias[1:2, part * D : (part + 1) * D]
    def norm_one_back(r):
        rs = pl.ds(r, 128)
        hat = hat1[rs, :]
        normed = hat * prm[5:6, :] + prm[7:8, :]
        grad, clip_sum = clip_back(gacc[rs, :], normed, c2, i2)
        sums[18:19, :] += clip_sum
        grad = grad + sgrad[rs, :]
        sums[5:6, :] += colsum(grad * hat)
        sums[7:8, :] += colsum(grad)
        grad = norm_rows_back(grad, hat, rstd1[rs, 0:1], prm[5:6, :])
        acc[rs, :] = grad
        lo = grad.astype(bf16)
        mlow[rs, :] = lo
        sums[3:4, :] += colsum(lo.astype(f32))

    loop(4, 128, norm_one_back)

    def mix_back(c):
        cs = pl.ds(c, 256)
        g = dot_nt(mlow[...], wm[cs, :])
        grad, clip_sum = clip_back(g, ctx[:, cs], c1, i1)
        sums[17:18, cs] += clip_sum
        cgrad[:, cs] = grad.astype(bf16)

    loop(3, 256, mix_back)

    def attend_pair_back(u, carry):
        g = lax.div(u, 6)
        hp = lax.rem(u, 6)
        rs = pl.ds(pl.multiple_of(g * 256, 256), 256)
        q0 = pl.multiple_of(hp * 128, 128)
        k0 = pl.multiple_of(D + q0, 128)
        v0 = pl.multiple_of(2 * D + q0, 128)
        q = qkv[rs, pl.ds(q0, 128)]
        k = qkv[rs, pl.ds(k0, 128)]
        v = qkv[rs, pl.ds(v0, 128)]
        cg = cgrad[rs, pl.ds(q0, 128)]
        ok = valid[g] > 0.5
        pairs = pair[g] > 0.5
        dq, dk, dv = [], [], []
        for j in range(2):
            s, p = softmax(q, k, ok, j)
            ts = teach_scores[2 * hp + j, rs, :].astype(f32)
            second = pltpu.roll(ts[128:192], 128, 1)
            third = pltpu.roll(ts[192:256], 192, 1)
            moved = jnp.concatenate([ts[0:128], second, third], axis=0)
            ts = jnp.where(g > 0, moved, ts)
            gap = jnp.where(pairs, s - ts, 0.0)
            sums[16:17, 0:256] += colsum(gap * gap) * (0.5 / LONG_LEN)
            pg = dot_nt(pick(cg, j), v)
            sg = p * (pg - jnp.sum(pg * p, axis=1, keepdims=True)) + gap * (1.0 / LONG_LEN)
            sg = sg.astype(bf16)
            dv.append(dot_tn(p.astype(bf16), cg))
            dq.append(dot_nn(sg, k))
            dk.append(dot_tn(sg, q))
        scale = HEAD_DIM**-0.5
        dq = (jnp.where(first, dq[0], dq[1]) * scale).astype(bf16)
        dk = (jnp.where(first, dk[0], dk[1]) * scale).astype(bf16)
        dv = jnp.where(first, dv[0], dv[1]).astype(bf16)
        for index, (grad, at) in enumerate(((dq, q0), (dk, k0), (dv, v0))):
            qg[rs, pl.ds(at, 128)] = grad
            sums[index : index + 1, pl.ds(q0, 128)] += colsum(grad.astype(f32))
        return carry

    lax.fori_loop(0, 12, attend_pair_back, 0)

    def input_back(c):
        cs = pl.ds(c, 256)
        g = dot_nt(qg[...], wt[cs, :])
        grad, clip_sum = clip_back(g, hid[:, cs].astype(f32), c0, i0)
        sums[19:20, cs] += clip_sum
        input_grad[:, cs] = grad + acc[:, cs]

    loop(3, 256, input_back)
    at = lax.broadcasted_iota(jnp.int32, (1, D), 1)
    line = jnp.zeros((1, D), f32)
    for spot, value in enumerate(
        (sums[19:20, :], sums[17:18, :], sums[18:19, :], sums[14:15, :], sums[15:16, :] + sums[16:17, :])
    ):
        line = jnp.where(at == spot, jnp.sum(value), line)
    sums[13:14, :] = line


def layer(seq, live, level, words, small, hid, teach, teach_scores):
    vm = pl.BlockSpec(memory_space=pltpu.VMEM)
    sm = pl.BlockSpec(memory_space=pltpu.SMEM)
    sds = jax.ShapeDtypeStruct
    return pl.pallas_call(
        layer_kernel,
        out_shape=(
            sds((ROWS, D), bf16),
            sds((ROWS, D), f32),
            sds((D, ROWS), bf16),
            sds((D, ROWS), bf16),
            sds((D, ROWS), bf16),
            sds((D, ROWS), bf16),
            sds((ROWS, FF), bf16),
            sds((ROWS, FF), bf16),
            sds((ROWS, D), bf16),
            sds((ROWS, 3 * D), bf16),
            sds((24, D), f32),
        ),
        in_specs=[sm] * 3 + [vm] * 5,
        out_specs=(vm,) * 11,
        scratch_shapes=[
            pltpu.VMEM((D, 3 * D), bf16),
            pltpu.VMEM((D, D), bf16),
            pltpu.VMEM((D, FF), bf16),
            pltpu.VMEM((FF, D), bf16),
            pltpu.VMEM((16, D), f32),
            pltpu.VMEM((8, 3 * D), f32),
            pltpu.VMEM((8, FF), f32),
            pltpu.VMEM((ROWS, 3 * D), bf16),
            pltpu.VMEM((ROWS, D), bf16),
            pltpu.VMEM((ROWS, D), f32),
            pltpu.VMEM((ROWS, D), f32),
            pltpu.VMEM((ROWS, 128), f32),
            pltpu.VMEM((ROWS, FF), f32),
            pltpu.VMEM((ROWS, D), f32),
            pltpu.VMEM((ROWS, D), f32),
            pltpu.VMEM((ROWS, D), f32),
            pltpu.VMEM((ROWS, D), bf16),
            pltpu.VMEM((2, 256, 256), f32),
            pltpu.VMEM((2, 256, 256), f32),
        ],
        compiler_params=pltpu.CompilerParams(vmem_limit_bytes=VMEM_CAP),
        name="layer",
    )(seq, live, level, words, small, hid, teach, teach_scores)


def reduce_kernel(
    nlT, act, wlT, wg, clT, ml, xlT, qg, sums,
    fin, small_out,
    pt, rb, rx, ry, rz, sin,
    s1, r1, s2, r2, s3, r3, s4, r4, s5, r5, s6, r6, sms, smr,
):
    dp = lax.axis_index("dp")
    me = lax.axis_index("fsdp")
    x = lax.rem(dp, 2)
    y = lax.div(dp, 2)
    z = lax.div(me, 2)
    core = lax.rem(me, 2)
    flip_x = dp + 1 - 2 * x
    flip_y = dp + 2 - 4 * y

    def turns(k):
        odd = lax.rem(k, 2)
        one = flip_x * (1 - odd) + flip_y * odd
        two = flip_y * (1 - odd) + flip_x * odd
        a = x * (1 - odd) + y * odd
        b = y * (1 - odd) + x * odd
        return one, two, a, b

    def rows_at(start, count):
        return pl.ds(pl.multiple_of(start, 8), count)

    def core_copy(k):
        slot = lax.rem(k, SLOTS)
        return pltpu.make_async_remote_copy(
            src_ref=pt.at[slot, :, 1 - core], dst_ref=rb.at[slot], send_sem=s1.at[slot],
            recv_sem=r1.at[slot], device_id=(dp, z * 2 + 1 - core), device_id_type=MESH,
        )

    def one_copy(k):
        slot = lax.rem(k, SLOTS)
        one, two, a, b = turns(k)
        return pltpu.make_async_remote_copy(
            src_ref=pt.at[slot, :, core, rows_at((1 - a) * 48, 48)], dst_ref=rx.at[slot],
            send_sem=s2.at[slot], recv_sem=r2.at[slot], device_id=(one, me), device_id_type=MESH,
        )

    def two_copy(k):
        slot = lax.rem(k, SLOTS)
        one, two, a, b = turns(k)
        return pltpu.make_async_remote_copy(
            src_ref=pt.at[slot, :, core, rows_at(a * 48 + (1 - b) * 24, 24)], dst_ref=ry.at[slot],
            send_sem=s3.at[slot], recv_sem=r3.at[slot], device_id=(two, me), device_id_type=MESH,
        )

    def z_copy(k, hop):
        slot = lax.rem(k, SLOTS)
        one, two, a, b = turns(k)
        to = lax.rem(z + hop, 4)
        return pltpu.make_async_remote_copy(
            src_ref=pt.at[slot, to, core, rows_at(a * 48 + b * 24, 24)],
            dst_ref=rz.at[slot, hop - 1], send_sem=s4.at[slot, hop - 1],
            recv_sem=r4.at[slot, hop - 1], device_id=(dp, to * 2 + core), device_id_type=MESH,
        )

    def fin_rows(k, start, count):
        section = lax.div(k, 6)
        return fin.at[
            section, rows_at(start, count),
            pl.ds(pl.multiple_of(lax.rem(k, 6) * CHUNK, CHUNK), CHUNK),
        ]

    def back_two(k):
        slot = lax.rem(k, SLOTS)
        one, two, a, b = turns(k)
        ref = fin_rows(k, a * 48 + b * 24, 24)
        return pltpu.make_async_remote_copy(
            src_ref=ref, dst_ref=ref, send_sem=s5.at[slot], recv_sem=r5.at[slot],
            device_id=(two, me), device_id_type=MESH,
        )

    def back_one(k):
        slot = lax.rem(k, SLOTS)
        one, two, a, b = turns(k)
        ref = fin_rows(k, a * 48, 48)
        return pltpu.make_async_remote_copy(
            src_ref=ref, dst_ref=ref, send_sem=s6.at[slot], recv_sem=r6.at[slot],
            device_id=(one, me), device_id_type=MESH,
        )

    def small_copy(step):
        to = (
            (dp, z * 2 + 1 - core), (flip_x, me), (flip_y, me),
            (dp, lax.rem(z + 1, 4) * 2 + core), (dp, lax.rem(z + 2, 4) * 2 + core),
            (dp, lax.rem(z + 3, 4) * 2 + core),
        )[step]
        return pltpu.make_async_remote_copy(
            src_ref=small_out, dst_ref=sin.at[step], send_sem=sms.at[step],
            recv_sem=smr.at[step], device_id=to, device_id_type=MESH,
        )

    small_out[...] = sums[0:16, :]

    def tick(t, carry):
        @pl.when(t >= 6)
        def _():
            back_one(t - 6).wait()

        @pl.when((t >= 5) & (t < 5 + CHUNKS))
        def _():
            back_two(t - 5).wait()
            back_one(t - 5).start()

        @pl.when((t >= 4) & (t < 4 + CHUNKS))
        def _():
            k = t - 4
            slot = lax.rem(k, SLOTS)
            one, two, a, b = turns(k)
            for hop in (1, 2, 3):
                z_copy(k, hop).wait()
            total = pt[slot, z, core, rows_at(a * 48 + b * 24, 24), :]
            total = total + rz[slot, 0] + rz[slot, 1] + rz[slot, 2]
            fin[
                lax.div(k, 6), rows_at(a * 48 + b * 24, 24),
                pl.ds(pl.multiple_of(lax.rem(k, 6) * CHUNK, CHUNK), CHUNK),
            ] = total
            back_two(k).start()

        @pl.when((t >= 3) & (t < 3 + CHUNKS))
        def _():
            k = t - 3
            slot = lax.rem(k, SLOTS)
            one, two, a, b = turns(k)
            two_copy(k).wait()
            for q in range(4):
                pt[slot, q, core, rows_at(a * 48 + b * 24, 24), :] += ry[slot, q]
            for hop in (1, 2, 3):
                z_copy(k, hop).start()

        @pl.when((t >= 2) & (t < 2 + CHUNKS))
        def _():
            k = t - 2
            slot = lax.rem(k, SLOTS)
            one, two, a, b = turns(k)
            one_copy(k).wait()
            for q in range(4):
                pt[slot, q, core, rows_at(a * 48, 48), :] += rx[slot, q]
            two_copy(k).start()

        @pl.when((t >= 1) & (t < 1 + CHUNKS))
        def _():
            k = t - 1
            slot = lax.rem(k, SLOTS)
            core_copy(k).wait()
            for q in range(4):
                pt[slot, q, core] += rb[slot, q]
            one_copy(k).start()

        slot = lax.rem(t, SLOTS)

        @pl.when(t < 6)
        def _():
            j = lax.div(t, 2)
            rows = pl.ds(pl.multiple_of(lax.rem(t, 2) * 384, 384), 384)
            left = nlT[rows, :]
            for owner in range(8):
                cols = pl.ds(pl.multiple_of(owner * 384 + j * 128, 128), 128)
                got = dot_nn(left, act[:, cols])
                for part in range(4):
                    pt[slot, owner // 2, owner % 2, :, part * 128 : (part + 1) * 128] = got[
                        part * BLOCK : (part + 1) * BLOCK, :
                    ]

        def whole(left, right, half):
            got = dot_nn(left, right)
            for owner in range(8):
                pt[slot, owner // 2, owner % 2, :, half * 256 : (half + 1) * 256] = got[
                    owner * BLOCK : (owner + 1) * BLOCK, :
                ]

        @pl.when((t >= 6) & (t < 12))
        def _():
            for half in range(2):
                cols = pl.ds(pl.multiple_of((t - 6) * CHUNK + half * 256, 256), 256)
                whole(wlT[...], wg[:, cols], half)

        for half in range(2):
            part = (t - 12) * 2 + half

            @pl.when((part >= 0) & (part < 3))
            def _():
                cols = pl.ds(pl.multiple_of(part * 256, 256), 256)
                whole(clT[...], ml[:, cols], half)

            @pl.when((part >= 3) & (part < 12))
            def _():
                cols = pl.ds(pl.multiple_of((part - 3) * 256, 256), 256)
                whole(xlT[...], qg[:, cols], half)

        @pl.when(t < CHUNKS)
        def _():
            core_copy(t).start()

        @pl.when(t == 8)
        def _():
            small_copy(0).start()

        @pl.when(t == 10)
        def _():
            small_copy(0).wait()
            small_out[...] += sin[0]
            small_copy(1).start()

        @pl.when(t == 12)
        def _():
            small_copy(1).wait()
            small_out[...] += sin[1]
            small_copy(2).start()

        @pl.when(t == 14)
        def _():
            small_copy(2).wait()
            small_out[...] += sin[2]
            for step in (3, 4, 5):
                small_copy(step).start()

        @pl.when(t == 16)
        def _():
            for step in (3, 4, 5):
                small_copy(step).wait()
            small_out[...] = small_out[...] + sin[3] + sin[4] + sin[5]

        return carry

    lax.fori_loop(0, CHUNKS + 6, tick, 0)


def reduce_grads(nlT, act, wlT, wg, clT, ml, xlT, qg, sums):
    vm = pl.BlockSpec(memory_space=pltpu.VMEM)
    sds = jax.ShapeDtypeStruct
    dma = pltpu.SemaphoreType.DMA
    return pl.pallas_call(
        reduce_kernel,
        out_shape=(sds((3, BLOCK, FF), f32), sds((16, D), f32)),
        in_specs=[vm] * 9,
        out_specs=(vm, vm),
        scratch_shapes=[
            pltpu.VMEM((SLOTS, 4, 2, BLOCK, CHUNK), f32),
            pltpu.VMEM((SLOTS, 4, BLOCK, CHUNK), f32),
            pltpu.VMEM((SLOTS, 4, 48, CHUNK), f32),
            pltpu.VMEM((SLOTS, 4, 24, CHUNK), f32),
            pltpu.VMEM((SLOTS, 3, 24, CHUNK), f32),
            pltpu.VMEM((6, 16, D), f32),
        ]
        + [dma((SLOTS,))] * 6
        + [dma((SLOTS, 3))] * 2
        + [dma((SLOTS,))] * 4
        + [dma((6,))] * 2,
        compiler_params=pltpu.CompilerParams(has_side_effects=True, vmem_limit_bytes=VMEM_CAP),
        name="reduce_grads",
    )(nlT, act, wlT, wg, clT, ml, xlT, qg, sums)


def on_device_fast(
    hidden_in, teacher_hidden, teacher_scores, seq_lengths, live_counts, triple_latent,
    mixing_latent, widen_latent, narrow_latent, triple_bias, mixing_bias, widen_bias, narrow_bias,
    norm_gain, norm_shift, clip_level,
):
    words, small = gather(
        triple_latent, mixing_latent, widen_latent, narrow_latent, triple_bias,
        mixing_bias[None], widen_bias[None], narrow_bias[None], norm_gain, norm_shift,
    )
    teach_scores = jnp.transpose(teacher_scores, (1, 0, 2))
    out, input_grad, xlT, clT, wlT, nlT, act, wg, ml, qg, sums = layer(
        seq_lengths, live_counts, clip_level, words, small, hidden_in, teacher_hidden, teach_scores
    )
    fin, small_sum = reduce_grads(nlT, act, wlT, wg, clT, ml, xlT, qg, sums)
    narrow_sum = (
        fin[0].reshape(BLOCK, 3, 2, 4, 128).transpose(1, 4, 2, 3, 0).reshape(4 * BLOCK, D)
    )
    totals = (fin[2][:, D:], fin[2][:, :D], fin[1], narrow_sum)
    latents = (triple_latent, mixing_latent, widen_latent, narrow_latent)
    latent_grads = tuple(
        (
            jnp.where(jnp.abs(latent) <= 1.0, (total / math.sqrt(fan_in))[None], 0.0)
            for latent, total, fan_in in zip(latents, totals, (D, D, D, FF))
        )
    )
    me = lax.axis_index("fsdp")
    own = lax.dynamic_slice_in_dim(small_sum[0:9], me * BLOCK, BLOCK, 1)
    wide = lax.dynamic_slice_in_dim(small_sum[9:13].reshape(FF), me * 4 * BLOCK, 4 * BLOCK, 0)
    tokens = hidden_in.shape[0] * lax.axis_size("dp") * lax.axis_size("fsdp")
    return (
        out,
        small_sum[13, 4] / (tokens * D),
        input_grad,
        latent_grads[0],
        latent_grads[1],
        latent_grads[2],
        latent_grads[3],
        own[0:3],
        own[3],
        wide,
        own[4],
        own[5:7],
        own[7:9],
        small_sum[13, 0:4],
    )


def solution(mesh):
    in_specs = (
        P(("dp", "fsdp"), None),
        P(("dp", "fsdp"), None),
        P(("dp", "fsdp"), None, None),
        P(("dp", "fsdp"), None),
        P(("dp", "fsdp"), None),
        P(None, "fsdp", None),
        P(None, "fsdp", None),
        P(None, "fsdp", None),
        P(None, "fsdp", None),
        P(None, "fsdp"),
        P("fsdp"),
        P("fsdp"),
        P("fsdp"),
        P(None, "fsdp"),
        P(None, "fsdp"),
        P(),
    )
    out_specs = (
        P(("dp", "fsdp"), None),
        P(),
        P(("dp", "fsdp"), None),
        P(None, "fsdp", None),
        P(None, "fsdp", None),
        P(None, "fsdp", None),
        P(None, "fsdp", None),
        P(None, "fsdp"),
        P("fsdp"),
        P("fsdp"),
        P("fsdp"),
        P(None, "fsdp"),
        P(None, "fsdp"),
        P(),
    )
    fits = mesh.shape["dp"] == 4 and mesh.shape["fsdp"] == 8
    return jax.shard_map(
        on_device_fast if fits else on_device, mesh=mesh, in_specs=in_specs, out_specs=out_specs, check_vma=False
    )
```

```python
import math

import jax
import jax.numpy as jnp
from jax import lax
from jax.experimental import pallas as pl
from jax.experimental.pallas import tpu as pltpu
from jax.sharding import PartitionSpec as P

D = 768
HEADS = 12
HEAD_DIM = 64
FF = 3072
LONG_LEN = 256
MID_LEN = 128
SHORT_LEN = 64
LONG_SLOTS = 1
MID_SLOTS = 1
SHORT_SLOTS = 2


bit_count = 32
norm_epsilon = 1e-12
masked_fill = -1e30


def soft_clip(values, clip_at):
    return clip_at * jnp.tanh(values / clip_at)


def layer_norm(values, gain_row, shift_row):
    center = values - jnp.mean(values, axis=-1, keepdims=True)
    variance = jnp.mean(center * center, axis=-1, keepdims=True)
    return center * lax.rsqrt(variance + norm_epsilon) * gain_row + shift_row


def gelu_exact(values):
    return 0.5 * values * (1.0 + lax.erf(values * (1.0 / math.sqrt(2.0))))


def pack_signs(latent):
    halves, row_count, columns = latent.shape
    sign_bits = (
        (latent > 0).astype(jnp.int32).reshape(halves, row_count, columns // bit_count, bit_count)
    )
    places = jnp.arange(bit_count, dtype=jnp.int32)
    return jnp.sum(jnp.left_shift(sign_bits, places), axis=-1, dtype=jnp.int32)


def unpack_weight(sign_words, scales):
    halves, row_count, word_count = sign_words.shape
    places = jnp.arange(bit_count, dtype=jnp.int32)
    sign_bits = jnp.bitwise_and(jnp.right_shift(sign_words[..., None], places), 1)
    sign_values = (
        (2 * sign_bits - 1).astype(jnp.float32).reshape(halves, row_count, word_count * bit_count)
    )
    return (scales[0][:, None] * sign_values[0] + scales[1][:, None] * sign_values[1]).astype(
        jnp.bfloat16
    )


def bucket_shapes():
    return ((LONG_SLOTS, LONG_LEN), (MID_SLOTS, MID_LEN), (SHORT_SLOTS, SHORT_LEN))


def bucket_masks(lengths, live_count, slot_count, bucket_len):
    places = jnp.arange(bucket_len, dtype=jnp.int32)
    key_ok = places[None, :] < lengths[:, None]
    query_ok = jnp.logical_and(
        key_ok, jnp.arange(slot_count, dtype=jnp.int32)[:, None] < live_count
    )
    return (key_ok, query_ok)


def split_heads(block, slot_count, bucket_len):
    return block.reshape(slot_count, bucket_len, HEADS, HEAD_DIM)


def bucket_scores(qkv_rows, teacher_rows, key_ok, query_ok, slot_count, bucket_len):
    queries = split_heads(qkv_rows[:, :D], slot_count, bucket_len)
    keys_part = split_heads(qkv_rows[:, D : 2 * D], slot_count, bucket_len)
    scores = jnp.einsum(
        "sqhd,skhd->shqk", queries, keys_part, preferred_element_type=jnp.float32
    ) * HEAD_DIM ** (-0.5)
    masked = jnp.where(key_ok[:, None, None, :], scores, masked_fill)
    teacher = jnp.transpose(
        teacher_rows.reshape(slot_count, bucket_len, HEADS, LONG_LEN)[..., :bucket_len],
        (0, 2, 1, 3),
    ).astype(jnp.float32)
    pair_ok = jnp.logical_and(query_ok[:, None, :, None], key_ok[:, None, None, :])
    score_gap = jnp.where(pair_ok, scores - teacher, 0.0)
    return (queries, keys_part, masked, score_gap)


def attend(qkv_rows, teacher_rows, key_ok, query_ok, slot_count, bucket_len):
    queries, keys_part, masked, score_gap = bucket_scores(
        qkv_rows, teacher_rows, key_ok, query_ok, slot_count, bucket_len
    )
    values_part = split_heads(qkv_rows[:, 2 * D :], slot_count, bucket_len)
    row_top = jnp.max(masked, axis=-1, keepdims=True)
    exponent = jnp.exp(masked - row_top)
    exp_total = jnp.sum(exponent, axis=-1, keepdims=True)
    attention = exponent / exp_total
    context = jnp.einsum(
        "shqk,skhd->sqhd",
        attention.astype(jnp.bfloat16),
        values_part,
        preferred_element_type=jnp.float32,
    )
    distill = 0.5 / LONG_LEN * jnp.sum(score_gap * score_gap)
    return (context.reshape(slot_count * bucket_len, D), row_top + jnp.log(exp_total), distill)


def attend_back(
    qkv_rows, teacher_rows, key_ok, query_ok, slot_count, bucket_len, log_total, context_grad
):
    queries, keys_part, masked, score_gap = bucket_scores(
        qkv_rows, teacher_rows, key_ok, query_ok, slot_count, bucket_len
    )
    values_part = split_heads(qkv_rows[:, 2 * D :], slot_count, bucket_len)
    attention = jnp.exp(masked - log_total)
    grad_heads = split_heads(context_grad, slot_count, bucket_len)
    values_grad = jnp.einsum(
        "shqk,sqhd->skhd",
        attention.astype(jnp.bfloat16),
        grad_heads,
        preferred_element_type=jnp.float32,
    )
    weight_grad = jnp.einsum(
        "sqhd,skhd->shqk", grad_heads, values_part, preferred_element_type=jnp.float32
    )
    score_grad = attention * (
        weight_grad - jnp.sum(weight_grad * attention, axis=-1, keepdims=True)
    ) + score_gap * (1.0 / LONG_LEN)
    score_low = score_grad.astype(jnp.bfloat16)
    score_scale = HEAD_DIM ** (-0.5)
    queries_grad = (
        jnp.einsum("shqk,skhd->sqhd", score_low, keys_part, preferred_element_type=jnp.float32)
        * score_scale
    )
    keys_grad = (
        jnp.einsum("shqk,sqhd->skhd", score_low, queries, preferred_element_type=jnp.float32)
        * score_scale
    )
    row_count = slot_count * bucket_len
    return jnp.concatenate(
        [
            queries_grad.reshape(row_count, D),
            keys_grad.reshape(row_count, D),
            values_grad.reshape(row_count, D),
        ],
        axis=-1,
    )


def on_device(
    hidden_in,
    teacher_hidden,
    teacher_scores,
    seq_lengths,
    live_counts,
    triple_latent,
    mixing_latent,
    widen_latent,
    narrow_latent,
    triple_bias,
    mixing_bias,
    widen_bias,
    narrow_bias,
    norm_gain,
    norm_shift,
    clip_level,
):
    latents = (triple_latent, mixing_latent, widen_latent, narrow_latent)
    fan_ins = (D, D, D, FF)
    own_scales = tuple(
        (
            jnp.mean(jnp.abs(latent), axis=-1) / math.sqrt(fan_in)
            for latent, fan_in in zip(latents, fan_ins)
        )
    )
    packed = tuple((pack_signs(latent) for latent in latents))
    gathered = (
        lax.all_gather(packed[0], "fsdp", axis=1, tiled=True),
        lax.all_gather(packed[1], "fsdp", axis=1, tiled=True),
        lax.all_gather(packed[2], "fsdp", axis=1, tiled=True),
        lax.all_gather(packed[3], "fsdp", axis=1, tiled=True),
    )
    factors = (
        lax.all_gather(own_scales[0], "fsdp", axis=1, tiled=True),
        lax.all_gather(own_scales[1], "fsdp", axis=1, tiled=True),
        lax.all_gather(own_scales[2], "fsdp", axis=1, tiled=True),
        lax.all_gather(own_scales[3], "fsdp", axis=1, tiled=True),
        lax.all_gather(triple_bias, "fsdp", axis=1, tiled=True),
        lax.all_gather(mixing_bias, "fsdp", axis=0, tiled=True),
        lax.all_gather(widen_bias, "fsdp", axis=0, tiled=True),
        lax.all_gather(narrow_bias, "fsdp", axis=0, tiled=True),
        lax.all_gather(norm_gain, "fsdp", axis=1, tiled=True),
        lax.all_gather(norm_shift, "fsdp", axis=1, tiled=True),
    )
    scales = factors[:4]
    triple_rows, full_mixing_bias, full_widen_bias, full_narrow_bias, gains, shifts = factors[4:]
    full_triple_bias = triple_rows.reshape(3 * D)
    weights = tuple(
        (unpack_weight(words_part, scale_part) for words_part, scale_part in zip(gathered, scales))
    )
    inputs = hidden_in.astype(jnp.float32)
    inputs_low = soft_clip(inputs, clip_level[0]).astype(jnp.bfloat16)
    qkv_all = (
        jnp.dot(inputs_low, weights[0], preferred_element_type=jnp.float32) + full_triple_bias
    ).astype(jnp.bfloat16)
    lengths = seq_lengths[0]
    counts = live_counts[0]
    plans = []
    row_start = 0
    slot_start = 0
    for bucket, shape_pair in enumerate(bucket_shapes()):
        slot_count, bucket_len = shape_pair
        key_ok, query_ok = bucket_masks(
            lengths[slot_start : slot_start + slot_count], counts[bucket], slot_count, bucket_len
        )
        plans.append(
            (
                row_start,
                row_start + slot_count * bucket_len,
                slot_count,
                bucket_len,
                key_ok,
                query_ok,
            )
        )
        row_start = row_start + slot_count * bucket_len
        slot_start = slot_start + slot_count
    contexts = []
    log_totals = []
    distill_sum = 0.0
    for plan in plans:
        row_begin, row_end, slot_count, bucket_len, key_ok, query_ok = plan
        context, log_total, distill = attend(
            qkv_all[row_begin:row_end],
            teacher_scores[row_begin:row_end],
            key_ok,
            query_ok,
            slot_count,
            bucket_len,
        )
        contexts.append(context)
        log_totals.append(log_total)
        distill_sum = distill_sum + distill
    context = jnp.concatenate(contexts, axis=0)
    token_ok = jnp.concatenate([plan[5].reshape(-1) for plan in plans])
    context_low = soft_clip(context, clip_level[1]).astype(jnp.bfloat16)
    mixed = jnp.dot(context_low, weights[1], preferred_element_type=jnp.float32) + full_mixing_bias
    first_sum = inputs + mixed
    first_norm = layer_norm(first_sum, gains[0], shifts[0])
    widen_low = soft_clip(first_norm, clip_level[2]).astype(jnp.bfloat16)
    widened = jnp.dot(widen_low, weights[2], preferred_element_type=jnp.float32) + full_widen_bias
    activated = gelu_exact(widened)
    activated_low = soft_clip(activated, clip_level[3]).astype(jnp.bfloat16)
    narrowed = (
        jnp.dot(activated_low, weights[3], preferred_element_type=jnp.float32) + full_narrow_bias
    )
    second_sum = first_norm + narrowed
    out_full = layer_norm(second_sum, gains[1], shifts[1])
    out_gap = jnp.where(token_ok[:, None], out_full - teacher_hidden.astype(jnp.float32), 0.0)
    loss_local = 0.5 * jnp.sum(out_gap * out_gap) + distill_sum
    regathered = (
        lax.all_gather(packed[0], "fsdp", axis=1, tiled=True),
        lax.all_gather(packed[1], "fsdp", axis=1, tiled=True),
        lax.all_gather(packed[2], "fsdp", axis=1, tiled=True),
        lax.all_gather(packed[3], "fsdp", axis=1, tiled=True),
    )
    back_weights = tuple(
        (
            unpack_weight(words_part, scale_part)
            for words_part, scale_part in zip(regathered, scales)
        )
    )
    _, second_back = jax.vjp(layer_norm, second_sum, gains[1], shifts[1])
    second_grad, gain_two, shift_two = second_back(out_gap)
    narrow_low = second_grad.astype(jnp.bfloat16)
    narrow_weight_grad = jnp.einsum(
        "rf,rd->fd", activated_low, narrow_low, preferred_element_type=jnp.float32
    )
    act_low_grad = jnp.einsum(
        "rd,fd->rf", narrow_low, back_weights[3], preferred_element_type=jnp.float32
    )
    _, clip_three_back = jax.vjp(soft_clip, activated, clip_level[3])
    act_grad, clip_three = clip_three_back(act_low_grad)
    _, gelu_back = jax.vjp(gelu_exact, widened)
    (widened_grad,) = gelu_back(act_grad)
    widen_grad_low = widened_grad.astype(jnp.bfloat16)
    widen_weight_grad = jnp.einsum(
        "rd,rf->df", widen_low, widen_grad_low, preferred_element_type=jnp.float32
    )
    norm_low_grad = jnp.einsum(
        "rf,df->rd", widen_grad_low, back_weights[2], preferred_element_type=jnp.float32
    )
    _, clip_two_back = jax.vjp(soft_clip, first_norm, clip_level[2])
    norm_grad, clip_two = clip_two_back(norm_low_grad)
    norm_grad = norm_grad + second_grad
    _, first_back = jax.vjp(layer_norm, first_sum, gains[0], shifts[0])
    first_grad, gain_one, shift_one = first_back(norm_grad)
    mixed_low = first_grad.astype(jnp.bfloat16)
    mixing_weight_grad = jnp.einsum(
        "rc,rd->cd", context_low, mixed_low, preferred_element_type=jnp.float32
    )
    context_low_grad = jnp.einsum(
        "rd,cd->rc", mixed_low, back_weights[1], preferred_element_type=jnp.float32
    )
    _, clip_one_back = jax.vjp(soft_clip, context, clip_level[1])
    context_grad, clip_one = clip_one_back(context_low_grad)
    context_grad_low = context_grad.astype(jnp.bfloat16)
    qkv_grads = []
    for plan, log_total in zip(plans, log_totals):
        row_begin, row_end, slot_count, bucket_len, key_ok, query_ok = plan
        qkv_grads.append(
            attend_back(
                qkv_all[row_begin:row_end],
                teacher_scores[row_begin:row_end],
                key_ok,
                query_ok,
                slot_count,
                bucket_len,
                log_total,
                context_grad_low[row_begin:row_end],
            )
        )
    qkv_grad_low = jnp.concatenate(qkv_grads, axis=0).astype(jnp.bfloat16)
    triple_weight_grad = jnp.einsum(
        "rd,re->de", inputs_low, qkv_grad_low, preferred_element_type=jnp.float32
    )
    input_low_grad = jnp.einsum(
        "re,de->rd", qkv_grad_low, back_weights[0], preferred_element_type=jnp.float32
    )
    _, clip_zero_back = jax.vjp(soft_clip, inputs, clip_level[0])
    input_side, clip_zero = clip_zero_back(input_low_grad)
    input_grad = input_side + first_grad
    bias_sums = (
        jnp.sum(qkv_grad_low, axis=0, dtype=jnp.float32).reshape(3, D),
        jnp.sum(mixed_low, axis=0, dtype=jnp.float32),
        jnp.sum(widen_grad_low, axis=0, dtype=jnp.float32),
        jnp.sum(narrow_low, axis=0, dtype=jnp.float32),
    )
    row_shares = (
        lax.psum_scatter(triple_weight_grad, "fsdp", scatter_dimension=0, tiled=True),
        lax.psum_scatter(mixing_weight_grad, "fsdp", scatter_dimension=0, tiled=True),
        lax.psum_scatter(widen_weight_grad, "fsdp", scatter_dimension=0, tiled=True),
        lax.psum_scatter(narrow_weight_grad, "fsdp", scatter_dimension=0, tiled=True),
    )
    totals = lax.psum((row_shares[0], row_shares[1], row_shares[2], row_shares[3]), "dp")
    small_sums = lax.psum(
        (
            bias_sums[0],
            bias_sums[1],
            bias_sums[2],
            bias_sums[3],
            jnp.stack([gain_one, gain_two]),
            jnp.stack([shift_one, shift_two]),
            jnp.stack([clip_zero, clip_one, clip_two, clip_three]),
            loss_local,
        ),
        ("dp", "fsdp"),
    )
    shard_index = lax.axis_index("fsdp")
    shard_parts = lax.axis_size("fsdp")

    def own_part(vector, along):
        share_width = vector.shape[along] // shard_parts
        return lax.dynamic_slice_in_dim(vector, shard_index * share_width, share_width, along)

    latent_grads = tuple(
        (
            jnp.where(jnp.abs(latent) <= 1.0, (total / math.sqrt(fan_in))[None], 0.0)
            for latent, total, fan_in in zip(latents, totals, fan_ins)
        )
    )
    loss = small_sums[7] / (hidden_in.shape[0] * D * lax.axis_size("dp") * shard_parts)
    return (
        out_full.astype(jnp.bfloat16),
        loss,
        input_grad,
        latent_grads[0],
        latent_grads[1],
        latent_grads[2],
        latent_grads[3],
        own_part(small_sums[0], 1),
        own_part(small_sums[1], 0),
        own_part(small_sums[2], 0),
        own_part(small_sums[3], 0),
        own_part(small_sums[4], 1),
        own_part(small_sums[5], 1),
        small_sums[6],
    )


bf16 = jnp.bfloat16
f32 = jnp.float32
MESH = pl.DeviceIdType.MESH
VMEM_CAP = 60 * 1024 * 1024
LAYER_CAP = 63 * 1024 * 1024
ROWS = LONG_SLOTS * LONG_LEN + MID_SLOTS * MID_LEN + SHORT_SLOTS * SHORT_LEN
BLOCK = 96
CHUNK = 512
CHUNKS = 18
SLOTS = 4


def dot_nn(a, b):
    return lax.dot_general(a, b, (((1,), (0,)), ((), ())), preferred_element_type=f32)


def dot_nt(a, b):
    return lax.dot_general(a, b, (((1,), (1,)), ((), ())), preferred_element_type=f32)


def dot_tn(a, b):
    return lax.dot_general(a, b, (((0,), (0,)), ((), ())), preferred_element_type=f32)


def loop(count, step, body):
    def run(i, carry):
        body(pl.multiple_of(i * step, step))
        return carry

    lax.fori_loop(0, count, run, 0)


def latent_piece(refs, block, half, group):
    triple, mixing, widen, narrow = refs
    rows = pl.ds(group * 8, 8)
    if block < 3:
        return triple[half, rows, block * D : (block + 1) * D]
    if block == 3:
        return mixing[half, rows, :]
    if block < 8:
        return widen[half, rows, (block - 4) * D : (block - 3) * D]
    return narrow[half, pl.ds((block - 8) * BLOCK + group * 8, 8), :]


def plane_of(block, half, group):
    place = block * 24 + half * 12 + group
    bit = place % 32
    return place // 32, (1 << bit) if bit < 31 else -(1 << 31)


def gather_kernel(
    triple, mixing, widen, narrow, tb, mb, wb, nb, gain, shift,
    words, small, spread, wsend, wrecv, ssend, srecv, cwsend, cwrecv, cssend, csrecv,
):
    dp = lax.axis_index("dp")
    me = lax.axis_index("fsdp")
    z = lax.div(me, 2)
    core = lax.rem(me, 2)
    refs = (triple, mixing, widen, narrow)
    masks = [[] for _ in range(9)]
    for block in range(12):
        for half in range(2):
            for group in range(12):
                word, bit = plane_of(block, half, group)
                masks[word].append((block, half, group, bit))
    for word in range(9):
        total = jnp.zeros((8, D), jnp.int32)
        for block, half, group, bit in masks[word]:
            piece = latent_piece(refs, block, half, group)
            total = total | jnp.where(piece > 0, jnp.int32(bit), jnp.int32(0))
        words[me, word * 8 : (word + 1) * 8, :] = total
    lane = lax.broadcasted_iota(jnp.int32, (8, 128), 1)

    def scale_rows(group, carry):
        tile = jnp.zeros((8, 128), f32)
        rows = pl.ds(pl.multiple_of(group * 8, 8), 8)
        for half in range(2):
            for index in range(7):
                if index == 0:
                    part = triple[half, rows, :]
                elif index == 1:
                    part = mixing[half, rows, :]
                elif index == 2:
                    part = widen[half, rows, :]
                else:
                    part = narrow[
                        half, pl.ds(pl.multiple_of((index - 3) * BLOCK + group * 8, 8), 8), :
                    ]
                fan = FF if index >= 3 else D
                mean = jnp.sum(jnp.abs(part), axis=1, keepdims=True) * (1.0 / part.shape[1])
                tile = jnp.where(lane == index * 2 + half, mean / math.sqrt(fan), tile)
        small[me, rows, :] = tile
        return carry

    lax.fori_loop(0, 12, scale_rows, 0)
    spread[...] = jnp.zeros_like(spread)
    spread[0:3, 0:BLOCK] = tb[...]
    spread[3:4, 0:BLOCK] = mb[...]
    spread[4:5, 0:BLOCK] = nb[...]
    spread[5:7, 0:BLOCK] = gain[...]
    spread[7:9, 0:BLOCK] = shift[...]
    spread[16:17, 0 : 4 * BLOCK] = wb[...]
    placed = pltpu.roll(spread[0:16, :], me * BLOCK, 1)
    wide = pltpu.roll(spread[16:24, :], core * (4 * BLOCK), 1)
    row = lax.broadcasted_iota(jnp.int32, (16, D), 0)
    wide_rows = jnp.broadcast_to(wide[0:1, :], (16, D))
    placed = placed + jnp.where(row == 9 + z, wide_rows, 0.0)
    for part in range(6):
        small[me, 96 + part * 16 : 112 + part * 16, :] = placed[:, part * 128 : (part + 1) * 128]

    def over_z(hop, ref, send, recv):
        peer = lax.rem(z + hop, 4) * 2 + core
        return pltpu.make_async_remote_copy(
            src_ref=ref.at[me], dst_ref=ref.at[me], send_sem=send.at[hop - 1],
            recv_sem=recv.at[hop - 1], device_id=(dp, peer), device_id_type=MESH,
        )

    def over_core(hop, ref, send, recv):
        owner = lax.rem(z + 4 - hop, 4) * 2 + core
        return pltpu.make_async_remote_copy(
            src_ref=ref.at[owner], dst_ref=ref.at[owner], send_sem=send.at[hop],
            recv_sem=recv.at[hop], device_id=(dp, z * 2 + 1 - core), device_id_type=MESH,
        )

    for hop in (1, 2, 3):
        over_z(hop, small, ssend, srecv).start()
    for hop in (1, 2, 3):
        over_z(hop, words, wsend, wrecv).start()
    over_core(0, small, cssend, csrecv).start()
    over_core(0, words, cwsend, cwrecv).start()
    for hop in (1, 2, 3):
        over_z(hop, small, ssend, srecv).wait()
        over_core(hop, small, cssend, csrecv).start()
    for hop in (1, 2, 3):
        over_z(hop, words, wsend, wrecv).wait()
        over_core(hop, words, cwsend, cwrecv).start()
    for hop in range(4):
        over_core(hop, small, cssend, csrecv).wait()
        over_core(hop, words, cwsend, cwrecv).wait()


def gather(triple, mixing, widen, narrow, tb, mb, wb, nb, gain, shift):
    vm = pl.BlockSpec(memory_space=pltpu.VMEM)
    return pl.pallas_call(
        gather_kernel,
        out_shape=(
            jax.ShapeDtypeStruct((8, 72, D), jnp.int32),
            jax.ShapeDtypeStruct((8, 192, 128), f32),
        ),
        in_specs=[vm] * 10,
        out_specs=(vm, vm),
        scratch_shapes=[pltpu.VMEM((24, D), f32)]
        + [pltpu.SemaphoreType.DMA((3,))] * 4
        + [pltpu.SemaphoreType.DMA((4,))] * 4,
        compiler_params=pltpu.CompilerParams(has_side_effects=True, vmem_limit_bytes=VMEM_CAP),
        name="gather_weights",
    )(triple, mixing, widen, narrow, tb, mb, wb, nb, gain, shift)


def unpack_block(words, small, block, dst):
    index = 0 if block < 3 else 1 if block == 3 else 2 if block < 8 else block - 5

    def one(owner, carry):
        for pair in range(6):
            parts = []
            for group in (2 * pair, 2 * pair + 1):
                total = None
                for half in range(2):
                    word, bit = plane_of(block, half, group)
                    bits = words[owner, word * 8 : (word + 1) * 8, :] & jnp.int32(bit)
                    column = index * 2 + half
                    scale = jnp.broadcast_to(
                        small[owner, group * 8 : (group + 1) * 8, column : column + 1], (8, D)
                    )
                    value = jnp.where(bits != 0, scale, -scale)
                    total = value if total is None else total + value
                parts.append(total)
            tile = jnp.concatenate(parts, axis=0).astype(bf16)
            if block < 8:
                start = owner * BLOCK + pair * 16
            else:
                start = owner * (4 * BLOCK) + (block - 8) * BLOCK + pair * 16
            rows = pl.ds(pl.multiple_of(start, 16), 16)
            if block < 3:
                dst[rows, block * D : (block + 1) * D] = tile
            elif block < 8 and block > 3:
                dst[rows, (block - 4) * D : (block - 3) * D] = tile
            else:
                dst[rows, :] = tile
        return carry

    lax.fori_loop(0, 8, one, 0)


def clip_back(grad, value, level, inverse):
    u = value * inverse
    t = jnp.tanh(u)
    slope = 1.0 - t * t
    return grad * slope, jnp.sum(grad * (t - u * slope), axis=0, keepdims=True)


def norm_rows(v):
    center = v - jnp.mean(v, axis=1, keepdims=True)
    variance = jnp.mean(center * center, axis=1, keepdims=True)
    rstd = lax.rsqrt(variance + norm_epsilon)
    return center * rstd, rstd


def norm_rows_back(grad, hat, rstd, gain_row):
    g = grad * gain_row
    return rstd * (
        g - jnp.mean(g, axis=1, keepdims=True) - hat * jnp.mean(g * hat, axis=1, keepdims=True)
    )


def colsum(v):
    return jnp.sum(v, axis=0, keepdims=True)


HALF_ROOT = 1.0 / math.sqrt(2.0)
DENSITY = 1.0 / math.sqrt(2.0 * math.pi)


def layer_kernel(
    seq, live, level, words, small, hid, teach, teach_scores,
    out, acc, fin, small_out,
    wt, wm, ww, wn, prm, bias, wbias, qkv, low, ctx, hat1, rstd1, widened, act, wg, sgrad,
    cgrad, valid, pair, xlT, clT, wlT, nlT, sums, tbuf, pt, rb, rx, ry, rz, sin,
    s1, r1, s2, r2, s3, r3, s4, r4, s5, r5, s6, r6, sms, smr, tsem,
):
    c0, c1, c2, c3 = level[0], level[1], level[2], level[3]
    i0, i1, i2, i3 = 1.0 / c0, 1.0 / c1, 1.0 / c2, 1.0 / c3
    for part in range(6):
        total = small[0, 96 + part * 16 : 112 + part * 16, :]
        for owner in range(1, 8):
            total = total + small[owner, 96 + part * 16 : 112 + part * 16, :]
        prm[:, part * 128 : (part + 1) * 128] = total
    for part in range(3):
        bias[0:1, part * D : (part + 1) * D] = prm[part : part + 1, :]
    for part in range(4):
        wbias[0:1, part * D : (part + 1) * D] = prm[9 + part : 10 + part, :]
    sums[...] = jnp.zeros_like(sums)
    row = lax.broadcasted_iota(jnp.int32, (256, 256), 0)
    col = lax.broadcasted_iota(jnp.int32, (256, 256), 1)
    key_ok = col < seq[0, 0]
    query_ok = row < seq[0, 0] * live[0, 0]
    valid[0] = jnp.where(key_ok, 1.0, 0.0)
    pair[0] = jnp.where(key_ok & query_ok, 1.0, 0.0)

    def in_slots(at):
        mid = (at < 128) & (at < seq[0, 1])
        one = (at >= 128) & (at < 192) & (at - 128 < seq[0, 2])
        two = (at >= 192) & (at - 192 < seq[0, 3])
        return mid, one, two

    km, ko, kt = in_slots(col)
    qm, qo, qt = in_slots(row)
    key_ok = (km & (row < 128)) | (ko & (row >= 128) & (row < 192)) | (kt & (row >= 192))
    live_mid = row * 0 + live[0, 1] > 0
    live_one = row * 0 + live[0, 2] > 0
    live_two = row * 0 + live[0, 2] > 1
    query_ok = (qm & live_mid) | (qo & live_one) | (qt & live_two)
    valid[1] = jnp.where(key_ok, 1.0, 0.0)
    pair[1] = jnp.where(key_ok & query_ok, 1.0, 0.0)
    ones = jnp.where(query_ok, 1.0, 0.0)

    for block in range(12):
        unpack_block(
            words, small, block, wt if block < 3 else wm if block == 3 else ww if block < 8 else wn
        )

    def clip_in(r):
        x = hid[pl.ds(r, 128), :].astype(f32)
        lo = (c0 * jnp.tanh(x * i0)).astype(bf16)
        low[pl.ds(r, 128), :] = lo
        xlT[:, pl.ds(r, 128)] = lo.T

    loop(4, 128, clip_in)

    def qkv_cols(c):
        cs = pl.ds(c, 256)
        qkv[:, cs] = (dot_nn(low[...], wt[:, cs]) + bias[0:1, cs]).astype(bf16)

    loop(9, 256, qkv_cols)
    lane = lax.broadcasted_iota(jnp.int32, (256, 128), 1)
    first = lane < 64

    def pick(v, j):
        return jnp.where(first, v, jnp.zeros_like(v)) if j == 0 else jnp.where(first, jnp.zeros_like(v), v)

    def softmax(q, k, ok, j):
        s = dot_nt(pick(q, j), k) * (HEAD_DIM**-0.5)
        masked = jnp.where(ok, s, masked_fill)
        e = jnp.exp(masked - jnp.max(masked, axis=1, keepdims=True))
        return s, e / jnp.sum(e, axis=1, keepdims=True)

    def attend_pair(u, carry):
        g = lax.div(u, 6)
        hp = lax.rem(u, 6)
        rs = pl.ds(pl.multiple_of(g * 256, 256), 256)
        qs = pl.multiple_of(hp * 128, 128)
        q = qkv[rs, pl.ds(qs, 128)]
        k = qkv[rs, pl.ds(pl.multiple_of(D + qs, 128), 128)]
        v = qkv[rs, pl.ds(pl.multiple_of(2 * D + qs, 128), 128)]
        ok = valid[g] > 0.5
        parts = []
        for j in range(2):
            s, p = softmax(q, k, ok, j)
            parts.append(dot_nn(p.astype(bf16), v))
        ctx[rs, pl.ds(qs, 128)] = jnp.where(first, parts[0], parts[1])
        return carry

    lax.fori_loop(0, 12, attend_pair, 0)

    def clip_ctx(r):
        lo = (c1 * jnp.tanh(ctx[pl.ds(r, 128), :] * i1)).astype(bf16)
        low[pl.ds(r, 128), :] = lo
        clT[:, pl.ds(r, 128)] = lo.T

    loop(4, 128, clip_ctx)

    def mix_cols(c):
        cs = pl.ds(c, 256)
        acc[:, cs] = dot_nn(low[...], wm[:, cs]) + prm[3:4, cs] + hid[:, cs].astype(f32)

    loop(3, 256, mix_cols)

    def norm_one(r):
        rs = pl.ds(r, 128)
        hat, rstd = norm_rows(acc[rs, :])
        hat1[rs, :] = hat
        rstd1[rs, :] = jnp.broadcast_to(rstd, (128, 128))
        normed = hat * prm[5:6, :] + prm[7:8, :]
        lo = (c2 * jnp.tanh(normed * i2)).astype(bf16)
        low[rs, :] = lo
        wlT[:, rs] = lo.T
        acc[rs, :] = normed + prm[4:5, :]

    loop(4, 128, norm_one)

    def feed(c):
        cs = pl.ds(c, 512)
        w = dot_nn(low[...], ww[:, cs]) + wbias[0:1, cs]
        widened[:, cs] = w
        a = 0.5 * w * (1.0 + lax.erf(w * HALF_ROOT))
        lo = (c3 * jnp.tanh(a * i3)).astype(bf16)
        act[:, cs] = lo
        acc[...] += dot_nn(lo, wn[cs, :])

    loop(6, 512, feed)

    def norm_two(r):
        rs = pl.ds(r, 128)
        hat, rstd = norm_rows(acc[rs, :])
        full = hat * prm[6:7, :] + prm[8:9, :]
        out[rs, :] = full.astype(bf16)
        at = lax.broadcasted_iota(jnp.int32, (128, D), 0) + r
        l0, l1, l2, l3 = seq[0, 0] * live[0, 0], seq[0, 1], seq[0, 2], seq[0, 3]
        l1 = jnp.where(live[0, 1] > 0, l1, 0)
        l2 = jnp.where(live[0, 2] > 0, l2, 0)
        l3 = jnp.where(live[0, 2] > 1, l3, 0)
        ok = (at < l0) | ((at >= 256) & (at < 256 + l1)) | ((at >= 384) & (at < 384 + l2))
        ok = ok | ((at >= 448) & (at < 448 + l3))
        gap = jnp.where(ok, full - teach[rs, :].astype(f32), 0.0)
        sums[15:16, :] += colsum(gap * gap) * 0.5
        sums[6:7, :] += colsum(gap * hat)
        sums[8:9, :] += colsum(gap)
        grad = norm_rows_back(gap, hat, rstd, prm[6:7, :])
        sgrad[rs, :] = grad
        acc[rs, :] = jnp.zeros((128, D), f32)
        lo = grad.astype(bf16)
        low[rs, :] = lo
        nlT[:, rs] = lo.T
        sums[4:5, :] += colsum(lo.astype(f32))

    loop(4, 128, norm_two)

    def feed_back(t):
        cs = pl.ds(pl.multiple_of(t * 512, 512), 512)
        g = dot_nt(low[...], wn[cs, :])
        w = widened[:, cs]
        e = 0.5 * (1.0 + lax.erf(w * HALF_ROOT))
        a = w * e
        u = a * i3
        th = jnp.tanh(u)
        slope = 1.0 - th * th
        clip_sum = colsum(g * (th - u * slope))
        sums[14:15, 0:512] += clip_sum
        back = g * slope * (e + w * (DENSITY * jnp.exp(-0.5 * w * w)))
        lo = back.astype(bf16)
        wg[:, cs] = lo
        wbias[1:2, cs] = colsum(lo.astype(f32))
        acc[...] += dot_nt(lo, ww[:, cs])

    def norm_one_back(r):
        rs = pl.ds(r, 128)
        hat = hat1[rs, :]
        normed = hat * prm[5:6, :] + prm[7:8, :]
        grad, clip_sum = clip_back(acc[rs, :], normed, c2, i2)
        sums[18:19, :] += clip_sum
        grad = grad + sgrad[rs, :]
        sums[5:6, :] += colsum(grad * hat)
        sums[7:8, :] += colsum(grad)
        grad = norm_rows_back(grad, hat, rstd1[rs, 0:1], prm[5:6, :])
        acc[rs, :] = grad
        lo = grad.astype(bf16)
        low[rs, :] = lo
        sums[3:4, :] += colsum(lo.astype(f32))

    def mix_back(c):
        cs = pl.ds(c, 256)
        g = dot_nt(low[...], wm[cs, :])
        grad, clip_sum = clip_back(g, ctx[:, cs], c1, i1)
        sums[17:18, cs] += clip_sum
        cgrad[:, cs] = grad.astype(bf16)

    def scores_copy(u, slot):
        g = lax.div(u, 6)
        hp = lax.rem(u, 6)
        rs = pl.ds(pl.multiple_of(g * 256, 256), 256)
        return pltpu.make_async_copy(
            teach_scores.at[pl.ds(2 * hp, 2), rs], tbuf.at[slot], tsem.at[slot]
        )

    def attend_pair_back(u, slot):
        g = lax.div(u, 6)
        hp = lax.rem(u, 6)
        rs = pl.ds(pl.multiple_of(g * 256, 256), 256)
        q0 = pl.multiple_of(hp * 128, 128)
        k0 = pl.multiple_of(D + q0, 128)
        v0 = pl.multiple_of(2 * D + q0, 128)
        q = qkv[rs, pl.ds(q0, 128)]
        k = qkv[rs, pl.ds(k0, 128)]
        v = qkv[rs, pl.ds(v0, 128)]
        cg = cgrad[rs, pl.ds(q0, 128)]
        ok = valid[g] > 0.5
        pairs = pair[g] > 0.5
        dq, dk, dv = [], [], []
        for j in range(2):
            s, p = softmax(q, k, ok, j)
            ts = tbuf[slot, j].astype(f32)
            second = pltpu.roll(ts[128:192], 128, 1)
            third = pltpu.roll(ts[192:256], 192, 1)
            moved = jnp.concatenate([ts[0:128], second, third], axis=0)
            ts = jnp.where(g > 0, moved, ts)
            gap = jnp.where(pairs, s - ts, 0.0)
            sums[16:17, 0:256] += colsum(gap * gap) * (0.5 / LONG_LEN)
            pg = dot_nt(pick(cg, j), v)
            sg = p * (pg - jnp.sum(pg * p, axis=1, keepdims=True)) + gap * (1.0 / LONG_LEN)
            sg = sg.astype(bf16)
            dv.append(dot_tn(p.astype(bf16), cg))
            dq.append(dot_nn(sg, k))
            dk.append(dot_tn(sg, q))
        scale = HEAD_DIM**-0.5
        dq = (jnp.where(first, dq[0], dq[1]) * scale).astype(bf16)
        dk = (jnp.where(first, dk[0], dk[1]) * scale).astype(bf16)
        dv = jnp.where(first, dv[0], dv[1]).astype(bf16)
        for index, (grad, at) in enumerate(((dq, q0), (dk, k0), (dv, v0))):
            qkv[rs, pl.ds(at, 128)] = grad
            sums[index : index + 1, pl.ds(q0, 128)] += colsum(grad.astype(f32))

    def input_back(c):
        cs = pl.ds(c, 256)
        g = dot_nt(qkv[...], wt[cs, :])
        grad, clip_sum = clip_back(g, hid[:, cs].astype(f32), c0, i0)
        sums[19:20, cs] += clip_sum
        acc[:, cs] += grad

    def close_sums():
        for part in range(4):
            sums[9 + part : 10 + part, :] = wbias[1:2, part * D : (part + 1) * D]
        at = lax.broadcasted_iota(jnp.int32, (1, D), 1)
        line = jnp.zeros((1, D), f32)
        for spot, value in enumerate(
            (
                sums[19:20, :], sums[17:18, :], sums[18:19, :], sums[14:15, :],
                sums[15:16, :] + sums[16:17, :],
            )
        ):
            line = jnp.where(at == spot, jnp.sum(value), line)
        sums[13:14, :] = line
        small_out[...] = sums[0:16, :]

    dp = lax.axis_index("dp")
    me = lax.axis_index("fsdp")
    x = lax.rem(dp, 2)
    y = lax.div(dp, 2)
    z = lax.div(me, 2)
    core = lax.rem(me, 2)
    over_x = (dp + 1 - 2 * x, me)
    over_y = (dp + 2 - 4 * y, me)
    over_core = (dp, z * 2 + 1 - core)
    firsts = (over_x, over_y)
    seconds = (over_y, over_x)

    def cols_of(p):
        return pl.ds(p * 256, 256)

    def remote(src, dst, send, recv, to):
        return pltpu.make_async_remote_copy(
            src_ref=src, dst_ref=dst, send_sem=send, recv_sem=recv, device_id=to,
            device_id_type=MESH,
        )

    def core_copy(k):
        slot = lax.rem(k, SLOTS)
        return remote(pt.at[slot, :, 1 - core], rb.at[lax.rem(k, 2)], s1.at[slot], r1.at[slot], over_core)

    def one_copy(k, p):
        slot = lax.rem(k, SLOTS)
        if p == 0:
            src = pt.at[slot, :, core, 1 - x, :, :, cols_of(p)]
        else:
            src = pt.at[slot, :, core, :, 1 - y, :, cols_of(p)]
        return remote(src, rx.at[lax.rem(k, 2), p], s2.at[slot, p], r2.at[slot, p], firsts[p])

    def two_copy(k, p):
        slot = lax.rem(k, SLOTS)
        if p == 0:
            src = pt.at[slot, :, core, x, 1 - y, :, cols_of(p)]
        else:
            src = pt.at[slot, :, core, 1 - x, y, :, cols_of(p)]
        return remote(src, ry.at[lax.rem(k, 2), p], s3.at[slot, p], r3.at[slot, p], seconds[p])

    def z_copy(k, hop):
        slot = lax.rem(k, SLOTS)
        to = lax.rem(z + hop, 4)
        return remote(
            pt.at[slot, to, core, x, y], rz.at[lax.rem(k, 2), hop - 1], s4.at[slot, hop - 1],
            r4.at[slot, hop - 1], (dp, to * 2 + core),
        )

    def fin_cols(k, start, count):
        return pl.ds(pl.multiple_of(lax.rem(k, 6) * CHUNK + start, count), count)

    def back_two(k, p):
        slot = lax.rem(k, SLOTS)
        ref = fin.at[lax.div(k, 6), x, y, :, fin_cols(k, p * 256, 256)]
        return remote(ref, ref, s5.at[slot, p], r5.at[slot, p], seconds[p])

    def back_one(k, p):
        slot = lax.rem(k, SLOTS)
        if p == 0:
            ref = fin.at[lax.div(k, 6), x, :, :, fin_cols(k, p * 256, 256)]
        else:
            ref = fin.at[lax.div(k, 6), :, y, :, fin_cols(k, p * 256, 256)]
        return remote(ref, ref, s6.at[slot, p], r6.at[slot, p], firsts[p])

    def small_copy(step):
        to = (
            over_core, over_x, over_y, (dp, lax.rem(z + 1, 4) * 2 + core),
            (dp, lax.rem(z + 2, 4) * 2 + core), (dp, lax.rem(z + 3, 4) * 2 + core),
        )[step]
        return remote(small_out, sin.at[step], sms.at[step], smr.at[step], to)

    def tick(t, carry):
        @pl.when(t >= 6)
        def _():
            for p in range(2):
                back_one(t - 6, p).wait()

        @pl.when((t >= 5) & (t < 5 + CHUNKS))
        def _():
            for p in range(2):
                back_two(t - 5, p).wait()
                back_one(t - 5, p).start()

        @pl.when((t >= 4) & (t < 4 + CHUNKS))
        def _():
            k = t - 4
            slot = lax.rem(k, SLOTS)
            for hop in (1, 2, 3):
                z_copy(k, hop).wait()
            duo = lax.rem(k, 2)
            total = pt[slot, z, core, x, y] + rz[duo, 0] + rz[duo, 1] + rz[duo, 2]
            fin[lax.div(k, 6), x, y, :, fin_cols(k, 0, CHUNK)] = total
            for p in range(2):
                back_two(k, p).start()

        @pl.when((t >= 3) & (t < 3 + CHUNKS))
        def _():
            k = t - 3
            slot = lax.rem(k, SLOTS)
            for p in range(2):
                two_copy(k, p).wait()
                for q in range(4):
                    pt[slot, q, core, x, y, :, cols_of(p)] += ry[lax.rem(k, 2), p, q]
            for hop in (1, 2, 3):
                z_copy(k, hop).start()

        @pl.when((t >= 2) & (t < 2 + CHUNKS))
        def _():
            k = t - 2
            slot = lax.rem(k, SLOTS)
            for p in range(2):
                one_copy(k, p).wait()
                for q in range(4):
                    for i in range(2):
                        if p == 0:
                            pt[slot, q, core, x, i, :, cols_of(p)] += rx[lax.rem(k, 2), p, q, i]
                        else:
                            pt[slot, q, core, i, y, :, cols_of(p)] += rx[lax.rem(k, 2), p, q, i]
                two_copy(k, p).start()

        @pl.when((t >= 1) & (t < 1 + CHUNKS))
        def _():
            k = t - 1
            slot = lax.rem(k, SLOTS)
            core_copy(k).wait()
            for q in range(4):
                pt[slot, q, core] += rb[lax.rem(k, 2), q]
            for p in range(2):
                one_copy(k, p).start()

        slot = lax.rem(t, SLOTS)

        def put(owner, cols, block):
            for i in range(2):
                for j in range(2):
                    at = (i * 2 + j) * 24
                    pt[slot, owner // 2, owner % 2, i, j, :, cols] = block[at : at + 24, :]

        @pl.when(t < 6)
        def _():
            j = lax.div(t, 2)
            rows = pl.ds(pl.multiple_of(lax.rem(t, 2) * 384, 384), 384)
            left = nlT[rows, :]
            for owner in range(8):
                cols = pl.ds(pl.multiple_of(owner * 384 + j * 128, 128), 128)
                got = dot_nn(left, act[:, cols])
                for part in range(4):
                    put(owner, pl.ds(part * 128, 128), got[part * BLOCK : (part + 1) * BLOCK, :])

        def whole(left, right, half):
            got = dot_nn(left, right)
            for owner in range(8):
                put(owner, pl.ds(half * 256, 256), got[owner * BLOCK : (owner + 1) * BLOCK, :])

        @pl.when((t >= 6) & (t < 12))
        def _():
            for half in range(2):
                cols = pl.ds(pl.multiple_of((t - 6) * CHUNK + half * 256, 256), 256)
                whole(wlT[...], wg[:, cols], half)

        for half in range(2):
            part = (t - 12) * 2 + half

            @pl.when((part >= 0) & (part < 3))
            def _():
                cols = pl.ds(pl.multiple_of(part * 256, 256), 256)
                whole(clT[...], low[:, cols], half)

            @pl.when((part >= 3) & (part < 12))
            def _():
                cols = pl.ds(pl.multiple_of((part - 3) * 256, 256), 256)
                whole(xlT[...], qkv[:, cols], half)

        @pl.when(t < CHUNKS)
        def _():
            core_copy(t).start()

        @pl.when(t < 6)
        def _():
            feed_back(t)

        @pl.when(t == 6)
        def _():
            for slot in range(2):
                scores_copy(slot, slot).start()
            loop(4, 128, norm_one_back)
            loop(3, 256, mix_back)

        @pl.when((t >= 7) & (t < 13))
        def _():
            for slot in range(2):
                u = (t - 7) * 2 + slot
                scores_copy(u, slot).wait()
                attend_pair_back(u, slot)

                @pl.when(t < 12)
                def _():
                    scores_copy(u + 2, slot).start()

        @pl.when((t >= 13) & (t < 16))
        def _():
            input_back(pl.multiple_of((t - 13) * 256, 256))

        @pl.when(t == 16)
        def _():
            close_sums()
            small_copy(0).start()

        @pl.when(t == 17)
        def _():
            small_copy(0).wait()
            small_out[...] += sin[0]
            small_copy(1).start()

        @pl.when(t == 18)
        def _():
            small_copy(1).wait()
            small_out[...] += sin[1]
            small_copy(2).start()

        @pl.when(t == 19)
        def _():
            small_copy(2).wait()
            small_out[...] += sin[2]
            for step in (3, 4, 5):
                small_copy(step).start()

        @pl.when(t == 20)
        def _():
            for step in (3, 4, 5):
                small_copy(step).wait()
            small_out[...] = small_out[...] + sin[3] + sin[4] + sin[5]

        return carry

    lax.fori_loop(0, CHUNKS + 6, tick, 0)


def layer(seq, live, level, words, small, hid, teach, teach_scores):
    vm = pl.BlockSpec(memory_space=pltpu.VMEM)
    sm = pl.BlockSpec(memory_space=pltpu.SMEM)
    sds = jax.ShapeDtypeStruct
    dma = pltpu.SemaphoreType.DMA
    return pl.pallas_call(
        layer_kernel,
        out_shape=(
            sds((ROWS, D), bf16),
            sds((ROWS, D), f32),
            sds((3, 2, 2, 24, FF), f32),
            sds((16, D), f32),
        ),
        in_specs=[sm] * 3 + [vm] * 4 + [pl.BlockSpec(memory_space=pl.ANY)],
        out_specs=(vm,) * 4,
        scratch_shapes=[
            pltpu.VMEM((D, 3 * D), bf16),
            pltpu.VMEM((D, D), bf16),
            pltpu.VMEM((D, FF), bf16),
            pltpu.VMEM((FF, D), bf16),
            pltpu.VMEM((16, D), f32),
            pltpu.VMEM((8, 3 * D), f32),
            pltpu.VMEM((8, FF), f32),
            pltpu.VMEM((ROWS, 3 * D), bf16),
            pltpu.VMEM((ROWS, D), bf16),
            pltpu.VMEM((ROWS, D), f32),
            pltpu.VMEM((ROWS, D), f32),
            pltpu.VMEM((ROWS, 128), f32),
            pltpu.VMEM((ROWS, FF), f32),
            pltpu.VMEM((ROWS, FF), bf16),
            pltpu.VMEM((ROWS, FF), bf16),
            pltpu.VMEM((ROWS, D), f32),
            pltpu.VMEM((ROWS, D), bf16),
            pltpu.VMEM((2, 256, 256), f32),
            pltpu.VMEM((2, 256, 256), f32),
            pltpu.VMEM((D, ROWS), bf16),
            pltpu.VMEM((D, ROWS), bf16),
            pltpu.VMEM((D, ROWS), bf16),
            pltpu.VMEM((D, ROWS), bf16),
            pltpu.VMEM((24, D), f32),
            pltpu.VMEM((2, 2, 256, 256), bf16),
            pltpu.VMEM((SLOTS, 4, 2, 2, 2, 24, CHUNK), f32),
            pltpu.VMEM((2, 4, 2, 2, 24, CHUNK), f32),
            pltpu.VMEM((2, 2, 4, 2, 24, 256), f32),
            pltpu.VMEM((2, 2, 4, 24, 256), f32),
            pltpu.VMEM((2, 3, 24, CHUNK), f32),
            pltpu.VMEM((6, 16, D), f32),
        ]
        + [dma((SLOTS,))] * 2
        + [dma((SLOTS, 2))] * 4
        + [dma((SLOTS, 3))] * 2
        + [dma((SLOTS, 2))] * 4
        + [dma((6,))] * 2
        + [dma((2,))],
        compiler_params=pltpu.CompilerParams(has_side_effects=True, vmem_limit_bytes=LAYER_CAP),
        name="layer",
    )(seq, live, level, words, small, hid, teach, teach_scores)


def on_device_fast(
    hidden_in, teacher_hidden, teacher_scores, seq_lengths, live_counts, triple_latent,
    mixing_latent, widen_latent, narrow_latent, triple_bias, mixing_bias, widen_bias, narrow_bias,
    norm_gain, norm_shift, clip_level,
):
    words, small = gather(
        triple_latent, mixing_latent, widen_latent, narrow_latent, triple_bias,
        mixing_bias[None], widen_bias[None], narrow_bias[None], norm_gain, norm_shift,
    )
    teach_scores = jnp.transpose(teacher_scores, (1, 0, 2))
    out, input_grad, fin, small_sum = layer(
        seq_lengths, live_counts, clip_level, words, small, hidden_in, teacher_hidden, teach_scores
    )
    fin = fin.reshape(3, BLOCK, FF)
    narrow_sum = (
        fin[0].reshape(BLOCK, 3, 2, 4, 128).transpose(1, 4, 2, 3, 0).reshape(4 * BLOCK, D)
    )
    totals = (fin[2][:, D:], fin[2][:, :D], fin[1], narrow_sum)
    latents = (triple_latent, mixing_latent, widen_latent, narrow_latent)
    latent_grads = tuple(
        (
            jnp.where(jnp.abs(latent) <= 1.0, (total / math.sqrt(fan_in))[None], 0.0)
            for latent, total, fan_in in zip(latents, totals, (D, D, D, FF))
        )
    )
    me = lax.axis_index("fsdp")
    own = lax.dynamic_slice_in_dim(small_sum[0:9], me * BLOCK, BLOCK, 1)
    wide = lax.dynamic_slice_in_dim(small_sum[9:13].reshape(FF), me * 4 * BLOCK, 4 * BLOCK, 0)
    tokens = hidden_in.shape[0] * lax.axis_size("dp") * lax.axis_size("fsdp")
    return (
        out,
        small_sum[13, 4] / (tokens * D),
        input_grad,
        latent_grads[0],
        latent_grads[1],
        latent_grads[2],
        latent_grads[3],
        own[0:3],
        own[3],
        wide,
        own[4],
        own[5:7],
        own[7:9],
        small_sum[13, 0:4],
    )


def solution(mesh):
    in_specs = (
        P(("dp", "fsdp"), None),
        P(("dp", "fsdp"), None),
        P(("dp", "fsdp"), None, None),
        P(("dp", "fsdp"), None),
        P(("dp", "fsdp"), None),
        P(None, "fsdp", None),
        P(None, "fsdp", None),
        P(None, "fsdp", None),
        P(None, "fsdp", None),
        P(None, "fsdp"),
        P("fsdp"),
        P("fsdp"),
        P("fsdp"),
        P(None, "fsdp"),
        P(None, "fsdp"),
        P(),
    )
    out_specs = (
        P(("dp", "fsdp"), None),
        P(),
        P(("dp", "fsdp"), None),
        P(None, "fsdp", None),
        P(None, "fsdp", None),
        P(None, "fsdp", None),
        P(None, "fsdp", None),
        P(None, "fsdp"),
        P("fsdp"),
        P("fsdp"),
        P("fsdp"),
        P(None, "fsdp"),
        P(None, "fsdp"),
        P(),
    )
    fits = mesh.shape["dp"] == 4 and mesh.shape["fsdp"] == 8
    return jax.shard_map(
        on_device_fast if fits else on_device, mesh=mesh, in_specs=in_specs, out_specs=out_specs, check_vma=False
    )
```

```python
import math

import jax
import jax.numpy as jnp
from jax import lax
from jax.experimental import pallas as pl
from jax.experimental.pallas import tpu as pltpu
from jax.sharding import PartitionSpec as P

D = 768
HEADS = 12
HEAD_DIM = 64
FF = 3072
LONG_LEN = 256
MID_LEN = 128
SHORT_LEN = 64
LONG_SLOTS = 1
MID_SLOTS = 1
SHORT_SLOTS = 2


bit_count = 32
norm_epsilon = 1e-12
masked_fill = -1e30


def soft_clip(values, clip_at):
    return clip_at * jnp.tanh(values / clip_at)


def layer_norm(values, gain_row, shift_row):
    center = values - jnp.mean(values, axis=-1, keepdims=True)
    variance = jnp.mean(center * center, axis=-1, keepdims=True)
    return center * lax.rsqrt(variance + norm_epsilon) * gain_row + shift_row


def gelu_exact(values):
    return 0.5 * values * (1.0 + lax.erf(values * (1.0 / math.sqrt(2.0))))


def pack_signs(latent):
    halves, row_count, columns = latent.shape
    sign_bits = (
        (latent > 0).astype(jnp.int32).reshape(halves, row_count, columns // bit_count, bit_count)
    )
    places = jnp.arange(bit_count, dtype=jnp.int32)
    return jnp.sum(jnp.left_shift(sign_bits, places), axis=-1, dtype=jnp.int32)


def unpack_weight(sign_words, scales):
    halves, row_count, word_count = sign_words.shape
    places = jnp.arange(bit_count, dtype=jnp.int32)
    sign_bits = jnp.bitwise_and(jnp.right_shift(sign_words[..., None], places), 1)
    sign_values = (
        (2 * sign_bits - 1).astype(jnp.float32).reshape(halves, row_count, word_count * bit_count)
    )
    return (scales[0][:, None] * sign_values[0] + scales[1][:, None] * sign_values[1]).astype(
        jnp.bfloat16
    )


def bucket_shapes():
    return ((LONG_SLOTS, LONG_LEN), (MID_SLOTS, MID_LEN), (SHORT_SLOTS, SHORT_LEN))


def bucket_masks(lengths, live_count, slot_count, bucket_len):
    places = jnp.arange(bucket_len, dtype=jnp.int32)
    key_ok = places[None, :] < lengths[:, None]
    query_ok = jnp.logical_and(
        key_ok, jnp.arange(slot_count, dtype=jnp.int32)[:, None] < live_count
    )
    return (key_ok, query_ok)


def split_heads(block, slot_count, bucket_len):
    return block.reshape(slot_count, bucket_len, HEADS, HEAD_DIM)


def bucket_scores(qkv_rows, teacher_rows, key_ok, query_ok, slot_count, bucket_len):
    queries = split_heads(qkv_rows[:, :D], slot_count, bucket_len)
    keys_part = split_heads(qkv_rows[:, D : 2 * D], slot_count, bucket_len)
    scores = jnp.einsum(
        "sqhd,skhd->shqk", queries, keys_part, preferred_element_type=jnp.float32
    ) * HEAD_DIM ** (-0.5)
    masked = jnp.where(key_ok[:, None, None, :], scores, masked_fill)
    teacher = jnp.transpose(
        teacher_rows.reshape(slot_count, bucket_len, HEADS, LONG_LEN)[..., :bucket_len],
        (0, 2, 1, 3),
    ).astype(jnp.float32)
    pair_ok = jnp.logical_and(query_ok[:, None, :, None], key_ok[:, None, None, :])
    score_gap = jnp.where(pair_ok, scores - teacher, 0.0)
    return (queries, keys_part, masked, score_gap)


def attend(qkv_rows, teacher_rows, key_ok, query_ok, slot_count, bucket_len):
    queries, keys_part, masked, score_gap = bucket_scores(
        qkv_rows, teacher_rows, key_ok, query_ok, slot_count, bucket_len
    )
    values_part = split_heads(qkv_rows[:, 2 * D :], slot_count, bucket_len)
    row_top = jnp.max(masked, axis=-1, keepdims=True)
    exponent = jnp.exp(masked - row_top)
    exp_total = jnp.sum(exponent, axis=-1, keepdims=True)
    attention = exponent / exp_total
    context = jnp.einsum(
        "shqk,skhd->sqhd",
        attention.astype(jnp.bfloat16),
        values_part,
        preferred_element_type=jnp.float32,
    )
    distill = 0.5 / LONG_LEN * jnp.sum(score_gap * score_gap)
    return (context.reshape(slot_count * bucket_len, D), row_top + jnp.log(exp_total), distill)


def attend_back(
    qkv_rows, teacher_rows, key_ok, query_ok, slot_count, bucket_len, log_total, context_grad
):
    queries, keys_part, masked, score_gap = bucket_scores(
        qkv_rows, teacher_rows, key_ok, query_ok, slot_count, bucket_len
    )
    values_part = split_heads(qkv_rows[:, 2 * D :], slot_count, bucket_len)
    attention = jnp.exp(masked - log_total)
    grad_heads = split_heads(context_grad, slot_count, bucket_len)
    values_grad = jnp.einsum(
        "shqk,sqhd->skhd",
        attention.astype(jnp.bfloat16),
        grad_heads,
        preferred_element_type=jnp.float32,
    )
    weight_grad = jnp.einsum(
        "sqhd,skhd->shqk", grad_heads, values_part, preferred_element_type=jnp.float32
    )
    score_grad = attention * (
        weight_grad - jnp.sum(weight_grad * attention, axis=-1, keepdims=True)
    ) + score_gap * (1.0 / LONG_LEN)
    score_low = score_grad.astype(jnp.bfloat16)
    score_scale = HEAD_DIM ** (-0.5)
    queries_grad = (
        jnp.einsum("shqk,skhd->sqhd", score_low, keys_part, preferred_element_type=jnp.float32)
        * score_scale
    )
    keys_grad = (
        jnp.einsum("shqk,sqhd->skhd", score_low, queries, preferred_element_type=jnp.float32)
        * score_scale
    )
    row_count = slot_count * bucket_len
    return jnp.concatenate(
        [
            queries_grad.reshape(row_count, D),
            keys_grad.reshape(row_count, D),
            values_grad.reshape(row_count, D),
        ],
        axis=-1,
    )


def on_device(
    hidden_in,
    teacher_hidden,
    teacher_scores,
    seq_lengths,
    live_counts,
    triple_latent,
    mixing_latent,
    widen_latent,
    narrow_latent,
    triple_bias,
    mixing_bias,
    widen_bias,
    narrow_bias,
    norm_gain,
    norm_shift,
    clip_level,
):
    latents = (triple_latent, mixing_latent, widen_latent, narrow_latent)
    fan_ins = (D, D, D, FF)
    own_scales = tuple(
        (
            jnp.mean(jnp.abs(latent), axis=-1) / math.sqrt(fan_in)
            for latent, fan_in in zip(latents, fan_ins)
        )
    )
    packed = tuple((pack_signs(latent) for latent in latents))
    gathered = (
        lax.all_gather(packed[0], "fsdp", axis=1, tiled=True),
        lax.all_gather(packed[1], "fsdp", axis=1, tiled=True),
        lax.all_gather(packed[2], "fsdp", axis=1, tiled=True),
        lax.all_gather(packed[3], "fsdp", axis=1, tiled=True),
    )
    factors = (
        lax.all_gather(own_scales[0], "fsdp", axis=1, tiled=True),
        lax.all_gather(own_scales[1], "fsdp", axis=1, tiled=True),
        lax.all_gather(own_scales[2], "fsdp", axis=1, tiled=True),
        lax.all_gather(own_scales[3], "fsdp", axis=1, tiled=True),
        lax.all_gather(triple_bias, "fsdp", axis=1, tiled=True),
        lax.all_gather(mixing_bias, "fsdp", axis=0, tiled=True),
        lax.all_gather(widen_bias, "fsdp", axis=0, tiled=True),
        lax.all_gather(narrow_bias, "fsdp", axis=0, tiled=True),
        lax.all_gather(norm_gain, "fsdp", axis=1, tiled=True),
        lax.all_gather(norm_shift, "fsdp", axis=1, tiled=True),
    )
    scales = factors[:4]
    triple_rows, full_mixing_bias, full_widen_bias, full_narrow_bias, gains, shifts = factors[4:]
    full_triple_bias = triple_rows.reshape(3 * D)
    weights = tuple(
        (unpack_weight(words_part, scale_part) for words_part, scale_part in zip(gathered, scales))
    )
    inputs = hidden_in.astype(jnp.float32)
    inputs_low = soft_clip(inputs, clip_level[0]).astype(jnp.bfloat16)
    qkv_all = (
        jnp.dot(inputs_low, weights[0], preferred_element_type=jnp.float32) + full_triple_bias
    ).astype(jnp.bfloat16)
    lengths = seq_lengths[0]
    counts = live_counts[0]
    plans = []
    row_start = 0
    slot_start = 0
    for bucket, shape_pair in enumerate(bucket_shapes()):
        slot_count, bucket_len = shape_pair
        key_ok, query_ok = bucket_masks(
            lengths[slot_start : slot_start + slot_count], counts[bucket], slot_count, bucket_len
        )
        plans.append(
            (
                row_start,
                row_start + slot_count * bucket_len,
                slot_count,
                bucket_len,
                key_ok,
                query_ok,
            )
        )
        row_start = row_start + slot_count * bucket_len
        slot_start = slot_start + slot_count
    contexts = []
    log_totals = []
    distill_sum = 0.0
    for plan in plans:
        row_begin, row_end, slot_count, bucket_len, key_ok, query_ok = plan
        context, log_total, distill = attend(
            qkv_all[row_begin:row_end],
            teacher_scores[row_begin:row_end],
            key_ok,
            query_ok,
            slot_count,
            bucket_len,
        )
        contexts.append(context)
        log_totals.append(log_total)
        distill_sum = distill_sum + distill
    context = jnp.concatenate(contexts, axis=0)
    token_ok = jnp.concatenate([plan[5].reshape(-1) for plan in plans])
    context_low = soft_clip(context, clip_level[1]).astype(jnp.bfloat16)
    mixed = jnp.dot(context_low, weights[1], preferred_element_type=jnp.float32) + full_mixing_bias
    first_sum = inputs + mixed
    first_norm = layer_norm(first_sum, gains[0], shifts[0])
    widen_low = soft_clip(first_norm, clip_level[2]).astype(jnp.bfloat16)
    widened = jnp.dot(widen_low, weights[2], preferred_element_type=jnp.float32) + full_widen_bias
    activated = gelu_exact(widened)
    activated_low = soft_clip(activated, clip_level[3]).astype(jnp.bfloat16)
    narrowed = (
        jnp.dot(activated_low, weights[3], preferred_element_type=jnp.float32) + full_narrow_bias
    )
    second_sum = first_norm + narrowed
    out_full = layer_norm(second_sum, gains[1], shifts[1])
    out_gap = jnp.where(token_ok[:, None], out_full - teacher_hidden.astype(jnp.float32), 0.0)
    loss_local = 0.5 * jnp.sum(out_gap * out_gap) + distill_sum
    regathered = (
        lax.all_gather(packed[0], "fsdp", axis=1, tiled=True),
        lax.all_gather(packed[1], "fsdp", axis=1, tiled=True),
        lax.all_gather(packed[2], "fsdp", axis=1, tiled=True),
        lax.all_gather(packed[3], "fsdp", axis=1, tiled=True),
    )
    back_weights = tuple(
        (
            unpack_weight(words_part, scale_part)
            for words_part, scale_part in zip(regathered, scales)
        )
    )
    _, second_back = jax.vjp(layer_norm, second_sum, gains[1], shifts[1])
    second_grad, gain_two, shift_two = second_back(out_gap)
    narrow_low = second_grad.astype(jnp.bfloat16)
    narrow_weight_grad = jnp.einsum(
        "rf,rd->fd", activated_low, narrow_low, preferred_element_type=jnp.float32
    )
    act_low_grad = jnp.einsum(
        "rd,fd->rf", narrow_low, back_weights[3], preferred_element_type=jnp.float32
    )
    _, clip_three_back = jax.vjp(soft_clip, activated, clip_level[3])
    act_grad, clip_three = clip_three_back(act_low_grad)
    _, gelu_back = jax.vjp(gelu_exact, widened)
    (widened_grad,) = gelu_back(act_grad)
    widen_grad_low = widened_grad.astype(jnp.bfloat16)
    widen_weight_grad = jnp.einsum(
        "rd,rf->df", widen_low, widen_grad_low, preferred_element_type=jnp.float32
    )
    norm_low_grad = jnp.einsum(
        "rf,df->rd", widen_grad_low, back_weights[2], preferred_element_type=jnp.float32
    )
    _, clip_two_back = jax.vjp(soft_clip, first_norm, clip_level[2])
    norm_grad, clip_two = clip_two_back(norm_low_grad)
    norm_grad = norm_grad + second_grad
    _, first_back = jax.vjp(layer_norm, first_sum, gains[0], shifts[0])
    first_grad, gain_one, shift_one = first_back(norm_grad)
    mixed_low = first_grad.astype(jnp.bfloat16)
    mixing_weight_grad = jnp.einsum(
        "rc,rd->cd", context_low, mixed_low, preferred_element_type=jnp.float32
    )
    context_low_grad = jnp.einsum(
        "rd,cd->rc", mixed_low, back_weights[1], preferred_element_type=jnp.float32
    )
    _, clip_one_back = jax.vjp(soft_clip, context, clip_level[1])
    context_grad, clip_one = clip_one_back(context_low_grad)
    context_grad_low = context_grad.astype(jnp.bfloat16)
    qkv_grads = []
    for plan, log_total in zip(plans, log_totals):
        row_begin, row_end, slot_count, bucket_len, key_ok, query_ok = plan
        qkv_grads.append(
            attend_back(
                qkv_all[row_begin:row_end],
                teacher_scores[row_begin:row_end],
                key_ok,
                query_ok,
                slot_count,
                bucket_len,
                log_total,
                context_grad_low[row_begin:row_end],
            )
        )
    qkv_grad_low = jnp.concatenate(qkv_grads, axis=0).astype(jnp.bfloat16)
    triple_weight_grad = jnp.einsum(
        "rd,re->de", inputs_low, qkv_grad_low, preferred_element_type=jnp.float32
    )
    input_low_grad = jnp.einsum(
        "re,de->rd", qkv_grad_low, back_weights[0], preferred_element_type=jnp.float32
    )
    _, clip_zero_back = jax.vjp(soft_clip, inputs, clip_level[0])
    input_side, clip_zero = clip_zero_back(input_low_grad)
    input_grad = input_side + first_grad
    bias_sums = (
        jnp.sum(qkv_grad_low, axis=0, dtype=jnp.float32).reshape(3, D),
        jnp.sum(mixed_low, axis=0, dtype=jnp.float32),
        jnp.sum(widen_grad_low, axis=0, dtype=jnp.float32),
        jnp.sum(narrow_low, axis=0, dtype=jnp.float32),
    )
    row_shares = (
        lax.psum_scatter(triple_weight_grad, "fsdp", scatter_dimension=0, tiled=True),
        lax.psum_scatter(mixing_weight_grad, "fsdp", scatter_dimension=0, tiled=True),
        lax.psum_scatter(widen_weight_grad, "fsdp", scatter_dimension=0, tiled=True),
        lax.psum_scatter(narrow_weight_grad, "fsdp", scatter_dimension=0, tiled=True),
    )
    totals = lax.psum((row_shares[0], row_shares[1], row_shares[2], row_shares[3]), "dp")
    small_sums = lax.psum(
        (
            bias_sums[0],
            bias_sums[1],
            bias_sums[2],
            bias_sums[3],
            jnp.stack([gain_one, gain_two]),
            jnp.stack([shift_one, shift_two]),
            jnp.stack([clip_zero, clip_one, clip_two, clip_three]),
            loss_local,
        ),
        ("dp", "fsdp"),
    )
    shard_index = lax.axis_index("fsdp")
    shard_parts = lax.axis_size("fsdp")

    def own_part(vector, along):
        share_width = vector.shape[along] // shard_parts
        return lax.dynamic_slice_in_dim(vector, shard_index * share_width, share_width, along)

    latent_grads = tuple(
        (
            jnp.where(jnp.abs(latent) <= 1.0, (total / math.sqrt(fan_in))[None], 0.0)
            for latent, total, fan_in in zip(latents, totals, fan_ins)
        )
    )
    loss = small_sums[7] / (hidden_in.shape[0] * D * lax.axis_size("dp") * shard_parts)
    return (
        out_full.astype(jnp.bfloat16),
        loss,
        input_grad,
        latent_grads[0],
        latent_grads[1],
        latent_grads[2],
        latent_grads[3],
        own_part(small_sums[0], 1),
        own_part(small_sums[1], 0),
        own_part(small_sums[2], 0),
        own_part(small_sums[3], 0),
        own_part(small_sums[4], 1),
        own_part(small_sums[5], 1),
        small_sums[6],
    )


bf16 = jnp.bfloat16
f32 = jnp.float32
MESH = pl.DeviceIdType.MESH
VMEM_CAP = 60 * 1024 * 1024
LAYER_CAP = 63 * 1024 * 1024
ROWS = LONG_SLOTS * LONG_LEN + MID_SLOTS * MID_LEN + SHORT_SLOTS * SHORT_LEN
BLOCK = 96
CHUNK = 512
HALF = CHUNK // 2
SECTION = FF // CHUNK
CHUNKS = 3 * SECTION
SLOTS = 4


def dot_nn(a, b):
    return lax.dot_general(a, b, (((1,), (0,)), ((), ())), preferred_element_type=f32)


def dot_nt(a, b):
    return lax.dot_general(a, b, (((1,), (1,)), ((), ())), preferred_element_type=f32)


def dot_tn(a, b):
    return lax.dot_general(a, b, (((0,), (0,)), ((), ())), preferred_element_type=f32)


def loop(count, step, body):
    def run(i, carry):
        body(pl.multiple_of(i * step, step))
        return carry

    lax.fori_loop(0, count, run, 0)


def plane_of(block, half, group):
    place = block * 24 + half * 12 + group
    bit = place % 32
    return place // 32, (1 << bit) if bit < 31 else -(1 << 31)


def unpack_block(words, scl, block, dst):
    index = 0 if block < 3 else 1 if block == 3 else 2 if block < 8 else block - 5

    def one(owner, carry):
        for pair in range(6):
            parts = []
            for group in (2 * pair, 2 * pair + 1):
                total = None
                for half in range(2):
                    word, bit = plane_of(block, half, group)
                    bits = words[owner, word * 8 : (word + 1) * 8, :] & jnp.int32(bit)
                    column = index * 2 + half
                    scale = jnp.broadcast_to(
                        scl[owner, group * 8 : (group + 1) * 8, column : column + 1], (8, D)
                    )
                    value = jnp.where(bits != 0, scale, -scale)
                    total = value if total is None else total + value
                parts.append(total)
            tile = jnp.concatenate(parts, axis=0).astype(bf16)
            if block < 8:
                start = owner * BLOCK + pair * 16
            else:
                start = owner * (4 * BLOCK) + (block - 8) * BLOCK + pair * 16
            rows = pl.ds(pl.multiple_of(start, 16), 16)
            if block < 3:
                dst[rows, block * D : (block + 1) * D] = tile
            elif block < 8 and block > 3:
                dst[rows, (block - 4) * D : (block - 3) * D] = tile
            else:
                dst[rows, :] = tile
        return carry

    lax.fori_loop(0, 8, one, 0)


def clip_back(grad, value, level, inverse):
    u = value * inverse
    t = jnp.tanh(u)
    slope = 1.0 - t * t
    return grad * slope, jnp.sum(grad * (t - u * slope), axis=0, keepdims=True)


def norm_rows(v):
    center = v - jnp.mean(v, axis=1, keepdims=True)
    variance = jnp.mean(center * center, axis=1, keepdims=True)
    rstd = lax.rsqrt(variance + norm_epsilon)
    return center * rstd, rstd


def norm_rows_back(grad, hat, rstd, gain_row):
    g = grad * gain_row
    return rstd * (
        g - jnp.mean(g, axis=1, keepdims=True) - hat * jnp.mean(g * hat, axis=1, keepdims=True)
    )


def colsum(v):
    return jnp.sum(v, axis=0, keepdims=True)


HALF_ROOT = 1.0 / math.sqrt(2.0)
DENSITY = 1.0 / math.sqrt(2.0 * math.pi)


def layer_kernel(
    seq, live, level, tb, mb, wb, nb, gain, shift, hid, teach, teach_scores, tl, ml, wl, nl,
    out, acc, fin, small_out,
    words, small, scl, spread,
    wt, wm, ww, wn, prm, bias, wbias, qkv, low, ctx, hat1, rstd1, widened, act, wg, sgrad,
    cgrad, valid, pair, xlT, clT, wlT, nlT, sums, tbuf, pt, rb, rx, rz, rf, held, ry, sin,
    s1, r1, s2, r2, s3, r3, s4, r4, s5, r5, s6, r6, s7, r7, sms, smr, tsem, lsem, zs, zr, cs_, cr_,
):
    dp = lax.axis_index("dp")
    me = lax.axis_index("fsdp")
    x = lax.rem(dp, 2)
    y = lax.div(dp, 2)
    z = lax.div(me, 2)
    core = lax.rem(me, 2)
    over_x = (dp + 1 - 2 * x, me)
    over_y = (dp + 2 - 4 * y, me)
    over_core = (dp, z * 2 + 1 - core)

    def remote(src, dst, send, recv, to):
        return pltpu.make_async_remote_copy(
            src_ref=src, dst_ref=dst, send_sem=send, recv_sem=recv, device_id=to,
            device_id_type=MESH,
        )

    greet = pltpu.get_barrier_semaphore()
    for to in (over_core, over_x, over_y) + tuple(
        (dp, lax.rem(z + hop, 4) * 2 + core) for hop in (1, 2, 3)
    ):
        pl.semaphore_signal(greet, inc=1, device_id=to, device_id_type=MESH)

    loads = []
    for half in range(2):
        band = slice(192 + half * BLOCK, 192 + (half + 1) * BLOCK)
        loads.append([
            pltpu.make_async_copy(tl.at[half], widened.at[band, 0 : 3 * D], lsem.at[half, 0]),
            pltpu.make_async_copy(ml.at[half], widened.at[band, 3 * D : FF], lsem.at[half, 1]),
            pltpu.make_async_copy(
                wl.at[half], widened.at[half * BLOCK : (half + 1) * BLOCK, :], lsem.at[half, 2]
            ),
            pltpu.make_async_copy(
                nl.at[half], (ctx if half == 0 else sgrad).at[0 : 4 * BLOCK, :], lsem.at[half, 3]
            ),
        ])
    for index in range(4):
        for half in range(2):
            loads[half][index].start()

    def latent_piece(block, half, group):
        if block < 4:
            rows = pl.ds(192 + half * BLOCK + group * 8, 8)
            return widened[rows, block * D : (block + 1) * D]
        if block < 8:
            return widened[pl.ds(half * BLOCK + group * 8, 8), (block - 4) * D : (block - 3) * D]
        rows = pl.ds((block - 8) * BLOCK + group * 8, 8)
        return (ctx if half == 0 else sgrad)[rows, :]

    planes = [[] for _ in range(9)]
    for block in range(12):
        for half in range(2):
            for group in range(12):
                word, bit = plane_of(block, half, group)
                planes[word].append((block, half, group, bit))

    def pack(word):
        total = jnp.zeros((8, D), jnp.int32)
        for block, half, group, bit in planes[word]:
            piece = latent_piece(block, half, group)
            total = total | jnp.where(piece > 0, jnp.int32(bit), jnp.int32(0))
        words[me, word * 8 : (word + 1) * 8, :] = total

    def part_of(owner, index):
        return small.at[owner] if index == 3 else words.at[owner, index * 24 : (index + 1) * 24]

    def z_send(index, hop):
        ref = part_of(me, index)
        peer = lax.rem(z + hop, 4) * 2 + core
        return remote(ref, ref, zs.at[index, hop - 1], zr.at[index, hop - 1], (dp, peer))

    def core_send(index, hop):
        ref = part_of(lax.rem(z + 4 - hop, 4) * 2 + core, index)
        return remote(ref, ref, cs_.at[index, hop], cr_.at[index, hop], over_core)

    def send_out(index):
        for hop in (2, 1, 3):
            z_send(index, hop).start()
        core_send(index, 0).start()

    def pass_on(index):
        for hop in (1, 3, 2):
            z_send(index, hop).wait()
            core_send(index, hop).start()

    def all_here(index):
        for hop in range(4):
            core_send(index, hop).wait()

    for half in range(2):
        loads[half][0].wait()
        loads[half][1].wait()
    for word in range(3):
        pack(word)
    pl.semaphore_wait(greet, 6)
    send_out(0)
    for half in range(2):
        loads[half][2].wait()
        loads[half][3].wait()
    slot_lane = lax.broadcasted_iota(jnp.int32, (8, 128), 1)

    def scale_rows(group):
        tile = jnp.zeros((8, 128), f32)
        for half in range(2):
            rows = pl.ds(pl.multiple_of(192 + half * BLOCK + group, 8), 8)
            for index in range(7):
                if index == 0:
                    part = widened[rows, 0 : 3 * D]
                elif index == 1:
                    part = widened[rows, 3 * D : FF]
                elif index == 2:
                    part = widened[pl.ds(pl.multiple_of(half * BLOCK + group, 8), 8), :]
                else:
                    at = pl.ds(pl.multiple_of((index - 3) * BLOCK + group, 8), 8)
                    part = (ctx if half == 0 else sgrad)[at, :]
                fan = FF if index >= 3 else D
                mean = jnp.sum(jnp.abs(part), axis=1, keepdims=True) * (1.0 / part.shape[1])
                tile = jnp.where(slot_lane == index * 2 + half, mean / math.sqrt(fan), tile)
        spread[pl.ds(group, 8), :] = tile

    loop(12, 8, scale_rows)
    spread[BLOCK:128, :] = jnp.zeros((128 - BLOCK, 128), f32)
    small[me, 0:16, :] = spread[...].T[0:16, :]
    small[me, 16:32, :] = jnp.zeros((16, 128), f32)
    small[me, 16:19, 0:BLOCK] = tb[...]
    small[me, 19:20, 0:BLOCK] = mb[...]
    small[me, 20:21, 0:BLOCK] = nb[...]
    small[me, 21:23, 0:BLOCK] = gain[...]
    small[me, 23:25, 0:BLOCK] = shift[...]
    for part in range(3):
        small[me, 25 + part : 26 + part, :] = wb[:, part * 128 : (part + 1) * 128]
    send_out(3)
    for word in range(3, 6):
        pack(word)
    send_out(1)
    for word in range(6, 9):
        pack(word)
    send_out(2)
    c0, c1, c2, c3 = level[0], level[1], level[2], level[3]
    i0, i1, i2, i3 = 1.0 / c0, 1.0 / c1, 1.0 / c2, 1.0 / c3
    sums[...] = jnp.zeros_like(sums)
    row = lax.broadcasted_iota(jnp.int32, (256, 256), 0)
    col = lax.broadcasted_iota(jnp.int32, (256, 256), 1)
    key_ok = col < seq[0, 0]
    query_ok = row < seq[0, 0] * live[0, 0]
    valid[0] = jnp.where(key_ok, 1.0, 0.0)
    pair[0] = jnp.where(key_ok & query_ok, 1.0, 0.0)

    def in_slots(at):
        mid = (at < 128) & (at < seq[0, 1])
        one = (at >= 128) & (at < 192) & (at - 128 < seq[0, 2])
        two = (at >= 192) & (at - 192 < seq[0, 3])
        return mid, one, two

    km, ko, kt = in_slots(col)
    qm, qo, qt = in_slots(row)
    key_ok = (km & (row < 128)) | (ko & (row >= 128) & (row < 192)) | (kt & (row >= 192))
    live_mid = row * 0 + live[0, 1] > 0
    live_one = row * 0 + live[0, 2] > 0
    live_two = row * 0 + live[0, 2] > 1
    query_ok = (qm & live_mid) | (qo & live_one) | (qt & live_two)
    valid[1] = jnp.where(key_ok, 1.0, 0.0)
    pair[1] = jnp.where(key_ok & query_ok, 1.0, 0.0)
    ones = jnp.where(query_ok, 1.0, 0.0)

    def clip_in(r):
        x = hid[pl.ds(r, 128), :].astype(f32)
        lo = (c0 * jnp.tanh(x * i0)).astype(bf16)
        low[pl.ds(r, 128), :] = lo
        xlT[:, pl.ds(r, 128)] = lo.T

    loop(4, 128, clip_in)
    pass_on(0)
    pass_on(3)
    all_here(3)
    total = jnp.zeros((16, D), f32)
    param_lane = lax.broadcasted_iota(jnp.int32, (16, 128), 1)
    for owner in range(8):
        turned = jnp.concatenate([small[owner, 0:16, :], jnp.zeros((112, 128), f32)], axis=0).T
        scl[owner] = turned[0:BLOCK, :]
        piece = jnp.where(param_lane < BLOCK, small[owner, 16:32, :], 0.0)
        wide = jnp.concatenate([piece, jnp.zeros((16, D - 128), f32)], axis=1)
        total = total + (pltpu.roll(wide, owner * BLOCK, 1) if owner else wide)
        for part in range(3):
            at = owner * 4 * BLOCK + part * 128
            wbias[0:1, at : at + 128] = small[owner, 25 + part : 26 + part, :]
    prm[...] = total
    for part in range(3):
        bias[0:1, part * D : (part + 1) * D] = prm[part : part + 1, :]
    all_here(0)
    for block in range(3):
        unpack_block(words, scl, block, wt)

    def qkv_cols(c):
        cs = pl.ds(c, 256)
        qkv[:, cs] = (dot_nn(low[...], wt[:, cs]) + bias[0:1, cs]).astype(bf16)

    loop(9, 256, qkv_cols)
    pass_on(1)
    lane = lax.broadcasted_iota(jnp.int32, (256, 128), 1)
    first = lane < 64

    def pick(v, j):
        return jnp.where(first, v, jnp.zeros_like(v)) if j == 0 else jnp.where(first, jnp.zeros_like(v), v)

    def softmax(q, k, ok, j):
        s = dot_nt(pick(q, j), k) * (HEAD_DIM**-0.5)
        masked = jnp.where(ok, s, masked_fill)
        e = jnp.exp(masked - jnp.max(masked, axis=1, keepdims=True))
        return s, e / jnp.sum(e, axis=1, keepdims=True)

    def attend_pair(u, carry):
        g = lax.div(u, 6)
        hp = lax.rem(u, 6)
        rs = pl.ds(pl.multiple_of(g * 256, 256), 256)
        qs = pl.multiple_of(hp * 128, 128)
        q = qkv[rs, pl.ds(qs, 128)]
        k = qkv[rs, pl.ds(pl.multiple_of(D + qs, 128), 128)]
        v = qkv[rs, pl.ds(pl.multiple_of(2 * D + qs, 128), 128)]
        ok = valid[g] > 0.5
        parts = []
        for j in range(2):
            s, p = softmax(q, k, ok, j)
            parts.append(dot_nn(p.astype(bf16), v))
        ctx[rs, pl.ds(qs, 128)] = jnp.where(first, parts[0], parts[1])
        return carry

    lax.fori_loop(0, 12, attend_pair, 0)
    pass_on(2)
    unpack_block(words, scl, 3, wm)

    def clip_ctx(r):
        lo = (c1 * jnp.tanh(ctx[pl.ds(r, 128), :] * i1)).astype(bf16)
        low[pl.ds(r, 128), :] = lo
        clT[:, pl.ds(r, 128)] = lo.T

    loop(4, 128, clip_ctx)

    def mix_cols(c):
        cs = pl.ds(c, 256)
        acc[:, cs] = dot_nn(low[...], wm[:, cs]) + prm[3:4, cs] + hid[:, cs].astype(f32)

    loop(3, 256, mix_cols)

    def norm_one(r):
        rs = pl.ds(r, 128)
        hat, rstd = norm_rows(acc[rs, :])
        hat1[rs, :] = hat
        rstd1[rs, :] = jnp.broadcast_to(rstd, (128, 128))
        normed = hat * prm[5:6, :] + prm[7:8, :]
        lo = (c2 * jnp.tanh(normed * i2)).astype(bf16)
        low[rs, :] = lo
        wlT[:, rs] = lo.T
        acc[rs, :] = normed + prm[4:5, :]

    loop(4, 128, norm_one)
    all_here(1)
    for block in range(4, 8):
        unpack_block(words, scl, block, ww)
    all_here(2)
    for block in range(8, 12):
        unpack_block(words, scl, block, wn)

    def feed(c):
        cs = pl.ds(c, 512)

        def feed_rows(r):
            rs = pl.ds(r, 256)
            w = dot_nn(low[rs, :], ww[:, cs]) + wbias[0:1, cs]
            widened[rs, cs] = w
            a = 0.5 * w * (1.0 + lax.erf(w * HALF_ROOT))
            lo = (c3 * jnp.tanh(a * i3)).astype(bf16)
            act[rs, cs] = lo
            acc[rs, :] += dot_nn(lo, wn[cs, :])

        loop(2, 256, feed_rows)

    loop(6, 512, feed)

    def norm_two(r):
        rs = pl.ds(r, 128)
        hat, rstd = norm_rows(acc[rs, :])
        full = hat * prm[6:7, :] + prm[8:9, :]
        out[rs, :] = full.astype(bf16)
        at = lax.broadcasted_iota(jnp.int32, (128, D), 0) + r
        l0, l1, l2, l3 = seq[0, 0] * live[0, 0], seq[0, 1], seq[0, 2], seq[0, 3]
        l1 = jnp.where(live[0, 1] > 0, l1, 0)
        l2 = jnp.where(live[0, 2] > 0, l2, 0)
        l3 = jnp.where(live[0, 2] > 1, l3, 0)
        ok = (at < l0) | ((at >= 256) & (at < 256 + l1)) | ((at >= 384) & (at < 384 + l2))
        ok = ok | ((at >= 448) & (at < 448 + l3))
        gap = jnp.where(ok, full - teach[rs, :].astype(f32), 0.0)
        sums[15:16, :] += colsum(gap * gap) * 0.5
        sums[6:7, :] += colsum(gap * hat)
        sums[8:9, :] += colsum(gap)
        grad = norm_rows_back(gap, hat, rstd, prm[6:7, :])
        sgrad[rs, :] = grad
        acc[rs, :] = jnp.zeros((128, D), f32)
        lo = grad.astype(bf16)
        low[rs, :] = lo
        nlT[:, rs] = lo.T
        sums[4:5, :] += colsum(lo.astype(f32))

    loop(4, 128, norm_two)

    def feed_back(t):
        cs = pl.ds(pl.multiple_of(t * CHUNK, CHUNK), CHUNK)
        wbias[1:2, cs] = jnp.zeros((1, CHUNK), f32)

        def feed_back_rows(r):
            rs = pl.ds(r, 256)
            g = dot_nt(low[rs, :], wn[cs, :])
            w = widened[rs, cs]
            e = 0.5 * (1.0 + lax.erf(w * HALF_ROOT))
            a = w * e
            u = a * i3
            th = jnp.tanh(u)
            slope = 1.0 - th * th
            sums[14:15, 0:CHUNK] += colsum(g * (th - u * slope))
            back = g * slope * (e + w * (DENSITY * jnp.exp(-0.5 * w * w)))
            lo = back.astype(bf16)
            wg[rs, cs] = lo
            wbias[1:2, cs] += colsum(lo.astype(f32))
            acc[rs, :] += dot_nt(lo, ww[:, cs])

        loop(2, 256, feed_back_rows)

    def norm_one_back(r):
        rs = pl.ds(r, 128)
        hat = hat1[rs, :]
        normed = hat * prm[5:6, :] + prm[7:8, :]
        grad, clip_sum = clip_back(acc[rs, :], normed, c2, i2)
        sums[18:19, :] += clip_sum
        grad = grad + sgrad[rs, :]
        sums[5:6, :] += colsum(grad * hat)
        sums[7:8, :] += colsum(grad)
        grad = norm_rows_back(grad, hat, rstd1[rs, 0:1], prm[5:6, :])
        acc[rs, :] = grad
        lo = grad.astype(bf16)
        low[rs, :] = lo
        sums[3:4, :] += colsum(lo.astype(f32))

    def mix_back(c):
        cs = pl.ds(c, 256)
        g = dot_nt(low[...], wm[cs, :])
        grad, clip_sum = clip_back(g, ctx[:, cs], c1, i1)
        sums[17:18, cs] += clip_sum
        cgrad[:, cs] = grad.astype(bf16)

    def scores_copy(u, slot):
        g = lax.div(u, 6)
        hp = lax.rem(u, 6)
        rs = pl.ds(pl.multiple_of(g * 256, 256), 256)
        return pltpu.make_async_copy(
            teach_scores.at[pl.ds(2 * hp, 2), rs], tbuf.at[slot], tsem.at[slot]
        )

    def attend_pair_back(u, slot):
        g = lax.div(u, 6)
        hp = lax.rem(u, 6)
        rs = pl.ds(pl.multiple_of(g * 256, 256), 256)
        q0 = pl.multiple_of(hp * 128, 128)
        k0 = pl.multiple_of(D + q0, 128)
        v0 = pl.multiple_of(2 * D + q0, 128)
        q = qkv[rs, pl.ds(q0, 128)]
        k = qkv[rs, pl.ds(k0, 128)]
        v = qkv[rs, pl.ds(v0, 128)]
        cg = cgrad[rs, pl.ds(q0, 128)]
        ok = valid[g] > 0.5
        pairs = pair[g] > 0.5
        dq, dk, dv = [], [], []
        for j in range(2):
            s, p = softmax(q, k, ok, j)
            ts = tbuf[slot, j].astype(f32)
            second = pltpu.roll(ts[128:192], 128, 1)
            third = pltpu.roll(ts[192:256], 192, 1)
            moved = jnp.concatenate([ts[0:128], second, third], axis=0)
            ts = jnp.where(g > 0, moved, ts)
            gap = jnp.where(pairs, s - ts, 0.0)
            sums[16:17, 0:256] += colsum(gap * gap) * (0.5 / LONG_LEN)
            pg = dot_nt(pick(cg, j), v)
            sg = p * (pg - jnp.sum(pg * p, axis=1, keepdims=True)) + gap * (1.0 / LONG_LEN)
            sg = sg.astype(bf16)
            dv.append(dot_tn(p.astype(bf16), cg))
            dq.append(dot_nn(sg, k))
            dk.append(dot_tn(sg, q))
        scale = HEAD_DIM**-0.5
        dq = (jnp.where(first, dq[0], dq[1]) * scale).astype(bf16)
        dk = (jnp.where(first, dk[0], dk[1]) * scale).astype(bf16)
        dv = jnp.where(first, dv[0], dv[1]).astype(bf16)
        for index, (grad, at) in enumerate(((dq, q0), (dk, k0), (dv, v0))):
            qkv[rs, pl.ds(at, 128)] = grad
            sums[index : index + 1, pl.ds(q0, 128)] += colsum(grad.astype(f32))

    def input_back(c):
        cs = pl.ds(c, 256)
        g = dot_nt(qkv[...], wt[cs, :])
        grad, clip_sum = clip_back(g, hid[:, cs].astype(f32), c0, i0)
        sums[19:20, cs] += clip_sum
        acc[:, cs] += grad

    def close_sums():
        for part in range(4):
            sums[9 + part : 10 + part, :] = wbias[1:2, part * D : (part + 1) * D]
        at = lax.broadcasted_iota(jnp.int32, (1, D), 1)
        line = jnp.zeros((1, D), f32)
        for spot, value in enumerate(
            (
                sums[19:20, :], sums[17:18, :], sums[18:19, :], sums[14:15, :],
                sums[15:16, :] + sums[16:17, :],
            )
        ):
            line = jnp.where(at == spot, jnp.sum(value), line)
        sums[13:14, :] = line
        small_out[...] = sums[0:16, :]

    firsts = (over_x, over_y)
    seconds = (over_y, over_x)
    cols = (pl.ds(0, HALF), pl.ds(HALF, HALF))
    outer = (z == 0) | (z == 3)
    inner = (z == 1) | (z == 2)
    near = z + 1 - 2 * lax.rem(z, 2)
    beyond = 1 - lax.div(z, 2)

    def on_z(to):
        return (dp, to * 2 + core)

    def core_copy(k):
        slot, duo = lax.rem(k, SLOTS), lax.rem(k, 2)
        return remote(pt.at[slot, :, 1 - core], rb.at[duo], s1.at[slot], r1.at[slot], over_core)

    def first_copy(k, p):
        slot, duo = lax.rem(k, SLOTS), lax.rem(k, 2)
        if p == 0:
            src = pt.at[slot, :, core, 1 - x, :, :, cols[p]]
        else:
            src = pt.at[slot, :, core, :, 1 - y, :, cols[p]]
        return remote(src, rx.at[duo, p], s2.at[slot, p], r2.at[slot, p], firsts[p])

    def own_rows(slot, blocks, p):
        if p == 0:
            return pt.at[slot, blocks, core, x, :, :, cols[p]]
        return pt.at[slot, blocks, core, :, y, :, cols[p]]

    def in_copy(k, p):
        slot, duo = lax.rem(k, SLOTS), lax.rem(k, 2)
        src = own_rows(slot, pl.ds(beyond, 3), p)
        return remote(src, rz.at[duo, p], s3.at[slot, p], r3.at[slot, p], on_z(near))

    def out_copy(k, p, kind):
        slot = lax.rem(k, SLOTS)
        to = (near, 3 - z, lax.rem(z + 2, 4))[kind]
        return remote(
            own_rows(slot, to, p), rf.at[slot, min(kind, 1), p], s4.at[slot, kind, p],
            r4.at[slot, min(kind, 1), p], on_z(to),
        )

    def second_copy(k, p):
        slot, duo = lax.rem(k, SLOTS), lax.rem(k, 2)
        src = held.at[duo, p, 1 - y if p == 0 else 1 - x]
        return remote(src, ry.at[duo, p], s5.at[slot, p], r5.at[slot, p], seconds[p])

    def fin_cols(k, start, count):
        return pl.ds(pl.multiple_of(lax.rem(k, SECTION) * CHUNK + start, 128), count)

    def back_second(k, p):
        slot = lax.rem(k, SLOTS)
        ref = fin.at[lax.div(k, SECTION), x, y, :, fin_cols(k, p * HALF, HALF)]
        return remote(ref, ref, s6.at[slot, p], r6.at[slot, p], seconds[p])

    def back_first(k, p):
        slot = lax.rem(k, SLOTS)
        if p == 0:
            ref = fin.at[lax.div(k, SECTION), x, :, :, fin_cols(k, p * HALF, HALF)]
        else:
            ref = fin.at[lax.div(k, SECTION), :, y, :, fin_cols(k, p * HALF, HALF)]
        return remote(ref, ref, s7.at[slot, p], r7.at[slot, p], firsts[p])

    def small_copy(step):
        to = (
            over_core, over_x, over_y, on_z(lax.rem(z + 1, 4)), on_z(lax.rem(z + 2, 4)),
            on_z(lax.rem(z + 3, 4)),
        )[step]
        return remote(small_out, sin.at[step], sms.at[step], smr.at[step], to)

    def tick(t, carry):
        def stage(lag):
            return (t >= lag) & (t < lag + CHUNKS)

        @pl.when(stage(7))
        def _():
            for p in range(2):
                back_first(t - 7, p).wait()

        @pl.when(stage(6))
        def _():
            for p in range(2):
                back_second(t - 6, p).wait()
                back_first(t - 6, p).start()

        @pl.when(stage(5))
        def _():
            k = t - 5
            duo = lax.rem(k, 2)
            for p in range(2):
                second_copy(k, p).wait()
                total = held[duo, p, y if p == 0 else x] + ry[duo, p]
                fin[lax.div(k, SECTION), x, y, :, fin_cols(k, p * HALF, HALF)] = total
                back_second(k, p).start()

        @pl.when(stage(4) & outer)
        def _():
            k = t - 4
            slot, duo = lax.rem(k, SLOTS), lax.rem(k, 2)
            for p in range(2):
                out_copy(k, p, 0).wait_recv()
                out_copy(k, p, 2).wait_recv()
                for i in range(2):
                    own = (
                        pt[slot, z, core, x, i, :, cols[p]]
                        if p == 0
                        else pt[slot, z, core, i, y, :, cols[p]]
                    )
                    held[duo, p, i] = own + rf[slot, 0, p, i] + rf[slot, 1, p, i]

        @pl.when(stage(4) & inner)
        def _():
            k = t - 4
            slot, duo = lax.rem(k, SLOTS), lax.rem(k, 2)
            for p in range(2):
                out_copy(k, p, 1).wait()
                out_copy(k, p, 0).wait_send()
                out_copy(k, p, 2).wait_send()
                for i in range(2):
                    own = (
                        pt[slot, z, core, x, i, :, cols[p]]
                        if p == 0
                        else pt[slot, z, core, i, y, :, cols[p]]
                    )
                    held[duo, p, i] = own + rf[slot, 1, p, i]

        @pl.when(stage(4))
        def _():
            for p in range(2):
                second_copy(t - 4, p).start()

        @pl.when(stage(3) & outer)
        def _():
            for p in range(2):
                in_copy(t - 3, p).wait_send()

        @pl.when(stage(3) & inner)
        def _():
            k = t - 3
            slot, duo = lax.rem(k, SLOTS), lax.rem(k, 2)
            for p in range(2):
                in_copy(k, p).wait_recv()
                for q in range(3):
                    for i in range(2):
                        if p == 0:
                            pt[slot, beyond + q, core, x, i, :, cols[p]] += rz[duo, p, q, i]
                        else:
                            pt[slot, beyond + q, core, i, y, :, cols[p]] += rz[duo, p, q, i]
                for kind in (2, 1, 0):
                    out_copy(k, p, kind).start()

        @pl.when(stage(2))
        def _():
            k = t - 2
            slot, duo = lax.rem(k, SLOTS), lax.rem(k, 2)
            for p in range(2):
                first_copy(k, p).wait()
                for q in range(4):
                    for i in range(2):
                        if p == 0:
                            pt[slot, q, core, x, i, :, cols[p]] += rx[duo, p, q, i]
                        else:
                            pt[slot, q, core, i, y, :, cols[p]] += rx[duo, p, q, i]

                @pl.when(outer)
                def _():
                    in_copy(k, p).start()

        @pl.when(stage(1))
        def _():
            k = t - 1
            slot, duo = lax.rem(k, SLOTS), lax.rem(k, 2)
            core_copy(k).wait()
            for q in range(4):
                pt[slot, q, core] += rb[duo, q]
            for p in range(2):
                first_copy(k, p).start()

        slot = lax.rem(t, SLOTS)

        def put(owner, cs, block):
            for i in range(2):
                for j in range(2):
                    at = (i * 2 + j) * 24
                    pt[slot, owner // 2, owner % 2, i, j, :, cs] = block[at : at + 24, :]

        pieces = CHUNK // 128
        turns = 8 // pieces

        @pl.when(t < SECTION)
        def _():
            j = lax.div(t, turns)
            count = pieces * BLOCK
            left = nlT[pl.ds(pl.multiple_of(lax.rem(t, turns) * count, count), count), :]
            for owner in range(8):
                cs = pl.ds(pl.multiple_of(owner * 384 + j * 128, 128), 128)
                got = dot_nn(left, act[:, cs])
                for part in range(pieces):
                    put(owner, pl.ds(part * 128, 128), got[part * BLOCK : (part + 1) * BLOCK, :])

        def whole(left, right, half):
            got = dot_nn(left, right)
            for owner in range(8):
                put(owner, pl.ds(half * 256, 256), got[owner * BLOCK : (owner + 1) * BLOCK, :])

        for half in range(CHUNK // 256):

            @pl.when((t >= SECTION) & (t < 2 * SECTION))
            def _():
                cs = pl.ds(pl.multiple_of((t - SECTION) * CHUNK + half * 256, 256), 256)
                whole(wlT[...], wg[:, cs], half)

            part = (t - 2 * SECTION) * (CHUNK // 256) + half

            @pl.when((part >= 0) & (part < 3))
            def _():
                whole(clT[...], low[:, pl.ds(pl.multiple_of(part * 256, 256), 256)], half)

            @pl.when((part >= 3) & (part < 12))
            def _():
                whole(xlT[...], qkv[:, pl.ds(pl.multiple_of((part - 3) * 256, 256), 256)], half)

        @pl.when(t < CHUNKS)
        def _():
            core_copy(t).start()

        units = 12 // SECTION
        begin = SECTION + 1

        @pl.when(t < SECTION)
        def _():
            feed_back(t)

        @pl.when(t == SECTION)
        def _():
            for slot in range(2):
                scores_copy(slot, slot).start()
            loop(4, 128, norm_one_back)
            loop(3, 256, mix_back)

        @pl.when((t >= begin) & (t < begin + SECTION))
        def _():
            for index in range(units):
                u = (t - begin) * units + index
                at = lax.rem(u, 2)
                scores_copy(u, at).wait()
                attend_pair_back(u, at)

                @pl.when(u < 10)
                def _():
                    scores_copy(u + 2, at).start()

        done = begin + SECTION

        @pl.when((t >= done) & (t < done + 3))
        def _():
            input_back(pl.multiple_of((t - done) * 256, 256))

        @pl.when(t == done + 3)
        def _():
            close_sums()
            small_copy(0).start()

        @pl.when(t == done + 4)
        def _():
            small_copy(0).wait()
            small_out[...] += sin[0]
            small_copy(1).start()

        @pl.when(t == done + 5)
        def _():
            small_copy(1).wait()
            small_out[...] += sin[1]
            small_copy(2).start()

        @pl.when(t == done + 6)
        def _():
            small_copy(2).wait()
            small_out[...] += sin[2]
            for step in (3, 4, 5):
                small_copy(step).start()

        @pl.when(t == done + 7)
        def _():
            for step in (3, 4, 5):
                small_copy(step).wait()
            small_out[...] = small_out[...] + sin[3] + sin[4] + sin[5]

        return carry

    lax.fori_loop(0, CHUNKS + 7, tick, 0)


def layer(*args):
    vm = pl.BlockSpec(memory_space=pltpu.VMEM)
    sm = pl.BlockSpec(memory_space=pltpu.SMEM)
    sds = jax.ShapeDtypeStruct
    dma = pltpu.SemaphoreType.DMA
    return pl.pallas_call(
        layer_kernel,
        out_shape=(
            sds((ROWS, D), bf16),
            sds((ROWS, D), f32),
            sds((3, 2, 2, 24, FF), f32),
            sds((16, D), f32),
        ),
        in_specs=[sm] * 3 + [vm] * 8 + [pl.BlockSpec(memory_space=pl.ANY)] * 5,
        out_specs=(vm,) * 4,
        scratch_shapes=[
            pltpu.VMEM((8, 72, D), jnp.int32),
            pltpu.VMEM((8, 32, 128), f32),
            pltpu.VMEM((8, BLOCK, 128), f32),
            pltpu.VMEM((128, 128), f32),
            pltpu.VMEM((D, 3 * D), bf16),
            pltpu.VMEM((D, D), bf16),
            pltpu.VMEM((D, FF), bf16),
            pltpu.VMEM((FF, D), bf16),
            pltpu.VMEM((16, D), f32),
            pltpu.VMEM((8, 3 * D), f32),
            pltpu.VMEM((8, FF), f32),
            pltpu.VMEM((ROWS, 3 * D), bf16),
            pltpu.VMEM((ROWS, D), bf16),
            pltpu.VMEM((ROWS, D), f32),
            pltpu.VMEM((ROWS, D), f32),
            pltpu.VMEM((ROWS, 128), f32),
            pltpu.VMEM((ROWS, FF), f32),
            pltpu.VMEM((ROWS, FF), bf16),
            pltpu.VMEM((ROWS, FF), bf16),
            pltpu.VMEM((ROWS, D), f32),
            pltpu.VMEM((ROWS, D), bf16),
            pltpu.VMEM((2, 256, 256), f32),
            pltpu.VMEM((2, 256, 256), f32),
            pltpu.VMEM((D, ROWS), bf16),
            pltpu.VMEM((D, ROWS), bf16),
            pltpu.VMEM((D, ROWS), bf16),
            pltpu.VMEM((D, ROWS), bf16),
            pltpu.VMEM((24, D), f32),
            pltpu.VMEM((2, 2, 256, 256), bf16),
            pltpu.VMEM((SLOTS, 4, 2, 2, 2, 24, CHUNK), f32),
            pltpu.VMEM((2, 4, 2, 2, 24, CHUNK), f32),
            pltpu.VMEM((2, 2, 4, 2, 24, HALF), f32),
            pltpu.VMEM((2, 2, 3, 2, 24, HALF), f32),
            pltpu.VMEM((SLOTS, 2, 2, 2, 24, HALF), f32),
            pltpu.VMEM((2, 2, 2, 24, HALF), f32),
            pltpu.VMEM((2, 2, 24, HALF), f32),
            pltpu.VMEM((6, 16, D), f32),
        ]
        + [dma((SLOTS,))] * 2
        + [dma((SLOTS, 2))] * 4
        + [dma((SLOTS, 3, 2)), dma((SLOTS, 2, 2))]
        + [dma((SLOTS, 2))] * 6
        + [dma((6,))] * 2
        + [dma((2,)), dma((2, 4)), dma((4, 3)), dma((4, 3)), dma((4, 4)), dma((4, 4))],
        compiler_params=pltpu.CompilerParams(collective_id=0, has_side_effects=True, vmem_limit_bytes=LAYER_CAP),
        name="layer",
    )(*args)


def finish_kernel(
    count, fin, small, tl, ml, wl, nl,
    tg, mg, wg, ng, tb, mb, wb, nb, gain, shift, clips, loss,
    fbuf, tin, min_, win, nin, tout, mout, wout, nout, fsem, isem, osem,
):
    fcopies = [pltpu.make_async_copy(fin.at[i], fbuf.at[i], fsem.at[i]) for i in range(3)]
    icopies, ocopies = [], []
    for half in range(2):
        for index, (src, dst) in enumerate(((nl, nin), (wl, win), (ml, min_), (tl, tin))):
            at = index * 2 + half
            icopies.append(pltpu.make_async_copy(src.at[half], dst.at[half], isem.at[at]))
    for half in range(2):
        for index, (src, dst) in enumerate(((nout, ng), (wout, wg), (mout, mg), (tout, tg))):
            at = index * 2 + half
            ocopies.append(pltpu.make_async_copy(src.at[half], dst.at[half], osem.at[at]))
    for index in range(4):
        if index < 3:
            fcopies[index].start()
        icopies[index].start()
        icopies[index + 4].start()
    me = lax.axis_index("fsdp")
    z = lax.div(me, 2)
    core = lax.rem(me, 2)
    own = pltpu.roll(small[...], lax.rem(8 - me, 8) * BLOCK, 1)
    tb[...] = own[0:3, 0:BLOCK]
    mb[...] = own[3:4, 0:BLOCK]
    nb[...] = own[4:5, 0:BLOCK]
    gain[...] = own[5:7, 0:BLOCK]
    shift[...] = own[7:9, 0:BLOCK]
    wide = pltpu.roll(small[...], core * (4 * BLOCK), 1)
    row = lax.broadcasted_iota(jnp.int32, (16, D), 0)
    picked = jnp.sum(jnp.where(row == 9 + z, wide, 0.0), axis=0, keepdims=True)
    wb[...] = picked[:, 0 : 4 * BLOCK]
    line = small[13:14, :]
    lane = lax.broadcasted_iota(jnp.int32, (1, D), 1)
    for spot in range(4):
        clips[spot] = jnp.sum(jnp.where(lane == spot, line, 0.0))
    loss[0, 0] = jnp.sum(jnp.where(lane == 4, line, 0.0)) * count[0]

    def keep(latent, total, fan):
        return jnp.where(jnp.abs(latent) <= 1.0, total * (1.0 / math.sqrt(fan)), 0.0)

    def arrived(index):
        icopies[index].wait()
        icopies[index + 4].wait()

    def leave(index):
        ocopies[index].start()
        ocopies[index + 4].start()

    fcopies[0].wait()
    arrived(0)
    for j in range(3):
        for i in range(2):
            tiles = range((j * 2 + i) * 4, (j * 2 + i) * 4 + 4)
            parts = [fbuf[0, :, tile * 128 : (tile + 1) * 128] for tile in tiles]
            total = jnp.concatenate(parts, axis=0).T
            rows = slice(j * 128, (j + 1) * 128)
            cols = slice(i * 384, (i + 1) * 384)
            for half in range(2):
                nout[half, rows, cols] = keep(nin[half, rows, cols], total, FF)
    leave(0)
    fcopies[1].wait()
    arrived(1)
    for half in range(2):
        wout[half] = keep(win[half], fbuf[1], D)
    leave(1)
    fcopies[2].wait()
    arrived(2)
    for half in range(2):
        mout[half] = keep(min_[half], fbuf[2, :, 0:D], D)
    leave(2)
    arrived(3)
    for half in range(2):
        tout[half] = keep(tin[half], fbuf[2, :, D:], D)
    leave(3)
    for copy in ocopies:
        copy.wait()


def finish(count, fin, small, tl, ml, wl, nl):
    vm = pl.BlockSpec(memory_space=pltpu.VMEM)
    sm = pl.BlockSpec(memory_space=pltpu.SMEM)
    hbm = pl.BlockSpec(memory_space=pl.ANY)
    sds = jax.ShapeDtypeStruct
    shapes = [v.shape for v in (tl, ml, wl, nl)]
    dma = pltpu.SemaphoreType.DMA
    return pl.pallas_call(
        finish_kernel,
        out_shape=[sds(v, f32) for v in shapes]
        + [
            sds((3, BLOCK), f32), sds((1, BLOCK), f32), sds((1, 4 * BLOCK), f32),
            sds((1, BLOCK), f32), sds((2, BLOCK), f32), sds((2, BLOCK), f32),
            sds((4,), f32), sds((1, 1), f32),
        ],
        in_specs=[sm, hbm, vm] + [hbm] * 4,
        out_specs=[hbm] * 4 + [vm] * 6 + [sm] * 2,
        scratch_shapes=[pltpu.VMEM((3, BLOCK, FF), f32)]
        + [pltpu.VMEM(v, f32) for v in shapes] * 2
        + [dma((3,)), dma((8,)), dma((8,))],
        compiler_params=pltpu.CompilerParams(vmem_limit_bytes=VMEM_CAP),
        name="finish",
    )(count, fin, small, tl, ml, wl, nl)


def on_device_fast(
    hidden_in, teacher_hidden, teacher_scores, seq_lengths, live_counts, triple_latent,
    mixing_latent, widen_latent, narrow_latent, triple_bias, mixing_bias, widen_bias, narrow_bias,
    norm_gain, norm_shift, clip_level,
):
    out, input_grad, fin, small_sum = layer(
        seq_lengths, live_counts, clip_level, triple_bias, mixing_bias[None], widen_bias[None],
        narrow_bias[None], norm_gain, norm_shift, hidden_in, teacher_hidden,
        jnp.transpose(teacher_scores, (1, 0, 2)), triple_latent, mixing_latent, widen_latent,
        narrow_latent,
    )
    fin = fin.reshape(3, BLOCK, FF)
    tokens = hidden_in.shape[0] * lax.axis_size("dp") * lax.axis_size("fsdp")
    count = jnp.full((1,), 1.0 / (tokens * D), f32)
    tg, mg, wg, ng, tb, mb, wb, nb, gain, shift, clips, loss = finish(
        count, fin, small_sum, triple_latent, mixing_latent, widen_latent, narrow_latent
    )
    return (
        out, loss.reshape(()), input_grad, tg, mg, wg, ng, tb, mb.reshape(BLOCK),
        wb.reshape(4 * BLOCK), nb.reshape(BLOCK), gain, shift, clips,
    )


def solution(mesh):
    in_specs = (
        P(("dp", "fsdp"), None),
        P(("dp", "fsdp"), None),
        P(("dp", "fsdp"), None, None),
        P(("dp", "fsdp"), None),
        P(("dp", "fsdp"), None),
        P(None, "fsdp", None),
        P(None, "fsdp", None),
        P(None, "fsdp", None),
        P(None, "fsdp", None),
        P(None, "fsdp"),
        P("fsdp"),
        P("fsdp"),
        P("fsdp"),
        P(None, "fsdp"),
        P(None, "fsdp"),
        P(),
    )
    out_specs = (
        P(("dp", "fsdp"), None),
        P(),
        P(("dp", "fsdp"), None),
        P(None, "fsdp", None),
        P(None, "fsdp", None),
        P(None, "fsdp", None),
        P(None, "fsdp", None),
        P(None, "fsdp"),
        P("fsdp"),
        P("fsdp"),
        P("fsdp"),
        P(None, "fsdp"),
        P(None, "fsdp"),
        P(),
    )
    fits = mesh.shape["dp"] == 4 and mesh.shape["fsdp"] == 8
    return jax.shard_map(
        on_device_fast if fits else on_device, mesh=mesh, in_specs=in_specs, out_specs=out_specs, check_vma=False
    )
```

```python
import math

import jax
import jax.numpy as jnp
from jax import lax
from jax.experimental import pallas as pl
from jax.experimental.pallas import tpu as pltpu
from jax.sharding import PartitionSpec as P

D = 768
HEADS = 12
HEAD_DIM = 64
FF = 3072
LONG_LEN = 256
MID_LEN = 128
SHORT_LEN = 64
LONG_SLOTS = 1
MID_SLOTS = 1
SHORT_SLOTS = 2


bit_count = 32
norm_epsilon = 1e-12
masked_fill = -1e30


def soft_clip(values, clip_at):
    return clip_at * jnp.tanh(values / clip_at)


def layer_norm(values, gain_row, shift_row):
    center = values - jnp.mean(values, axis=-1, keepdims=True)
    variance = jnp.mean(center * center, axis=-1, keepdims=True)
    return center * lax.rsqrt(variance + norm_epsilon) * gain_row + shift_row


def gelu_exact(values):
    return 0.5 * values * (1.0 + lax.erf(values * (1.0 / math.sqrt(2.0))))


def pack_signs(latent):
    halves, row_count, columns = latent.shape
    sign_bits = (
        (latent > 0).astype(jnp.int32).reshape(halves, row_count, columns // bit_count, bit_count)
    )
    places = jnp.arange(bit_count, dtype=jnp.int32)
    return jnp.sum(jnp.left_shift(sign_bits, places), axis=-1, dtype=jnp.int32)


def unpack_weight(sign_words, scales):
    halves, row_count, word_count = sign_words.shape
    places = jnp.arange(bit_count, dtype=jnp.int32)
    sign_bits = jnp.bitwise_and(jnp.right_shift(sign_words[..., None], places), 1)
    sign_values = (
        (2 * sign_bits - 1).astype(jnp.float32).reshape(halves, row_count, word_count * bit_count)
    )
    return (scales[0][:, None] * sign_values[0] + scales[1][:, None] * sign_values[1]).astype(
        jnp.bfloat16
    )


def bucket_shapes():
    return ((LONG_SLOTS, LONG_LEN), (MID_SLOTS, MID_LEN), (SHORT_SLOTS, SHORT_LEN))


def bucket_masks(lengths, live_count, slot_count, bucket_len):
    places = jnp.arange(bucket_len, dtype=jnp.int32)
    key_ok = places[None, :] < lengths[:, None]
    query_ok = jnp.logical_and(
        key_ok, jnp.arange(slot_count, dtype=jnp.int32)[:, None] < live_count
    )
    return (key_ok, query_ok)


def split_heads(block, slot_count, bucket_len):
    return block.reshape(slot_count, bucket_len, HEADS, HEAD_DIM)


def bucket_scores(qkv_rows, teacher_rows, key_ok, query_ok, slot_count, bucket_len):
    queries = split_heads(qkv_rows[:, :D], slot_count, bucket_len)
    keys_part = split_heads(qkv_rows[:, D : 2 * D], slot_count, bucket_len)
    scores = jnp.einsum(
        "sqhd,skhd->shqk", queries, keys_part, preferred_element_type=jnp.float32
    ) * HEAD_DIM ** (-0.5)
    masked = jnp.where(key_ok[:, None, None, :], scores, masked_fill)
    teacher = jnp.transpose(
        teacher_rows.reshape(slot_count, bucket_len, HEADS, LONG_LEN)[..., :bucket_len],
        (0, 2, 1, 3),
    ).astype(jnp.float32)
    pair_ok = jnp.logical_and(query_ok[:, None, :, None], key_ok[:, None, None, :])
    score_gap = jnp.where(pair_ok, scores - teacher, 0.0)
    return (queries, keys_part, masked, score_gap)


def attend(qkv_rows, teacher_rows, key_ok, query_ok, slot_count, bucket_len):
    queries, keys_part, masked, score_gap = bucket_scores(
        qkv_rows, teacher_rows, key_ok, query_ok, slot_count, bucket_len
    )
    values_part = split_heads(qkv_rows[:, 2 * D :], slot_count, bucket_len)
    row_top = jnp.max(masked, axis=-1, keepdims=True)
    exponent = jnp.exp(masked - row_top)
    exp_total = jnp.sum(exponent, axis=-1, keepdims=True)
    attention = exponent / exp_total
    context = jnp.einsum(
        "shqk,skhd->sqhd",
        attention.astype(jnp.bfloat16),
        values_part,
        preferred_element_type=jnp.float32,
    )
    distill = 0.5 / LONG_LEN * jnp.sum(score_gap * score_gap)
    return (context.reshape(slot_count * bucket_len, D), row_top + jnp.log(exp_total), distill)


def attend_back(
    qkv_rows, teacher_rows, key_ok, query_ok, slot_count, bucket_len, log_total, context_grad
):
    queries, keys_part, masked, score_gap = bucket_scores(
        qkv_rows, teacher_rows, key_ok, query_ok, slot_count, bucket_len
    )
    values_part = split_heads(qkv_rows[:, 2 * D :], slot_count, bucket_len)
    attention = jnp.exp(masked - log_total)
    grad_heads = split_heads(context_grad, slot_count, bucket_len)
    values_grad = jnp.einsum(
        "shqk,sqhd->skhd",
        attention.astype(jnp.bfloat16),
        grad_heads,
        preferred_element_type=jnp.float32,
    )
    weight_grad = jnp.einsum(
        "sqhd,skhd->shqk", grad_heads, values_part, preferred_element_type=jnp.float32
    )
    score_grad = attention * (
        weight_grad - jnp.sum(weight_grad * attention, axis=-1, keepdims=True)
    ) + score_gap * (1.0 / LONG_LEN)
    score_low = score_grad.astype(jnp.bfloat16)
    score_scale = HEAD_DIM ** (-0.5)
    queries_grad = (
        jnp.einsum("shqk,skhd->sqhd", score_low, keys_part, preferred_element_type=jnp.float32)
        * score_scale
    )
    keys_grad = (
        jnp.einsum("shqk,sqhd->skhd", score_low, queries, preferred_element_type=jnp.float32)
        * score_scale
    )
    row_count = slot_count * bucket_len
    return jnp.concatenate(
        [
            queries_grad.reshape(row_count, D),
            keys_grad.reshape(row_count, D),
            values_grad.reshape(row_count, D),
        ],
        axis=-1,
    )


def on_device(
    hidden_in,
    teacher_hidden,
    teacher_scores,
    seq_lengths,
    live_counts,
    triple_latent,
    mixing_latent,
    widen_latent,
    narrow_latent,
    triple_bias,
    mixing_bias,
    widen_bias,
    narrow_bias,
    norm_gain,
    norm_shift,
    clip_level,
):
    latents = (triple_latent, mixing_latent, widen_latent, narrow_latent)
    fan_ins = (D, D, D, FF)
    own_scales = tuple(
        (
            jnp.mean(jnp.abs(latent), axis=-1) / math.sqrt(fan_in)
            for latent, fan_in in zip(latents, fan_ins)
        )
    )
    packed = tuple((pack_signs(latent) for latent in latents))
    gathered = (
        lax.all_gather(packed[0], "fsdp", axis=1, tiled=True),
        lax.all_gather(packed[1], "fsdp", axis=1, tiled=True),
        lax.all_gather(packed[2], "fsdp", axis=1, tiled=True),
        lax.all_gather(packed[3], "fsdp", axis=1, tiled=True),
    )
    factors = (
        lax.all_gather(own_scales[0], "fsdp", axis=1, tiled=True),
        lax.all_gather(own_scales[1], "fsdp", axis=1, tiled=True),
        lax.all_gather(own_scales[2], "fsdp", axis=1, tiled=True),
        lax.all_gather(own_scales[3], "fsdp", axis=1, tiled=True),
        lax.all_gather(triple_bias, "fsdp", axis=1, tiled=True),
        lax.all_gather(mixing_bias, "fsdp", axis=0, tiled=True),
        lax.all_gather(widen_bias, "fsdp", axis=0, tiled=True),
        lax.all_gather(narrow_bias, "fsdp", axis=0, tiled=True),
        lax.all_gather(norm_gain, "fsdp", axis=1, tiled=True),
        lax.all_gather(norm_shift, "fsdp", axis=1, tiled=True),
    )
    scales = factors[:4]
    triple_rows, full_mixing_bias, full_widen_bias, full_narrow_bias, gains, shifts = factors[4:]
    full_triple_bias = triple_rows.reshape(3 * D)
    weights = tuple(
        (unpack_weight(words_part, scale_part) for words_part, scale_part in zip(gathered, scales))
    )
    inputs = hidden_in.astype(jnp.float32)
    inputs_low = soft_clip(inputs, clip_level[0]).astype(jnp.bfloat16)
    qkv_all = (
        jnp.dot(inputs_low, weights[0], preferred_element_type=jnp.float32) + full_triple_bias
    ).astype(jnp.bfloat16)
    lengths = seq_lengths[0]
    counts = live_counts[0]
    plans = []
    row_start = 0
    slot_start = 0
    for bucket, shape_pair in enumerate(bucket_shapes()):
        slot_count, bucket_len = shape_pair
        key_ok, query_ok = bucket_masks(
            lengths[slot_start : slot_start + slot_count], counts[bucket], slot_count, bucket_len
        )
        plans.append(
            (
                row_start,
                row_start + slot_count * bucket_len,
                slot_count,
                bucket_len,
                key_ok,
                query_ok,
            )
        )
        row_start = row_start + slot_count * bucket_len
        slot_start = slot_start + slot_count
    contexts = []
    log_totals = []
    distill_sum = 0.0
    for plan in plans:
        row_begin, row_end, slot_count, bucket_len, key_ok, query_ok = plan
        context, log_total, distill = attend(
            qkv_all[row_begin:row_end],
            teacher_scores[row_begin:row_end],
            key_ok,
            query_ok,
            slot_count,
            bucket_len,
        )
        contexts.append(context)
        log_totals.append(log_total)
        distill_sum = distill_sum + distill
    context = jnp.concatenate(contexts, axis=0)
    token_ok = jnp.concatenate([plan[5].reshape(-1) for plan in plans])
    context_low = soft_clip(context, clip_level[1]).astype(jnp.bfloat16)
    mixed = jnp.dot(context_low, weights[1], preferred_element_type=jnp.float32) + full_mixing_bias
    first_sum = inputs + mixed
    first_norm = layer_norm(first_sum, gains[0], shifts[0])
    widen_low = soft_clip(first_norm, clip_level[2]).astype(jnp.bfloat16)
    widened = jnp.dot(widen_low, weights[2], preferred_element_type=jnp.float32) + full_widen_bias
    activated = gelu_exact(widened)
    activated_low = soft_clip(activated, clip_level[3]).astype(jnp.bfloat16)
    narrowed = (
        jnp.dot(activated_low, weights[3], preferred_element_type=jnp.float32) + full_narrow_bias
    )
    second_sum = first_norm + narrowed
    out_full = layer_norm(second_sum, gains[1], shifts[1])
    out_gap = jnp.where(token_ok[:, None], out_full - teacher_hidden.astype(jnp.float32), 0.0)
    loss_local = 0.5 * jnp.sum(out_gap * out_gap) + distill_sum
    regathered = (
        lax.all_gather(packed[0], "fsdp", axis=1, tiled=True),
        lax.all_gather(packed[1], "fsdp", axis=1, tiled=True),
        lax.all_gather(packed[2], "fsdp", axis=1, tiled=True),
        lax.all_gather(packed[3], "fsdp", axis=1, tiled=True),
    )
    back_weights = tuple(
        (
            unpack_weight(words_part, scale_part)
            for words_part, scale_part in zip(regathered, scales)
        )
    )
    _, second_back = jax.vjp(layer_norm, second_sum, gains[1], shifts[1])
    second_grad, gain_two, shift_two = second_back(out_gap)
    narrow_low = second_grad.astype(jnp.bfloat16)
    narrow_weight_grad = jnp.einsum(
        "rf,rd->fd", activated_low, narrow_low, preferred_element_type=jnp.float32
    )
    act_low_grad = jnp.einsum(
        "rd,fd->rf", narrow_low, back_weights[3], preferred_element_type=jnp.float32
    )
    _, clip_three_back = jax.vjp(soft_clip, activated, clip_level[3])
    act_grad, clip_three = clip_three_back(act_low_grad)
    _, gelu_back = jax.vjp(gelu_exact, widened)
    (widened_grad,) = gelu_back(act_grad)
    widen_grad_low = widened_grad.astype(jnp.bfloat16)
    widen_weight_grad = jnp.einsum(
        "rd,rf->df", widen_low, widen_grad_low, preferred_element_type=jnp.float32
    )
    norm_low_grad = jnp.einsum(
        "rf,df->rd", widen_grad_low, back_weights[2], preferred_element_type=jnp.float32
    )
    _, clip_two_back = jax.vjp(soft_clip, first_norm, clip_level[2])
    norm_grad, clip_two = clip_two_back(norm_low_grad)
    norm_grad = norm_grad + second_grad
    _, first_back = jax.vjp(layer_norm, first_sum, gains[0], shifts[0])
    first_grad, gain_one, shift_one = first_back(norm_grad)
    mixed_low = first_grad.astype(jnp.bfloat16)
    mixing_weight_grad = jnp.einsum(
        "rc,rd->cd", context_low, mixed_low, preferred_element_type=jnp.float32
    )
    context_low_grad = jnp.einsum(
        "rd,cd->rc", mixed_low, back_weights[1], preferred_element_type=jnp.float32
    )
    _, clip_one_back = jax.vjp(soft_clip, context, clip_level[1])
    context_grad, clip_one = clip_one_back(context_low_grad)
    context_grad_low = context_grad.astype(jnp.bfloat16)
    qkv_grads = []
    for plan, log_total in zip(plans, log_totals):
        row_begin, row_end, slot_count, bucket_len, key_ok, query_ok = plan
        qkv_grads.append(
            attend_back(
                qkv_all[row_begin:row_end],
                teacher_scores[row_begin:row_end],
                key_ok,
                query_ok,
                slot_count,
                bucket_len,
                log_total,
                context_grad_low[row_begin:row_end],
            )
        )
    qkv_grad_low = jnp.concatenate(qkv_grads, axis=0).astype(jnp.bfloat16)
    triple_weight_grad = jnp.einsum(
        "rd,re->de", inputs_low, qkv_grad_low, preferred_element_type=jnp.float32
    )
    input_low_grad = jnp.einsum(
        "re,de->rd", qkv_grad_low, back_weights[0], preferred_element_type=jnp.float32
    )
    _, clip_zero_back = jax.vjp(soft_clip, inputs, clip_level[0])
    input_side, clip_zero = clip_zero_back(input_low_grad)
    input_grad = input_side + first_grad
    bias_sums = (
        jnp.sum(qkv_grad_low, axis=0, dtype=jnp.float32).reshape(3, D),
        jnp.sum(mixed_low, axis=0, dtype=jnp.float32),
        jnp.sum(widen_grad_low, axis=0, dtype=jnp.float32),
        jnp.sum(narrow_low, axis=0, dtype=jnp.float32),
    )
    row_shares = (
        lax.psum_scatter(triple_weight_grad, "fsdp", scatter_dimension=0, tiled=True),
        lax.psum_scatter(mixing_weight_grad, "fsdp", scatter_dimension=0, tiled=True),
        lax.psum_scatter(widen_weight_grad, "fsdp", scatter_dimension=0, tiled=True),
        lax.psum_scatter(narrow_weight_grad, "fsdp", scatter_dimension=0, tiled=True),
    )
    totals = lax.psum((row_shares[0], row_shares[1], row_shares[2], row_shares[3]), "dp")
    small_sums = lax.psum(
        (
            bias_sums[0],
            bias_sums[1],
            bias_sums[2],
            bias_sums[3],
            jnp.stack([gain_one, gain_two]),
            jnp.stack([shift_one, shift_two]),
            jnp.stack([clip_zero, clip_one, clip_two, clip_three]),
            loss_local,
        ),
        ("dp", "fsdp"),
    )
    shard_index = lax.axis_index("fsdp")
    shard_parts = lax.axis_size("fsdp")

    def own_part(vector, along):
        share_width = vector.shape[along] // shard_parts
        return lax.dynamic_slice_in_dim(vector, shard_index * share_width, share_width, along)

    latent_grads = tuple(
        (
            jnp.where(jnp.abs(latent) <= 1.0, (total / math.sqrt(fan_in))[None], 0.0)
            for latent, total, fan_in in zip(latents, totals, fan_ins)
        )
    )
    loss = small_sums[7] / (hidden_in.shape[0] * D * lax.axis_size("dp") * shard_parts)
    return (
        out_full.astype(jnp.bfloat16),
        loss,
        input_grad,
        latent_grads[0],
        latent_grads[1],
        latent_grads[2],
        latent_grads[3],
        own_part(small_sums[0], 1),
        own_part(small_sums[1], 0),
        own_part(small_sums[2], 0),
        own_part(small_sums[3], 0),
        own_part(small_sums[4], 1),
        own_part(small_sums[5], 1),
        small_sums[6],
    )


bf16 = jnp.bfloat16
f32 = jnp.float32
MESH = pl.DeviceIdType.MESH
VMEM_CAP = 60 * 1024 * 1024
LAYER_CAP = 63 * 1024 * 1024
ROWS = LONG_SLOTS * LONG_LEN + MID_SLOTS * MID_LEN + SHORT_SLOTS * SHORT_LEN
BLOCK = 96
CHUNK = 512
HALF = CHUNK // 2
SECTION = FF // CHUNK
WIDE = 3 * SECTION - 1
CHUNKS = WIDE + 2
SLOTS = 4


def dot_nn(a, b):
    return lax.dot_general(a, b, (((1,), (0,)), ((), ())), preferred_element_type=f32)


def dot_nt(a, b):
    return lax.dot_general(a, b, (((1,), (1,)), ((), ())), preferred_element_type=f32)


def dot_tn(a, b):
    return lax.dot_general(a, b, (((0,), (0,)), ((), ())), preferred_element_type=f32)


def loop(count, step, body):
    def run(i, carry):
        body(pl.multiple_of(i * step, step))
        return carry

    lax.fori_loop(0, count, run, 0)


def plane_of(block, half, group):
    place = block * 24 + half * 12 + group
    bit = place % 32
    return place // 32, (1 << bit) if bit < 31 else -(1 << 31)


def unpack_block(words, scl, block, dst):
    def one(owner, carry):
        unpack_owner(words, scl, block, dst, owner)
        return carry

    lax.fori_loop(0, 8, one, 0)


def unpack_owner(words, scl, block, dst, owner):
    index = 0 if block < 3 else 1 if block == 3 else 2 if block < 8 else block - 5

    for pair in range(6):
        parts = []
        for group in (2 * pair, 2 * pair + 1):
            total = None
            for half in range(2):
                word, bit = plane_of(block, half, group)
                bits = words[owner, word * 8 : (word + 1) * 8, :] & jnp.int32(bit)
                column = index * 2 + half
                scale = jnp.broadcast_to(
                    scl[owner, group * 8 : (group + 1) * 8, column : column + 1], (8, D)
                )
                value = jnp.where(bits != 0, scale, -scale)
                total = value if total is None else total + value
            parts.append(total)
        tile = jnp.concatenate(parts, axis=0).astype(bf16)
        if block < 8:
            start = owner * BLOCK + pair * 16
        else:
            start = owner * (4 * BLOCK) + (block - 8) * BLOCK + pair * 16
        rows = pl.ds(pl.multiple_of(start, 16), 16)
        if block < 3:
            dst[rows, block * D : (block + 1) * D] = tile
        elif block < 8 and block > 3:
            dst[rows, (block - 4) * D : (block - 3) * D] = tile
        else:
            dst[rows, :] = tile


def clip_back(grad, value, level, inverse):
    u = value * inverse
    t = jnp.tanh(u)
    slope = 1.0 - t * t
    return grad * slope, jnp.sum(grad * (t - u * slope), axis=0, keepdims=True)


def norm_rows(v):
    center = v - jnp.mean(v, axis=1, keepdims=True)
    variance = jnp.mean(center * center, axis=1, keepdims=True)
    rstd = lax.rsqrt(variance + norm_epsilon)
    return center * rstd, rstd


def norm_rows_back(grad, hat, rstd, gain_row):
    g = grad * gain_row
    return rstd * (
        g - jnp.mean(g, axis=1, keepdims=True) - hat * jnp.mean(g * hat, axis=1, keepdims=True)
    )


def colsum(v):
    return jnp.sum(v, axis=0, keepdims=True)


HALF_ROOT = 1.0 / math.sqrt(2.0)
DENSITY = 1.0 / math.sqrt(2.0 * math.pi)


def layer_kernel(
    seq, live, level, tb, mb, wb, nb, gain, shift, hid, teach, teach_scores, tl, ml, wl, nl,
    out, acc, fin, small_out,
    words, small, scl, spread,
    wt, wm, ww, wn, prm, bias, wbias, qkv, low, ctx, hat1, rstd1, widened, act, wg, sgrad,
    cgrad, valid, pair, xlT, clT, wlT, nlT, sums, tbuf, pt, rb, rx, rz, rf, held, ry, sin,
    s1, r1, s2, r2, s3, r3, s4, r4, s5, r5, s6, r6, sms, smr, tsem, lsem, zs, zr, cs_, cr_, hsem,
):
    dp = lax.axis_index("dp")
    me = lax.axis_index("fsdp")
    x = lax.rem(dp, 2)
    y = lax.div(dp, 2)
    z = lax.div(me, 2)
    core = lax.rem(me, 2)
    over_x = (dp + 1 - 2 * x, me)
    over_y = (dp + 2 - 4 * y, me)
    over_core = (dp, z * 2 + 1 - core)

    def remote(src, dst, send, recv, to):
        return pltpu.make_async_remote_copy(
            src_ref=src, dst_ref=dst, send_sem=send, recv_sem=recv, device_id=to,
            device_id_type=MESH,
        )

    greet = pltpu.get_barrier_semaphore()
    for to in (over_core, over_x, over_y) + tuple(
        (dp, lax.rem(z + hop, 4) * 2 + core) for hop in (1, 2, 3)
    ):
        pl.semaphore_signal(greet, inc=1, device_id=to, device_id_type=MESH)

    teach_load = pltpu.make_async_copy(teach, cgrad, hsem.at[0])

    loads = []
    for half in range(2):
        band = slice(192 + half * BLOCK, 192 + (half + 1) * BLOCK)
        loads.append([
            pltpu.make_async_copy(tl.at[half], widened.at[band, 0 : 3 * D], lsem.at[half, 0]),
            pltpu.make_async_copy(ml.at[half], widened.at[band, 3 * D : FF], lsem.at[half, 1]),
            pltpu.make_async_copy(
                wl.at[half], widened.at[half * BLOCK : (half + 1) * BLOCK, :], lsem.at[half, 2]
            ),
            pltpu.make_async_copy(
                nl.at[half], (ctx if half == 0 else sgrad).at[0 : 4 * BLOCK, :], lsem.at[half, 3]
            ),
        ])
    for index in range(4):
        for half in range(2):
            loads[half][index].start()
    teach_load.start()

    def latent_piece(block, half, group):
        if block < 4:
            rows = pl.ds(192 + half * BLOCK + group * 8, 8)
            return widened[rows, block * D : (block + 1) * D]
        if block < 8:
            return widened[pl.ds(half * BLOCK + group * 8, 8), (block - 4) * D : (block - 3) * D]
        rows = pl.ds((block - 8) * BLOCK + group * 8, 8)
        return (ctx if half == 0 else sgrad)[rows, :]

    planes = [[] for _ in range(9)]
    for block in range(12):
        for half in range(2):
            for group in range(12):
                word, bit = plane_of(block, half, group)
                planes[word].append((block, half, group, bit))

    def pack(word):
        total = jnp.zeros((8, D), jnp.int32)
        for block, half, group, bit in planes[word]:
            piece = latent_piece(block, half, group)
            total = total | jnp.where(piece > 0, jnp.int32(bit), jnp.int32(0))
        words[me, word * 8 : (word + 1) * 8, :] = total

    def part_of(owner, index):
        return small.at[owner] if index == 3 else words.at[owner, index * 24 : (index + 1) * 24]

    def z_send(index, hop):
        ref = part_of(me, index)
        peer = lax.rem(z + hop, 4) * 2 + core
        return remote(ref, ref, zs.at[index, hop - 1], zr.at[index, hop - 1], (dp, peer))

    def core_send(index, hop):
        ref = part_of(lax.rem(z + 4 - hop, 4) * 2 + core, index)
        return remote(ref, ref, cs_.at[index, hop], cr_.at[index, hop], over_core)

    def send_out(index):
        for hop in (2, 1, 3):
            z_send(index, hop).start()
        core_send(index, 0).start()

    def pass_on(index):
        for hop in (1, 3, 2):
            z_send(index, hop).wait()
            core_send(index, hop).start()

    def all_here(index):
        for hop in range(4):
            core_send(index, hop).wait()

    for half in range(2):
        loads[half][0].wait()
        loads[half][1].wait()
    for word in range(3):
        pack(word)
    pl.semaphore_wait(greet, 6)
    send_out(0)
    for half in range(2):
        loads[half][2].wait()
        loads[half][3].wait()
    slot_lane = lax.broadcasted_iota(jnp.int32, (8, 128), 1)

    def scale_rows(group):
        tile = jnp.zeros((8, 128), f32)
        for half in range(2):
            rows = pl.ds(pl.multiple_of(192 + half * BLOCK + group, 8), 8)
            for index in range(7):
                if index == 0:
                    part = widened[rows, 0 : 3 * D]
                elif index == 1:
                    part = widened[rows, 3 * D : FF]
                elif index == 2:
                    part = widened[pl.ds(pl.multiple_of(half * BLOCK + group, 8), 8), :]
                else:
                    at = pl.ds(pl.multiple_of((index - 3) * BLOCK + group, 8), 8)
                    part = (ctx if half == 0 else sgrad)[at, :]
                fan = FF if index >= 3 else D
                mean = jnp.sum(jnp.abs(part), axis=1, keepdims=True) * (1.0 / part.shape[1])
                tile = jnp.where(slot_lane == index * 2 + half, mean / math.sqrt(fan), tile)
        spread[pl.ds(group, 8), :] = tile

    loop(12, 8, scale_rows)
    spread[BLOCK:128, :] = jnp.zeros((128 - BLOCK, 128), f32)
    small[me, 0:16, :] = spread[...].T[0:16, :]
    small[me, 16:32, :] = jnp.zeros((16, 128), f32)
    small[me, 16:19, 0:BLOCK] = tb[...]
    small[me, 19:20, 0:BLOCK] = mb[...]
    small[me, 20:21, 0:BLOCK] = nb[...]
    small[me, 21:23, 0:BLOCK] = gain[...]
    small[me, 23:25, 0:BLOCK] = shift[...]
    for part in range(3):
        small[me, 25 + part : 26 + part, :] = wb[:, part * 128 : (part + 1) * 128]
    send_out(3)
    for word in range(3, 9):
        pack(word)
    c0, c1, c2, c3 = level[0], level[1], level[2], level[3]
    i0, i1, i2, i3 = 1.0 / c0, 1.0 / c1, 1.0 / c2, 1.0 / c3
    sums[...] = jnp.zeros_like(sums)
    row = lax.broadcasted_iota(jnp.int32, (256, 256), 0)
    col = lax.broadcasted_iota(jnp.int32, (256, 256), 1)
    key_ok = col < seq[0, 0]
    query_ok = row < seq[0, 0] * live[0, 0]
    valid[0] = jnp.where(key_ok, 1.0, 0.0)
    pair[0] = jnp.where(key_ok & query_ok, 1.0, 0.0)

    def in_slots(at):
        mid = (at < 128) & (at < seq[0, 1])
        one = (at >= 128) & (at < 192) & (at - 128 < seq[0, 2])
        two = (at >= 192) & (at - 192 < seq[0, 3])
        return mid, one, two

    km, ko, kt = in_slots(col)
    qm, qo, qt = in_slots(row)
    key_ok = (km & (row < 128)) | (ko & (row >= 128) & (row < 192)) | (kt & (row >= 192))
    live_mid = row * 0 + live[0, 1] > 0
    live_one = row * 0 + live[0, 2] > 0
    live_two = row * 0 + live[0, 2] > 1
    query_ok = (qm & live_mid) | (qo & live_one) | (qt & live_two)
    valid[1] = jnp.where(key_ok, 1.0, 0.0)
    pair[1] = jnp.where(key_ok & query_ok, 1.0, 0.0)
    ones = jnp.where(query_ok, 1.0, 0.0)

    def clip_in(r):
        x = hid[pl.ds(r, 128), :].astype(f32)
        lo = (c0 * jnp.tanh(x * i0)).astype(bf16)
        low[pl.ds(r, 128), :] = lo

    loop(4, 128, clip_in)
    pass_on(3)
    all_here(3)
    total = jnp.zeros((16, D), f32)
    param_lane = lax.broadcasted_iota(jnp.int32, (16, 128), 1)
    for owner in range(8):
        turned = jnp.concatenate([small[owner, 0:16, :], jnp.zeros((112, 128), f32)], axis=0).T
        scl[owner] = turned[0:BLOCK, :]
        piece = jnp.where(param_lane < BLOCK, small[owner, 16:32, :], 0.0)
        wide = jnp.concatenate([piece, jnp.zeros((16, D - 128), f32)], axis=1)
        total = total + (pltpu.roll(wide, owner * BLOCK, 1) if owner else wide)
        for part in range(3):
            at = owner * 4 * BLOCK + part * 128
            wbias[0:1, at : at + 128] = small[owner, 25 + part : 26 + part, :]
    prm[...] = total
    for part in range(3):
        bias[0:1, part * D : (part + 1) * D] = prm[part : part + 1, :]
    def same_core(hop, carry):
        @pl.when(hop > 0)
        def _():
            z_send(0, hop).wait()
            core_send(0, hop).start()

        for block in range(3):
            unpack_owner(words, scl, block, wt, lax.rem(z + 4 - hop, 4) * 2 + core)
        return carry

    def other_core(hop, carry):
        core_send(0, hop).wait()
        for block in range(3):
            unpack_owner(words, scl, block, wt, lax.rem(z + 4 - hop, 4) * 2 + 1 - core)
        return carry

    lax.fori_loop(0, 4, same_core, 0)
    send_out(1)
    lax.fori_loop(0, 4, other_core, 0)

    for part in range(9):
        cs = slice(part * 256, (part + 1) * 256)
        qkv[:, cs] = (dot_nn(low[...], wt[:, cs]) + bias[0:1, cs]).astype(bf16)
    send_out(2)
    lane = lax.broadcasted_iota(jnp.int32, (256, 128), 1)
    first = lane < 64

    def pick(v, j):
        return jnp.where(first, v, jnp.zeros_like(v)) if j == 0 else jnp.where(first, jnp.zeros_like(v), v)

    def softmax(q, k, ok, j):
        s = dot_nt(pick(q, j), k) * (HEAD_DIM**-0.5)
        masked = jnp.where(ok, s, masked_fill)
        e = jnp.exp(masked - jnp.max(masked, axis=1, keepdims=True))
        return s, e / jnp.sum(e, axis=1, keepdims=True)

    for g in range(2):
        for c in range(0, D, 128):
            rs = slice(g * 256, (g + 1) * 256)
            q, k, v = (qkv[rs, at + c : at + c + 128] for at in (0, D, 2 * D))
            ok = valid[g] > 0.5
            parts = []
            for j in range(2):
                s, p = softmax(q, k, ok, j)
                parts.append(dot_nn(p.astype(bf16), v))
            ctx[rs, c : c + 128] = jnp.where(first, parts[0], parts[1])
    pass_on(1)
    unpack_block(words, scl, 3, wm)

    def clip_ctx(r):
        lo = (c1 * jnp.tanh(ctx[pl.ds(r, 128), :] * i1)).astype(bf16)
        low[pl.ds(r, 128), :] = lo

    loop(4, 128, clip_ctx)

    for part in range(3):
        cs = slice(part * 256, (part + 1) * 256)
        acc[:, cs] = dot_nn(low[...], wm[:, cs]) + prm[3:4, cs] + hid[:, cs].astype(f32)

    def norm_one(r):
        rs = pl.ds(r, 128)
        hat, rstd = norm_rows(acc[rs, :])
        hat1[rs, :] = hat
        rstd1[rs, :] = jnp.broadcast_to(rstd, (128, 128))
        normed = hat * prm[5:6, :] + prm[7:8, :]
        lo = (c2 * jnp.tanh(normed * i2)).astype(bf16)
        low[rs, :] = lo
        acc[rs, :] = normed + prm[4:5, :]

    loop(4, 128, norm_one)
    all_here(1)
    pass_on(2)
    for block in range(4, 8):
        unpack_block(words, scl, block, ww)
    all_here(2)
    for block in range(8, 12):
        unpack_block(words, scl, block, wn)

    for t in range(8):
        if t < 6:
            cs = slice(t * 512, (t + 1) * 512)
            widened[:, cs] = dot_nn(low[...], ww[:, cs]) + wbias[0:1, cs]
        if 1 <= t <= 6:
            cs = slice((t - 1) * 512, t * 512)
            for r in range(0, ROWS, 64):
                w = widened[r : r + 64, cs]
                a = 0.5 * w * (1.0 + lax.erf(w * HALF_ROOT))
                act[r : r + 64, cs] = (c3 * jnp.tanh(a * i3)).astype(bf16)
        if t >= 2:
            cs = slice((t - 2) * 512, (t - 1) * 512)
            acc[...] += dot_nn(act[:, cs], wn[cs, :])

    teach_load.wait()

    def norm_two(r):
        rs = pl.ds(r, 128)
        hat, rstd = norm_rows(acc[rs, :])
        full = hat * prm[6:7, :] + prm[8:9, :]
        out[rs, :] = full.astype(bf16)
        at = lax.broadcasted_iota(jnp.int32, (128, D), 0) + r
        l0, l1, l2, l3 = seq[0, 0] * live[0, 0], seq[0, 1], seq[0, 2], seq[0, 3]
        l1 = jnp.where(live[0, 1] > 0, l1, 0)
        l2 = jnp.where(live[0, 2] > 0, l2, 0)
        l3 = jnp.where(live[0, 2] > 1, l3, 0)
        ok = (at < l0) | ((at >= 256) & (at < 256 + l1)) | ((at >= 384) & (at < 384 + l2))
        ok = ok | ((at >= 448) & (at < 448 + l3))
        gap = jnp.where(ok, full - cgrad[rs, :].astype(f32), 0.0)
        sums[15:16, :] += colsum(gap * gap) * 0.5
        sums[6:7, :] += colsum(gap * hat)
        sums[8:9, :] += colsum(gap)
        grad = norm_rows_back(gap, hat, rstd, prm[6:7, :])
        sgrad[rs, :] = grad
        acc[rs, :] = jnp.zeros((128, D), f32)
        lo = grad.astype(bf16)
        low[rs, :] = lo
        nlT[:, rs] = lo.T
        sums[4:5, :] += colsum(lo.astype(f32))

    loop(4, 128, norm_two)

    def feed_back(t):
        cs = pl.ds(pl.multiple_of(t * CHUNK, CHUNK), CHUNK)
        wbias[1:2, cs] = jnp.zeros((1, CHUNK), f32)

        def feed_back_rows(r):
            rs = pl.ds(r, 256)
            g = dot_nt(low[rs, :], wn[cs, :])
            w = widened[rs, cs]
            e = 0.5 * (1.0 + lax.erf(w * HALF_ROOT))
            a = w * e
            u = a * i3
            th = jnp.tanh(u)
            slope = 1.0 - th * th
            sums[14:15, 0:CHUNK] += colsum(g * (th - u * slope))
            back = g * slope * (e + w * (DENSITY * jnp.exp(-0.5 * w * w)))
            lo = back.astype(bf16)
            wg[rs, cs] = lo
            wbias[1:2, cs] += colsum(lo.astype(f32))
            acc[rs, :] += dot_nt(lo, ww[:, cs])

        loop(2, 256, feed_back_rows)

    def turn_widen(r):
        rs = pl.ds(r, 128)
        normed = hat1[rs, :] * prm[5:6, :] + prm[7:8, :]
        wlT[:, rs] = (c2 * jnp.tanh(normed * i2)).astype(bf16).T

    def turn_context(r):
        clT[:, pl.ds(r, 128)] = (c1 * jnp.tanh(ctx[pl.ds(r, 128), :] * i1)).astype(bf16).T

    def turn_inputs(r):
        v = hid[pl.ds(r, 128), :].astype(f32)
        xlT[:, pl.ds(r, 128)] = (c0 * jnp.tanh(v * i0)).astype(bf16).T

    def norm_one_back(r):
        rs = pl.ds(r, 128)
        hat = hat1[rs, :]
        normed = hat * prm[5:6, :] + prm[7:8, :]
        grad, clip_sum = clip_back(acc[rs, :], normed, c2, i2)
        sums[18:19, :] += clip_sum
        grad = grad + sgrad[rs, :]
        sums[5:6, :] += colsum(grad * hat)
        sums[7:8, :] += colsum(grad)
        grad = norm_rows_back(grad, hat, rstd1[rs, 0:1], prm[5:6, :])
        acc[rs, :] = grad
        lo = grad.astype(bf16)
        low[rs, :] = lo
        sums[3:4, :] += colsum(lo.astype(f32))

    def mix_back(c):
        cs = pl.ds(c, 256)
        g = dot_nt(low[...], wm[cs, :])
        grad, clip_sum = clip_back(g, ctx[:, cs], c1, i1)
        sums[17:18, cs] += clip_sum
        cgrad[:, cs] = grad.astype(bf16)

    def scores_copy(u, slot):
        g = lax.div(u, 6)
        hp = lax.rem(u, 6)
        rs = pl.ds(pl.multiple_of(g * 256, 256), 256)
        return pltpu.make_async_copy(
            teach_scores.at[pl.ds(2 * hp, 2), rs], tbuf.at[slot], tsem.at[slot]
        )

    def attend_pair_back(u, slot):
        g = lax.div(u, 6)
        hp = lax.rem(u, 6)
        rs = pl.ds(pl.multiple_of(g * 256, 256), 256)
        q0 = pl.multiple_of(hp * 128, 128)
        k0 = pl.multiple_of(D + q0, 128)
        v0 = pl.multiple_of(2 * D + q0, 128)
        q = qkv[rs, pl.ds(q0, 128)]
        k = qkv[rs, pl.ds(k0, 128)]
        v = qkv[rs, pl.ds(v0, 128)]
        cg = cgrad[rs, pl.ds(q0, 128)]
        ok = valid[g] > 0.5
        pairs = pair[g] > 0.5
        dq, dk, dv = [], [], []
        for j in range(2):
            s, p = softmax(q, k, ok, j)
            ts = tbuf[slot, j].astype(f32)
            second = pltpu.roll(ts[128:192], 128, 1)
            third = pltpu.roll(ts[192:256], 192, 1)
            moved = jnp.concatenate([ts[0:128], second, third], axis=0)
            ts = jnp.where(g > 0, moved, ts)
            gap = jnp.where(pairs, s - ts, 0.0)
            sums[16:17, 0:256] += colsum(gap * gap) * (0.5 / LONG_LEN)
            pg = dot_nt(pick(cg, j), v)
            sg = p * (pg - jnp.sum(pg * p, axis=1, keepdims=True)) + gap * (1.0 / LONG_LEN)
            sg = sg.astype(bf16)
            dv.append(dot_tn(p.astype(bf16), cg))
            dq.append(dot_nn(sg, k))
            dk.append(dot_tn(sg, q))
        scale = HEAD_DIM**-0.5
        dq = (jnp.where(first, dq[0], dq[1]) * scale).astype(bf16)
        dk = (jnp.where(first, dk[0], dk[1]) * scale).astype(bf16)
        dv = jnp.where(first, dv[0], dv[1]).astype(bf16)
        for index, (grad, at) in enumerate(((dq, q0), (dk, k0), (dv, v0))):
            qkv[rs, pl.ds(at, 128)] = grad
            sums[index : index + 1, pl.ds(q0, 128)] += colsum(grad.astype(f32))

    def input_back(c):
        cs = pl.ds(c, 256)
        g = dot_nt(qkv[...], wt[cs, :])
        grad, clip_sum = clip_back(g, hid[:, cs].astype(f32), c0, i0)
        sums[19:20, cs] += clip_sum
        acc[:, cs] += grad

    def close_sums():
        for part in range(4):
            sums[9 + part : 10 + part, :] = wbias[1:2, part * D : (part + 1) * D]
        at = lax.broadcasted_iota(jnp.int32, (1, D), 1)
        line = jnp.zeros((1, D), f32)
        for spot, value in enumerate(
            (
                sums[19:20, :], sums[17:18, :], sums[18:19, :], sums[14:15, :],
                sums[15:16, :] + sums[16:17, :],
            )
        ):
            line = jnp.where(at == spot, jnp.sum(value), line)
        sums[13:14, :] = line
        small_out[...] = sums[0:16, :]

    firsts = (over_x, over_y)
    seconds = (over_y, over_x)
    outer = (z == 0) | (z == 3)
    inner = (z == 1) | (z == 2)
    near = z + 1 - 2 * lax.rem(z, 2)
    beyond = 1 - lax.div(z, 2)

    def on_z(to):
        return (dp, to * 2 + core)

    def lanes(p, w):
        return pl.ds(p * (w // 2), w // 2)

    def core_copy(k, w):
        slot, duo = lax.rem(k, SLOTS), lax.rem(k, 2)
        cs = pl.ds(0, w)
        return remote(
            pt.at[slot, :, 1 - core, :, :, :, cs], rb.at[duo, :, :, :, :, cs], s1.at[slot],
            r1.at[slot], over_core,
        )

    def own_rows(slot, blocks, p, w, mine):
        i = (x if p == 0 else y) if mine else (1 - x if p == 0 else 1 - y)
        if p == 0:
            return pt.at[slot, blocks, core, i, :, :, lanes(p, w)]
        return pt.at[slot, blocks, core, :, i, :, lanes(p, w)]

    def first_copy(k, w, p):
        slot, duo = lax.rem(k, SLOTS), lax.rem(k, 2)
        src = own_rows(slot, pl.ds(0, 4), p, w, False)
        dst = rx.at[duo, p, :, :, :, lanes(0, w)]
        return remote(src, dst, s2.at[slot, p], r2.at[slot, p], firsts[p])

    def in_copy(k, w, p):
        slot, duo = lax.rem(k, SLOTS), lax.rem(k, 2)
        src = own_rows(slot, pl.ds(beyond, 3), p, w, True)
        dst = rz.at[duo, p, :, :, :, lanes(0, w)]
        return remote(src, dst, s3.at[slot, p], r3.at[slot, p], on_z(near))

    def out_copy(k, w, p, kind):
        slot = lax.rem(k, SLOTS)
        to = (near, 3 - z, lax.rem(z + 2, 4))[kind]
        return remote(
            own_rows(slot, to, p, w, True), rf.at[slot, min(kind, 1), p, :, :, lanes(0, w)],
            s4.at[slot, kind, p], r4.at[slot, min(kind, 1), p], on_z(to),
        )

    def second_copy(k, w, p):
        slot, duo = lax.rem(k, SLOTS), lax.rem(k, 2)
        cs = lanes(0, w)
        return remote(
            held.at[duo, p, :, :, cs], ry.at[duo, p, :, :, cs], s5.at[slot, p], r5.at[slot, p],
            seconds[p],
        )

    def fin_at(k, w, p, rows):
        if w == CHUNK:
            flat = k * CHUNK
        else:
            flat = WIDE * CHUNK + (k - WIDE) * w
        cs = pl.ds(pl.multiple_of(lax.rem(flat, FF) + p * (w // 2), 128), w // 2)
        return (lax.div(flat, FF), *((x, rows) if p == 0 else (rows, y)), slice(None), cs)

    def back_first(k, w, p):
        slot = lax.rem(k, SLOTS)
        ref = fin.at[fin_at(k, w, p, slice(None))]
        return remote(ref, ref, s6.at[slot, p], r6.at[slot, p], firsts[p])

    def small_copy(step):
        to = (
            over_core, over_x, over_y, on_z(lax.rem(z + 1, 4)), on_z(lax.rem(z + 2, 4)),
            on_z(lax.rem(z + 3, 4)),
        )[step]
        return remote(small_out, sin.at[step], sms.at[step], smr.at[step], to)

    def finish_first(k, w):
        for p in range(2):
            back_first(k, w, p).wait()

    def finish_second(k, w):
        duo = lax.rem(k, 2)
        for p in range(2):
            second_copy(k, w, p).wait()
            for i in range(2):
                cs = lanes(0, w)
                fin[fin_at(k, w, p, i)] = held[duo, p, i, :, cs] + ry[duo, p, i, :, cs]
            back_first(k, w, p).start()

    def finish_out(k, w):
        slot, duo = lax.rem(k, SLOTS), lax.rem(k, 2)
        cs = lanes(0, w)

        @pl.when(outer)
        def _():
            for p in range(2):
                out_copy(k, w, p, 0).wait_recv()
                out_copy(k, w, p, 2).wait_recv()
                for i in range(2):
                    at = (x, i) if p == 0 else (i, y)
                    own = pt[(slot, z, core, *at, slice(None), lanes(p, w))]
                    held[duo, p, i, :, cs] = (
                        own + rf[slot, 0, p, i, :, cs] + rf[slot, 1, p, i, :, cs]
                    )

        @pl.when(inner)
        def _():
            for p in range(2):
                out_copy(k, w, p, 1).wait()
                out_copy(k, w, p, 0).wait_send()
                out_copy(k, w, p, 2).wait_send()
                for i in range(2):
                    at = (x, i) if p == 0 else (i, y)
                    own = pt[(slot, z, core, *at, slice(None), lanes(p, w))]
                    held[duo, p, i, :, cs] = own + rf[slot, 1, p, i, :, cs]

        for p in range(2):
            second_copy(k, w, p).start()

    def finish_in(k, w):
        slot, duo = lax.rem(k, SLOTS), lax.rem(k, 2)

        @pl.when(outer)
        def _():
            for p in range(2):
                in_copy(k, w, p).wait_send()

        @pl.when(inner)
        def _():
            for p in range(2):
                in_copy(k, w, p).wait_recv()
                for q in range(3):
                    for i in range(2):
                        at = (x, i) if p == 0 else (i, y)
                        at = (slot, beyond + q, core, *at, slice(None), lanes(p, w))
                        pt[at] += rz[duo, p, q, i, :, lanes(0, w)]
                for kind in (2, 1, 0):
                    out_copy(k, w, p, kind).start()

    def finish_one(k, w):
        slot, duo = lax.rem(k, SLOTS), lax.rem(k, 2)
        for p in range(2):
            first_copy(k, w, p).wait()
            for q in range(4):
                for i in range(2):
                    at = (x, i) if p == 0 else (i, y)
                    at = (slot, q, core, *at, slice(None), lanes(p, w))
                    pt[at] += rx[duo, p, q, i, :, lanes(0, w)]

            @pl.when(outer)
            def _():
                in_copy(k, w, p).start()

    def finish_core(k, w):
        slot, duo = lax.rem(k, SLOTS), lax.rem(k, 2)
        core_copy(k, w).wait()
        cs = pl.ds(0, w)
        for q in range(4):
            pt[slot, q, core, :, :, :, cs] += rb[duo, q, :, :, :, cs]
        for p in range(2):
            first_copy(k, w, p).start()

    stages = (
        (6, finish_first), (5, finish_second), (4, finish_out), (3, finish_in), (2, finish_one),
        (1, finish_core),
    )

    def tick(t, carry):
        for lag, step in stages:

            @pl.when((t >= lag) & (t < lag + WIDE))
            def _():
                step(t - lag, CHUNK)

            @pl.when((t >= lag + WIDE) & (t < lag + CHUNKS))
            def _():
                step(t - lag, HALF)

        slot = lax.rem(t, SLOTS)

        def put(owner, cs, block):
            for i in range(2):
                for j in range(2):
                    at = (i * 2 + j) * 24
                    pt[slot, owner // 2, owner % 2, i, j, :, cs] = block[at : at + 24, :]

        pieces = CHUNK // 128
        turns = 8 // pieces

        @pl.when(t < SECTION)
        def _():
            j = lax.div(t, turns)
            count = pieces * BLOCK
            left = nlT[pl.ds(pl.multiple_of(lax.rem(t, turns) * count, count), count), :]
            for owner in range(8):
                cs = pl.ds(pl.multiple_of(owner * 384 + j * 128, 128), 128)
                got = dot_nn(left, act[:, cs])
                for part in range(pieces):
                    put(owner, pl.ds(part * 128, 128), got[part * BLOCK : (part + 1) * BLOCK, :])

        def whole(left, right, half):
            got = dot_nn(left, right)
            for owner in range(8):
                put(owner, pl.ds(half * 256, 256), got[owner * BLOCK : (owner + 1) * BLOCK, :])

        for half in range(2):

            @pl.when((t >= SECTION) & (t < 2 * SECTION))
            def _():
                cs = pl.ds(pl.multiple_of((t - SECTION) * CHUNK + half * 256, 256), 256)
                whole(wlT[...], wg[:, cs], half)

            part = (t - 2 * SECTION) * 2 + half

            @pl.when((part >= 0) & (part < 3))
            def _():
                whole(clT[...], low[:, pl.ds(pl.multiple_of(part * 256, 256), 256)], half)

            @pl.when((part >= 3) & (part < 10))
            def _():
                whole(xlT[...], qkv[:, pl.ds(pl.multiple_of((part - 3) * 256, 256), 256)], half)

        @pl.when(t < WIDE)
        def _():
            core_copy(t, CHUNK).start()

        @pl.when((t >= WIDE) & (t < CHUNKS))
        def _():
            cs = pl.ds(pl.multiple_of((t - WIDE + 7) * 256, 256), 256)
            whole(xlT[...], qkv[:, cs], 0)
            core_copy(t, HALF).start()

        for when, turn in ((3, turn_inputs), (4, turn_context), (5, turn_widen)):

            @pl.when(t == when)
            def _():
                loop(4, 128, turn)

        units = 12 // SECTION
        begin = SECTION + 1

        @pl.when(t < SECTION)
        def _():
            feed_back(t)

        @pl.when(t == SECTION)
        def _():
            for slot in range(2):
                scores_copy(slot, slot).start()
            loop(4, 128, norm_one_back)
            loop(3, 256, mix_back)

        @pl.when((t >= begin) & (t < begin + SECTION))
        def _():
            for index in range(units):
                u = (t - begin) * units + index
                at = lax.rem(u, 2)
                scores_copy(u, at).wait()
                attend_pair_back(u, at)

                @pl.when(u < 10)
                def _():
                    scores_copy(u + 2, at).start()

        done = begin + SECTION

        @pl.when((t >= done) & (t < done + 3))
        def _():
            input_back(pl.multiple_of((t - done) * 256, 256))

        @pl.when(t == done + 3)
        def _():
            close_sums()
            small_copy(0).start()

        @pl.when(t == done + 4)
        def _():
            small_copy(0).wait()
            small_out[...] += sin[0]
            small_copy(1).start()

        @pl.when(t == done + 5)
        def _():
            small_copy(1).wait()
            small_out[...] += sin[1]
            small_copy(2).start()

        @pl.when(t == done + 6)
        def _():
            small_copy(2).wait()
            small_out[...] += sin[2]
            for step in (3, 4, 5):
                small_copy(step).start()

        @pl.when(t == done + 7)
        def _():
            for step in (3, 4, 5):
                small_copy(step).wait()
            small_out[...] = small_out[...] + sin[3] + sin[4] + sin[5]

        return carry

    lax.fori_loop(0, CHUNKS + 6, tick, 0)


def layer(*args):
    vm = pl.BlockSpec(memory_space=pltpu.VMEM)
    sm = pl.BlockSpec(memory_space=pltpu.SMEM)
    sds = jax.ShapeDtypeStruct
    dma = pltpu.SemaphoreType.DMA
    return pl.pallas_call(
        layer_kernel,
        out_shape=(
            sds((ROWS, D), bf16),
            sds((ROWS, D), f32),
            sds((3, 2, 2, 24, FF), f32),
            sds((16, D), f32),
        ),
        in_specs=[sm] * 3 + [vm] * 7 + [pl.BlockSpec(memory_space=pl.ANY)] * 6,
        out_specs=(vm,) * 4,
        scratch_shapes=[
            pltpu.VMEM((8, 72, D), jnp.int32),
            pltpu.VMEM((8, 32, 128), f32),
            pltpu.VMEM((8, BLOCK, 128), f32),
            pltpu.VMEM((128, 128), f32),
            pltpu.VMEM((D, 3 * D), bf16),
            pltpu.VMEM((D, D), bf16),
            pltpu.VMEM((D, FF), bf16),
            pltpu.VMEM((FF, D), bf16),
            pltpu.VMEM((16, D), f32),
            pltpu.VMEM((8, 3 * D), f32),
            pltpu.VMEM((8, FF), f32),
            pltpu.VMEM((ROWS, 3 * D), bf16),
            pltpu.VMEM((ROWS, D), bf16),
            pltpu.VMEM((ROWS, D), f32),
            pltpu.VMEM((ROWS, D), f32),
            pltpu.VMEM((ROWS, 128), f32),
            pltpu.VMEM((ROWS, FF), f32),
            pltpu.VMEM((ROWS, FF), bf16),
            pltpu.VMEM((ROWS, FF), bf16),
            pltpu.VMEM((ROWS, D), f32),
            pltpu.VMEM((ROWS, D), bf16),
            pltpu.VMEM((2, 256, 256), f32),
            pltpu.VMEM((2, 256, 256), f32),
            pltpu.VMEM((D, ROWS), bf16),
            pltpu.VMEM((D, ROWS), bf16),
            pltpu.VMEM((D, ROWS), bf16),
            pltpu.VMEM((D, ROWS), bf16),
            pltpu.VMEM((24, D), f32),
            pltpu.VMEM((2, 2, 256, 256), bf16),
            pltpu.VMEM((SLOTS, 4, 2, 2, 2, 24, CHUNK), f32),
            pltpu.VMEM((2, 4, 2, 2, 24, CHUNK), f32),
            pltpu.VMEM((2, 2, 4, 2, 24, HALF), f32),
            pltpu.VMEM((2, 2, 3, 2, 24, HALF), f32),
            pltpu.VMEM((SLOTS, 2, 2, 2, 24, HALF), f32),
            pltpu.VMEM((2, 2, 2, 24, HALF), f32),
            pltpu.VMEM((2, 2, 2, 24, HALF), f32),
            pltpu.VMEM((6, 16, D), f32),
        ]
        + [dma((SLOTS,))] * 2
        + [dma((SLOTS, 2))] * 4
        + [dma((SLOTS, 3, 2)), dma((SLOTS, 2, 2))]
        + [dma((SLOTS, 2))] * 4
        + [dma((6,))] * 2
        + [dma((2,)), dma((2, 4)), dma((4, 3)), dma((4, 3)), dma((4, 4)), dma((4, 4)), dma((1,))],
        compiler_params=pltpu.CompilerParams(collective_id=0, has_side_effects=True, vmem_limit_bytes=LAYER_CAP),
        name="layer",
    )(*args)


def finish_kernel(
    count, fin, small, tl, ml, wl, nl,
    tg, mg, wg, ng, tb, mb, wb, nb, gain, shift, clips, loss,
    fbuf, tin, min_, win, nin, tout, mout, wout, nout, fsem, isem, osem,
):
    fcopies = [pltpu.make_async_copy(fin.at[i], fbuf.at[i], fsem.at[i]) for i in range(3)]
    icopies, ocopies = [], []
    for half in range(2):
        for index, (src, dst) in enumerate(((nl, nin), (wl, win), (ml, min_), (tl, tin))):
            at = index * 2 + half
            icopies.append(pltpu.make_async_copy(src.at[half], dst.at[half], isem.at[at]))
    for half in range(2):
        for index, (src, dst) in enumerate(((nout, ng), (wout, wg), (mout, mg), (tout, tg))):
            at = index * 2 + half
            ocopies.append(pltpu.make_async_copy(src.at[half], dst.at[half], osem.at[at]))
    for index in range(4):
        if index < 3:
            fcopies[index].start()
        icopies[index].start()
        icopies[index + 4].start()
    me = lax.axis_index("fsdp")
    z = lax.div(me, 2)
    core = lax.rem(me, 2)
    own = pltpu.roll(small[...], lax.rem(8 - me, 8) * BLOCK, 1)
    tb[...] = own[0:3, 0:BLOCK]
    mb[...] = own[3:4, 0:BLOCK]
    nb[...] = own[4:5, 0:BLOCK]
    gain[...] = own[5:7, 0:BLOCK]
    shift[...] = own[7:9, 0:BLOCK]
    wide = pltpu.roll(small[...], core * (4 * BLOCK), 1)
    row = lax.broadcasted_iota(jnp.int32, (16, D), 0)
    picked = jnp.sum(jnp.where(row == 9 + z, wide, 0.0), axis=0, keepdims=True)
    wb[...] = picked[:, 0 : 4 * BLOCK]
    line = small[13:14, :]
    lane = lax.broadcasted_iota(jnp.int32, (1, D), 1)
    for spot in range(4):
        clips[spot] = jnp.sum(jnp.where(lane == spot, line, 0.0))
    loss[0, 0] = jnp.sum(jnp.where(lane == 4, line, 0.0)) * count[0]

    def keep(latent, total, fan):
        return jnp.where(jnp.abs(latent) <= 1.0, total * (1.0 / math.sqrt(fan)), 0.0)

    def arrived(index):
        icopies[index].wait()
        icopies[index + 4].wait()

    def leave(index):
        ocopies[index].start()
        ocopies[index + 4].start()

    fcopies[0].wait()
    arrived(0)
    for j in range(3):
        for i in range(2):
            tiles = range((j * 2 + i) * 4, (j * 2 + i) * 4 + 4)
            parts = [fbuf[0, :, tile * 128 : (tile + 1) * 128] for tile in tiles]
            total = jnp.concatenate(parts, axis=0).T
            rows = slice(j * 128, (j + 1) * 128)
            cols = slice(i * 384, (i + 1) * 384)
            for half in range(2):
                nout[half, rows, cols] = keep(nin[half, rows, cols], total, FF)
    leave(0)
    fcopies[1].wait()
    arrived(1)
    for half in range(2):
        wout[half] = keep(win[half], fbuf[1], D)
    leave(1)
    fcopies[2].wait()
    arrived(2)
    for half in range(2):
        mout[half] = keep(min_[half], fbuf[2, :, 0:D], D)
    leave(2)
    arrived(3)
    for half in range(2):
        tout[half] = keep(tin[half], fbuf[2, :, D:], D)
    leave(3)
    for copy in ocopies:
        copy.wait()


def finish(count, fin, small, tl, ml, wl, nl):
    vm = pl.BlockSpec(memory_space=pltpu.VMEM)
    sm = pl.BlockSpec(memory_space=pltpu.SMEM)
    hbm = pl.BlockSpec(memory_space=pl.ANY)
    sds = jax.ShapeDtypeStruct
    shapes = [v.shape for v in (tl, ml, wl, nl)]
    dma = pltpu.SemaphoreType.DMA
    return pl.pallas_call(
        finish_kernel,
        out_shape=[sds(v, f32) for v in shapes]
        + [
            sds((3, BLOCK), f32), sds((1, BLOCK), f32), sds((1, 4 * BLOCK), f32),
            sds((1, BLOCK), f32), sds((2, BLOCK), f32), sds((2, BLOCK), f32),
            sds((4,), f32), sds((1, 1), f32),
        ],
        in_specs=[sm, hbm, vm] + [hbm] * 4,
        out_specs=[hbm] * 4 + [vm] * 6 + [sm] * 2,
        scratch_shapes=[pltpu.VMEM((3, BLOCK, FF), f32)]
        + [pltpu.VMEM(v, f32) for v in shapes] * 2
        + [dma((3,)), dma((8,)), dma((8,))],
        compiler_params=pltpu.CompilerParams(vmem_limit_bytes=VMEM_CAP),
        name="finish",
    )(count, fin, small, tl, ml, wl, nl)


def on_device_fast(
    hidden_in, teacher_hidden, teacher_scores, seq_lengths, live_counts, triple_latent,
    mixing_latent, widen_latent, narrow_latent, triple_bias, mixing_bias, widen_bias, narrow_bias,
    norm_gain, norm_shift, clip_level,
):
    out, input_grad, fin, small_sum = layer(
        seq_lengths, live_counts, clip_level, triple_bias, mixing_bias[None], widen_bias[None],
        narrow_bias[None], norm_gain, norm_shift, hidden_in, teacher_hidden,
        jnp.transpose(teacher_scores, (1, 0, 2)), triple_latent, mixing_latent, widen_latent,
        narrow_latent,
    )
    fin = fin.reshape(3, BLOCK, FF)
    tokens = hidden_in.shape[0] * lax.axis_size("dp") * lax.axis_size("fsdp")
    count = jnp.full((1,), 1.0 / (tokens * D), f32)
    tg, mg, wg, ng, tb, mb, wb, nb, gain, shift, clips, loss = finish(
        count, fin, small_sum, triple_latent, mixing_latent, widen_latent, narrow_latent
    )
    return (
        out, loss.reshape(()), input_grad, tg, mg, wg, ng, tb, mb.reshape(BLOCK),
        wb.reshape(4 * BLOCK), nb.reshape(BLOCK), gain, shift, clips,
    )


def solution(mesh):
    in_specs = (
        P(("dp", "fsdp"), None),
        P(("dp", "fsdp"), None),
        P(("dp", "fsdp"), None, None),
        P(("dp", "fsdp"), None),
        P(("dp", "fsdp"), None),
        P(None, "fsdp", None),
        P(None, "fsdp", None),
        P(None, "fsdp", None),
        P(None, "fsdp", None),
        P(None, "fsdp"),
        P("fsdp"),
        P("fsdp"),
        P("fsdp"),
        P(None, "fsdp"),
        P(None, "fsdp"),
        P(),
    )
    out_specs = (
        P(("dp", "fsdp"), None),
        P(),
        P(("dp", "fsdp"), None),
        P(None, "fsdp", None),
        P(None, "fsdp", None),
        P(None, "fsdp", None),
        P(None, "fsdp", None),
        P(None, "fsdp"),
        P("fsdp"),
        P("fsdp"),
        P("fsdp"),
        P(None, "fsdp"),
        P(None, "fsdp"),
        P(),
    )
    fits = mesh.shape["dp"] == 4 and mesh.shape["fsdp"] == 8
    return jax.shard_map(
        on_device_fast if fits else on_device, mesh=mesh, in_specs=in_specs, out_specs=out_specs, check_vma=False
    )
```

```python
import math

import jax
import jax.numpy as jnp
from jax import lax
from jax.experimental import pallas as pl
from jax.experimental.pallas import tpu as pltpu
from jax.sharding import PartitionSpec as P

D = 768
HEADS = 12
HEAD_DIM = 64
FF = 3072
LONG_LEN = 256
MID_LEN = 128
SHORT_LEN = 64
LONG_SLOTS = 1
MID_SLOTS = 1
SHORT_SLOTS = 2


bit_count = 32
norm_epsilon = 1e-12
masked_fill = -1e30


def soft_clip(values, clip_at):
    return clip_at * jnp.tanh(values / clip_at)


def layer_norm(values, gain_row, shift_row):
    center = values - jnp.mean(values, axis=-1, keepdims=True)
    variance = jnp.mean(center * center, axis=-1, keepdims=True)
    return center * lax.rsqrt(variance + norm_epsilon) * gain_row + shift_row


def gelu_exact(values):
    return 0.5 * values * (1.0 + lax.erf(values * (1.0 / math.sqrt(2.0))))


def pack_signs(latent):
    halves, row_count, columns = latent.shape
    sign_bits = (
        (latent > 0).astype(jnp.int32).reshape(halves, row_count, columns // bit_count, bit_count)
    )
    places = jnp.arange(bit_count, dtype=jnp.int32)
    return jnp.sum(jnp.left_shift(sign_bits, places), axis=-1, dtype=jnp.int32)


def unpack_weight(sign_words, scales):
    halves, row_count, word_count = sign_words.shape
    places = jnp.arange(bit_count, dtype=jnp.int32)
    sign_bits = jnp.bitwise_and(jnp.right_shift(sign_words[..., None], places), 1)
    sign_values = (
        (2 * sign_bits - 1).astype(jnp.float32).reshape(halves, row_count, word_count * bit_count)
    )
    return (scales[0][:, None] * sign_values[0] + scales[1][:, None] * sign_values[1]).astype(
        jnp.bfloat16
    )


def bucket_shapes():
    return ((LONG_SLOTS, LONG_LEN), (MID_SLOTS, MID_LEN), (SHORT_SLOTS, SHORT_LEN))


def bucket_masks(lengths, live_count, slot_count, bucket_len):
    places = jnp.arange(bucket_len, dtype=jnp.int32)
    key_ok = places[None, :] < lengths[:, None]
    query_ok = jnp.logical_and(
        key_ok, jnp.arange(slot_count, dtype=jnp.int32)[:, None] < live_count
    )
    return (key_ok, query_ok)


def split_heads(block, slot_count, bucket_len):
    return block.reshape(slot_count, bucket_len, HEADS, HEAD_DIM)


def bucket_scores(qkv_rows, teacher_rows, key_ok, query_ok, slot_count, bucket_len):
    queries = split_heads(qkv_rows[:, :D], slot_count, bucket_len)
    keys_part = split_heads(qkv_rows[:, D : 2 * D], slot_count, bucket_len)
    scores = jnp.einsum(
        "sqhd,skhd->shqk", queries, keys_part, preferred_element_type=jnp.float32
    ) * HEAD_DIM ** (-0.5)
    masked = jnp.where(key_ok[:, None, None, :], scores, masked_fill)
    teacher = jnp.transpose(
        teacher_rows.reshape(slot_count, bucket_len, HEADS, LONG_LEN)[..., :bucket_len],
        (0, 2, 1, 3),
    ).astype(jnp.float32)
    pair_ok = jnp.logical_and(query_ok[:, None, :, None], key_ok[:, None, None, :])
    score_gap = jnp.where(pair_ok, scores - teacher, 0.0)
    return (queries, keys_part, masked, score_gap)


def attend(qkv_rows, teacher_rows, key_ok, query_ok, slot_count, bucket_len):
    queries, keys_part, masked, score_gap = bucket_scores(
        qkv_rows, teacher_rows, key_ok, query_ok, slot_count, bucket_len
    )
    values_part = split_heads(qkv_rows[:, 2 * D :], slot_count, bucket_len)
    row_top = jnp.max(masked, axis=-1, keepdims=True)
    exponent = jnp.exp(masked - row_top)
    exp_total = jnp.sum(exponent, axis=-1, keepdims=True)
    attention = exponent / exp_total
    context = jnp.einsum(
        "shqk,skhd->sqhd",
        attention.astype(jnp.bfloat16),
        values_part,
        preferred_element_type=jnp.float32,
    )
    distill = 0.5 / LONG_LEN * jnp.sum(score_gap * score_gap)
    return (context.reshape(slot_count * bucket_len, D), row_top + jnp.log(exp_total), distill)


def attend_back(
    qkv_rows, teacher_rows, key_ok, query_ok, slot_count, bucket_len, log_total, context_grad
):
    queries, keys_part, masked, score_gap = bucket_scores(
        qkv_rows, teacher_rows, key_ok, query_ok, slot_count, bucket_len
    )
    values_part = split_heads(qkv_rows[:, 2 * D :], slot_count, bucket_len)
    attention = jnp.exp(masked - log_total)
    grad_heads = split_heads(context_grad, slot_count, bucket_len)
    values_grad = jnp.einsum(
        "shqk,sqhd->skhd",
        attention.astype(jnp.bfloat16),
        grad_heads,
        preferred_element_type=jnp.float32,
    )
    weight_grad = jnp.einsum(
        "sqhd,skhd->shqk", grad_heads, values_part, preferred_element_type=jnp.float32
    )
    score_grad = attention * (
        weight_grad - jnp.sum(weight_grad * attention, axis=-1, keepdims=True)
    ) + score_gap * (1.0 / LONG_LEN)
    score_low = score_grad.astype(jnp.bfloat16)
    score_scale = HEAD_DIM ** (-0.5)
    queries_grad = (
        jnp.einsum("shqk,skhd->sqhd", score_low, keys_part, preferred_element_type=jnp.float32)
        * score_scale
    )
    keys_grad = (
        jnp.einsum("shqk,sqhd->skhd", score_low, queries, preferred_element_type=jnp.float32)
        * score_scale
    )
    row_count = slot_count * bucket_len
    return jnp.concatenate(
        [
            queries_grad.reshape(row_count, D),
            keys_grad.reshape(row_count, D),
            values_grad.reshape(row_count, D),
        ],
        axis=-1,
    )


def on_device(
    hidden_in,
    teacher_hidden,
    teacher_scores,
    seq_lengths,
    live_counts,
    triple_latent,
    mixing_latent,
    widen_latent,
    narrow_latent,
    triple_bias,
    mixing_bias,
    widen_bias,
    narrow_bias,
    norm_gain,
    norm_shift,
    clip_level,
):
    latents = (triple_latent, mixing_latent, widen_latent, narrow_latent)
    fan_ins = (D, D, D, FF)
    own_scales = tuple(
        (
            jnp.mean(jnp.abs(latent), axis=-1) / math.sqrt(fan_in)
            for latent, fan_in in zip(latents, fan_ins)
        )
    )
    packed = tuple((pack_signs(latent) for latent in latents))
    gathered = (
        lax.all_gather(packed[0], "fsdp", axis=1, tiled=True),
        lax.all_gather(packed[1], "fsdp", axis=1, tiled=True),
        lax.all_gather(packed[2], "fsdp", axis=1, tiled=True),
        lax.all_gather(packed[3], "fsdp", axis=1, tiled=True),
    )
    factors = (
        lax.all_gather(own_scales[0], "fsdp", axis=1, tiled=True),
        lax.all_gather(own_scales[1], "fsdp", axis=1, tiled=True),
        lax.all_gather(own_scales[2], "fsdp", axis=1, tiled=True),
        lax.all_gather(own_scales[3], "fsdp", axis=1, tiled=True),
        lax.all_gather(triple_bias, "fsdp", axis=1, tiled=True),
        lax.all_gather(mixing_bias, "fsdp", axis=0, tiled=True),
        lax.all_gather(widen_bias, "fsdp", axis=0, tiled=True),
        lax.all_gather(narrow_bias, "fsdp", axis=0, tiled=True),
        lax.all_gather(norm_gain, "fsdp", axis=1, tiled=True),
        lax.all_gather(norm_shift, "fsdp", axis=1, tiled=True),
    )
    scales = factors[:4]
    triple_rows, full_mixing_bias, full_widen_bias, full_narrow_bias, gains, shifts = factors[4:]
    full_triple_bias = triple_rows.reshape(3 * D)
    weights = tuple(
        (unpack_weight(words_part, scale_part) for words_part, scale_part in zip(gathered, scales))
    )
    inputs = hidden_in.astype(jnp.float32)
    inputs_low = soft_clip(inputs, clip_level[0]).astype(jnp.bfloat16)
    qkv_all = (
        jnp.dot(inputs_low, weights[0], preferred_element_type=jnp.float32) + full_triple_bias
    ).astype(jnp.bfloat16)
    lengths = seq_lengths[0]
    counts = live_counts[0]
    plans = []
    row_start = 0
    slot_start = 0
    for bucket, shape_pair in enumerate(bucket_shapes()):
        slot_count, bucket_len = shape_pair
        key_ok, query_ok = bucket_masks(
            lengths[slot_start : slot_start + slot_count], counts[bucket], slot_count, bucket_len
        )
        plans.append(
            (
                row_start,
                row_start + slot_count * bucket_len,
                slot_count,
                bucket_len,
                key_ok,
                query_ok,
            )
        )
        row_start = row_start + slot_count * bucket_len
        slot_start = slot_start + slot_count
    contexts = []
    log_totals = []
    distill_sum = 0.0
    for plan in plans:
        row_begin, row_end, slot_count, bucket_len, key_ok, query_ok = plan
        context, log_total, distill = attend(
            qkv_all[row_begin:row_end],
            teacher_scores[row_begin:row_end],
            key_ok,
            query_ok,
            slot_count,
            bucket_len,
        )
        contexts.append(context)
        log_totals.append(log_total)
        distill_sum = distill_sum + distill
    context = jnp.concatenate(contexts, axis=0)
    token_ok = jnp.concatenate([plan[5].reshape(-1) for plan in plans])
    context_low = soft_clip(context, clip_level[1]).astype(jnp.bfloat16)
    mixed = jnp.dot(context_low, weights[1], preferred_element_type=jnp.float32) + full_mixing_bias
    first_sum = inputs + mixed
    first_norm = layer_norm(first_sum, gains[0], shifts[0])
    widen_low = soft_clip(first_norm, clip_level[2]).astype(jnp.bfloat16)
    widened = jnp.dot(widen_low, weights[2], preferred_element_type=jnp.float32) + full_widen_bias
    activated = gelu_exact(widened)
    activated_low = soft_clip(activated, clip_level[3]).astype(jnp.bfloat16)
    narrowed = (
        jnp.dot(activated_low, weights[3], preferred_element_type=jnp.float32) + full_narrow_bias
    )
    second_sum = first_norm + narrowed
    out_full = layer_norm(second_sum, gains[1], shifts[1])
    out_gap = jnp.where(token_ok[:, None], out_full - teacher_hidden.astype(jnp.float32), 0.0)
    loss_local = 0.5 * jnp.sum(out_gap * out_gap) + distill_sum
    regathered = (
        lax.all_gather(packed[0], "fsdp", axis=1, tiled=True),
        lax.all_gather(packed[1], "fsdp", axis=1, tiled=True),
        lax.all_gather(packed[2], "fsdp", axis=1, tiled=True),
        lax.all_gather(packed[3], "fsdp", axis=1, tiled=True),
    )
    back_weights = tuple(
        (
            unpack_weight(words_part, scale_part)
            for words_part, scale_part in zip(regathered, scales)
        )
    )
    _, second_back = jax.vjp(layer_norm, second_sum, gains[1], shifts[1])
    second_grad, gain_two, shift_two = second_back(out_gap)
    narrow_low = second_grad.astype(jnp.bfloat16)
    narrow_weight_grad = jnp.einsum(
        "rf,rd->fd", activated_low, narrow_low, preferred_element_type=jnp.float32
    )
    act_low_grad = jnp.einsum(
        "rd,fd->rf", narrow_low, back_weights[3], preferred_element_type=jnp.float32
    )
    _, clip_three_back = jax.vjp(soft_clip, activated, clip_level[3])
    act_grad, clip_three = clip_three_back(act_low_grad)
    _, gelu_back = jax.vjp(gelu_exact, widened)
    (widened_grad,) = gelu_back(act_grad)
    widen_grad_low = widened_grad.astype(jnp.bfloat16)
    widen_weight_grad = jnp.einsum(
        "rd,rf->df", widen_low, widen_grad_low, preferred_element_type=jnp.float32
    )
    norm_low_grad = jnp.einsum(
        "rf,df->rd", widen_grad_low, back_weights[2], preferred_element_type=jnp.float32
    )
    _, clip_two_back = jax.vjp(soft_clip, first_norm, clip_level[2])
    norm_grad, clip_two = clip_two_back(norm_low_grad)
    norm_grad = norm_grad + second_grad
    _, first_back = jax.vjp(layer_norm, first_sum, gains[0], shifts[0])
    first_grad, gain_one, shift_one = first_back(norm_grad)
    mixed_low = first_grad.astype(jnp.bfloat16)
    mixing_weight_grad = jnp.einsum(
        "rc,rd->cd", context_low, mixed_low, preferred_element_type=jnp.float32
    )
    context_low_grad = jnp.einsum(
        "rd,cd->rc", mixed_low, back_weights[1], preferred_element_type=jnp.float32
    )
    _, clip_one_back = jax.vjp(soft_clip, context, clip_level[1])
    context_grad, clip_one = clip_one_back(context_low_grad)
    context_grad_low = context_grad.astype(jnp.bfloat16)
    qkv_grads = []
    for plan, log_total in zip(plans, log_totals):
        row_begin, row_end, slot_count, bucket_len, key_ok, query_ok = plan
        qkv_grads.append(
            attend_back(
                qkv_all[row_begin:row_end],
                teacher_scores[row_begin:row_end],
                key_ok,
                query_ok,
                slot_count,
                bucket_len,
                log_total,
                context_grad_low[row_begin:row_end],
            )
        )
    qkv_grad_low = jnp.concatenate(qkv_grads, axis=0).astype(jnp.bfloat16)
    triple_weight_grad = jnp.einsum(
        "rd,re->de", inputs_low, qkv_grad_low, preferred_element_type=jnp.float32
    )
    input_low_grad = jnp.einsum(
        "re,de->rd", qkv_grad_low, back_weights[0], preferred_element_type=jnp.float32
    )
    _, clip_zero_back = jax.vjp(soft_clip, inputs, clip_level[0])
    input_side, clip_zero = clip_zero_back(input_low_grad)
    input_grad = input_side + first_grad
    bias_sums = (
        jnp.sum(qkv_grad_low, axis=0, dtype=jnp.float32).reshape(3, D),
        jnp.sum(mixed_low, axis=0, dtype=jnp.float32),
        jnp.sum(widen_grad_low, axis=0, dtype=jnp.float32),
        jnp.sum(narrow_low, axis=0, dtype=jnp.float32),
    )
    row_shares = (
        lax.psum_scatter(triple_weight_grad, "fsdp", scatter_dimension=0, tiled=True),
        lax.psum_scatter(mixing_weight_grad, "fsdp", scatter_dimension=0, tiled=True),
        lax.psum_scatter(widen_weight_grad, "fsdp", scatter_dimension=0, tiled=True),
        lax.psum_scatter(narrow_weight_grad, "fsdp", scatter_dimension=0, tiled=True),
    )
    totals = lax.psum((row_shares[0], row_shares[1], row_shares[2], row_shares[3]), "dp")
    small_sums = lax.psum(
        (
            bias_sums[0],
            bias_sums[1],
            bias_sums[2],
            bias_sums[3],
            jnp.stack([gain_one, gain_two]),
            jnp.stack([shift_one, shift_two]),
            jnp.stack([clip_zero, clip_one, clip_two, clip_three]),
            loss_local,
        ),
        ("dp", "fsdp"),
    )
    shard_index = lax.axis_index("fsdp")
    shard_parts = lax.axis_size("fsdp")

    def own_part(vector, along):
        share_width = vector.shape[along] // shard_parts
        return lax.dynamic_slice_in_dim(vector, shard_index * share_width, share_width, along)

    latent_grads = tuple(
        (
            jnp.where(jnp.abs(latent) <= 1.0, (total / math.sqrt(fan_in))[None], 0.0)
            for latent, total, fan_in in zip(latents, totals, fan_ins)
        )
    )
    loss = small_sums[7] / (hidden_in.shape[0] * D * lax.axis_size("dp") * shard_parts)
    return (
        out_full.astype(jnp.bfloat16),
        loss,
        input_grad,
        latent_grads[0],
        latent_grads[1],
        latent_grads[2],
        latent_grads[3],
        own_part(small_sums[0], 1),
        own_part(small_sums[1], 0),
        own_part(small_sums[2], 0),
        own_part(small_sums[3], 0),
        own_part(small_sums[4], 1),
        own_part(small_sums[5], 1),
        small_sums[6],
    )


bf16 = jnp.bfloat16
f32 = jnp.float32
MESH = pl.DeviceIdType.MESH
VMEM_CAP = 60 * 1024 * 1024
LAYER_CAP = 63 * 1024 * 1024
ROWS = LONG_SLOTS * LONG_LEN + MID_SLOTS * MID_LEN + SHORT_SLOTS * SHORT_LEN
BLOCK = 96
CHUNK = 512
HALF = CHUNK // 2
SECTION = FF // CHUNK
WIDE = 3 * SECTION - 1
CHUNKS = WIDE + 2
SLOTS = 4


def dot_nn(a, b):
    return lax.dot_general(a, b, (((1,), (0,)), ((), ())), preferred_element_type=f32)


def dot_nt(a, b):
    return lax.dot_general(a, b, (((1,), (1,)), ((), ())), preferred_element_type=f32)


def dot_tn(a, b):
    return lax.dot_general(a, b, (((0,), (0,)), ((), ())), preferred_element_type=f32)


def loop(count, step, body):
    def run(i, carry):
        body(pl.multiple_of(i * step, step))
        return carry

    lax.fori_loop(0, count, run, 0)


def plane_of(block, half, group):
    place = block * 24 + half * 12 + group
    bit = place % 32
    return place // 32, (1 << bit) if bit < 31 else -(1 << 31)


def unpack_block(words, scl, block, dst):
    def one(owner, carry):
        unpack_owner(words, scl, block, dst, owner)
        return carry

    lax.fori_loop(0, 8, one, 0)


def unpack_owner(words, scl, block, dst, owner):
    index = 0 if block < 3 else 1 if block == 3 else 2 if block < 8 else block - 5

    for pair in range(6):
        parts = []
        for group in (2 * pair, 2 * pair + 1):
            total = None
            for half in range(2):
                word, bit = plane_of(block, half, group)
                bits = words[owner, word * 8 : (word + 1) * 8, :] & jnp.int32(bit)
                column = index * 2 + half
                scale = jnp.broadcast_to(
                    scl[owner, group * 8 : (group + 1) * 8, column : column + 1], (8, D)
                )
                value = jnp.where(bits != 0, scale, -scale)
                total = value if total is None else total + value
            parts.append(total)
        tile = jnp.concatenate(parts, axis=0).astype(bf16)
        if block < 8:
            start = owner * BLOCK + pair * 16
        else:
            start = owner * (4 * BLOCK) + (block - 8) * BLOCK + pair * 16
        rows = pl.ds(pl.multiple_of(start, 16), 16)
        if block < 3:
            dst[rows, block * D : (block + 1) * D] = tile
        elif block < 8 and block > 3:
            dst[rows, (block - 4) * D : (block - 3) * D] = tile
        else:
            dst[rows, :] = tile


def clip_back(grad, value, level, inverse):
    u = value * inverse
    t = jnp.tanh(u)
    slope = 1.0 - t * t
    return grad * slope, jnp.sum(grad * (t - u * slope), axis=0, keepdims=True)


def norm_rows(v):
    center = v - jnp.mean(v, axis=1, keepdims=True)
    variance = jnp.mean(center * center, axis=1, keepdims=True)
    rstd = lax.rsqrt(variance + norm_epsilon)
    return center * rstd, rstd


def norm_rows_back(grad, hat, rstd, gain_row):
    g = grad * gain_row
    return rstd * (
        g - jnp.mean(g, axis=1, keepdims=True) - hat * jnp.mean(g * hat, axis=1, keepdims=True)
    )


def colsum(v):
    return jnp.sum(v, axis=0, keepdims=True)


HALF_ROOT = 1.0 / math.sqrt(2.0)
DENSITY = 1.0 / math.sqrt(2.0 * math.pi)


def layer_kernel(
    seq, live, level, tb, mb, wb, nb, gain, shift, hid_in, teach, teach_scores, tl, ml, wl, nl,
    out_to, acc_to, fin_to, kept_to, small_out,
    out, acc, fin, kept, hid, words, small, scl, spread,
    wt, wm, ww, wn, prm, bias, wbias, qkv, low, ctx, hat1, rstd1, widened, act, wg, sgrad,
    cgrad, valid, pair, xlT, clT, wlT, nlT, sums, tbuf, pt, rb, rx, rz, rf, held, ry, rd, sin,
    s1, r1, s2, r2, s3, r3, s4, r4, s5, r5, s6, r6, sms, smr, tsem, lsem, zs, zr, cs_, cr_, hsem, fsem, s7, r7,
):
    dp = lax.axis_index("dp")
    me = lax.axis_index("fsdp")
    x = lax.rem(dp, 2)
    y = lax.div(dp, 2)
    z = lax.div(me, 2)
    core = lax.rem(me, 2)
    over_x = (dp + 1 - 2 * x, me)
    over_y = (dp + 2 - 4 * y, me)
    over_core = (dp, z * 2 + 1 - core)

    def remote(src, dst, send, recv, to):
        return pltpu.make_async_remote_copy(
            src_ref=src, dst_ref=dst, send_sem=send, recv_sem=recv, device_id=to,
            device_id_type=MESH,
        )

    greet = pltpu.get_barrier_semaphore()
    for to in (over_core, over_x, over_y) + tuple(
        (dp, lax.rem(z + hop, 4) * 2 + core) for hop in (1, 2, 3)
    ):
        pl.semaphore_signal(greet, inc=1, device_id=to, device_id_type=MESH)

    teach_load = pltpu.make_async_copy(teach, cgrad, hsem.at[0])
    hid_load = pltpu.make_async_copy(hid_in, hid, hsem.at[1])
    out_save = pltpu.make_async_copy(out, out_to, hsem.at[2])
    acc_save = pltpu.make_async_copy(acc, acc_to, hsem.at[3])
    kept_save = pltpu.make_async_copy(kept, kept_to, hsem.at[4])

    loads = []
    for half in range(2):
        band = slice(192 + half * BLOCK, 192 + (half + 1) * BLOCK)
        loads.append([
            pltpu.make_async_copy(tl.at[half], widened.at[band, 0 : 3 * D], lsem.at[half, 0]),
            pltpu.make_async_copy(ml.at[half], widened.at[band, 3 * D : FF], lsem.at[half, 1]),
            pltpu.make_async_copy(
                wl.at[half], widened.at[half * BLOCK : (half + 1) * BLOCK, :], lsem.at[half, 2]
            ),
            pltpu.make_async_copy(
                nl.at[half], (ctx if half == 0 else sgrad).at[0 : 4 * BLOCK, :], lsem.at[half, 3]
            ),
        ])
    for index in range(4):
        for half in range(2):
            loads[half][index].start()
    hid_load.start()
    teach_load.start()

    def latent_piece(block, half, group):
        if block < 4:
            rows = pl.ds(192 + half * BLOCK + group * 8, 8)
            return widened[rows, block * D : (block + 1) * D]
        if block < 8:
            return widened[pl.ds(half * BLOCK + group * 8, 8), (block - 4) * D : (block - 3) * D]
        rows = pl.ds((block - 8) * BLOCK + group * 8, 8)
        return (ctx if half == 0 else sgrad)[rows, :]

    planes = [[] for _ in range(9)]
    for block in range(12):
        for half in range(2):
            for group in range(12):
                word, bit = plane_of(block, half, group)
                planes[word].append((block, half, group, bit))

    def pack(word):
        total = jnp.zeros((8, D), jnp.int32)
        for block, half, group, bit in planes[word]:
            piece = latent_piece(block, half, group)
            total = total | jnp.where(piece > 0, jnp.int32(bit), jnp.int32(0))
        words[me, word * 8 : (word + 1) * 8, :] = total

    def pack_kept(word):
        total = jnp.zeros((8, D), jnp.int32)
        for block, half, group, bit in planes[word]:
            piece = jnp.abs(latent_piece(block, half, group))
            total = total | jnp.where(piece <= 1.0, jnp.int32(bit), jnp.int32(0))
        kept[word * 8 : (word + 1) * 8, :] = total

    def part_of(owner, index):
        return small.at[owner] if index == 3 else words.at[owner, index * 24 : (index + 1) * 24]

    def z_send(index, hop):
        ref = part_of(me, index)
        peer = lax.rem(z + hop, 4) * 2 + core
        return remote(ref, ref, zs.at[index, hop - 1], zr.at[index, hop - 1], (dp, peer))

    def core_send(index, hop):
        ref = part_of(lax.rem(z + 4 - hop, 4) * 2 + core, index)
        return remote(ref, ref, cs_.at[index, hop], cr_.at[index, hop], over_core)

    def send_out(index):
        for hop in (2, 1, 3):
            z_send(index, hop).start()
        core_send(index, 0).start()

    def pass_on(index):
        for hop in (1, 3, 2):
            z_send(index, hop).wait()
            core_send(index, hop).start()

    def all_here(index):
        for hop in range(4):
            core_send(index, hop).wait()

    for half in range(2):
        loads[half][0].wait()
        loads[half][1].wait()
    for word in range(3):
        pack(word)
    pl.semaphore_wait(greet, 6)
    send_out(0)
    for half in range(2):
        loads[half][2].wait()
        loads[half][3].wait()
    slot_lane = lax.broadcasted_iota(jnp.int32, (8, 128), 1)

    def scale_rows(group):
        tile = jnp.zeros((8, 128), f32)
        for half in range(2):
            rows = pl.ds(pl.multiple_of(192 + half * BLOCK + group, 8), 8)
            for index in range(7):
                if index == 0:
                    part = widened[rows, 0 : 3 * D]
                elif index == 1:
                    part = widened[rows, 3 * D : FF]
                elif index == 2:
                    part = widened[pl.ds(pl.multiple_of(half * BLOCK + group, 8), 8), :]
                else:
                    at = pl.ds(pl.multiple_of((index - 3) * BLOCK + group, 8), 8)
                    part = (ctx if half == 0 else sgrad)[at, :]
                fan = FF if index >= 3 else D
                mean = jnp.sum(jnp.abs(part), axis=1, keepdims=True) * (1.0 / part.shape[1])
                tile = jnp.where(slot_lane == index * 2 + half, mean / math.sqrt(fan), tile)
        spread[pl.ds(group, 8), :] = tile

    loop(12, 8, scale_rows)
    spread[BLOCK:128, :] = jnp.zeros((128 - BLOCK, 128), f32)
    small[me, 0:16, :] = spread[...].T[0:16, :]
    small[me, 16:32, :] = jnp.zeros((16, 128), f32)
    small[me, 16:19, 0:BLOCK] = tb[...]
    small[me, 19:20, 0:BLOCK] = mb[...]
    small[me, 20:21, 0:BLOCK] = nb[...]
    small[me, 21:23, 0:BLOCK] = gain[...]
    small[me, 23:25, 0:BLOCK] = shift[...]
    for part in range(3):
        small[me, 25 + part : 26 + part, :] = wb[part * 128 : (part + 1) * 128].reshape(1, 128)
    send_out(3)
    for word in range(3, 9):
        pack(word)
    for word in range(9):
        pack_kept(word)
    kept_save.start()
    c0, c1, c2, c3 = level[0], level[1], level[2], level[3]
    i0, i1, i2, i3 = 1.0 / c0, 1.0 / c1, 1.0 / c2, 1.0 / c3
    sums[...] = jnp.zeros_like(sums)
    row = lax.broadcasted_iota(jnp.int32, (256, 256), 0)
    col = lax.broadcasted_iota(jnp.int32, (256, 256), 1)
    key_ok = col < seq[0, 0]
    query_ok = row < seq[0, 0] * live[0, 0]
    valid[0] = jnp.where(key_ok, 1.0, 0.0)
    pair[0] = jnp.where(key_ok & query_ok, 1.0, 0.0)

    def in_slots(at):
        mid = (at < 128) & (at < seq[0, 1])
        one = (at >= 128) & (at < 192) & (at - 128 < seq[0, 2])
        two = (at >= 192) & (at - 192 < seq[0, 3])
        return mid, one, two

    km, ko, kt = in_slots(col)
    qm, qo, qt = in_slots(row)
    key_ok = (km & (row < 128)) | (ko & (row >= 128) & (row < 192)) | (kt & (row >= 192))
    live_mid = row * 0 + live[0, 1] > 0
    live_one = row * 0 + live[0, 2] > 0
    live_two = row * 0 + live[0, 2] > 1
    query_ok = (qm & live_mid) | (qo & live_one) | (qt & live_two)
    valid[1] = jnp.where(key_ok, 1.0, 0.0)
    pair[1] = jnp.where(key_ok & query_ok, 1.0, 0.0)
    ones = jnp.where(query_ok, 1.0, 0.0)

    def clip_in(r):
        x = hid[pl.ds(r, 128), :].astype(f32)
        lo = (c0 * jnp.tanh(x * i0)).astype(bf16)
        low[pl.ds(r, 128), :] = lo

    hid_load.wait()
    loop(4, 128, clip_in)
    pass_on(3)
    all_here(3)
    total = jnp.zeros((16, D), f32)
    param_lane = lax.broadcasted_iota(jnp.int32, (16, 128), 1)
    for owner in range(8):
        turned = jnp.concatenate([small[owner, 0:16, :], jnp.zeros((112, 128), f32)], axis=0).T
        scl[owner] = turned[0:BLOCK, :]
        piece = jnp.where(param_lane < BLOCK, small[owner, 16:32, :], 0.0)
        wide = jnp.concatenate([piece, jnp.zeros((16, D - 128), f32)], axis=1)
        total = total + (pltpu.roll(wide, owner * BLOCK, 1) if owner else wide)
        for part in range(3):
            at = owner * 4 * BLOCK + part * 128
            wbias[0:1, at : at + 128] = small[owner, 25 + part : 26 + part, :]
    prm[...] = total
    for part in range(3):
        bias[0:1, part * D : (part + 1) * D] = prm[part : part + 1, :]
    def same_core(hop, carry):
        @pl.when(hop > 0)
        def _():
            z_send(0, hop).wait()
            core_send(0, hop).start()

        for block in range(3):
            unpack_owner(words, scl, block, wt, lax.rem(z + 4 - hop, 4) * 2 + core)
        return carry

    def other_core(hop, carry):
        core_send(0, hop).wait()
        for block in range(3):
            unpack_owner(words, scl, block, wt, lax.rem(z + 4 - hop, 4) * 2 + 1 - core)
        return carry

    lax.fori_loop(0, 4, same_core, 0)
    send_out(1)
    lax.fori_loop(0, 4, other_core, 0)

    for part in range(9):
        cs = slice(part * 256, (part + 1) * 256)
        qkv[:, cs] = (dot_nn(low[...], wt[:, cs]) + bias[0:1, cs]).astype(bf16)
    send_out(2)
    lane = lax.broadcasted_iota(jnp.int32, (256, 128), 1)
    first = lane < 64

    def pick(v, j):
        return jnp.where(first, v, jnp.zeros_like(v)) if j == 0 else jnp.where(first, jnp.zeros_like(v), v)

    def softmax(q, k, ok, j):
        s = dot_nt(pick(q, j), k) * (HEAD_DIM**-0.5)
        masked = jnp.where(ok, s, masked_fill)
        e = jnp.exp(masked - jnp.max(masked, axis=1, keepdims=True))
        return s, e / jnp.sum(e, axis=1, keepdims=True)

    for g in range(2):
        for c in range(0, D, 128):
            rs = slice(g * 256, (g + 1) * 256)
            q, k, v = (qkv[rs, at + c : at + c + 128] for at in (0, D, 2 * D))
            ok = valid[g] > 0.5
            parts = []
            for j in range(2):
                s, p = softmax(q, k, ok, j)
                parts.append(dot_nn(p.astype(bf16), v))
            ctx[rs, c : c + 128] = jnp.where(first, parts[0], parts[1])
    pass_on(1)
    unpack_block(words, scl, 3, wm)

    def clip_ctx(r):
        lo = (c1 * jnp.tanh(ctx[pl.ds(r, 128), :] * i1)).astype(bf16)
        low[pl.ds(r, 128), :] = lo

    loop(4, 128, clip_ctx)

    for part in range(3):
        cs = slice(part * 256, (part + 1) * 256)
        acc[:, cs] = dot_nn(low[...], wm[:, cs]) + prm[3:4, cs] + hid[:, cs].astype(f32)

    def norm_one(r):
        rs = pl.ds(r, 128)
        hat, rstd = norm_rows(acc[rs, :])
        hat1[rs, :] = hat
        rstd1[rs, :] = jnp.broadcast_to(rstd, (128, 128))
        normed = hat * prm[5:6, :] + prm[7:8, :]
        lo = (c2 * jnp.tanh(normed * i2)).astype(bf16)
        low[rs, :] = lo
        acc[rs, :] = normed + prm[4:5, :]

    loop(4, 128, norm_one)
    all_here(1)
    pass_on(2)
    for block in range(4, 8):
        unpack_block(words, scl, block, ww)
    all_here(2)
    for block in range(8, 12):
        unpack_block(words, scl, block, wn)

    for t in range(8):
        if t < 6:
            cs = slice(t * 512, (t + 1) * 512)
            widened[:, cs] = dot_nn(low[...], ww[:, cs]) + wbias[0:1, cs]
        if 1 <= t <= 6:
            cs = slice((t - 1) * 512, t * 512)
            for r in range(0, ROWS, 64):
                w = widened[r : r + 64, cs]
                a = 0.5 * w * (1.0 + lax.erf(w * HALF_ROOT))
                act[r : r + 64, cs] = (c3 * jnp.tanh(a * i3)).astype(bf16)
        if t >= 2:
            cs = slice((t - 2) * 512, (t - 1) * 512)
            acc[...] += dot_nn(act[:, cs], wn[cs, :])

    teach_load.wait()

    def norm_two(r):
        rs = pl.ds(r, 128)
        hat, rstd = norm_rows(acc[rs, :])
        full = hat * prm[6:7, :] + prm[8:9, :]
        out[rs, :] = full.astype(bf16)
        at = lax.broadcasted_iota(jnp.int32, (128, D), 0) + r
        l0, l1, l2, l3 = seq[0, 0] * live[0, 0], seq[0, 1], seq[0, 2], seq[0, 3]
        l1 = jnp.where(live[0, 1] > 0, l1, 0)
        l2 = jnp.where(live[0, 2] > 0, l2, 0)
        l3 = jnp.where(live[0, 2] > 1, l3, 0)
        ok = (at < l0) | ((at >= 256) & (at < 256 + l1)) | ((at >= 384) & (at < 384 + l2))
        ok = ok | ((at >= 448) & (at < 448 + l3))
        gap = jnp.where(ok, full - cgrad[rs, :].astype(f32), 0.0)
        sums[15:16, :] += colsum(gap * gap) * 0.5
        sums[6:7, :] += colsum(gap * hat)
        sums[8:9, :] += colsum(gap)
        grad = norm_rows_back(gap, hat, rstd, prm[6:7, :])
        sgrad[rs, :] = grad
        acc[rs, :] = jnp.zeros((128, D), f32)
        lo = grad.astype(bf16)
        low[rs, :] = lo
        nlT[:, rs] = lo.T
        sums[4:5, :] += colsum(lo.astype(f32))

    loop(4, 128, norm_two)
    out_save.start()

    def feed_back(t):
        cs = pl.ds(pl.multiple_of(t * CHUNK, CHUNK), CHUNK)
        wbias[1:2, cs] = jnp.zeros((1, CHUNK), f32)

        def feed_back_rows(r):
            rs = pl.ds(r, 256)
            g = dot_nt(low[rs, :], wn[cs, :])
            w = widened[rs, cs]
            e = 0.5 * (1.0 + lax.erf(w * HALF_ROOT))
            a = w * e
            u = a * i3
            th = jnp.tanh(u)
            slope = 1.0 - th * th
            sums[14:15, 0:CHUNK] += colsum(g * (th - u * slope))
            back = g * slope * (e + w * (DENSITY * jnp.exp(-0.5 * w * w)))
            lo = back.astype(bf16)
            wg[rs, cs] = lo
            wbias[1:2, cs] += colsum(lo.astype(f32))
            acc[rs, :] += dot_nt(lo, ww[:, cs])

        loop(2, 256, feed_back_rows)

    def turn_widen(r):
        rs = pl.ds(r, 128)
        normed = hat1[rs, :] * prm[5:6, :] + prm[7:8, :]
        wlT[:, rs] = (c2 * jnp.tanh(normed * i2)).astype(bf16).T

    def turn_context(r):
        clT[:, pl.ds(r, 128)] = (c1 * jnp.tanh(ctx[pl.ds(r, 128), :] * i1)).astype(bf16).T

    def turn_inputs(r):
        v = hid[pl.ds(r, 128), :].astype(f32)
        xlT[:, pl.ds(r, 128)] = (c0 * jnp.tanh(v * i0)).astype(bf16).T

    def norm_one_back(r):
        rs = pl.ds(r, 128)
        hat = hat1[rs, :]
        normed = hat * prm[5:6, :] + prm[7:8, :]
        grad, clip_sum = clip_back(acc[rs, :], normed, c2, i2)
        sums[18:19, :] += clip_sum
        grad = grad + sgrad[rs, :]
        sums[5:6, :] += colsum(grad * hat)
        sums[7:8, :] += colsum(grad)
        grad = norm_rows_back(grad, hat, rstd1[rs, 0:1], prm[5:6, :])
        acc[rs, :] = grad
        lo = grad.astype(bf16)
        low[rs, :] = lo
        sums[3:4, :] += colsum(lo.astype(f32))

    def mix_back(c):
        cs = pl.ds(c, 256)
        g = dot_nt(low[...], wm[cs, :])
        grad, clip_sum = clip_back(g, ctx[:, cs], c1, i1)
        sums[17:18, cs] += clip_sum
        cgrad[:, cs] = grad.astype(bf16)

    def scores_copy(u, slot):
        g = lax.div(u, 6)
        hp = lax.rem(u, 6)
        rs = pl.ds(pl.multiple_of(g * 256, 256), 256)
        return pltpu.make_async_copy(
            teach_scores.at[pl.ds(2 * hp, 2), rs], tbuf.at[slot], tsem.at[slot]
        )

    def attend_pair_back(u, slot):
        g = lax.div(u, 6)
        hp = lax.rem(u, 6)
        rs = pl.ds(pl.multiple_of(g * 256, 256), 256)
        q0 = pl.multiple_of(hp * 128, 128)
        k0 = pl.multiple_of(D + q0, 128)
        v0 = pl.multiple_of(2 * D + q0, 128)
        q = qkv[rs, pl.ds(q0, 128)]
        k = qkv[rs, pl.ds(k0, 128)]
        v = qkv[rs, pl.ds(v0, 128)]
        cg = cgrad[rs, pl.ds(q0, 128)]
        ok = valid[g] > 0.5
        pairs = pair[g] > 0.5
        dq, dk, dv = [], [], []
        for j in range(2):
            s, p = softmax(q, k, ok, j)
            ts = tbuf[slot, j].astype(f32)
            second = pltpu.roll(ts[128:192], 128, 1)
            third = pltpu.roll(ts[192:256], 192, 1)
            moved = jnp.concatenate([ts[0:128], second, third], axis=0)
            ts = jnp.where(g > 0, moved, ts)
            gap = jnp.where(pairs, s - ts, 0.0)
            sums[16:17, 0:256] += colsum(gap * gap) * (0.5 / LONG_LEN)
            pg = dot_nt(pick(cg, j), v)
            sg = p * (pg - jnp.sum(pg * p, axis=1, keepdims=True)) + gap * (1.0 / LONG_LEN)
            sg = sg.astype(bf16)
            dv.append(dot_tn(p.astype(bf16), cg))
            dq.append(dot_nn(sg, k))
            dk.append(dot_tn(sg, q))
        scale = HEAD_DIM**-0.5
        dq = (jnp.where(first, dq[0], dq[1]) * scale).astype(bf16)
        dk = (jnp.where(first, dk[0], dk[1]) * scale).astype(bf16)
        dv = jnp.where(first, dv[0], dv[1]).astype(bf16)
        for index, (grad, at) in enumerate(((dq, q0), (dk, k0), (dv, v0))):
            qkv[rs, pl.ds(at, 128)] = grad
            sums[index : index + 1, pl.ds(q0, 128)] += colsum(grad.astype(f32))

    def input_back(c):
        cs = pl.ds(c, 256)
        g = dot_nt(qkv[...], wt[cs, :])
        grad, clip_sum = clip_back(g, hid[:, cs].astype(f32), c0, i0)
        sums[19:20, cs] += clip_sum
        acc[:, cs] += grad

    def close_sums():
        for part in range(4):
            sums[9 + part : 10 + part, :] = wbias[1:2, part * D : (part + 1) * D]
        at = lax.broadcasted_iota(jnp.int32, (1, D), 1)
        line = jnp.zeros((1, D), f32)
        for spot, value in enumerate(
            (
                sums[19:20, :], sums[17:18, :], sums[18:19, :], sums[14:15, :],
                sums[15:16, :] + sums[16:17, :],
            )
        ):
            line = jnp.where(at == spot, jnp.sum(value), line)
        sums[13:14, :] = line
        small_out[...] = sums[0:16, :]

    firsts = (over_x, over_y)
    seconds = (over_y, over_x)
    outer = (z == 0) | (z == 3)
    inner = (z == 1) | (z == 2)
    near = z + 1 - 2 * lax.rem(z, 2)
    beyond = 1 - lax.div(z, 2)

    def on_z(to):
        return (dp, to * 2 + core)

    def lanes(p, w):
        return pl.ds(p * (w // 2), w // 2)

    def core_copy(k, w):
        slot, duo = lax.rem(k, SLOTS), lax.rem(k, 2)
        cs = pl.ds(0, w)
        return remote(
            pt.at[slot, :, 1 - core, :, :, :, cs], rb.at[duo, :, :, :, :, cs], s1.at[slot],
            r1.at[slot], over_core,
        )

    def own_rows(slot, blocks, p, w, mine):
        i = (x if p == 0 else y) if mine else (1 - x if p == 0 else 1 - y)
        if p == 0:
            return pt.at[slot, blocks, core, i, :, :, lanes(p, w)]
        return pt.at[slot, blocks, core, :, i, :, lanes(p, w)]

    def first_copy(k, w, p):
        slot, duo = lax.rem(k, SLOTS), lax.rem(k, 2)
        src = own_rows(slot, pl.ds(0, 4), p, w, False)
        dst = rx.at[duo, p, :, :, :, lanes(0, w)]
        return remote(src, dst, s2.at[slot, p], r2.at[slot, p], firsts[p])

    def in_copy(k, w, p):
        slot, duo = lax.rem(k, SLOTS), lax.rem(k, 2)
        src = own_rows(slot, pl.ds(beyond, 3), p, w, True)
        dst = rz.at[duo, p, :, :, :, lanes(0, w)]
        return remote(src, dst, s3.at[slot, p], r3.at[slot, p], on_z(near))

    def out_copy(k, w, p, kind):
        slot = lax.rem(k, SLOTS)
        to = (near, 3 - z, lax.rem(z + 2, 4))[kind]
        return remote(
            own_rows(slot, to, p, w, True), rf.at[slot, min(kind, 1), p, :, :, lanes(0, w)],
            s4.at[slot, kind, p], r4.at[slot, min(kind, 1), p], on_z(to),
        )

    def direct_copy(p, hop):
        to = lax.rem(z + hop, 4)
        return remote(
            own_rows((CHUNKS - 1) % SLOTS, to, p, HALF, True), rd.at[hop - 1, p],
            s7.at[hop - 1, p], r7.at[hop - 1, p], on_z(to),
        )

    def room_of(k):
        return 2 if isinstance(k, int) else lax.rem(k, 2)

    def second_copy(k, w, p):
        slot, duo = lax.rem(k, SLOTS), room_of(k)
        cs = lanes(0, w)
        return remote(
            held.at[duo, p, :, :, cs], ry.at[duo, p, :, :, cs], s5.at[slot, p], r5.at[slot, p],
            seconds[p],
        )

    def fin_at(k, w, p, rows):
        if w == CHUNK:
            flat = k * CHUNK
        else:
            flat = WIDE * CHUNK + (k - WIDE) * w
        cs = pl.ds(pl.multiple_of(lax.rem(flat, FF) + p * (w // 2), 128), w // 2)
        return (lax.div(flat, FF), *((x, rows) if p == 0 else (rows, y)), slice(None), cs)

    def back_first(k, w, p):
        slot = lax.rem(k, SLOTS)
        ref = fin.at[fin_at(k, w, p, slice(None))]
        return remote(ref, ref, s6.at[slot, p], r6.at[slot, p], firsts[p])

    def small_copy(step):
        to = (
            over_core, over_x, over_y, on_z(lax.rem(z + 1, 4)), on_z(lax.rem(z + 2, 4)),
            on_z(lax.rem(z + 3, 4)),
        )[step]
        return remote(small_out, sin.at[step], sms.at[step], smr.at[step], to)

    def finish_first(k, w):
        for p in range(2):
            back_first(k, w, p).wait()
        fin_save(k, w).start()

    def fin_save(k, w):
        if w == CHUNK:
            flat = k * CHUNK
        else:
            flat = WIDE * CHUNK + (k - WIDE) * w
        cs = pl.ds(pl.multiple_of(lax.rem(flat, FF), 128), w)
        at = (lax.div(flat, FF), slice(None), slice(None), slice(None), cs)
        return pltpu.make_async_copy(fin.at[at], fin_to.at[at], fsem.at[lax.rem(k, SLOTS)])

    def finish_save(k, w):
        fin_save(k, w).wait()

    def finish_second(k, w):
        duo = room_of(k)
        for p in range(2):
            second_copy(k, w, p).wait()
            for i in range(2):
                cs = lanes(0, w)
                fin[fin_at(k, w, p, i)] = held[duo, p, i, :, cs] + ry[duo, p, i, :, cs]
            back_first(k, w, p).start()

    def finish_out(k, w):
        slot, duo = lax.rem(k, SLOTS), lax.rem(k, 2)
        cs = lanes(0, w)

        @pl.when(outer)
        def _():
            for p in range(2):
                out_copy(k, w, p, 0).wait_recv()
                out_copy(k, w, p, 2).wait_recv()
                for i in range(2):
                    at = (x, i) if p == 0 else (i, y)
                    own = pt[(slot, z, core, *at, slice(None), lanes(p, w))]
                    held[duo, p, i, :, cs] = (
                        own + rf[slot, 0, p, i, :, cs] + rf[slot, 1, p, i, :, cs]
                    )

        @pl.when(inner)
        def _():
            for p in range(2):
                out_copy(k, w, p, 1).wait()
                out_copy(k, w, p, 0).wait_send()
                out_copy(k, w, p, 2).wait_send()
                for i in range(2):
                    at = (x, i) if p == 0 else (i, y)
                    own = pt[(slot, z, core, *at, slice(None), lanes(p, w))]
                    held[duo, p, i, :, cs] = own + rf[slot, 1, p, i, :, cs]

        for p in range(2):
            second_copy(k, w, p).start()

    def finish_in(k, w):
        slot, duo = lax.rem(k, SLOTS), lax.rem(k, 2)

        @pl.when(outer)
        def _():
            for p in range(2):
                in_copy(k, w, p).wait_send()

        @pl.when(inner)
        def _():
            for p in range(2):
                in_copy(k, w, p).wait_recv()
                for q in range(3):
                    for i in range(2):
                        at = (x, i) if p == 0 else (i, y)
                        at = (slot, beyond + q, core, *at, slice(None), lanes(p, w))
                        pt[at] += rz[duo, p, q, i, :, lanes(0, w)]
                for kind in (2, 1, 0):
                    out_copy(k, w, p, kind).start()

    def add_first(k, w, p):
        slot, duo = lax.rem(k, SLOTS), lax.rem(k, 2)
        first_copy(k, w, p).wait()
        for q in range(4):
            for i in range(2):
                at = (x, i) if p == 0 else (i, y)
                at = (slot, q, core, *at, slice(None), lanes(p, w))
                pt[at] += rx[duo, p, q, i, :, lanes(0, w)]

    def finish_one(k, w):
        for p in range(2):
            add_first(k, w, p)

            @pl.when(outer)
            def _():
                in_copy(k, w, p).start()

    def last_one():
        for p in range(2):
            add_first(CHUNKS - 1, HALF, p)
            for hop in (2, 1, 3):
                direct_copy(p, hop).start()

    def last_direct():
        slot = (CHUNKS - 1) % SLOTS
        for p in range(2):
            for hop in (1, 3, 2):
                direct_copy(p, hop).wait()
            for i in range(2):
                at = (x, i) if p == 0 else (i, y)
                own = pt[(slot, z, core, *at, slice(None), lanes(p, HALF))]
                held[2, p, i, :, lanes(0, HALF)] = own + rd[0, p, i] + rd[1, p, i] + rd[2, p, i]
            second_copy(CHUNKS - 1, HALF, p).start()

    def finish_core(k, w):
        slot, duo = lax.rem(k, SLOTS), lax.rem(k, 2)
        core_copy(k, w).wait()
        cs = pl.ds(0, w)
        for q in range(4):
            pt[slot, q, core, :, :, :, cs] += rb[duo, q, :, :, :, cs]
        for p in range(2):
            first_copy(k, w, p).start()

    stages = (
        (7, finish_save), (6, finish_first), (5, finish_second), (4, finish_out), (3, finish_in),
        (2, finish_one), (1, finish_core),
    )
    last = CHUNKS - 1
    last_stages = {
        5: lambda: finish_second(last, HALF), 4: last_direct, 2: last_one,
        6: lambda: finish_first(last, HALF), 1: lambda: finish_core(last, HALF),
    }

    def tick(t, carry):
        for lag, step in stages:

            @pl.when((t >= lag) & (t < lag + WIDE))
            def _():
                step(t - lag, CHUNK)

            @pl.when(t == lag + WIDE)
            def _():
                step(t - lag, HALF)

            if lag in last_stages:

                @pl.when(t == last + lag - (1 if lag > 2 else 0))
                def _():
                    last_stages[lag]()

        slot = lax.rem(t, SLOTS)

        def put(owner, cs, block):
            for i in range(2):
                for j in range(2):
                    at = (i * 2 + j) * 24
                    pt[slot, owner // 2, owner % 2, i, j, :, cs] = block[at : at + 24, :]

        pieces = CHUNK // 128
        turns = 8 // pieces

        @pl.when(t < SECTION)
        def _():
            j = lax.div(t, turns)
            count = pieces * BLOCK
            left = nlT[pl.ds(pl.multiple_of(lax.rem(t, turns) * count, count), count), :]
            for owner in range(8):
                cs = pl.ds(pl.multiple_of(owner * 384 + j * 128, 128), 128)
                got = dot_nn(left, act[:, cs])
                for part in range(pieces):
                    put(owner, pl.ds(part * 128, 128), got[part * BLOCK : (part + 1) * BLOCK, :])

        def whole(left, right, half):
            got = dot_nn(left, right)
            for owner in range(8):
                put(owner, pl.ds(half * 256, 256), got[owner * BLOCK : (owner + 1) * BLOCK, :])

        for half in range(2):

            @pl.when((t >= SECTION) & (t < 2 * SECTION))
            def _():
                cs = pl.ds(pl.multiple_of((t - SECTION) * CHUNK + half * 256, 256), 256)
                whole(wlT[...], wg[:, cs], half)

            part = (t - 2 * SECTION) * 2 + half

            @pl.when((part >= 0) & (part < 3))
            def _():
                whole(clT[...], low[:, pl.ds(pl.multiple_of(part * 256, 256), 256)], half)

            @pl.when((part >= 3) & (part < 10))
            def _():
                whole(xlT[...], qkv[:, pl.ds(pl.multiple_of((part - 3) * 256, 256), 256)], half)

        @pl.when(t < WIDE)
        def _():
            core_copy(t, CHUNK).start()

        @pl.when((t >= WIDE) & (t < CHUNKS))
        def _():
            cs = pl.ds(pl.multiple_of((t - WIDE + 7) * 256, 256), 256)
            whole(xlT[...], qkv[:, cs], 0)
            core_copy(t, HALF).start()

        for when, turn in ((2, turn_inputs), (3, turn_context), (4, turn_widen)):

            @pl.when(t == when)
            def _():
                loop(4, 128, turn)

        units = 12 // SECTION
        begin = SECTION + 1

        @pl.when((t >= 1) & (t < SECTION))
        def _():
            feed_back(t - 1)

        @pl.when(t == SECTION - 1)
        def _():
            feed_back(t)

        @pl.when(t == SECTION)
        def _():
            for slot in range(2):
                scores_copy(slot, slot).start()
            loop(4, 128, norm_one_back)
            loop(3, 256, mix_back)

        @pl.when((t >= begin) & (t < begin + SECTION))
        def _():
            for index in range(units):
                u = (t - begin) * units + index
                at = lax.rem(u, 2)
                scores_copy(u, at).wait()
                attend_pair_back(u, at)

                @pl.when(u < 10)
                def _():
                    scores_copy(u + 2, at).start()

        done = begin + SECTION

        @pl.when((t >= done) & (t < done + 3))
        def _():
            input_back(pl.multiple_of((t - done) * 256, 256))

        @pl.when(t == done + 3)
        def _():
            acc_save.start()
            close_sums()
            small_copy(0).start()

        @pl.when(t == done + 4)
        def _():
            small_copy(0).wait()
            small_out[...] += sin[0]
            small_copy(1).start()

        @pl.when(t == done + 5)
        def _():
            small_copy(1).wait()
            small_out[...] += sin[1]
            small_copy(2).start()

        @pl.when(t == done + 6)
        def _():
            small_copy(2).wait()
            small_out[...] += sin[2]
            for step in (3, 4, 5):
                small_copy(step).start()

        @pl.when(t == done + 7)
        def _():
            for step in (3, 4, 5):
                small_copy(step).wait()
            small_out[...] = small_out[...] + sin[3] + sin[4] + sin[5]

        return carry

    lax.fori_loop(0, CHUNKS + 5, tick, 0)
    fin_save(WIDE, HALF).wait()
    fin_save(last, HALF).wait()
    for copy in (out_save, acc_save, kept_save):
        copy.wait()


def layer(*args):
    vm = pl.BlockSpec(memory_space=pltpu.VMEM)
    sm = pl.BlockSpec(memory_space=pltpu.SMEM)
    sds = jax.ShapeDtypeStruct
    dma = pltpu.SemaphoreType.DMA
    return pl.pallas_call(
        layer_kernel,
        out_shape=(
            sds((ROWS, D), bf16),
            sds((ROWS, D), f32),
            sds((3, 2, 2, 24, FF), f32),
            sds((72, D), jnp.int32),
            sds((16, D), f32),
        ),
        in_specs=[sm] * 3 + [vm] * 6 + [pl.BlockSpec(memory_space=pl.ANY)] * 7,
        out_specs=(pl.BlockSpec(memory_space=pl.ANY),) * 4 + (vm,),
        scratch_shapes=[
            pltpu.VMEM((ROWS, D), bf16),
            pltpu.VMEM((ROWS, D), f32),
            pltpu.VMEM((3, 2, 2, 24, FF), f32),
            pltpu.VMEM((72, D), jnp.int32),
            pltpu.VMEM((ROWS, D), bf16),
            pltpu.VMEM((8, 72, D), jnp.int32),
            pltpu.VMEM((8, 32, 128), f32),
            pltpu.VMEM((8, BLOCK, 128), f32),
            pltpu.VMEM((128, 128), f32),
            pltpu.VMEM((D, 3 * D), bf16),
            pltpu.VMEM((D, D), bf16),
            pltpu.VMEM((D, FF), bf16),
            pltpu.VMEM((FF, D), bf16),
            pltpu.VMEM((16, D), f32),
            pltpu.VMEM((8, 3 * D), f32),
            pltpu.VMEM((8, FF), f32),
            pltpu.VMEM((ROWS, 3 * D), bf16),
            pltpu.VMEM((ROWS, D), bf16),
            pltpu.VMEM((ROWS, D), f32),
            pltpu.VMEM((ROWS, D), f32),
            pltpu.VMEM((ROWS, 128), f32),
            pltpu.VMEM((ROWS, FF), f32),
            pltpu.VMEM((ROWS, FF), bf16),
            pltpu.VMEM((ROWS, FF), bf16),
            pltpu.VMEM((ROWS, D), f32),
            pltpu.VMEM((ROWS, D), bf16),
            pltpu.VMEM((2, 256, 256), f32),
            pltpu.VMEM((2, 256, 256), f32),
            pltpu.VMEM((D, ROWS), bf16),
            pltpu.VMEM((D, ROWS), bf16),
            pltpu.VMEM((D, ROWS), bf16),
            pltpu.VMEM((D, ROWS), bf16),
            pltpu.VMEM((24, D), f32),
            pltpu.VMEM((2, 2, 256, 256), bf16),
            pltpu.VMEM((SLOTS, 4, 2, 2, 2, 24, CHUNK), f32),
            pltpu.VMEM((2, 4, 2, 2, 24, CHUNK), f32),
            pltpu.VMEM((2, 2, 4, 2, 24, HALF), f32),
            pltpu.VMEM((2, 2, 3, 2, 24, HALF), f32),
            pltpu.VMEM((SLOTS, 2, 2, 2, 24, HALF), f32),
            pltpu.VMEM((3, 2, 2, 24, HALF), f32),
            pltpu.VMEM((3, 2, 2, 24, HALF), f32),
            pltpu.VMEM((3, 2, 2, 24, HALF // 2), f32),
            pltpu.VMEM((6, 16, D), f32),
        ]
        + [dma((SLOTS,))] * 2
        + [dma((SLOTS, 2))] * 4
        + [dma((SLOTS, 3, 2)), dma((SLOTS, 2, 2))]
        + [dma((SLOTS, 2))] * 4
        + [dma((6,))] * 2
        + [dma((2,)), dma((2, 4)), dma((4, 3)), dma((4, 3)), dma((4, 4)), dma((4, 4)), dma((5,)), dma((SLOTS,)), dma((3, 2)), dma((3, 2))],
        compiler_params=pltpu.CompilerParams(collective_id=0, has_side_effects=True, vmem_limit_bytes=LAYER_CAP),
        name="layer",
    )(*args)


def finish_kernel(
    count, small, kept, fin, tg, mg, wg, ng, tb, mb, wb, nb, gain, shift, clips, loss,
    fbuf, turned, tout, mout, wout, nout, fsem, osem,
):
    fcopies = [pltpu.make_async_copy(fin.at[i], fbuf.at[i], fsem.at[i]) for i in range(3)]
    ocopies = []
    for half in range(2):
        for index, (src, dst) in enumerate(((nout, ng), (wout, wg), (mout, mg), (tout, tg))):
            at = index * 2 + half
            ocopies.append(pltpu.make_async_copy(src.at[half], dst.at[half], osem.at[at]))
    for index in (1, 2, 0):
        fcopies[index].start()
    me = lax.axis_index("fsdp")
    z = lax.div(me, 2)
    core = lax.rem(me, 2)
    own = pltpu.roll(small[...], lax.rem(8 - me, 8) * BLOCK, 1)
    tb[...] = own[0:3, 0:BLOCK]
    mb[...] = own[3:4, 0:BLOCK]
    nb[...] = own[4:5, 0:BLOCK]
    gain[...] = own[5:7, 0:BLOCK]
    shift[...] = own[7:9, 0:BLOCK]
    wide = pltpu.roll(small[...], core * (4 * BLOCK), 1)
    row = lax.broadcasted_iota(jnp.int32, (16, D), 0)
    picked = jnp.sum(jnp.where(row == 9 + z, wide, 0.0), axis=0, keepdims=True)
    wb[...] = picked[:, 0 : 4 * BLOCK]
    line = small[13:14, :]
    lane = lax.broadcasted_iota(jnp.int32, (1, D), 1)
    for spot in range(4):
        clips[spot] = jnp.sum(jnp.where(lane == spot, line, 0.0))
    loss[0] = jnp.sum(jnp.where(lane == 4, line, 0.0)) * count[0]

    def keep(block, half, group, total, fan):
        word, bit = plane_of(block, half, group)
        bits = kept[word * 8 : (word + 1) * 8, :] & jnp.int32(bit)
        return jnp.where(bits != 0, total * (1.0 / math.sqrt(fan)), 0.0)

    def spread_out(blocks, half, dst, src, at):
        for index, block in enumerate(blocks):
            cols = slice(index * D, (index + 1) * D)
            for group in range(12):
                rows = slice(group * 8, (group + 1) * 8)
                total = src[rows, at + index * D : at + (index + 1) * D]
                dst[half, rows, cols] = keep(block, half, group, total, D)

    def leave(index, half):
        ocopies[index + 4 * half].start()

    fcopies[1].wait()
    for half in range(2):
        spread_out(range(4, 8), half, wout, fbuf.at[1], 0)
        leave(1, half)
    fcopies[2].wait()
    for half in range(2):
        spread_out(range(3), half, tout, fbuf.at[2], D)
        leave(3, half)
    for half in range(2):
        spread_out(range(3, 4), half, mout, fbuf.at[2], 0)
        leave(2, half)
    fcopies[0].wait()
    for j in range(3):
        for i in range(2):
            tiles = range((j * 2 + i) * 4, (j * 2 + i) * 4 + 4)
            parts = [fbuf[0, :, tile * 128 : (tile + 1) * 128] for tile in tiles]
            total = jnp.concatenate(parts, axis=0).T
            turned[j * 128 : (j + 1) * 128, i * 384 : (i + 1) * 384] = total
    for half in range(2):
        for block in range(8, 12):
            for group in range(12):
                rows = slice((block - 8) * BLOCK + group * 8, (block - 8) * BLOCK + group * 8 + 8)
                nout[half, rows, :] = keep(block, half, group, turned[rows, :], FF)
        leave(0, half)
    for copy in ocopies:
        copy.wait()


def finish(count, small, kept, fin):
    vm = pl.BlockSpec(memory_space=pltpu.VMEM)
    sm = pl.BlockSpec(memory_space=pltpu.SMEM)
    hbm = pl.BlockSpec(memory_space=pl.ANY)
    sds = jax.ShapeDtypeStruct
    shapes = [(2, BLOCK, 3 * D), (2, BLOCK, D), (2, BLOCK, FF), (2, 4 * BLOCK, D)]
    dma = pltpu.SemaphoreType.DMA
    return pl.pallas_call(
        finish_kernel,
        out_shape=[sds(v, f32) for v in shapes]
        + [
            sds((3, BLOCK), f32), sds((1, BLOCK), f32), sds((1, 4 * BLOCK), f32),
            sds((1, BLOCK), f32), sds((2, BLOCK), f32), sds((2, BLOCK), f32),
            sds((4,), f32), sds((1,), f32),
        ],
        in_specs=[sm, vm, vm, hbm],
        out_specs=[hbm] * 4 + [vm] * 6 + [sm] * 2,
        scratch_shapes=[pltpu.VMEM((3, BLOCK, FF), f32), pltpu.VMEM((4 * BLOCK, D), f32)]
        + [pltpu.VMEM(v, f32) for v in shapes]
        + [dma((3,)), dma((8,))],
        compiler_params=pltpu.CompilerParams(vmem_limit_bytes=VMEM_CAP),
        name="finish",
    )(count, small, kept, fin)


def on_device_fast(
    hidden_in, teacher_hidden, teacher_scores, seq_lengths, live_counts, triple_latent,
    mixing_latent, widen_latent, narrow_latent, triple_bias, mixing_bias, widen_bias, narrow_bias,
    norm_gain, norm_shift, clip_level,
):
    out, input_grad, fin, kept, small_sum = layer(
        seq_lengths, live_counts, clip_level, triple_bias, mixing_bias[None], widen_bias,
        narrow_bias[None], norm_gain, norm_shift, hidden_in, teacher_hidden,
        jnp.transpose(teacher_scores, (1, 0, 2)), triple_latent, mixing_latent, widen_latent,
        narrow_latent,
    )
    fin = fin.reshape(3, BLOCK, FF)
    tokens = hidden_in.shape[0] * lax.axis_size("dp") * lax.axis_size("fsdp")
    count = jnp.full((1,), 1.0 / (tokens * D), f32)
    tg, mg, wg, ng, tb, mb, wb, nb, gain, shift, clips, loss = finish(
        count, small_sum, kept, fin
    )
    return (
        out, loss[0], input_grad, tg, mg, wg, ng, tb, mb.reshape(BLOCK),
        wb.reshape(4 * BLOCK), nb.reshape(BLOCK), gain, shift, clips,
    )


def solution(mesh):
    in_specs = (
        P(("dp", "fsdp"), None),
        P(("dp", "fsdp"), None),
        P(("dp", "fsdp"), None, None),
        P(("dp", "fsdp"), None),
        P(("dp", "fsdp"), None),
        P(None, "fsdp", None),
        P(None, "fsdp", None),
        P(None, "fsdp", None),
        P(None, "fsdp", None),
        P(None, "fsdp"),
        P("fsdp"),
        P("fsdp"),
        P("fsdp"),
        P(None, "fsdp"),
        P(None, "fsdp"),
        P(),
    )
    out_specs = (
        P(("dp", "fsdp"), None),
        P(),
        P(("dp", "fsdp"), None),
        P(None, "fsdp", None),
        P(None, "fsdp", None),
        P(None, "fsdp", None),
        P(None, "fsdp", None),
        P(None, "fsdp"),
        P("fsdp"),
        P("fsdp"),
        P("fsdp"),
        P(None, "fsdp"),
        P(None, "fsdp"),
        P(),
    )
    fits = mesh.shape["dp"] == 4 and mesh.shape["fsdp"] == 8
    return jax.shard_map(
        on_device_fast if fits else on_device, mesh=mesh, in_specs=in_specs, out_specs=out_specs, check_vma=False
    )
```

```python
import math

import jax
import jax.numpy as jnp
from jax import lax
from jax.experimental import pallas as pl
from jax.experimental.pallas import tpu as pltpu
from jax.sharding import PartitionSpec as P

D = 768
HEADS = 12
HEAD_DIM = 64
FF = 3072
LONG_LEN = 256
MID_LEN = 128
SHORT_LEN = 64
LONG_SLOTS = 1
MID_SLOTS = 1
SHORT_SLOTS = 2


bit_count = 32
norm_epsilon = 1e-12
masked_fill = -1e30


def soft_clip(values, clip_at):
    return clip_at * jnp.tanh(values / clip_at)


def layer_norm(values, gain_row, shift_row):
    center = values - jnp.mean(values, axis=-1, keepdims=True)
    variance = jnp.mean(center * center, axis=-1, keepdims=True)
    return center * lax.rsqrt(variance + norm_epsilon) * gain_row + shift_row


def gelu_exact(values):
    return 0.5 * values * (1.0 + lax.erf(values * (1.0 / math.sqrt(2.0))))


def pack_signs(latent):
    halves, row_count, columns = latent.shape
    sign_bits = (
        (latent > 0).astype(jnp.int32).reshape(halves, row_count, columns // bit_count, bit_count)
    )
    places = jnp.arange(bit_count, dtype=jnp.int32)
    return jnp.sum(jnp.left_shift(sign_bits, places), axis=-1, dtype=jnp.int32)


def unpack_weight(sign_words, scales):
    halves, row_count, word_count = sign_words.shape
    places = jnp.arange(bit_count, dtype=jnp.int32)
    sign_bits = jnp.bitwise_and(jnp.right_shift(sign_words[..., None], places), 1)
    sign_values = (
        (2 * sign_bits - 1).astype(jnp.float32).reshape(halves, row_count, word_count * bit_count)
    )
    return (scales[0][:, None] * sign_values[0] + scales[1][:, None] * sign_values[1]).astype(
        jnp.bfloat16
    )


def bucket_shapes():
    return ((LONG_SLOTS, LONG_LEN), (MID_SLOTS, MID_LEN), (SHORT_SLOTS, SHORT_LEN))


def bucket_masks(lengths, live_count, slot_count, bucket_len):
    places = jnp.arange(bucket_len, dtype=jnp.int32)
    key_ok = places[None, :] < lengths[:, None]
    query_ok = jnp.logical_and(
        key_ok, jnp.arange(slot_count, dtype=jnp.int32)[:, None] < live_count
    )
    return (key_ok, query_ok)


def split_heads(block, slot_count, bucket_len):
    return block.reshape(slot_count, bucket_len, HEADS, HEAD_DIM)


def bucket_scores(qkv_rows, teacher_rows, key_ok, query_ok, slot_count, bucket_len):
    queries = split_heads(qkv_rows[:, :D], slot_count, bucket_len)
    keys_part = split_heads(qkv_rows[:, D : 2 * D], slot_count, bucket_len)
    scores = jnp.einsum(
        "sqhd,skhd->shqk", queries, keys_part, preferred_element_type=jnp.float32
    ) * HEAD_DIM ** (-0.5)
    masked = jnp.where(key_ok[:, None, None, :], scores, masked_fill)
    teacher = jnp.transpose(
        teacher_rows.reshape(slot_count, bucket_len, HEADS, LONG_LEN)[..., :bucket_len],
        (0, 2, 1, 3),
    ).astype(jnp.float32)
    pair_ok = jnp.logical_and(query_ok[:, None, :, None], key_ok[:, None, None, :])
    score_gap = jnp.where(pair_ok, scores - teacher, 0.0)
    return (queries, keys_part, masked, score_gap)


def attend(qkv_rows, teacher_rows, key_ok, query_ok, slot_count, bucket_len):
    queries, keys_part, masked, score_gap = bucket_scores(
        qkv_rows, teacher_rows, key_ok, query_ok, slot_count, bucket_len
    )
    values_part = split_heads(qkv_rows[:, 2 * D :], slot_count, bucket_len)
    row_top = jnp.max(masked, axis=-1, keepdims=True)
    exponent = jnp.exp(masked - row_top)
    exp_total = jnp.sum(exponent, axis=-1, keepdims=True)
    attention = exponent / exp_total
    context = jnp.einsum(
        "shqk,skhd->sqhd",
        attention.astype(jnp.bfloat16),
        values_part,
        preferred_element_type=jnp.float32,
    )
    distill = 0.5 / LONG_LEN * jnp.sum(score_gap * score_gap)
    return (context.reshape(slot_count * bucket_len, D), row_top + jnp.log(exp_total), distill)


def attend_back(
    qkv_rows, teacher_rows, key_ok, query_ok, slot_count, bucket_len, log_total, context_grad
):
    queries, keys_part, masked, score_gap = bucket_scores(
        qkv_rows, teacher_rows, key_ok, query_ok, slot_count, bucket_len
    )
    values_part = split_heads(qkv_rows[:, 2 * D :], slot_count, bucket_len)
    attention = jnp.exp(masked - log_total)
    grad_heads = split_heads(context_grad, slot_count, bucket_len)
    values_grad = jnp.einsum(
        "shqk,sqhd->skhd",
        attention.astype(jnp.bfloat16),
        grad_heads,
        preferred_element_type=jnp.float32,
    )
    weight_grad = jnp.einsum(
        "sqhd,skhd->shqk", grad_heads, values_part, preferred_element_type=jnp.float32
    )
    score_grad = attention * (
        weight_grad - jnp.sum(weight_grad * attention, axis=-1, keepdims=True)
    ) + score_gap * (1.0 / LONG_LEN)
    score_low = score_grad.astype(jnp.bfloat16)
    score_scale = HEAD_DIM ** (-0.5)
    queries_grad = (
        jnp.einsum("shqk,skhd->sqhd", score_low, keys_part, preferred_element_type=jnp.float32)
        * score_scale
    )
    keys_grad = (
        jnp.einsum("shqk,sqhd->skhd", score_low, queries, preferred_element_type=jnp.float32)
        * score_scale
    )
    row_count = slot_count * bucket_len
    return jnp.concatenate(
        [
            queries_grad.reshape(row_count, D),
            keys_grad.reshape(row_count, D),
            values_grad.reshape(row_count, D),
        ],
        axis=-1,
    )


def on_device(
    hidden_in,
    teacher_hidden,
    teacher_scores,
    seq_lengths,
    live_counts,
    triple_latent,
    mixing_latent,
    widen_latent,
    narrow_latent,
    triple_bias,
    mixing_bias,
    widen_bias,
    narrow_bias,
    norm_gain,
    norm_shift,
    clip_level,
):
    latents = (triple_latent, mixing_latent, widen_latent, narrow_latent)
    fan_ins = (D, D, D, FF)
    own_scales = tuple(
        (
            jnp.mean(jnp.abs(latent), axis=-1) / math.sqrt(fan_in)
            for latent, fan_in in zip(latents, fan_ins)
        )
    )
    packed = tuple((pack_signs(latent) for latent in latents))
    gathered = (
        lax.all_gather(packed[0], "fsdp", axis=1, tiled=True),
        lax.all_gather(packed[1], "fsdp", axis=1, tiled=True),
        lax.all_gather(packed[2], "fsdp", axis=1, tiled=True),
        lax.all_gather(packed[3], "fsdp", axis=1, tiled=True),
    )
    factors = (
        lax.all_gather(own_scales[0], "fsdp", axis=1, tiled=True),
        lax.all_gather(own_scales[1], "fsdp", axis=1, tiled=True),
        lax.all_gather(own_scales[2], "fsdp", axis=1, tiled=True),
        lax.all_gather(own_scales[3], "fsdp", axis=1, tiled=True),
        lax.all_gather(triple_bias, "fsdp", axis=1, tiled=True),
        lax.all_gather(mixing_bias, "fsdp", axis=0, tiled=True),
        lax.all_gather(widen_bias, "fsdp", axis=0, tiled=True),
        lax.all_gather(narrow_bias, "fsdp", axis=0, tiled=True),
        lax.all_gather(norm_gain, "fsdp", axis=1, tiled=True),
        lax.all_gather(norm_shift, "fsdp", axis=1, tiled=True),
    )
    scales = factors[:4]
    triple_rows, full_mixing_bias, full_widen_bias, full_narrow_bias, gains, shifts = factors[4:]
    full_triple_bias = triple_rows.reshape(3 * D)
    weights = tuple(
        (unpack_weight(words_part, scale_part) for words_part, scale_part in zip(gathered, scales))
    )
    inputs = hidden_in.astype(jnp.float32)
    inputs_low = soft_clip(inputs, clip_level[0]).astype(jnp.bfloat16)
    qkv_all = (
        jnp.dot(inputs_low, weights[0], preferred_element_type=jnp.float32) + full_triple_bias
    ).astype(jnp.bfloat16)
    lengths = seq_lengths[0]
    counts = live_counts[0]
    plans = []
    row_start = 0
    slot_start = 0
    for bucket, shape_pair in enumerate(bucket_shapes()):
        slot_count, bucket_len = shape_pair
        key_ok, query_ok = bucket_masks(
            lengths[slot_start : slot_start + slot_count], counts[bucket], slot_count, bucket_len
        )
        plans.append(
            (
                row_start,
                row_start + slot_count * bucket_len,
                slot_count,
                bucket_len,
                key_ok,
                query_ok,
            )
        )
        row_start = row_start + slot_count * bucket_len
        slot_start = slot_start + slot_count
    contexts = []
    log_totals = []
    distill_sum = 0.0
    for plan in plans:
        row_begin, row_end, slot_count, bucket_len, key_ok, query_ok = plan
        context, log_total, distill = attend(
            qkv_all[row_begin:row_end],
            teacher_scores[row_begin:row_end],
            key_ok,
            query_ok,
            slot_count,
            bucket_len,
        )
        contexts.append(context)
        log_totals.append(log_total)
        distill_sum = distill_sum + distill
    context = jnp.concatenate(contexts, axis=0)
    token_ok = jnp.concatenate([plan[5].reshape(-1) for plan in plans])
    context_low = soft_clip(context, clip_level[1]).astype(jnp.bfloat16)
    mixed = jnp.dot(context_low, weights[1], preferred_element_type=jnp.float32) + full_mixing_bias
    first_sum = inputs + mixed
    first_norm = layer_norm(first_sum, gains[0], shifts[0])
    widen_low = soft_clip(first_norm, clip_level[2]).astype(jnp.bfloat16)
    widened = jnp.dot(widen_low, weights[2], preferred_element_type=jnp.float32) + full_widen_bias
    activated = gelu_exact(widened)
    activated_low = soft_clip(activated, clip_level[3]).astype(jnp.bfloat16)
    narrowed = (
        jnp.dot(activated_low, weights[3], preferred_element_type=jnp.float32) + full_narrow_bias
    )
    second_sum = first_norm + narrowed
    out_full = layer_norm(second_sum, gains[1], shifts[1])
    out_gap = jnp.where(token_ok[:, None], out_full - teacher_hidden.astype(jnp.float32), 0.0)
    loss_local = 0.5 * jnp.sum(out_gap * out_gap) + distill_sum
    regathered = (
        lax.all_gather(packed[0], "fsdp", axis=1, tiled=True),
        lax.all_gather(packed[1], "fsdp", axis=1, tiled=True),
        lax.all_gather(packed[2], "fsdp", axis=1, tiled=True),
        lax.all_gather(packed[3], "fsdp", axis=1, tiled=True),
    )
    back_weights = tuple(
        (
            unpack_weight(words_part, scale_part)
            for words_part, scale_part in zip(regathered, scales)
        )
    )
    _, second_back = jax.vjp(layer_norm, second_sum, gains[1], shifts[1])
    second_grad, gain_two, shift_two = second_back(out_gap)
    narrow_low = second_grad.astype(jnp.bfloat16)
    narrow_weight_grad = jnp.einsum(
        "rf,rd->fd", activated_low, narrow_low, preferred_element_type=jnp.float32
    )
    act_low_grad = jnp.einsum(
        "rd,fd->rf", narrow_low, back_weights[3], preferred_element_type=jnp.float32
    )
    _, clip_three_back = jax.vjp(soft_clip, activated, clip_level[3])
    act_grad, clip_three = clip_three_back(act_low_grad)
    _, gelu_back = jax.vjp(gelu_exact, widened)
    (widened_grad,) = gelu_back(act_grad)
    widen_grad_low = widened_grad.astype(jnp.bfloat16)
    widen_weight_grad = jnp.einsum(
        "rd,rf->df", widen_low, widen_grad_low, preferred_element_type=jnp.float32
    )
    norm_low_grad = jnp.einsum(
        "rf,df->rd", widen_grad_low, back_weights[2], preferred_element_type=jnp.float32
    )
    _, clip_two_back = jax.vjp(soft_clip, first_norm, clip_level[2])
    norm_grad, clip_two = clip_two_back(norm_low_grad)
    norm_grad = norm_grad + second_grad
    _, first_back = jax.vjp(layer_norm, first_sum, gains[0], shifts[0])
    first_grad, gain_one, shift_one = first_back(norm_grad)
    mixed_low = first_grad.astype(jnp.bfloat16)
    mixing_weight_grad = jnp.einsum(
        "rc,rd->cd", context_low, mixed_low, preferred_element_type=jnp.float32
    )
    context_low_grad = jnp.einsum(
        "rd,cd->rc", mixed_low, back_weights[1], preferred_element_type=jnp.float32
    )
    _, clip_one_back = jax.vjp(soft_clip, context, clip_level[1])
    context_grad, clip_one = clip_one_back(context_low_grad)
    context_grad_low = context_grad.astype(jnp.bfloat16)
    qkv_grads = []
    for plan, log_total in zip(plans, log_totals):
        row_begin, row_end, slot_count, bucket_len, key_ok, query_ok = plan
        qkv_grads.append(
            attend_back(
                qkv_all[row_begin:row_end],
                teacher_scores[row_begin:row_end],
                key_ok,
                query_ok,
                slot_count,
                bucket_len,
                log_total,
                context_grad_low[row_begin:row_end],
            )
        )
    qkv_grad_low = jnp.concatenate(qkv_grads, axis=0).astype(jnp.bfloat16)
    triple_weight_grad = jnp.einsum(
        "rd,re->de", inputs_low, qkv_grad_low, preferred_element_type=jnp.float32
    )
    input_low_grad = jnp.einsum(
        "re,de->rd", qkv_grad_low, back_weights[0], preferred_element_type=jnp.float32
    )
    _, clip_zero_back = jax.vjp(soft_clip, inputs, clip_level[0])
    input_side, clip_zero = clip_zero_back(input_low_grad)
    input_grad = input_side + first_grad
    bias_sums = (
        jnp.sum(qkv_grad_low, axis=0, dtype=jnp.float32).reshape(3, D),
        jnp.sum(mixed_low, axis=0, dtype=jnp.float32),
        jnp.sum(widen_grad_low, axis=0, dtype=jnp.float32),
        jnp.sum(narrow_low, axis=0, dtype=jnp.float32),
    )
    row_shares = (
        lax.psum_scatter(triple_weight_grad, "fsdp", scatter_dimension=0, tiled=True),
        lax.psum_scatter(mixing_weight_grad, "fsdp", scatter_dimension=0, tiled=True),
        lax.psum_scatter(widen_weight_grad, "fsdp", scatter_dimension=0, tiled=True),
        lax.psum_scatter(narrow_weight_grad, "fsdp", scatter_dimension=0, tiled=True),
    )
    totals = lax.psum((row_shares[0], row_shares[1], row_shares[2], row_shares[3]), "dp")
    small_sums = lax.psum(
        (
            bias_sums[0],
            bias_sums[1],
            bias_sums[2],
            bias_sums[3],
            jnp.stack([gain_one, gain_two]),
            jnp.stack([shift_one, shift_two]),
            jnp.stack([clip_zero, clip_one, clip_two, clip_three]),
            loss_local,
        ),
        ("dp", "fsdp"),
    )
    shard_index = lax.axis_index("fsdp")
    shard_parts = lax.axis_size("fsdp")

    def own_part(vector, along):
        share_width = vector.shape[along] // shard_parts
        return lax.dynamic_slice_in_dim(vector, shard_index * share_width, share_width, along)

    latent_grads = tuple(
        (
            jnp.where(jnp.abs(latent) <= 1.0, (total / math.sqrt(fan_in))[None], 0.0)
            for latent, total, fan_in in zip(latents, totals, fan_ins)
        )
    )
    loss = small_sums[7] / (hidden_in.shape[0] * D * lax.axis_size("dp") * shard_parts)
    return (
        out_full.astype(jnp.bfloat16),
        loss,
        input_grad,
        latent_grads[0],
        latent_grads[1],
        latent_grads[2],
        latent_grads[3],
        own_part(small_sums[0], 1),
        own_part(small_sums[1], 0),
        own_part(small_sums[2], 0),
        own_part(small_sums[3], 0),
        own_part(small_sums[4], 1),
        own_part(small_sums[5], 1),
        small_sums[6],
    )


bf16 = jnp.bfloat16
f32 = jnp.float32
MESH = pl.DeviceIdType.MESH
VMEM_CAP = 60 * 1024 * 1024
LAYER_CAP = 63 * 1024 * 1024
ROWS = LONG_SLOTS * LONG_LEN + MID_SLOTS * MID_LEN + SHORT_SLOTS * SHORT_LEN
BLOCK = 96
CHUNK = 512
HALF = CHUNK // 2
SECTION = FF // CHUNK
WIDE = 3 * SECTION - 1
CHUNKS = WIDE + 2
SLOTS = 4


def dot_nn(a, b):
    return lax.dot_general(a, b, (((1,), (0,)), ((), ())), preferred_element_type=f32)


def dot_nt(a, b):
    return lax.dot_general(a, b, (((1,), (1,)), ((), ())), preferred_element_type=f32)


def dot_tn(a, b):
    return lax.dot_general(a, b, (((0,), (0,)), ((), ())), preferred_element_type=f32)


def loop(count, step, body):
    def run(i, carry):
        body(pl.multiple_of(i * step, step))
        return carry

    lax.fori_loop(0, count, run, 0)


def plane_of(block, half, group):
    place = block * 24 + half * 12 + group
    bit = place % 32
    return place // 32, (1 << bit) if bit < 31 else -(1 << 31)


def unpack_blocks(words, scl, blocks, dst):
    def one(owner, carry):
        for block in blocks:
            unpack_owner(words, scl, block, dst, owner)
        return carry

    lax.fori_loop(0, 8, one, 0)


def unpack_owner(words, scl, block, dst, owner):
    index = 0 if block < 3 else 1 if block == 3 else 2 if block < 8 else block - 5

    for pair in range(6):
        parts = []
        for group in (2 * pair, 2 * pair + 1):
            total = None
            for half in range(2):
                word, bit = plane_of(block, half, group)
                bits = words[owner, word * 8 : (word + 1) * 8, :] & jnp.int32(bit)
                column = index * 2 + half
                scale = jnp.broadcast_to(
                    scl[owner, group * 8 : (group + 1) * 8, column : column + 1], (8, D)
                )
                value = jnp.where(bits != 0, scale, -scale)
                total = value if total is None else total + value
            parts.append(total)
        tile = jnp.concatenate(parts, axis=0).astype(bf16)
        if block < 8:
            start = owner * BLOCK + pair * 16
        else:
            start = owner * (4 * BLOCK) + (block - 8) * BLOCK + pair * 16
        rows = pl.ds(pl.multiple_of(start, 16), 16)
        if block < 3:
            dst[rows, block * D : (block + 1) * D] = tile
        elif block < 8 and block > 3:
            dst[rows, (block - 4) * D : (block - 3) * D] = tile
        else:
            dst[rows, :] = tile


def clip_back(grad, value, level, inverse):
    u = value * inverse
    t = jnp.tanh(u)
    slope = 1.0 - t * t
    return grad * slope, jnp.sum(grad * (t - u * slope), axis=0, keepdims=True)


def norm_rows(v):
    center = v - jnp.mean(v, axis=1, keepdims=True)
    variance = jnp.mean(center * center, axis=1, keepdims=True)
    rstd = lax.rsqrt(variance + norm_epsilon)
    return center * rstd, rstd


def norm_rows_back(grad, hat, rstd, gain_row):
    g = grad * gain_row
    return rstd * (
        g - jnp.mean(g, axis=1, keepdims=True) - hat * jnp.mean(g * hat, axis=1, keepdims=True)
    )


def colsum(v):
    return jnp.sum(v, axis=0, keepdims=True)


HALF_ROOT = 1.0 / math.sqrt(2.0)
DENSITY = 1.0 / math.sqrt(2.0 * math.pi)


def layer_kernel(
    seq, live, level, tb, mb, wb, nb, gain, shift, hid_in, teach, teach_scores, tl, ml, wl, nl,
    out_to, acc_to, fin_to, kept_to, small_out,
    out, acc, fin, kept, hid, words, small, scl, spread,
    wt, wm, ww, wn, prm, bias, wbias, qkv, low, ctx, hat1, rstd1, widened, act, wg, sgrad,
    cgrad, valid, pair, xlT, clT, wlT, nlT, sums, tbuf, pt, rb, rx, rz, rf, held, ry, rd, sin,
    s1, r1, s2, r2, s3, r3, s4, r4, s5, r5, s6, r6, sms, smr, tsem, lsem, zs, zr, cs_, cr_, hsem, fsem, s7, r7,
):
    dp = lax.axis_index("dp")
    me = lax.axis_index("fsdp")
    x = lax.rem(dp, 2)
    y = lax.div(dp, 2)
    z = lax.div(me, 2)
    core = lax.rem(me, 2)
    over_x = (dp + 1 - 2 * x, me)
    over_y = (dp + 2 - 4 * y, me)
    over_core = (dp, z * 2 + 1 - core)

    def remote(src, dst, send, recv, to):
        return pltpu.make_async_remote_copy(
            src_ref=src, dst_ref=dst, send_sem=send, recv_sem=recv, device_id=to,
            device_id_type=MESH,
        )

    greet = pltpu.get_barrier_semaphore()
    for to in (over_core, over_x, over_y) + tuple(
        (dp, lax.rem(z + hop, 4) * 2 + core) for hop in (1, 2, 3)
    ):
        pl.semaphore_signal(greet, inc=1, device_id=to, device_id_type=MESH)

    teach_load = pltpu.make_async_copy(teach, cgrad, hsem.at[0])
    hid_load = pltpu.make_async_copy(hid_in, hid, hsem.at[1])
    out_save = pltpu.make_async_copy(out, out_to, hsem.at[2])
    acc_save = pltpu.make_async_copy(acc, acc_to, hsem.at[3])
    kept_save = pltpu.make_async_copy(kept, kept_to, hsem.at[4])

    loads = []
    for half in range(2):
        band = slice(192 + half * BLOCK, 192 + (half + 1) * BLOCK)
        loads.append([
            pltpu.make_async_copy(tl.at[half], widened.at[band, 0 : 3 * D], lsem.at[half, 0]),
            pltpu.make_async_copy(ml.at[half], widened.at[band, 3 * D : FF], lsem.at[half, 1]),
            pltpu.make_async_copy(
                wl.at[half], widened.at[half * BLOCK : (half + 1) * BLOCK, :], lsem.at[half, 2]
            ),
            pltpu.make_async_copy(
                nl.at[half], (ctx if half == 0 else sgrad).at[0 : 4 * BLOCK, :], lsem.at[half, 3]
            ),
        ])
    for index in range(4):
        for half in range(2):
            loads[half][index].start()
    hid_load.start()
    teach_load.start()

    def latent_piece(block, half, group):
        if block < 4:
            rows = pl.ds(192 + half * BLOCK + group * 8, 8)
            return widened[rows, block * D : (block + 1) * D]
        if block < 8:
            return widened[pl.ds(half * BLOCK + group * 8, 8), (block - 4) * D : (block - 3) * D]
        rows = pl.ds((block - 8) * BLOCK + group * 8, 8)
        return (ctx if half == 0 else sgrad)[rows, :]

    planes = [[] for _ in range(9)]
    for block in range(12):
        for half in range(2):
            for group in range(12):
                word, bit = plane_of(block, half, group)
                planes[word].append((block, half, group, bit))

    def pack(word):
        total = jnp.zeros((8, D), jnp.int32)
        for block, half, group, bit in planes[word]:
            piece = latent_piece(block, half, group)
            total = total | jnp.where(piece > 0, jnp.int32(bit), jnp.int32(0))
        words[me, word * 8 : (word + 1) * 8, :] = total

    def pack_kept(word):
        total = jnp.zeros((8, D), jnp.int32)
        for block, half, group, bit in planes[word]:
            piece = jnp.abs(latent_piece(block, half, group))
            total = total | jnp.where(piece <= 1.0, jnp.int32(bit), jnp.int32(0))
        kept[word * 8 : (word + 1) * 8, :] = total

    def part_of(owner, index):
        return small.at[owner] if index == 3 else words.at[owner, index * 24 : (index + 1) * 24]

    def z_send(index, hop):
        ref = part_of(me, index)
        peer = lax.rem(z + hop, 4) * 2 + core
        return remote(ref, ref, zs.at[index, hop - 1], zr.at[index, hop - 1], (dp, peer))

    def core_send(index, hop):
        ref = part_of(lax.rem(z + 4 - hop, 4) * 2 + core, index)
        return remote(ref, ref, cs_.at[index, hop], cr_.at[index, hop], over_core)

    def send_out(index):
        for hop in (2, 1, 3):
            z_send(index, hop).start()
        core_send(index, 0).start()

    def pass_on(index):
        for hop in (1, 3, 2):
            z_send(index, hop).wait()
            core_send(index, hop).start()

    def all_here(index):
        for hop in range(4):
            core_send(index, hop).wait()

    for half in range(2):
        loads[half][0].wait()
        loads[half][1].wait()
    for word in range(3):
        pack(word)
    pl.semaphore_wait(greet, 6)
    send_out(0)
    for half in range(2):
        loads[half][2].wait()
        loads[half][3].wait()
    slot_lane = lax.broadcasted_iota(jnp.int32, (8, 128), 1)

    def scale_rows(pair):
        for part in range(2):
            scale_group(pl.multiple_of(pair + part * 8, 8))

    def scale_group(group):
        tile = jnp.zeros((8, 128), f32)
        for half in range(2):
            rows = pl.ds(pl.multiple_of(192 + half * BLOCK + group, 8), 8)
            for index in range(7):
                if index == 0:
                    part = widened[rows, 0 : 3 * D]
                elif index == 1:
                    part = widened[rows, 3 * D : FF]
                elif index == 2:
                    part = widened[pl.ds(pl.multiple_of(half * BLOCK + group, 8), 8), :]
                else:
                    at = pl.ds(pl.multiple_of((index - 3) * BLOCK + group, 8), 8)
                    part = (ctx if half == 0 else sgrad)[at, :]
                fan = FF if index >= 3 else D
                mean = jnp.sum(jnp.abs(part), axis=1, keepdims=True) * (1.0 / part.shape[1])
                tile = jnp.where(slot_lane == index * 2 + half, mean / math.sqrt(fan), tile)
        spread[pl.ds(group, 8), :] = tile

    loop(6, 16, scale_rows)
    spread[BLOCK:128, :] = jnp.zeros((128 - BLOCK, 128), f32)
    small[me, 0:16, :] = spread[...].T[0:16, :]
    small[me, 16:32, :] = jnp.zeros((16, 128), f32)
    small[me, 16:19, 0:BLOCK] = tb[...]
    small[me, 19:20, 0:BLOCK] = mb[...]
    small[me, 20:21, 0:BLOCK] = nb[...]
    small[me, 21:23, 0:BLOCK] = gain[...]
    small[me, 23:25, 0:BLOCK] = shift[...]
    for part in range(3):
        small[me, 25 + part : 26 + part, :] = wb[part * 128 : (part + 1) * 128].reshape(1, 128)
    send_out(3)
    for word in range(3, 9):
        pack(word)
    for word in range(9):
        pack_kept(word)
    kept_save.start()
    c0, c1, c2, c3 = level[0], level[1], level[2], level[3]
    i0, i1, i2, i3 = 1.0 / c0, 1.0 / c1, 1.0 / c2, 1.0 / c3
    sums[...] = jnp.zeros_like(sums)
    row = lax.broadcasted_iota(jnp.int32, (256, 256), 0)
    col = lax.broadcasted_iota(jnp.int32, (256, 256), 1)
    key_ok = col < seq[0, 0]
    query_ok = row < seq[0, 0] * live[0, 0]
    valid[0] = jnp.where(key_ok, 1.0, 0.0).astype(bf16)
    pair[0] = jnp.where(key_ok & query_ok, 1.0, 0.0).astype(bf16)

    def in_slots(at):
        mid = (at < 128) & (at < seq[0, 1])
        one = (at >= 128) & (at < 192) & (at - 128 < seq[0, 2])
        two = (at >= 192) & (at - 192 < seq[0, 3])
        return mid, one, two

    km, ko, kt = in_slots(col)
    qm, qo, qt = in_slots(row)
    key_ok = (km & (row < 128)) | (ko & (row >= 128) & (row < 192)) | (kt & (row >= 192))
    live_mid = row * 0 + live[0, 1] > 0
    live_one = row * 0 + live[0, 2] > 0
    live_two = row * 0 + live[0, 2] > 1
    query_ok = (qm & live_mid) | (qo & live_one) | (qt & live_two)
    valid[1] = jnp.where(key_ok, 1.0, 0.0).astype(bf16)
    pair[1] = jnp.where(key_ok & query_ok, 1.0, 0.0).astype(bf16)
    ones = jnp.where(query_ok, 1.0, 0.0)

    def clip_in(r):
        x = hid[pl.ds(r, 128), :].astype(f32)
        lo = (c0 * jnp.tanh(x * i0)).astype(bf16)
        low[pl.ds(r, 128), :] = lo

    hid_load.wait()
    for r in range(0, ROWS, 128):
        clip_in(r)
    pass_on(3)
    all_here(3)
    total = jnp.zeros((16, D), f32)
    param_lane = lax.broadcasted_iota(jnp.int32, (16, 128), 1)
    for owner in range(8):
        turned = jnp.concatenate([small[owner, 0:16, :], jnp.zeros((112, 128), f32)], axis=0).T
        scl[owner] = turned[0:BLOCK, :]
        piece = jnp.where(param_lane < BLOCK, small[owner, 16:32, :], 0.0)
        wide = jnp.concatenate([piece, jnp.zeros((16, D - 128), f32)], axis=1)
        total = total + (pltpu.roll(wide, owner * BLOCK, 1) if owner else wide)
        for part in range(3):
            at = owner * 4 * BLOCK + part * 128
            wbias[0:1, at : at + 128] = small[owner, 25 + part : 26 + part, :]
    prm[...] = total
    for part in range(3):
        bias[0:1, part * D : (part + 1) * D] = prm[part : part + 1, :]
    def same_core(hop, carry):
        @pl.when(hop > 0)
        def _():
            z_send(0, hop).wait()
            core_send(0, hop).start()

        for block in range(3):
            unpack_owner(words, scl, block, wt, lax.rem(z + 4 - hop, 4) * 2 + core)
        return carry

    def other_core(hop, carry):
        core_send(0, hop).wait()
        for block in range(3):
            unpack_owner(words, scl, block, wt, lax.rem(z + 4 - hop, 4) * 2 + 1 - core)
        return carry

    lax.fori_loop(0, 4, same_core, 0)
    send_out(1)
    lax.fori_loop(0, 4, other_core, 0)

    for part in range(9):
        cs = slice(part * 256, (part + 1) * 256)
        qkv[:, cs] = (dot_nn(low[...], wt[:, cs]) + bias[0:1, cs]).astype(bf16)
    send_out(2)
    lane = lax.broadcasted_iota(jnp.int32, (256, 128), 1)
    first = lane < 64

    def pick(v, j):
        return jnp.where(first, v, jnp.zeros_like(v)) if j == 0 else jnp.where(first, jnp.zeros_like(v), v)

    def softmax(q, k, ok, j):
        s = dot_nt(pick(q, j), k) * (HEAD_DIM**-0.5)
        masked = jnp.where(ok, s, masked_fill)
        e = jnp.exp(masked - jnp.max(masked, axis=1, keepdims=True))
        return s, e / jnp.sum(e, axis=1, keepdims=True)

    for g in range(2):
        for c in range(0, D, 128):
            rs = slice(g * 256, (g + 1) * 256)
            q, k, v = (qkv[rs, at + c : at + c + 128] for at in (0, D, 2 * D))
            ok = valid[g].astype(f32) > 0.5
            parts = []
            for j in range(2):
                s, p = softmax(q, k, ok, j)
                parts.append(dot_nn(p.astype(bf16), v))
            ctx[rs, c : c + 128] = jnp.where(first, parts[0], parts[1])
    pass_on(1)
    unpack_blocks(words, scl, (3,), wm)

    def clip_ctx(r):
        lo = (c1 * jnp.tanh(ctx[pl.ds(r, 128), :] * i1)).astype(bf16)
        low[pl.ds(r, 128), :] = lo

    for r in range(0, ROWS, 128):
        clip_ctx(r)

    for part in range(3):
        cs = slice(part * 256, (part + 1) * 256)
        acc[:, cs] = dot_nn(low[...], wm[:, cs]) + prm[3:4, cs] + hid[:, cs].astype(f32)

    def norm_one(r):
        rs = pl.ds(r, 128)
        hat, rstd = norm_rows(acc[rs, :])
        hat1[rs, :] = hat
        rstd1[rs, :] = jnp.broadcast_to(rstd, (128, 128))
        normed = hat * prm[5:6, :] + prm[7:8, :]
        lo = (c2 * jnp.tanh(normed * i2)).astype(bf16)
        low[rs, :] = lo
        acc[rs, :] = normed + prm[4:5, :]

    loop(4, 128, norm_one)
    all_here(1)
    pass_on(2)
    unpack_blocks(words, scl, range(4, 8), ww)
    all_here(2)

    for t in range(8):
        for owner in ((0, 1), (2,), (3,), (4,), (5,), (6,), (7,), ())[t]:
            for block in range(8, 12):
                unpack_owner(words, scl, block, wn, owner)
        if t < 6:
            cs = slice(t * 512, (t + 1) * 512)
            widened[:, cs] = dot_nn(low[...], ww[:, cs]) + wbias[0:1, cs]
        if 1 <= t <= 6:
            cs = slice((t - 1) * 512, t * 512)
            for r in range(0, ROWS, 64):
                w = widened[r : r + 64, cs]
                a = 0.5 * w * (1.0 + lax.erf(w * HALF_ROOT))
                act[r : r + 64, cs] = (c3 * jnp.tanh(a * i3)).astype(bf16)
        if t >= 2:
            cs = slice((t - 2) * 512, (t - 1) * 512)
            acc[...] += dot_nn(act[:, cs], wn[cs, :])

    teach_load.wait()

    def norm_two(r):
        rs = pl.ds(r, 128)
        hat, rstd = norm_rows(acc[rs, :])
        full = hat * prm[6:7, :] + prm[8:9, :]
        out[rs, :] = full.astype(bf16)
        at = lax.broadcasted_iota(jnp.int32, (128, D), 0) + r
        l0, l1, l2, l3 = seq[0, 0] * live[0, 0], seq[0, 1], seq[0, 2], seq[0, 3]
        l1 = jnp.where(live[0, 1] > 0, l1, 0)
        l2 = jnp.where(live[0, 2] > 0, l2, 0)
        l3 = jnp.where(live[0, 2] > 1, l3, 0)
        ok = (at < l0) | ((at >= 256) & (at < 256 + l1)) | ((at >= 384) & (at < 384 + l2))
        ok = ok | ((at >= 448) & (at < 448 + l3))
        gap = jnp.where(ok, full - cgrad[rs, :].astype(f32), 0.0)
        sums[15:16, :] += colsum(gap * gap) * 0.5
        sums[6:7, :] += colsum(gap * hat)
        sums[8:9, :] += colsum(gap)
        grad = norm_rows_back(gap, hat, rstd, prm[6:7, :])
        sgrad[rs, :] = grad
        acc[rs, :] = jnp.zeros((128, D), f32)
        lo = grad.astype(bf16)
        low[rs, :] = lo
        nlT[:, rs] = lo.T
        sums[4:5, :] += colsum(lo.astype(f32))

    loop(4, 128, norm_two)
    out_save.start()

    def feed_back(t):
        cs = pl.ds(pl.multiple_of(t * CHUNK, CHUNK), CHUNK)
        wbias[1:2, cs] = jnp.zeros((1, CHUNK), f32)

        def feed_back_rows(r):
            rs = pl.ds(r, 256)
            g = dot_nt(low[rs, :], wn[cs, :])
            w = widened[rs, cs]
            e = 0.5 * (1.0 + lax.erf(w * HALF_ROOT))
            a = w * e
            u = a * i3
            th = jnp.tanh(u)
            slope = 1.0 - th * th
            sums[14:15, 0:CHUNK] += colsum(g * (th - u * slope))
            back = g * slope * (e + w * (DENSITY * jnp.exp(-0.5 * w * w)))
            lo = back.astype(bf16)
            wg[rs, cs] = lo
            wbias[1:2, cs] += colsum(lo.astype(f32))
            acc[rs, :] += dot_nt(lo, ww[:, cs])

        loop(2, 256, feed_back_rows)

    def turn_widen(r):
        rs = pl.ds(r, 128)
        normed = hat1[rs, :] * prm[5:6, :] + prm[7:8, :]
        wlT[:, rs] = (c2 * jnp.tanh(normed * i2)).astype(bf16).T

    def turn_context(r):
        clT[:, pl.ds(r, 128)] = (c1 * jnp.tanh(ctx[pl.ds(r, 128), :] * i1)).astype(bf16).T

    def turn_inputs(r):
        v = hid[pl.ds(r, 128), :].astype(f32)
        xlT[:, pl.ds(r, 128)] = (c0 * jnp.tanh(v * i0)).astype(bf16).T

    def norm_one_back(r):
        rs = pl.ds(r, 128)
        hat = hat1[rs, :]
        normed = hat * prm[5:6, :] + prm[7:8, :]
        grad, clip_sum = clip_back(acc[rs, :], normed, c2, i2)
        sums[18:19, :] += clip_sum
        grad = grad + sgrad[rs, :]
        sums[5:6, :] += colsum(grad * hat)
        sums[7:8, :] += colsum(grad)
        grad = norm_rows_back(grad, hat, rstd1[rs, 0:1], prm[5:6, :])
        acc[rs, :] = grad
        lo = grad.astype(bf16)
        low[rs, :] = lo
        sums[3:4, :] += colsum(lo.astype(f32))

    def mix_back(c):
        cs = pl.ds(c, 256)
        g = dot_nt(low[...], wm[cs, :])
        grad, clip_sum = clip_back(g, ctx[:, cs], c1, i1)
        sums[17:18, cs] += clip_sum
        cgrad[:, cs] = grad.astype(bf16)

    def scores_copy(u, slot):
        g = lax.div(u, 6)
        hp = lax.rem(u, 6)
        rs = pl.ds(pl.multiple_of(g * 256, 256), 256)
        return pltpu.make_async_copy(
            teach_scores.at[pl.ds(2 * hp, 2), rs], tbuf.at[slot], tsem.at[slot]
        )

    def attend_pair_back(u, slot):
        g = lax.div(u, 6)
        hp = lax.rem(u, 6)
        rs = pl.ds(pl.multiple_of(g * 256, 256), 256)
        q0 = pl.multiple_of(hp * 128, 128)
        k0 = pl.multiple_of(D + q0, 128)
        v0 = pl.multiple_of(2 * D + q0, 128)
        q = qkv[rs, pl.ds(q0, 128)]
        k = qkv[rs, pl.ds(k0, 128)]
        v = qkv[rs, pl.ds(v0, 128)]
        cg = cgrad[rs, pl.ds(q0, 128)]
        ok = valid[g].astype(f32) > 0.5
        pairs = pair[g].astype(f32) > 0.5
        dq, dk, dv = [], [], []
        for j in range(2):
            s, p = softmax(q, k, ok, j)
            ts = tbuf[slot, j].astype(f32)
            second = pltpu.roll(ts[128:192], 128, 1)
            third = pltpu.roll(ts[192:256], 192, 1)
            moved = jnp.concatenate([ts[0:128], second, third], axis=0)
            ts = jnp.where(g > 0, moved, ts)
            gap = jnp.where(pairs, s - ts, 0.0)
            sums[16:17, 0:256] += colsum(gap * gap) * (0.5 / LONG_LEN)
            pg = dot_nt(pick(cg, j), v)
            sg = p * (pg - jnp.sum(pg * p, axis=1, keepdims=True)) + gap * (1.0 / LONG_LEN)
            sg = sg.astype(bf16)
            dv.append(dot_tn(p.astype(bf16), cg))
            dq.append(dot_nn(sg, k))
            dk.append(dot_tn(sg, q))
        scale = HEAD_DIM**-0.5
        dq = (jnp.where(first, dq[0], dq[1]) * scale).astype(bf16)
        dk = (jnp.where(first, dk[0], dk[1]) * scale).astype(bf16)
        dv = jnp.where(first, dv[0], dv[1]).astype(bf16)
        for index, (grad, at) in enumerate(((dq, q0), (dk, k0), (dv, v0))):
            qkv[rs, pl.ds(at, 128)] = grad
            sums[index : index + 1, pl.ds(q0, 128)] += colsum(grad.astype(f32))

    def input_back(c):
        cs = pl.ds(c, 256)
        g = dot_nt(qkv[...], wt[cs, :])
        grad, clip_sum = clip_back(g, hid[:, cs].astype(f32), c0, i0)
        sums[19:20, cs] += clip_sum
        acc[:, cs] += grad

    def close_sums():
        for part in range(4):
            sums[9 + part : 10 + part, :] = wbias[1:2, part * D : (part + 1) * D]
        at = lax.broadcasted_iota(jnp.int32, (1, D), 1)
        line = jnp.zeros((1, D), f32)
        for spot, value in enumerate(
            (
                sums[19:20, :], sums[17:18, :], sums[18:19, :], sums[14:15, :],
                sums[15:16, :] + sums[16:17, :],
            )
        ):
            line = jnp.where(at == spot, jnp.sum(value), line)
        sums[13:14, :] = line
        small_out[...] = sums[0:16, :]

    firsts = (over_x, over_y)
    seconds = (over_y, over_x)
    outer = (z == 0) | (z == 3)
    inner = (z == 1) | (z == 2)
    near = z + 1 - 2 * lax.rem(z, 2)
    beyond = 1 - lax.div(z, 2)

    def on_z(to):
        return (dp, to * 2 + core)

    def lanes(p, w):
        return pl.ds(p * (w // 2), w // 2)

    def core_copy(k, w):
        slot, duo = lax.rem(k, SLOTS), lax.rem(k, 2)
        cs = pl.ds(0, w)
        return remote(
            pt.at[slot, :, 1 - core, :, :, :, cs], rb.at[duo, :, :, :, :, cs], s1.at[slot],
            r1.at[slot], over_core,
        )

    def own_rows(slot, blocks, p, w, mine):
        i = (x if p == 0 else y) if mine else (1 - x if p == 0 else 1 - y)
        if p == 0:
            return pt.at[slot, blocks, core, i, :, :, lanes(p, w)]
        return pt.at[slot, blocks, core, :, i, :, lanes(p, w)]

    def first_copy(k, w, p):
        slot, duo = lax.rem(k, SLOTS), lax.rem(k, 2)
        src = own_rows(slot, pl.ds(0, 4), p, w, False)
        dst = rx.at[duo, p, :, :, :, lanes(0, w)]
        return remote(src, dst, s2.at[slot, p], r2.at[slot, p], firsts[p])

    def in_copy(k, w, p):
        slot, duo = lax.rem(k, SLOTS), lax.rem(k, 2)
        src = own_rows(slot, pl.ds(beyond, 3), p, w, True)
        dst = rz.at[duo, p, :, :, :, lanes(0, w)]
        return remote(src, dst, s3.at[slot, p], r3.at[slot, p], on_z(near))

    def out_copy(k, w, p, kind):
        slot = lax.rem(k, SLOTS)
        to = (near, 3 - z, lax.rem(z + 2, 4))[kind]
        return remote(
            own_rows(slot, to, p, w, True), rf.at[slot, min(kind, 1), p, :, :, lanes(0, w)],
            s4.at[slot, kind, p], r4.at[slot, min(kind, 1), p], on_z(to),
        )

    def direct_copy(p, hop):
        to = lax.rem(z + hop, 4)
        return remote(
            own_rows((CHUNKS - 1) % SLOTS, to, p, HALF, True), rd.at[hop - 1, p],
            s7.at[hop - 1, p], r7.at[hop - 1, p], on_z(to),
        )

    def room_of(k):
        return 2 if isinstance(k, int) else lax.rem(k, 2)

    def second_copy(k, w, p):
        slot, duo = lax.rem(k, SLOTS), room_of(k)
        cs = lanes(0, w)
        return remote(
            held.at[duo, p, :, :, cs], ry.at[duo, p, :, :, cs], s5.at[slot, p], r5.at[slot, p],
            seconds[p],
        )

    def fin_at(k, w, p, rows):
        if w == CHUNK:
            flat = k * CHUNK
        else:
            flat = WIDE * CHUNK + (k - WIDE) * w
        cs = pl.ds(pl.multiple_of(lax.rem(flat, FF) + p * (w // 2), 128), w // 2)
        return (lax.div(flat, FF), *((x, rows) if p == 0 else (rows, y)), slice(None), cs)

    def back_first(k, w, p):
        slot = lax.rem(k, SLOTS)
        ref = fin.at[fin_at(k, w, p, slice(None))]
        return remote(ref, ref, s6.at[slot, p], r6.at[slot, p], firsts[p])

    def small_copy(step):
        to = (
            over_core, over_x, over_y, on_z(lax.rem(z + 1, 4)), on_z(lax.rem(z + 2, 4)),
            on_z(lax.rem(z + 3, 4)),
        )[step]
        return remote(small_out, sin.at[step], sms.at[step], smr.at[step], to)

    def finish_first(k, w):
        for p in range(2):
            back_first(k, w, p).wait()
        fin_save(k, w).start()

    def fin_save(k, w):
        if w == CHUNK:
            flat = k * CHUNK
        else:
            flat = WIDE * CHUNK + (k - WIDE) * w
        cs = pl.ds(pl.multiple_of(lax.rem(flat, FF), 128), w)
        at = (lax.div(flat, FF), slice(None), slice(None), slice(None), cs)
        return pltpu.make_async_copy(fin.at[at], fin_to.at[at], fsem.at[lax.rem(k, SLOTS)])

    def finish_save(k, w):
        fin_save(k, w).wait()

    def finish_second(k, w):
        duo = room_of(k)
        for p in range(2):
            second_copy(k, w, p).wait()
            for i in range(2):
                cs = lanes(0, w)
                fin[fin_at(k, w, p, i)] = held[duo, p, i, :, cs] + ry[duo, p, i, :, cs]
            back_first(k, w, p).start()

    def finish_out(k, w):
        slot, duo = lax.rem(k, SLOTS), lax.rem(k, 2)
        cs = lanes(0, w)

        @pl.when(outer)
        def _():
            for p in range(2):
                out_copy(k, w, p, 0).wait_recv()
                out_copy(k, w, p, 2).wait_recv()
                for i in range(2):
                    at = (x, i) if p == 0 else (i, y)
                    own = pt[(slot, z, core, *at, slice(None), lanes(p, w))]
                    held[duo, p, i, :, cs] = (
                        own + rf[slot, 0, p, i, :, cs] + rf[slot, 1, p, i, :, cs]
                    )

        @pl.when(inner)
        def _():
            for p in range(2):
                out_copy(k, w, p, 1).wait()
                out_copy(k, w, p, 0).wait_send()
                out_copy(k, w, p, 2).wait_send()
                for i in range(2):
                    at = (x, i) if p == 0 else (i, y)
                    own = pt[(slot, z, core, *at, slice(None), lanes(p, w))]
                    held[duo, p, i, :, cs] = own + rf[slot, 1, p, i, :, cs]

        for p in range(2):
            second_copy(k, w, p).start()

    def finish_in(k, w):
        slot, duo = lax.rem(k, SLOTS), lax.rem(k, 2)

        @pl.when(outer)
        def _():
            for p in range(2):
                in_copy(k, w, p).wait_send()

        @pl.when(inner)
        def _():
            for p in range(2):
                in_copy(k, w, p).wait_recv()
                for q in range(3):
                    for i in range(2):
                        at = (x, i) if p == 0 else (i, y)
                        at = (slot, beyond + q, core, *at, slice(None), lanes(p, w))
                        pt[at] += rz[duo, p, q, i, :, lanes(0, w)]
                for kind in (2, 1, 0):
                    out_copy(k, w, p, kind).start()

    def add_first(k, w, p):
        slot, duo = lax.rem(k, SLOTS), lax.rem(k, 2)
        first_copy(k, w, p).wait()
        for q in range(4):
            for i in range(2):
                at = (x, i) if p == 0 else (i, y)
                at = (slot, q, core, *at, slice(None), lanes(p, w))
                pt[at] += rx[duo, p, q, i, :, lanes(0, w)]

    def finish_one(k, w):
        for p in range(2):
            add_first(k, w, p)

            @pl.when(outer)
            def _():
                in_copy(k, w, p).start()

    def last_one():
        for p in range(2):
            add_first(CHUNKS - 1, HALF, p)
            for hop in (2, 1, 3):
                direct_copy(p, hop).start()

    def last_direct():
        slot = (CHUNKS - 1) % SLOTS
        for p in range(2):
            for hop in (1, 3, 2):
                direct_copy(p, hop).wait()
            for i in range(2):
                at = (x, i) if p == 0 else (i, y)
                own = pt[(slot, z, core, *at, slice(None), lanes(p, HALF))]
                held[2, p, i, :, lanes(0, HALF)] = own + rd[0, p, i] + rd[1, p, i] + rd[2, p, i]
            second_copy(CHUNKS - 1, HALF, p).start()

    def finish_core(k, w):
        slot, duo = lax.rem(k, SLOTS), lax.rem(k, 2)
        core_copy(k, w).wait()
        cs = pl.ds(0, w)
        for q in range(4):
            pt[slot, q, core, :, :, :, cs] += rb[duo, q, :, :, :, cs]
        for p in range(2):
            first_copy(k, w, p).start()

    stages = (
        (7, finish_save), (6, finish_first), (5, finish_second), (4, finish_out), (3, finish_in),
        (2, finish_one), (1, finish_core),
    )
    last = CHUNKS - 1
    last_stages = {
        5: lambda: finish_second(last, HALF), 4: last_direct, 2: last_one,
        6: lambda: finish_first(last, HALF), 1: lambda: finish_core(last, HALF),
    }

    def tick(t, carry):
        for lag, step in stages:

            @pl.when((t >= lag) & (t < lag + WIDE))
            def _():
                step(t - lag, CHUNK)

            @pl.when(t == lag + WIDE)
            def _():
                step(t - lag, HALF)

            if lag in last_stages:

                @pl.when(t == last + lag - (1 if lag > 2 else 0))
                def _():
                    last_stages[lag]()

        slot = lax.rem(t, SLOTS)

        def put(owner, cs, block):
            for i in range(2):
                for j in range(2):
                    at = (i * 2 + j) * 24
                    pt[slot, owner // 2, owner % 2, i, j, :, cs] = block[at : at + 24, :]

        pieces = CHUNK // 128
        turns = 8 // pieces

        @pl.when(t < SECTION)
        def _():
            j = lax.div(t, turns)
            count = pieces * BLOCK
            left = nlT[pl.ds(pl.multiple_of(lax.rem(t, turns) * count, count), count), :]
            for owner in range(8):
                cs = pl.ds(pl.multiple_of(owner * 384 + j * 128, 128), 128)
                got = dot_nn(left, act[:, cs])
                for part in range(pieces):
                    put(owner, pl.ds(part * 128, 128), got[part * BLOCK : (part + 1) * BLOCK, :])

        def whole(left, right, half):
            got = dot_nn(left, right)
            for owner in range(8):
                put(owner, pl.ds(half * 256, 256), got[owner * BLOCK : (owner + 1) * BLOCK, :])

        for half in range(2):

            @pl.when((t >= SECTION) & (t < 2 * SECTION))
            def _():
                cs = pl.ds(pl.multiple_of((t - SECTION) * CHUNK + half * 256, 256), 256)
                whole(wlT[...], wg[:, cs], half)

            part = (t - 2 * SECTION) * 2 + half

            @pl.when((part >= 0) & (part < 3))
            def _():
                whole(clT[...], low[:, pl.ds(pl.multiple_of(part * 256, 256), 256)], half)

            @pl.when((part >= 3) & (part < 10))
            def _():
                whole(xlT[...], qkv[:, pl.ds(pl.multiple_of((part - 3) * 256, 256), 256)], half)

        @pl.when(t < WIDE)
        def _():
            core_copy(t, CHUNK).start()

        @pl.when((t >= WIDE) & (t < CHUNKS))
        def _():
            cs = pl.ds(pl.multiple_of((t - WIDE + 7) * 256, 256), 256)
            whole(xlT[...], qkv[:, cs], 0)
            core_copy(t, HALF).start()

        for when, turn in ((2, turn_inputs), (3, turn_context), (4, turn_widen)):

            @pl.when(t == when)
            def _():
                loop(4, 128, turn)

        units = 12 // SECTION
        begin = SECTION + 1

        @pl.when((t >= 1) & (t < SECTION))
        def _():
            feed_back(t - 1)

        @pl.when(t == SECTION - 1)
        def _():
            feed_back(t)

        @pl.when(t == SECTION)
        def _():
            for slot in range(2):
                scores_copy(slot, slot).start()
            loop(4, 128, norm_one_back)
            loop(3, 256, mix_back)

        @pl.when((t >= begin) & (t < begin + SECTION))
        def _():
            for index in range(units):
                u = (t - begin) * units + index
                at = lax.rem(u, 2)
                scores_copy(u, at).wait()
                attend_pair_back(u, at)

                @pl.when(u < 10)
                def _():
                    scores_copy(u + 2, at).start()

        done = begin + SECTION

        @pl.when((t >= done) & (t < done + 3))
        def _():
            input_back(pl.multiple_of((t - done) * 256, 256))

        @pl.when(t == done + 3)
        def _():
            acc_save.start()
            close_sums()
            small_copy(0).start()

        @pl.when(t == done + 4)
        def _():
            small_copy(0).wait()
            small_out[...] += sin[0]
            small_copy(1).start()

        @pl.when(t == done + 5)
        def _():
            small_copy(1).wait()
            small_out[...] += sin[1]
            small_copy(2).start()

        @pl.when(t == done + 6)
        def _():
            small_copy(2).wait()
            small_out[...] += sin[2]
            for step in (3, 4, 5):
                small_copy(step).start()

        @pl.when(t == done + 7)
        def _():
            for step in (3, 4, 5):
                small_copy(step).wait()
            small_out[...] = small_out[...] + sin[3] + sin[4] + sin[5]

        return carry

    lax.fori_loop(0, CHUNKS + 5, tick, 0)
    fin_save(WIDE, HALF).wait()
    fin_save(last, HALF).wait()
    for copy in (out_save, acc_save, kept_save):
        copy.wait()


def layer(*args):
    vm = pl.BlockSpec(memory_space=pltpu.VMEM)
    sm = pl.BlockSpec(memory_space=pltpu.SMEM)
    sds = jax.ShapeDtypeStruct
    dma = pltpu.SemaphoreType.DMA
    return pl.pallas_call(
        layer_kernel,
        out_shape=(
            sds((ROWS, D), bf16),
            sds((ROWS, D), f32),
            sds((3, 2, 2, 24, FF), f32),
            sds((72, D), jnp.int32),
            sds((16, D), f32),
        ),
        in_specs=[sm] * 3 + [vm] * 6 + [pl.BlockSpec(memory_space=pl.ANY)] * 7,
        out_specs=(pl.BlockSpec(memory_space=pl.ANY),) * 4 + (vm,),
        scratch_shapes=[
            pltpu.VMEM((ROWS, D), bf16),
            pltpu.VMEM((ROWS, D), f32),
            pltpu.VMEM((3, 2, 2, 24, FF), f32),
            pltpu.VMEM((72, D), jnp.int32),
            pltpu.VMEM((ROWS, D), bf16),
            pltpu.VMEM((8, 72, D), jnp.int32),
            pltpu.VMEM((8, 32, 128), f32),
            pltpu.VMEM((8, BLOCK, 128), f32),
            pltpu.VMEM((128, 128), f32),
            pltpu.VMEM((D, 3 * D), bf16),
            pltpu.VMEM((D, D), bf16),
            pltpu.VMEM((D, FF), bf16),
            pltpu.VMEM((FF, D), bf16),
            pltpu.VMEM((16, D), f32),
            pltpu.VMEM((8, 3 * D), f32),
            pltpu.VMEM((8, FF), f32),
            pltpu.VMEM((ROWS, 3 * D), bf16),
            pltpu.VMEM((ROWS, D), bf16),
            pltpu.VMEM((ROWS, D), f32),
            pltpu.VMEM((ROWS, D), f32),
            pltpu.VMEM((ROWS, 128), f32),
            pltpu.VMEM((ROWS, FF), f32),
            pltpu.VMEM((ROWS, FF), bf16),
            pltpu.VMEM((ROWS, FF), bf16),
            pltpu.VMEM((ROWS, D), f32),
            pltpu.VMEM((ROWS, D), bf16),
            pltpu.VMEM((2, 256, 256), bf16),
            pltpu.VMEM((2, 256, 256), bf16),
            pltpu.VMEM((D, ROWS), bf16),
            pltpu.VMEM((D, ROWS), bf16),
            pltpu.VMEM((D, ROWS), bf16),
            pltpu.VMEM((D, ROWS), bf16),
            pltpu.VMEM((24, D), f32),
            pltpu.VMEM((2, 2, 256, 256), bf16),
            pltpu.VMEM((SLOTS, 4, 2, 2, 2, 24, CHUNK), f32),
            pltpu.VMEM((2, 4, 2, 2, 24, CHUNK), f32),
            pltpu.VMEM((2, 2, 4, 2, 24, HALF), f32),
            pltpu.VMEM((2, 2, 3, 2, 24, HALF), f32),
            pltpu.VMEM((SLOTS, 2, 2, 2, 24, HALF), f32),
            pltpu.VMEM((3, 2, 2, 24, HALF), f32),
            pltpu.VMEM((3, 2, 2, 24, HALF), f32),
            pltpu.VMEM((3, 2, 2, 24, HALF // 2), f32),
            pltpu.VMEM((6, 16, D), f32),
        ]
        + [dma((SLOTS,))] * 2
        + [dma((SLOTS, 2))] * 4
        + [dma((SLOTS, 3, 2)), dma((SLOTS, 2, 2))]
        + [dma((SLOTS, 2))] * 4
        + [dma((6,))] * 2
        + [dma((2,)), dma((2, 4)), dma((4, 3)), dma((4, 3)), dma((4, 4)), dma((4, 4)), dma((5,)), dma((SLOTS,)), dma((3, 2)), dma((3, 2))],
        compiler_params=pltpu.CompilerParams(collective_id=0, has_side_effects=True, vmem_limit_bytes=LAYER_CAP),
        name="layer",
    )(*args)


def finish_kernel(
    count, small, kept, fin, out_in, grad_in, out, grad, tg, mg, wg, ng, tb, mb, wb, nb, gain, shift, clips, loss,
    fbuf, turned, tout, mout, wout, nout, obuf, gbuf, fsem, osem, psem,
):
    fcopies = [pltpu.make_async_copy(fin.at[i], fbuf.at[i], fsem.at[i]) for i in range(3)]
    ocopies = []
    for half in range(2):
        for index, (src, dst) in enumerate(((nout, ng), (wout, wg), (mout, mg), (tout, tg))):
            at = index * 2 + half
            ocopies.append(pltpu.make_async_copy(src.at[half], dst.at[half], osem.at[at]))
    for index in (1, 2, 0):
        fcopies[index].start()
    arrive = [
        pltpu.make_async_copy(out_in, obuf, psem.at[0]),
        pltpu.make_async_copy(grad_in, gbuf, psem.at[1]),
    ]
    depart = [
        pltpu.make_async_copy(obuf, out, psem.at[2]),
        pltpu.make_async_copy(gbuf, grad, psem.at[3]),
    ]
    for copy in arrive:
        copy.start()
    me = lax.axis_index("fsdp")
    z = lax.div(me, 2)
    core = lax.rem(me, 2)
    own = pltpu.roll(small[...], lax.rem(8 - me, 8) * BLOCK, 1)
    tb[...] = own[0:3, 0:BLOCK]
    mb[...] = own[3:4, 0:BLOCK]
    nb[...] = own[4:5, 0:BLOCK]
    gain[...] = own[5:7, 0:BLOCK]
    shift[...] = own[7:9, 0:BLOCK]
    wide = pltpu.roll(small[...], core * (4 * BLOCK), 1)
    row = lax.broadcasted_iota(jnp.int32, (16, D), 0)
    picked = jnp.sum(jnp.where(row == 9 + z, wide, 0.0), axis=0, keepdims=True)
    wb[...] = picked[:, 0 : 4 * BLOCK]
    line = small[13:14, :]
    lane = lax.broadcasted_iota(jnp.int32, (1, D), 1)
    for spot in range(4):
        clips[spot] = jnp.sum(jnp.where(lane == spot, line, 0.0))
    loss[...] = jnp.sum(jnp.where(lane == 4, line, 0.0)) * count[0]

    def keep(block, half, group, total, fan):
        word, bit = plane_of(block, half, group)
        bits = kept[word * 8 : (word + 1) * 8, :] & jnp.int32(bit)
        return jnp.where(bits != 0, total * (1.0 / math.sqrt(fan)), 0.0)

    def spread_out(blocks, half, dst, src, at):
        for index, block in enumerate(blocks):
            cols = slice(index * D, (index + 1) * D)
            for group in range(12):
                rows = slice(group * 8, (group + 1) * 8)
                total = src[rows, at + index * D : at + (index + 1) * D]
                dst[half, rows, cols] = keep(block, half, group, total, D)

    def leave(index, half):
        ocopies[index + 4 * half].start()

    fcopies[1].wait()
    for half in range(2):
        spread_out(range(4, 8), half, wout, fbuf.at[1], 0)
        leave(1, half)
    fcopies[2].wait()
    for half in range(2):
        spread_out(range(3), half, tout, fbuf.at[2], D)
        leave(3, half)
    for half in range(2):
        spread_out(range(3, 4), half, mout, fbuf.at[2], 0)
        leave(2, half)
    for index in range(2):
        arrive[index].wait()
        depart[index].start()
    fcopies[0].wait()
    for j in range(3):
        for i in range(2):
            tiles = range((j * 2 + i) * 4, (j * 2 + i) * 4 + 4)
            parts = [fbuf[0, :, tile * 128 : (tile + 1) * 128] for tile in tiles]
            total = jnp.concatenate(parts, axis=0).T
            turned[j * 128 : (j + 1) * 128, i * 384 : (i + 1) * 384] = total
    for half in range(2):
        for block in range(8, 12):
            for group in range(12):
                rows = slice((block - 8) * BLOCK + group * 8, (block - 8) * BLOCK + group * 8 + 8)
                nout[half, rows, :] = keep(block, half, group, turned[rows, :], FF)
        leave(0, half)
    for copy in depart + ocopies:
        copy.wait()


def finish(count, small, kept, fin, out, grad):
    vm = pl.BlockSpec(memory_space=pltpu.VMEM)
    sm = pl.BlockSpec(memory_space=pltpu.SMEM)
    hbm = pl.BlockSpec(memory_space=pl.ANY)
    sds = jax.ShapeDtypeStruct
    shapes = [(2, BLOCK, 3 * D), (2, BLOCK, D), (2, BLOCK, FF), (2, 4 * BLOCK, D)]
    dma = pltpu.SemaphoreType.DMA
    return pl.pallas_call(
        finish_kernel,
        out_shape=[sds((ROWS, D), bf16), sds((ROWS, D), f32)]
        + [sds(v, f32) for v in shapes]
        + [
            sds((3, BLOCK), f32), sds((1, BLOCK), f32), sds((1, 4 * BLOCK), f32),
            sds((1, BLOCK), f32), sds((2, BLOCK), f32), sds((2, BLOCK), f32),
            sds((4,), f32), sds((), f32),
        ],
        in_specs=[sm, vm, vm, hbm, hbm, hbm],
        out_specs=[hbm] * 6 + [vm] * 6 + [sm] * 2,
        scratch_shapes=[pltpu.VMEM((3, BLOCK, FF), f32), pltpu.VMEM((4 * BLOCK, D), f32)]
        + [pltpu.VMEM(v, f32) for v in shapes]
        + [pltpu.VMEM((ROWS, D), bf16), pltpu.VMEM((ROWS, D), f32)]
        + [dma((3,)), dma((8,)), dma((4,))],
        compiler_params=pltpu.CompilerParams(vmem_limit_bytes=VMEM_CAP),
        name="finish",
    )(count, small, kept, fin, out, grad)


def on_device_fast(
    hidden_in, teacher_hidden, teacher_scores, seq_lengths, live_counts, triple_latent,
    mixing_latent, widen_latent, narrow_latent, triple_bias, mixing_bias, widen_bias, narrow_bias,
    norm_gain, norm_shift, clip_level,
):
    out, input_grad, fin, kept, small_sum = layer(
        seq_lengths, live_counts, clip_level, triple_bias, mixing_bias[None], widen_bias,
        narrow_bias[None], norm_gain, norm_shift, hidden_in, teacher_hidden,
        jnp.transpose(teacher_scores, (1, 0, 2)), triple_latent, mixing_latent, widen_latent,
        narrow_latent,
    )
    fin = fin.reshape(3, BLOCK, FF)
    tokens = hidden_in.shape[0] * lax.axis_size("dp") * lax.axis_size("fsdp")
    count = jnp.full((1,), 1.0 / (tokens * D), f32)
    out, input_grad, tg, mg, wg, ng, tb, mb, wb, nb, gain, shift, clips, loss = finish(
        count, small_sum, kept, fin, out, input_grad
    )
    return (
        out, loss, input_grad, tg, mg, wg, ng, tb, mb.reshape(BLOCK),
        wb.reshape(4 * BLOCK), nb.reshape(BLOCK), gain, shift, clips,
    )


def solution(mesh):
    in_specs = (
        P(("dp", "fsdp"), None),
        P(("dp", "fsdp"), None),
        P(("dp", "fsdp"), None, None),
        P(("dp", "fsdp"), None),
        P(("dp", "fsdp"), None),
        P(None, "fsdp", None),
        P(None, "fsdp", None),
        P(None, "fsdp", None),
        P(None, "fsdp", None),
        P(None, "fsdp"),
        P("fsdp"),
        P("fsdp"),
        P("fsdp"),
        P(None, "fsdp"),
        P(None, "fsdp"),
        P(),
    )
    out_specs = (
        P(("dp", "fsdp"), None),
        P(),
        P(("dp", "fsdp"), None),
        P(None, "fsdp", None),
        P(None, "fsdp", None),
        P(None, "fsdp", None),
        P(None, "fsdp", None),
        P(None, "fsdp"),
        P("fsdp"),
        P("fsdp"),
        P("fsdp"),
        P(None, "fsdp"),
        P(None, "fsdp"),
        P(),
    )
    fits = mesh.shape["dp"] == 4 and mesh.shape["fsdp"] == 8
    return jax.shard_map(
        on_device_fast if fits else on_device, mesh=mesh, in_specs=in_specs, out_specs=out_specs, check_vma=False
    )
```

```python
import math

import jax
import jax.numpy as jnp
from jax import lax
from jax.experimental import pallas as pl
from jax.experimental.pallas import tpu as pltpu
from jax.sharding import PartitionSpec as P

D = 768
HEADS = 12
HEAD_DIM = 64
FF = 3072
LONG_LEN = 256
MID_LEN = 128
SHORT_LEN = 64
LONG_SLOTS = 1
MID_SLOTS = 1
SHORT_SLOTS = 2


bit_count = 32
norm_epsilon = 1e-12
masked_fill = -1e30


def soft_clip(values, clip_at):
    return clip_at * jnp.tanh(values / clip_at)


def layer_norm(values, gain_row, shift_row):
    center = values - jnp.mean(values, axis=-1, keepdims=True)
    variance = jnp.mean(center * center, axis=-1, keepdims=True)
    return center * lax.rsqrt(variance + norm_epsilon) * gain_row + shift_row


def gelu_exact(values):
    return 0.5 * values * (1.0 + lax.erf(values * (1.0 / math.sqrt(2.0))))


def pack_signs(latent):
    halves, row_count, columns = latent.shape
    sign_bits = (
        (latent > 0).astype(jnp.int32).reshape(halves, row_count, columns // bit_count, bit_count)
    )
    places = jnp.arange(bit_count, dtype=jnp.int32)
    return jnp.sum(jnp.left_shift(sign_bits, places), axis=-1, dtype=jnp.int32)


def unpack_weight(sign_words, scales):
    halves, row_count, word_count = sign_words.shape
    places = jnp.arange(bit_count, dtype=jnp.int32)
    sign_bits = jnp.bitwise_and(jnp.right_shift(sign_words[..., None], places), 1)
    sign_values = (
        (2 * sign_bits - 1).astype(jnp.float32).reshape(halves, row_count, word_count * bit_count)
    )
    return (scales[0][:, None] * sign_values[0] + scales[1][:, None] * sign_values[1]).astype(
        jnp.bfloat16
    )


def bucket_shapes():
    return ((LONG_SLOTS, LONG_LEN), (MID_SLOTS, MID_LEN), (SHORT_SLOTS, SHORT_LEN))


def bucket_masks(lengths, live_count, slot_count, bucket_len):
    places = jnp.arange(bucket_len, dtype=jnp.int32)
    key_ok = places[None, :] < lengths[:, None]
    query_ok = jnp.logical_and(
        key_ok, jnp.arange(slot_count, dtype=jnp.int32)[:, None] < live_count
    )
    return (key_ok, query_ok)


def split_heads(block, slot_count, bucket_len):
    return block.reshape(slot_count, bucket_len, HEADS, HEAD_DIM)


def bucket_scores(qkv_rows, teacher_rows, key_ok, query_ok, slot_count, bucket_len):
    queries = split_heads(qkv_rows[:, :D], slot_count, bucket_len)
    keys_part = split_heads(qkv_rows[:, D : 2 * D], slot_count, bucket_len)
    scores = jnp.einsum(
        "sqhd,skhd->shqk", queries, keys_part, preferred_element_type=jnp.float32
    ) * HEAD_DIM ** (-0.5)
    masked = jnp.where(key_ok[:, None, None, :], scores, masked_fill)
    teacher = jnp.transpose(
        teacher_rows.reshape(slot_count, bucket_len, HEADS, LONG_LEN)[..., :bucket_len],
        (0, 2, 1, 3),
    ).astype(jnp.float32)
    pair_ok = jnp.logical_and(query_ok[:, None, :, None], key_ok[:, None, None, :])
    score_gap = jnp.where(pair_ok, scores - teacher, 0.0)
    return (queries, keys_part, masked, score_gap)


def attend(qkv_rows, teacher_rows, key_ok, query_ok, slot_count, bucket_len):
    queries, keys_part, masked, score_gap = bucket_scores(
        qkv_rows, teacher_rows, key_ok, query_ok, slot_count, bucket_len
    )
    values_part = split_heads(qkv_rows[:, 2 * D :], slot_count, bucket_len)
    row_top = jnp.max(masked, axis=-1, keepdims=True)
    exponent = jnp.exp(masked - row_top)
    exp_total = jnp.sum(exponent, axis=-1, keepdims=True)
    attention = exponent / exp_total
    context = jnp.einsum(
        "shqk,skhd->sqhd",
        attention.astype(jnp.bfloat16),
        values_part,
        preferred_element_type=jnp.float32,
    )
    distill = 0.5 / LONG_LEN * jnp.sum(score_gap * score_gap)
    return (context.reshape(slot_count * bucket_len, D), row_top + jnp.log(exp_total), distill)


def attend_back(
    qkv_rows, teacher_rows, key_ok, query_ok, slot_count, bucket_len, log_total, context_grad
):
    queries, keys_part, masked, score_gap = bucket_scores(
        qkv_rows, teacher_rows, key_ok, query_ok, slot_count, bucket_len
    )
    values_part = split_heads(qkv_rows[:, 2 * D :], slot_count, bucket_len)
    attention = jnp.exp(masked - log_total)
    grad_heads = split_heads(context_grad, slot_count, bucket_len)
    values_grad = jnp.einsum(
        "shqk,sqhd->skhd",
        attention.astype(jnp.bfloat16),
        grad_heads,
        preferred_element_type=jnp.float32,
    )
    weight_grad = jnp.einsum(
        "sqhd,skhd->shqk", grad_heads, values_part, preferred_element_type=jnp.float32
    )
    score_grad = attention * (
        weight_grad - jnp.sum(weight_grad * attention, axis=-1, keepdims=True)
    ) + score_gap * (1.0 / LONG_LEN)
    score_low = score_grad.astype(jnp.bfloat16)
    score_scale = HEAD_DIM ** (-0.5)
    queries_grad = (
        jnp.einsum("shqk,skhd->sqhd", score_low, keys_part, preferred_element_type=jnp.float32)
        * score_scale
    )
    keys_grad = (
        jnp.einsum("shqk,sqhd->skhd", score_low, queries, preferred_element_type=jnp.float32)
        * score_scale
    )
    row_count = slot_count * bucket_len
    return jnp.concatenate(
        [
            queries_grad.reshape(row_count, D),
            keys_grad.reshape(row_count, D),
            values_grad.reshape(row_count, D),
        ],
        axis=-1,
    )


def on_device(
    hidden_in,
    teacher_hidden,
    teacher_scores,
    seq_lengths,
    live_counts,
    triple_latent,
    mixing_latent,
    widen_latent,
    narrow_latent,
    triple_bias,
    mixing_bias,
    widen_bias,
    narrow_bias,
    norm_gain,
    norm_shift,
    clip_level,
):
    latents = (triple_latent, mixing_latent, widen_latent, narrow_latent)
    fan_ins = (D, D, D, FF)
    own_scales = tuple(
        (
            jnp.mean(jnp.abs(latent), axis=-1) / math.sqrt(fan_in)
            for latent, fan_in in zip(latents, fan_ins)
        )
    )
    packed = tuple((pack_signs(latent) for latent in latents))
    gathered = (
        lax.all_gather(packed[0], "fsdp", axis=1, tiled=True),
        lax.all_gather(packed[1], "fsdp", axis=1, tiled=True),
        lax.all_gather(packed[2], "fsdp", axis=1, tiled=True),
        lax.all_gather(packed[3], "fsdp", axis=1, tiled=True),
    )
    factors = (
        lax.all_gather(own_scales[0], "fsdp", axis=1, tiled=True),
        lax.all_gather(own_scales[1], "fsdp", axis=1, tiled=True),
        lax.all_gather(own_scales[2], "fsdp", axis=1, tiled=True),
        lax.all_gather(own_scales[3], "fsdp", axis=1, tiled=True),
        lax.all_gather(triple_bias, "fsdp", axis=1, tiled=True),
        lax.all_gather(mixing_bias, "fsdp", axis=0, tiled=True),
        lax.all_gather(widen_bias, "fsdp", axis=0, tiled=True),
        lax.all_gather(narrow_bias, "fsdp", axis=0, tiled=True),
        lax.all_gather(norm_gain, "fsdp", axis=1, tiled=True),
        lax.all_gather(norm_shift, "fsdp", axis=1, tiled=True),
    )
    scales = factors[:4]
    triple_rows, full_mixing_bias, full_widen_bias, full_narrow_bias, gains, shifts = factors[4:]
    full_triple_bias = triple_rows.reshape(3 * D)
    weights = tuple(
        (unpack_weight(words_part, scale_part) for words_part, scale_part in zip(gathered, scales))
    )
    inputs = hidden_in.astype(jnp.float32)
    inputs_low = soft_clip(inputs, clip_level[0]).astype(jnp.bfloat16)
    qkv_all = (
        jnp.dot(inputs_low, weights[0], preferred_element_type=jnp.float32) + full_triple_bias
    ).astype(jnp.bfloat16)
    lengths = seq_lengths[0]
    counts = live_counts[0]
    plans = []
    row_start = 0
    slot_start = 0
    for bucket, shape_pair in enumerate(bucket_shapes()):
        slot_count, bucket_len = shape_pair
        key_ok, query_ok = bucket_masks(
            lengths[slot_start : slot_start + slot_count], counts[bucket], slot_count, bucket_len
        )
        plans.append(
            (
                row_start,
                row_start + slot_count * bucket_len,
                slot_count,
                bucket_len,
                key_ok,
                query_ok,
            )
        )
        row_start = row_start + slot_count * bucket_len
        slot_start = slot_start + slot_count
    contexts = []
    log_totals = []
    distill_sum = 0.0
    for plan in plans:
        row_begin, row_end, slot_count, bucket_len, key_ok, query_ok = plan
        context, log_total, distill = attend(
            qkv_all[row_begin:row_end],
            teacher_scores[row_begin:row_end],
            key_ok,
            query_ok,
            slot_count,
            bucket_len,
        )
        contexts.append(context)
        log_totals.append(log_total)
        distill_sum = distill_sum + distill
    context = jnp.concatenate(contexts, axis=0)
    token_ok = jnp.concatenate([plan[5].reshape(-1) for plan in plans])
    context_low = soft_clip(context, clip_level[1]).astype(jnp.bfloat16)
    mixed = jnp.dot(context_low, weights[1], preferred_element_type=jnp.float32) + full_mixing_bias
    first_sum = inputs + mixed
    first_norm = layer_norm(first_sum, gains[0], shifts[0])
    widen_low = soft_clip(first_norm, clip_level[2]).astype(jnp.bfloat16)
    widened = jnp.dot(widen_low, weights[2], preferred_element_type=jnp.float32) + full_widen_bias
    activated = gelu_exact(widened)
    activated_low = soft_clip(activated, clip_level[3]).astype(jnp.bfloat16)
    narrowed = (
        jnp.dot(activated_low, weights[3], preferred_element_type=jnp.float32) + full_narrow_bias
    )
    second_sum = first_norm + narrowed
    out_full = layer_norm(second_sum, gains[1], shifts[1])
    out_gap = jnp.where(token_ok[:, None], out_full - teacher_hidden.astype(jnp.float32), 0.0)
    loss_local = 0.5 * jnp.sum(out_gap * out_gap) + distill_sum
    regathered = (
        lax.all_gather(packed[0], "fsdp", axis=1, tiled=True),
        lax.all_gather(packed[1], "fsdp", axis=1, tiled=True),
        lax.all_gather(packed[2], "fsdp", axis=1, tiled=True),
        lax.all_gather(packed[3], "fsdp", axis=1, tiled=True),
    )
    back_weights = tuple(
        (
            unpack_weight(words_part, scale_part)
            for words_part, scale_part in zip(regathered, scales)
        )
    )
    _, second_back = jax.vjp(layer_norm, second_sum, gains[1], shifts[1])
    second_grad, gain_two, shift_two = second_back(out_gap)
    narrow_low = second_grad.astype(jnp.bfloat16)
    narrow_weight_grad = jnp.einsum(
        "rf,rd->fd", activated_low, narrow_low, preferred_element_type=jnp.float32
    )
    act_low_grad = jnp.einsum(
        "rd,fd->rf", narrow_low, back_weights[3], preferred_element_type=jnp.float32
    )
    _, clip_three_back = jax.vjp(soft_clip, activated, clip_level[3])
    act_grad, clip_three = clip_three_back(act_low_grad)
    _, gelu_back = jax.vjp(gelu_exact, widened)
    (widened_grad,) = gelu_back(act_grad)
    widen_grad_low = widened_grad.astype(jnp.bfloat16)
    widen_weight_grad = jnp.einsum(
        "rd,rf->df", widen_low, widen_grad_low, preferred_element_type=jnp.float32
    )
    norm_low_grad = jnp.einsum(
        "rf,df->rd", widen_grad_low, back_weights[2], preferred_element_type=jnp.float32
    )
    _, clip_two_back = jax.vjp(soft_clip, first_norm, clip_level[2])
    norm_grad, clip_two = clip_two_back(norm_low_grad)
    norm_grad = norm_grad + second_grad
    _, first_back = jax.vjp(layer_norm, first_sum, gains[0], shifts[0])
    first_grad, gain_one, shift_one = first_back(norm_grad)
    mixed_low = first_grad.astype(jnp.bfloat16)
    mixing_weight_grad = jnp.einsum(
        "rc,rd->cd", context_low, mixed_low, preferred_element_type=jnp.float32
    )
    context_low_grad = jnp.einsum(
        "rd,cd->rc", mixed_low, back_weights[1], preferred_element_type=jnp.float32
    )
    _, clip_one_back = jax.vjp(soft_clip, context, clip_level[1])
    context_grad, clip_one = clip_one_back(context_low_grad)
    context_grad_low = context_grad.astype(jnp.bfloat16)
    qkv_grads = []
    for plan, log_total in zip(plans, log_totals):
        row_begin, row_end, slot_count, bucket_len, key_ok, query_ok = plan
        qkv_grads.append(
            attend_back(
                qkv_all[row_begin:row_end],
                teacher_scores[row_begin:row_end],
                key_ok,
                query_ok,
                slot_count,
                bucket_len,
                log_total,
                context_grad_low[row_begin:row_end],
            )
        )
    qkv_grad_low = jnp.concatenate(qkv_grads, axis=0).astype(jnp.bfloat16)
    triple_weight_grad = jnp.einsum(
        "rd,re->de", inputs_low, qkv_grad_low, preferred_element_type=jnp.float32
    )
    input_low_grad = jnp.einsum(
        "re,de->rd", qkv_grad_low, back_weights[0], preferred_element_type=jnp.float32
    )
    _, clip_zero_back = jax.vjp(soft_clip, inputs, clip_level[0])
    input_side, clip_zero = clip_zero_back(input_low_grad)
    input_grad = input_side + first_grad
    bias_sums = (
        jnp.sum(qkv_grad_low, axis=0, dtype=jnp.float32).reshape(3, D),
        jnp.sum(mixed_low, axis=0, dtype=jnp.float32),
        jnp.sum(widen_grad_low, axis=0, dtype=jnp.float32),
        jnp.sum(narrow_low, axis=0, dtype=jnp.float32),
    )
    row_shares = (
        lax.psum_scatter(triple_weight_grad, "fsdp", scatter_dimension=0, tiled=True),
        lax.psum_scatter(mixing_weight_grad, "fsdp", scatter_dimension=0, tiled=True),
        lax.psum_scatter(widen_weight_grad, "fsdp", scatter_dimension=0, tiled=True),
        lax.psum_scatter(narrow_weight_grad, "fsdp", scatter_dimension=0, tiled=True),
    )
    totals = lax.psum((row_shares[0], row_shares[1], row_shares[2], row_shares[3]), "dp")
    small_sums = lax.psum(
        (
            bias_sums[0],
            bias_sums[1],
            bias_sums[2],
            bias_sums[3],
            jnp.stack([gain_one, gain_two]),
            jnp.stack([shift_one, shift_two]),
            jnp.stack([clip_zero, clip_one, clip_two, clip_three]),
            loss_local,
        ),
        ("dp", "fsdp"),
    )
    shard_index = lax.axis_index("fsdp")
    shard_parts = lax.axis_size("fsdp")

    def own_part(vector, along):
        share_width = vector.shape[along] // shard_parts
        return lax.dynamic_slice_in_dim(vector, shard_index * share_width, share_width, along)

    latent_grads = tuple(
        (
            jnp.where(jnp.abs(latent) <= 1.0, (total / math.sqrt(fan_in))[None], 0.0)
            for latent, total, fan_in in zip(latents, totals, fan_ins)
        )
    )
    loss = small_sums[7] / (hidden_in.shape[0] * D * lax.axis_size("dp") * shard_parts)
    return (
        out_full.astype(jnp.bfloat16),
        loss,
        input_grad,
        latent_grads[0],
        latent_grads[1],
        latent_grads[2],
        latent_grads[3],
        own_part(small_sums[0], 1),
        own_part(small_sums[1], 0),
        own_part(small_sums[2], 0),
        own_part(small_sums[3], 0),
        own_part(small_sums[4], 1),
        own_part(small_sums[5], 1),
        small_sums[6],
    )


bf16 = jnp.bfloat16
f32 = jnp.float32
MESH = pl.DeviceIdType.MESH
VMEM_CAP = 60 * 1024 * 1024
LAYER_CAP = 63 * 1024 * 1024
ROWS = LONG_SLOTS * LONG_LEN + MID_SLOTS * MID_LEN + SHORT_SLOTS * SHORT_LEN
BLOCK = 96
CHUNK = 512
HALF = CHUNK // 2
SECTION = FF // CHUNK
WIDE = 3 * SECTION - 1
CHUNKS = WIDE + 2
SLOTS = 4


def dot_nn(a, b):
    return lax.dot_general(a, b, (((1,), (0,)), ((), ())), preferred_element_type=f32)


def dot_nt(a, b):
    return lax.dot_general(a, b, (((1,), (1,)), ((), ())), preferred_element_type=f32)


def dot_tn(a, b):
    return lax.dot_general(a, b, (((0,), (0,)), ((), ())), preferred_element_type=f32)


def loop(count, step, body):
    def run(i, carry):
        body(pl.multiple_of(i * step, step))
        return carry

    lax.fori_loop(0, count, run, 0)


def plane_of(block, half, group):
    place = block * 24 + half * 12 + group
    bit = place % 32
    return place // 32, (1 << bit) if bit < 31 else -(1 << 31)


def unpack_blocks(words, scl, blocks, dst):
    def one(owner, carry):
        for block in blocks:
            unpack_owner(words, scl, block, dst, owner)
        return carry

    lax.fori_loop(0, 8, one, 0)


def unpack_owner(words, scl, block, dst, owner):
    index = 0 if block < 3 else 1 if block == 3 else 2 if block < 8 else block - 5

    for pair in range(6):
        parts = []
        for group in (2 * pair, 2 * pair + 1):
            total = None
            for half in range(2):
                word, bit = plane_of(block, half, group)
                bits = words[owner, word * 8 : (word + 1) * 8, :] & jnp.int32(bit)
                column = index * 2 + half
                scale = jnp.broadcast_to(
                    scl[owner, group * 8 : (group + 1) * 8, column : column + 1], (8, D)
                )
                value = jnp.where(bits != 0, scale, -scale)
                total = value if total is None else total + value
            parts.append(total)
        tile = jnp.concatenate(parts, axis=0).astype(bf16)
        if block < 8:
            start = owner * BLOCK + pair * 16
        else:
            start = owner * (4 * BLOCK) + (block - 8) * BLOCK + pair * 16
        rows = pl.ds(pl.multiple_of(start, 16), 16)
        if block < 3:
            dst[rows, block * D : (block + 1) * D] = tile
        elif block < 8 and block > 3:
            dst[rows, (block - 4) * D : (block - 3) * D] = tile
        else:
            dst[rows, :] = tile


def clip_back(grad, value, level, inverse):
    u = value * inverse
    t = jnp.tanh(u)
    slope = 1.0 - t * t
    return grad * slope, jnp.sum(grad * (t - u * slope), axis=0, keepdims=True)


def norm_rows(v):
    center = v - jnp.mean(v, axis=1, keepdims=True)
    variance = jnp.mean(center * center, axis=1, keepdims=True)
    rstd = lax.rsqrt(variance + norm_epsilon)
    return center * rstd, rstd


def norm_rows_back(grad, hat, rstd, gain_row):
    g = grad * gain_row
    return rstd * (
        g - jnp.mean(g, axis=1, keepdims=True) - hat * jnp.mean(g * hat, axis=1, keepdims=True)
    )


def colsum(v):
    return jnp.sum(v, axis=0, keepdims=True)


HALF_ROOT = 1.0 / math.sqrt(2.0)
DENSITY = 1.0 / math.sqrt(2.0 * math.pi)


def layer_kernel(
    seq, live, level, tb, mb, wb, nb, gain, shift, hid_in, teach, teach_scores, tl, ml, wl, nl,
    out_to, acc_to, fin_to, kept_to, small_out,
    out, acc, fin, kept, hid, words, small, scl, spread,
    wt, wm, ww, wn, prm, bias, wbias, qkv, low, ctx, hat1, rstd1, widened, act, wg, sgrad,
    cgrad, valid, pair, xlT, clT, wlT, nlT, sums, tbuf, pt, rb, rx, rz, rf, held, ry, rd, sin,
    s1, r1, s2, r2, s3, r3, s4, r4, s5, r5, s6, r6, sms, smr, tsem, lsem, zs, zr, cs_, cr_, hsem, fsem, s7, r7,
):
    dp = lax.axis_index("dp")
    me = lax.axis_index("fsdp")
    x = lax.rem(dp, 2)
    y = lax.div(dp, 2)
    z = lax.div(me, 2)
    core = lax.rem(me, 2)
    over_x = (dp + 1 - 2 * x, me)
    over_y = (dp + 2 - 4 * y, me)
    over_core = (dp, z * 2 + 1 - core)

    def remote(src, dst, send, recv, to):
        return pltpu.make_async_remote_copy(
            src_ref=src, dst_ref=dst, send_sem=send, recv_sem=recv, device_id=to,
            device_id_type=MESH,
        )

    greet = pltpu.get_barrier_semaphore()
    for to in (over_core, over_x, over_y) + tuple(
        (dp, lax.rem(z + hop, 4) * 2 + core) for hop in (1, 2, 3)
    ):
        pl.semaphore_signal(greet, inc=1, device_id=to, device_id_type=MESH)

    teach_load = pltpu.make_async_copy(teach, cgrad, hsem.at[0])
    hid_load = pltpu.make_async_copy(hid_in, hid, hsem.at[1])
    out_save = pltpu.make_async_copy(out, out_to, hsem.at[2])
    acc_save = pltpu.make_async_copy(acc, acc_to, hsem.at[3])
    kept_save = pltpu.make_async_copy(kept, kept_to, hsem.at[4])

    loads = []
    for half in range(2):
        band = slice(192 + half * BLOCK, 192 + (half + 1) * BLOCK)
        loads.append([
            pltpu.make_async_copy(tl.at[half], widened.at[band, 0 : 3 * D], lsem.at[half, 0]),
            pltpu.make_async_copy(ml.at[half], widened.at[band, 3 * D : FF], lsem.at[half, 1]),
            pltpu.make_async_copy(
                wl.at[half], widened.at[half * BLOCK : (half + 1) * BLOCK, :], lsem.at[half, 2]
            ),
            pltpu.make_async_copy(
                nl.at[half], (ctx if half == 0 else sgrad).at[0 : 4 * BLOCK, :], lsem.at[half, 3]
            ),
        ])
    for index in range(2):
        for half in range(2):
            loads[half][index].start()

    def latent_piece(block, half, group):
        if block < 4:
            rows = pl.ds(192 + half * BLOCK + group * 8, 8)
            return widened[rows, block * D : (block + 1) * D]
        if block < 8:
            return widened[pl.ds(half * BLOCK + group * 8, 8), (block - 4) * D : (block - 3) * D]
        rows = pl.ds((block - 8) * BLOCK + group * 8, 8)
        return (ctx if half == 0 else sgrad)[rows, :]

    planes = [[] for _ in range(9)]
    for block in range(12):
        for half in range(2):
            for group in range(12):
                word, bit = plane_of(block, half, group)
                planes[word].append((block, half, group, bit))

    def pack(word):
        total = jnp.zeros((8, D), jnp.int32)
        for block, half, group, bit in planes[word]:
            piece = latent_piece(block, half, group)
            total = total | jnp.where(piece > 0, jnp.int32(bit), jnp.int32(0))
        words[me, word * 8 : (word + 1) * 8, :] = total

    def pack_kept(word):
        total = jnp.zeros((8, D), jnp.int32)
        for block, half, group, bit in planes[word]:
            piece = jnp.abs(latent_piece(block, half, group))
            total = total | jnp.where(piece <= 1.0, jnp.int32(bit), jnp.int32(0))
        kept[word * 8 : (word + 1) * 8, :] = total

    def part_of(owner, index):
        return small.at[owner] if index == 3 else words.at[owner, index * 24 : (index + 1) * 24]

    def z_send(index, hop):
        ref = part_of(me, index)
        peer = lax.rem(z + hop, 4) * 2 + core
        return remote(ref, ref, zs.at[index, hop - 1], zr.at[index, hop - 1], (dp, peer))

    def core_send(index, hop):
        ref = part_of(lax.rem(z + 4 - hop, 4) * 2 + core, index)
        return remote(ref, ref, cs_.at[index, hop], cr_.at[index, hop], over_core)

    def send_out(index):
        for hop in (2, 1, 3):
            z_send(index, hop).start()
        core_send(index, 0).start()

    def pass_on(index):
        for hop in (1, 3, 2):
            z_send(index, hop).wait()
            core_send(index, hop).start()

    def all_here(index):
        for hop in range(4):
            core_send(index, hop).wait()

    for half in range(2):
        loads[half][0].wait()
        loads[half][1].wait()
    for index in range(2, 4):
        for half in range(2):
            loads[half][index].start()
    hid_load.start()
    teach_load.start()
    for word in range(3):
        pack(word)
    pl.semaphore_wait(greet, 6)
    send_out(0)
    for half in range(2):
        loads[half][2].wait()
        loads[half][3].wait()
    slot_lane = lax.broadcasted_iota(jnp.int32, (8, 128), 1)

    def scale_rows(pair):
        for part in range(2):
            scale_group(pl.multiple_of(pair + part * 8, 8))

    def scale_group(group):
        tile = jnp.zeros((8, 128), f32)
        for half in range(2):
            rows = pl.ds(pl.multiple_of(192 + half * BLOCK + group, 8), 8)
            for index in range(7):
                if index == 0:
                    part = widened[rows, 0 : 3 * D]
                elif index == 1:
                    part = widened[rows, 3 * D : FF]
                elif index == 2:
                    part = widened[pl.ds(pl.multiple_of(half * BLOCK + group, 8), 8), :]
                else:
                    at = pl.ds(pl.multiple_of((index - 3) * BLOCK + group, 8), 8)
                    part = (ctx if half == 0 else sgrad)[at, :]
                fan = FF if index >= 3 else D
                mean = jnp.sum(jnp.abs(part), axis=1, keepdims=True) * (1.0 / part.shape[1])
                tile = jnp.where(slot_lane == index * 2 + half, mean / math.sqrt(fan), tile)
        spread[pl.ds(group, 8), :] = tile

    loop(6, 16, scale_rows)
    spread[BLOCK:128, :] = jnp.zeros((128 - BLOCK, 128), f32)
    small[me, 0:16, :] = spread[...].T[0:16, :]
    small[me, 16:32, :] = jnp.zeros((16, 128), f32)
    small[me, 16:19, 0:BLOCK] = tb[...]
    small[me, 19:20, 0:BLOCK] = mb[...]
    small[me, 20:21, 0:BLOCK] = nb[...]
    small[me, 21:23, 0:BLOCK] = gain[...]
    small[me, 23:25, 0:BLOCK] = shift[...]
    for part in range(3):
        small[me, 25 + part : 26 + part, :] = wb[part * 128 : (part + 1) * 128].reshape(1, 128)
    send_out(3)
    for word in range(3, 9):
        pack(word)
    for word in range(9):
        pack_kept(word)
    kept_save.start()
    c0, c1, c2, c3 = level[0], level[1], level[2], level[3]
    i0, i1, i2, i3 = 1.0 / c0, 1.0 / c1, 1.0 / c2, 1.0 / c3
    sums[...] = jnp.zeros_like(sums)
    row = lax.broadcasted_iota(jnp.int32, (256, 256), 0)
    col = lax.broadcasted_iota(jnp.int32, (256, 256), 1)
    key_ok = col < seq[0, 0]
    query_ok = row < seq[0, 0] * live[0, 0]
    valid[0] = jnp.where(key_ok, 1.0, 0.0).astype(bf16)
    pair[0] = jnp.where(key_ok & query_ok, 1.0, 0.0).astype(bf16)

    def in_slots(at):
        mid = (at < 128) & (at < seq[0, 1])
        one = (at >= 128) & (at < 192) & (at - 128 < seq[0, 2])
        two = (at >= 192) & (at - 192 < seq[0, 3])
        return mid, one, two

    km, ko, kt = in_slots(col)
    qm, qo, qt = in_slots(row)
    key_ok = (km & (row < 128)) | (ko & (row >= 128) & (row < 192)) | (kt & (row >= 192))
    live_mid = row * 0 + live[0, 1] > 0
    live_one = row * 0 + live[0, 2] > 0
    live_two = row * 0 + live[0, 2] > 1
    query_ok = (qm & live_mid) | (qo & live_one) | (qt & live_two)
    valid[1] = jnp.where(key_ok, 1.0, 0.0).astype(bf16)
    pair[1] = jnp.where(key_ok & query_ok, 1.0, 0.0).astype(bf16)
    ones = jnp.where(query_ok, 1.0, 0.0)

    def clip_in(r):
        x = hid[pl.ds(r, 128), :].astype(f32)
        lo = (c0 * jnp.tanh(x * i0)).astype(bf16)
        low[pl.ds(r, 128), :] = lo

    hid_load.wait()
    for r in range(0, ROWS, 128):
        clip_in(r)
    pass_on(3)
    all_here(3)
    total = jnp.zeros((16, D), f32)
    param_lane = lax.broadcasted_iota(jnp.int32, (16, 128), 1)
    for owner in range(8):
        turned = jnp.concatenate([small[owner, 0:16, :], jnp.zeros((112, 128), f32)], axis=0).T
        scl[owner] = turned[0:BLOCK, :]
        piece = jnp.where(param_lane < BLOCK, small[owner, 16:32, :], 0.0)
        wide = jnp.concatenate([piece, jnp.zeros((16, D - 128), f32)], axis=1)
        total = total + (pltpu.roll(wide, owner * BLOCK, 1) if owner else wide)
        for part in range(3):
            at = owner * 4 * BLOCK + part * 128
            wbias[0:1, at : at + 128] = small[owner, 25 + part : 26 + part, :]
    prm[...] = total
    for part in range(3):
        bias[0:1, part * D : (part + 1) * D] = prm[part : part + 1, :]
    def same_core(hop, carry):
        @pl.when(hop > 0)
        def _():
            z_send(0, hop).wait()
            core_send(0, hop).start()

        for block in range(3):
            unpack_owner(words, scl, block, wt, lax.rem(z + 4 - hop, 4) * 2 + core)
        return carry

    def other_core(hop, carry):
        core_send(0, hop).wait()
        for block in range(3):
            unpack_owner(words, scl, block, wt, lax.rem(z + 4 - hop, 4) * 2 + 1 - core)
        return carry

    lax.fori_loop(0, 4, same_core, 0)
    send_out(1)
    lax.fori_loop(0, 4, other_core, 0)

    for part in range(9):
        cs = slice(part * 256, (part + 1) * 256)
        qkv[:, cs] = (dot_nn(low[...], wt[:, cs]) + bias[0:1, cs]).astype(bf16)
    send_out(2)
    lane = lax.broadcasted_iota(jnp.int32, (256, 128), 1)
    first = lane < 64

    def pick(v, j):
        return jnp.where(first, v, jnp.zeros_like(v)) if j == 0 else jnp.where(first, jnp.zeros_like(v), v)

    def softmax(q, k, ok, j):
        s = dot_nt(pick(q, j), k) * (HEAD_DIM**-0.5)
        masked = jnp.where(ok, s, masked_fill)
        e = jnp.exp(masked - jnp.max(masked, axis=1, keepdims=True))
        return s, e / jnp.sum(e, axis=1, keepdims=True)

    for g in range(2):
        for c in range(0, D, 128):
            rs = slice(g * 256, (g + 1) * 256)
            q, k, v = (qkv[rs, at + c : at + c + 128] for at in (0, D, 2 * D))
            ok = valid[g].astype(f32) > 0.5
            parts = []
            for j in range(2):
                s, p = softmax(q, k, ok, j)
                parts.append(dot_nn(p.astype(bf16), v))
            ctx[rs, c : c + 128] = jnp.where(first, parts[0], parts[1])
    pass_on(1)
    unpack_blocks(words, scl, (3,), wm)

    def clip_ctx(r):
        lo = (c1 * jnp.tanh(ctx[pl.ds(r, 128), :] * i1)).astype(bf16)
        low[pl.ds(r, 128), :] = lo

    for r in range(0, ROWS, 128):
        clip_ctx(r)

    for part in range(3):
        cs = slice(part * 256, (part + 1) * 256)
        acc[:, cs] = dot_nn(low[...], wm[:, cs]) + prm[3:4, cs] + hid[:, cs].astype(f32)

    def norm_one(r):
        rs = pl.ds(r, 128)
        hat, rstd = norm_rows(acc[rs, :])
        hat1[rs, :] = hat
        rstd1[rs, :] = jnp.broadcast_to(rstd, (128, 128))
        normed = hat * prm[5:6, :] + prm[7:8, :]
        lo = (c2 * jnp.tanh(normed * i2)).astype(bf16)
        low[rs, :] = lo
        acc[rs, :] = normed + prm[4:5, :]

    loop(4, 128, norm_one)
    all_here(1)
    pass_on(2)
    unpack_blocks(words, scl, range(4, 8), ww)
    all_here(2)

    for t in range(8):
        for owner in ((0, 1), (2,), (3,), (4,), (5,), (6,), (7,), ())[t]:
            for block in range(8, 12):
                unpack_owner(words, scl, block, wn, owner)
        if t < 6:
            cs = slice(t * 512, (t + 1) * 512)
            widened[:, cs] = dot_nn(low[...], ww[:, cs]) + wbias[0:1, cs]
        if 1 <= t <= 6:
            cs = slice((t - 1) * 512, t * 512)
            for r in range(0, ROWS, 64):
                w = widened[r : r + 64, cs]
                a = 0.5 * w * (1.0 + lax.erf(w * HALF_ROOT))
                act[r : r + 64, cs] = (c3 * jnp.tanh(a * i3)).astype(bf16)
        if t >= 2:
            cs = slice((t - 2) * 512, (t - 1) * 512)
            acc[...] += dot_nn(act[:, cs], wn[cs, :])

    teach_load.wait()

    def norm_two(r):
        rs = pl.ds(r, 128)
        hat, rstd = norm_rows(acc[rs, :])
        full = hat * prm[6:7, :] + prm[8:9, :]
        out[rs, :] = full.astype(bf16)
        at = lax.broadcasted_iota(jnp.int32, (128, D), 0) + r
        l0, l1, l2, l3 = seq[0, 0] * live[0, 0], seq[0, 1], seq[0, 2], seq[0, 3]
        l1 = jnp.where(live[0, 1] > 0, l1, 0)
        l2 = jnp.where(live[0, 2] > 0, l2, 0)
        l3 = jnp.where(live[0, 2] > 1, l3, 0)
        ok = (at < l0) | ((at >= 256) & (at < 256 + l1)) | ((at >= 384) & (at < 384 + l2))
        ok = ok | ((at >= 448) & (at < 448 + l3))
        gap = jnp.where(ok, full - cgrad[rs, :].astype(f32), 0.0)
        sums[15:16, :] += colsum(gap * gap) * 0.5
        sums[6:7, :] += colsum(gap * hat)
        sums[8:9, :] += colsum(gap)
        grad = norm_rows_back(gap, hat, rstd, prm[6:7, :])
        sgrad[rs, :] = grad
        acc[rs, :] = jnp.zeros((128, D), f32)
        lo = grad.astype(bf16)
        low[rs, :] = lo
        nlT[:, rs] = lo.T
        sums[4:5, :] += colsum(lo.astype(f32))

    loop(4, 128, norm_two)
    out_save.start()

    def feed_back(t):
        cs = pl.ds(pl.multiple_of(t * CHUNK, CHUNK), CHUNK)
        wbias[1:2, cs] = jnp.zeros((1, CHUNK), f32)

        def feed_back_rows(r):
            rs = pl.ds(r, 256)
            g = dot_nt(low[rs, :], wn[cs, :])
            w = widened[rs, cs]
            e = 0.5 * (1.0 + lax.erf(w * HALF_ROOT))
            a = w * e
            u = a * i3
            th = jnp.tanh(u)
            slope = 1.0 - th * th
            sums[14:15, 0:CHUNK] += colsum(g * (th - u * slope))
            back = g * slope * (e + w * (DENSITY * jnp.exp(-0.5 * w * w)))
            lo = back.astype(bf16)
            wg[rs, cs] = lo
            wbias[1:2, cs] += colsum(lo.astype(f32))
            acc[rs, :] += dot_nt(lo, ww[:, cs])

        loop(2, 256, feed_back_rows)

    def turn_widen(r):
        rs = pl.ds(r, 128)
        normed = hat1[rs, :] * prm[5:6, :] + prm[7:8, :]
        wlT[:, rs] = (c2 * jnp.tanh(normed * i2)).astype(bf16).T

    def turn_context(r):
        clT[:, pl.ds(r, 128)] = (c1 * jnp.tanh(ctx[pl.ds(r, 128), :] * i1)).astype(bf16).T

    def turn_inputs(r):
        v = hid[pl.ds(r, 128), :].astype(f32)
        xlT[:, pl.ds(r, 128)] = (c0 * jnp.tanh(v * i0)).astype(bf16).T

    def norm_one_back(r):
        rs = pl.ds(r, 128)
        hat = hat1[rs, :]
        normed = hat * prm[5:6, :] + prm[7:8, :]
        grad, clip_sum = clip_back(acc[rs, :], normed, c2, i2)
        sums[18:19, :] += clip_sum
        grad = grad + sgrad[rs, :]
        sums[5:6, :] += colsum(grad * hat)
        sums[7:8, :] += colsum(grad)
        grad = norm_rows_back(grad, hat, rstd1[rs, 0:1], prm[5:6, :])
        acc[rs, :] = grad
        lo = grad.astype(bf16)
        low[rs, :] = lo
        sums[3:4, :] += colsum(lo.astype(f32))

    def mix_back(c):
        cs = pl.ds(c, 256)
        g = dot_nt(low[...], wm[cs, :])
        grad, clip_sum = clip_back(g, ctx[:, cs], c1, i1)
        sums[17:18, cs] += clip_sum
        cgrad[:, cs] = grad.astype(bf16)

    def scores_copy(u, slot):
        g = lax.div(u, 6)
        hp = lax.rem(u, 6)
        rs = pl.ds(pl.multiple_of(g * 256, 256), 256)
        return pltpu.make_async_copy(
            teach_scores.at[pl.ds(2 * hp, 2), rs], tbuf.at[slot], tsem.at[slot]
        )

    def attend_pair_back(u, slot):
        g = lax.div(u, 6)
        hp = lax.rem(u, 6)
        rs = pl.ds(pl.multiple_of(g * 256, 256), 256)
        q0 = pl.multiple_of(hp * 128, 128)
        k0 = pl.multiple_of(D + q0, 128)
        v0 = pl.multiple_of(2 * D + q0, 128)
        q = qkv[rs, pl.ds(q0, 128)]
        k = qkv[rs, pl.ds(k0, 128)]
        v = qkv[rs, pl.ds(v0, 128)]
        cg = cgrad[rs, pl.ds(q0, 128)]
        ok = valid[g].astype(f32) > 0.5
        pairs = pair[g].astype(f32) > 0.5
        dq, dk, dv = [], [], []
        for j in range(2):
            s, p = softmax(q, k, ok, j)
            ts = tbuf[slot, j].astype(f32)
            second = pltpu.roll(ts[128:192], 128, 1)
            third = pltpu.roll(ts[192:256], 192, 1)
            moved = jnp.concatenate([ts[0:128], second, third], axis=0)
            ts = jnp.where(g > 0, moved, ts)
            gap = jnp.where(pairs, s - ts, 0.0)
            sums[16:17, 0:256] += colsum(gap * gap) * (0.5 / LONG_LEN)
            pg = dot_nt(pick(cg, j), v)
            sg = p * (pg - jnp.sum(pg * p, axis=1, keepdims=True)) + gap * (1.0 / LONG_LEN)
            sg = sg.astype(bf16)
            dv.append(dot_tn(p.astype(bf16), cg))
            dq.append(dot_nn(sg, k))
            dk.append(dot_tn(sg, q))
        scale = HEAD_DIM**-0.5
        dq = (jnp.where(first, dq[0], dq[1]) * scale).astype(bf16)
        dk = (jnp.where(first, dk[0], dk[1]) * scale).astype(bf16)
        dv = jnp.where(first, dv[0], dv[1]).astype(bf16)
        for index, (grad, at) in enumerate(((dq, q0), (dk, k0), (dv, v0))):
            qkv[rs, pl.ds(at, 128)] = grad
            sums[index : index + 1, pl.ds(q0, 128)] += colsum(grad.astype(f32))

    def input_back(c):
        cs = pl.ds(c, 256)
        g = dot_nt(qkv[...], wt[cs, :])
        grad, clip_sum = clip_back(g, hid[:, cs].astype(f32), c0, i0)
        sums[19:20, cs] += clip_sum
        acc[:, cs] += grad

    def close_sums():
        for part in range(4):
            sums[9 + part : 10 + part, :] = wbias[1:2, part * D : (part + 1) * D]
        at = lax.broadcasted_iota(jnp.int32, (1, D), 1)
        line = jnp.zeros((1, D), f32)
        for spot, value in enumerate(
            (
                sums[19:20, :], sums[17:18, :], sums[18:19, :], sums[14:15, :],
                sums[15:16, :] + sums[16:17, :],
            )
        ):
            line = jnp.where(at == spot, jnp.sum(value), line)
        sums[13:14, :] = line
        small_out[...] = sums[0:16, :]

    firsts = (over_x, over_y)
    seconds = (over_y, over_x)
    outer = (z == 0) | (z == 3)
    inner = (z == 1) | (z == 2)
    near = z + 1 - 2 * lax.rem(z, 2)
    beyond = 1 - lax.div(z, 2)

    def on_z(to):
        return (dp, to * 2 + core)

    def lanes(p, w):
        return pl.ds(p * (w // 2), w // 2)

    def core_copy(k, w):
        slot, duo = lax.rem(k, SLOTS), lax.rem(k, 2)
        cs = pl.ds(0, w)
        return remote(
            pt.at[slot, :, 1 - core, :, :, :, cs], rb.at[duo, :, :, :, :, cs], s1.at[slot],
            r1.at[slot], over_core,
        )

    def own_rows(slot, blocks, p, w, mine):
        i = (x if p == 0 else y) if mine else (1 - x if p == 0 else 1 - y)
        if p == 0:
            return pt.at[slot, blocks, core, i, :, :, lanes(p, w)]
        return pt.at[slot, blocks, core, :, i, :, lanes(p, w)]

    def first_copy(k, w, p):
        slot, duo = lax.rem(k, SLOTS), lax.rem(k, 2)
        src = own_rows(slot, pl.ds(0, 4), p, w, False)
        dst = rx.at[duo, p, :, :, :, lanes(0, w)]
        return remote(src, dst, s2.at[slot, p], r2.at[slot, p], firsts[p])

    def in_copy(k, w, p):
        slot, duo = lax.rem(k, SLOTS), lax.rem(k, 2)
        src = own_rows(slot, pl.ds(beyond, 3), p, w, True)
        dst = rz.at[duo, p, :, :, :, lanes(0, w)]
        return remote(src, dst, s3.at[slot, p], r3.at[slot, p], on_z(near))

    def out_copy(k, w, p, kind):
        slot = lax.rem(k, SLOTS)
        to = (near, 3 - z, lax.rem(z + 2, 4))[kind]
        return remote(
            own_rows(slot, to, p, w, True), rf.at[slot, min(kind, 1), p, :, :, lanes(0, w)],
            s4.at[slot, kind, p], r4.at[slot, min(kind, 1), p], on_z(to),
        )

    def direct_copy(p, hop):
        to = lax.rem(z + hop, 4)
        return remote(
            own_rows((CHUNKS - 1) % SLOTS, to, p, HALF, True), rd.at[hop - 1, p],
            s7.at[hop - 1, p], r7.at[hop - 1, p], on_z(to),
        )

    def room_of(k):
        return 2 if isinstance(k, int) else lax.rem(k, 2)

    def second_copy(k, w, p):
        slot, duo = lax.rem(k, SLOTS), room_of(k)
        cs = lanes(0, w)
        return remote(
            held.at[duo, p, :, :, cs], ry.at[duo, p, :, :, cs], s5.at[slot, p], r5.at[slot, p],
            seconds[p],
        )

    def fin_at(k, w, p, rows):
        if w == CHUNK:
            flat = k * CHUNK
        else:
            flat = WIDE * CHUNK + (k - WIDE) * w
        cs = pl.ds(pl.multiple_of(lax.rem(flat, FF) + p * (w // 2), 128), w // 2)
        return (lax.div(flat, FF), *((x, rows) if p == 0 else (rows, y)), slice(None), cs)

    def back_first(k, w, p):
        slot = lax.rem(k, SLOTS)
        ref = fin.at[fin_at(k, w, p, slice(None))]
        return remote(ref, ref, s6.at[slot, p], r6.at[slot, p], firsts[p])

    def small_copy(step):
        to = (
            over_core, over_x, over_y, on_z(lax.rem(z + 1, 4)), on_z(lax.rem(z + 2, 4)),
            on_z(lax.rem(z + 3, 4)),
        )[step]
        return remote(small_out, sin.at[step], sms.at[step], smr.at[step], to)

    def finish_first(k, w):
        for p in range(2):
            back_first(k, w, p).wait()
        fin_save(k, w).start()

    def fin_save(k, w):
        if w == CHUNK:
            flat = k * CHUNK
        else:
            flat = WIDE * CHUNK + (k - WIDE) * w
        cs = pl.ds(pl.multiple_of(lax.rem(flat, FF), 128), w)
        at = (lax.div(flat, FF), slice(None), slice(None), slice(None), cs)
        return pltpu.make_async_copy(fin.at[at], fin_to.at[at], fsem.at[lax.rem(k, SLOTS)])

    def finish_save(k, w):
        fin_save(k, w).wait()

    def finish_second(k, w):
        duo = room_of(k)
        for p in range(2):
            second_copy(k, w, p).wait()
            for i in range(2):
                cs = lanes(0, w)
                fin[fin_at(k, w, p, i)] = held[duo, p, i, :, cs] + ry[duo, p, i, :, cs]
            back_first(k, w, p).start()

    def finish_out(k, w):
        slot, duo = lax.rem(k, SLOTS), lax.rem(k, 2)
        cs = lanes(0, w)

        @pl.when(outer)
        def _():
            for p in range(2):
                out_copy(k, w, p, 0).wait_recv()
                out_copy(k, w, p, 2).wait_recv()
                for i in range(2):
                    at = (x, i) if p == 0 else (i, y)
                    own = pt[(slot, z, core, *at, slice(None), lanes(p, w))]
                    held[duo, p, i, :, cs] = (
                        own + rf[slot, 0, p, i, :, cs] + rf[slot, 1, p, i, :, cs]
                    )

        @pl.when(inner)
        def _():
            for p in range(2):
                out_copy(k, w, p, 1).wait()
                out_copy(k, w, p, 0).wait_send()
                out_copy(k, w, p, 2).wait_send()
                for i in range(2):
                    at = (x, i) if p == 0 else (i, y)
                    own = pt[(slot, z, core, *at, slice(None), lanes(p, w))]
                    held[duo, p, i, :, cs] = own + rf[slot, 1, p, i, :, cs]

        for p in range(2):
            second_copy(k, w, p).start()

    def finish_in(k, w):
        slot, duo = lax.rem(k, SLOTS), lax.rem(k, 2)

        @pl.when(outer)
        def _():
            for p in range(2):
                in_copy(k, w, p).wait_send()

        @pl.when(inner)
        def _():
            for p in range(2):
                in_copy(k, w, p).wait_recv()
                for q in range(3):
                    for i in range(2):
                        at = (x, i) if p == 0 else (i, y)
                        at = (slot, beyond + q, core, *at, slice(None), lanes(p, w))
                        pt[at] += rz[duo, p, q, i, :, lanes(0, w)]
                for kind in (2, 1, 0):
                    out_copy(k, w, p, kind).start()

    def add_first(k, w, p):
        slot, duo = lax.rem(k, SLOTS), lax.rem(k, 2)
        first_copy(k, w, p).wait()
        for q in range(4):
            for i in range(2):
                at = (x, i) if p == 0 else (i, y)
                at = (slot, q, core, *at, slice(None), lanes(p, w))
                pt[at] += rx[duo, p, q, i, :, lanes(0, w)]

    def finish_one(k, w):
        for p in range(2):
            add_first(k, w, p)

            @pl.when(outer)
            def _():
                in_copy(k, w, p).start()

    def last_one():
        for p in range(2):
            add_first(CHUNKS - 1, HALF, p)
            for hop in (2, 1, 3):
                direct_copy(p, hop).start()

    def last_direct():
        slot = (CHUNKS - 1) % SLOTS
        for p in range(2):
            for hop in (1, 3, 2):
                direct_copy(p, hop).wait()
            for i in range(2):
                at = (x, i) if p == 0 else (i, y)
                own = pt[(slot, z, core, *at, slice(None), lanes(p, HALF))]
                held[2, p, i, :, lanes(0, HALF)] = own + rd[0, p, i] + rd[1, p, i] + rd[2, p, i]
            second_copy(CHUNKS - 1, HALF, p).start()

    def finish_core(k, w):
        slot, duo = lax.rem(k, SLOTS), lax.rem(k, 2)
        core_copy(k, w).wait()
        cs = pl.ds(0, w)
        for q in range(4):
            pt[slot, q, core, :, :, :, cs] += rb[duo, q, :, :, :, cs]
        for p in range(2):
            first_copy(k, w, p).start()

    stages = (
        (7, finish_save), (6, finish_first), (5, finish_second), (4, finish_out), (3, finish_in),
        (2, finish_one), (1, finish_core),
    )
    last = CHUNKS - 1
    last_stages = {
        5: lambda: finish_second(last, HALF), 4: last_direct, 2: last_one,
        6: lambda: finish_first(last, HALF), 1: lambda: finish_core(last, HALF),
    }

    def tick(t, carry):
        for lag, step in stages:

            @pl.when((t >= lag) & (t < lag + WIDE))
            def _():
                step(t - lag, CHUNK)

            @pl.when(t == lag + WIDE)
            def _():
                step(t - lag, HALF)

            if lag in last_stages:

                @pl.when(t == last + lag - (1 if lag > 2 else 0))
                def _():
                    last_stages[lag]()

        slot = lax.rem(t, SLOTS)

        def put(owner, cs, block):
            for i in range(2):
                for j in range(2):
                    at = (i * 2 + j) * 24
                    pt[slot, owner // 2, owner % 2, i, j, :, cs] = block[at : at + 24, :]

        pieces = CHUNK // 128
        turns = 8 // pieces

        @pl.when(t < SECTION)
        def _():
            j = lax.div(t, turns)
            count = pieces * BLOCK
            left = nlT[pl.ds(pl.multiple_of(lax.rem(t, turns) * count, count), count), :]
            for owner in range(8):
                cs = pl.ds(pl.multiple_of(owner * 384 + j * 128, 128), 128)
                got = dot_nn(left, act[:, cs])
                for part in range(pieces):
                    put(owner, pl.ds(part * 128, 128), got[part * BLOCK : (part + 1) * BLOCK, :])

        def whole(left, right, half):
            got = dot_nn(left, right)
            for owner in range(8):
                put(owner, pl.ds(half * 256, 256), got[owner * BLOCK : (owner + 1) * BLOCK, :])

        for half in range(2):

            @pl.when((t >= SECTION) & (t < 2 * SECTION))
            def _():
                cs = pl.ds(pl.multiple_of((t - SECTION) * CHUNK + half * 256, 256), 256)
                whole(wlT[...], wg[:, cs], half)

            part = (t - 2 * SECTION) * 2 + half

            @pl.when((part >= 0) & (part < 3))
            def _():
                whole(clT[...], low[:, pl.ds(pl.multiple_of(part * 256, 256), 256)], half)

            @pl.when((part >= 3) & (part < 10))
            def _():
                whole(xlT[...], qkv[:, pl.ds(pl.multiple_of((part - 3) * 256, 256), 256)], half)

        @pl.when(t < WIDE)
        def _():
            core_copy(t, CHUNK).start()

        @pl.when((t >= WIDE) & (t < CHUNKS))
        def _():
            cs = pl.ds(pl.multiple_of((t - WIDE + 7) * 256, 256), 256)
            whole(xlT[...], qkv[:, cs], 0)
            core_copy(t, HALF).start()

        for when, turn in ((2, turn_inputs), (3, turn_context), (4, turn_widen)):

            @pl.when(t == when)
            def _():
                loop(4, 128, turn)

        units = 12 // SECTION
        begin = SECTION + 1

        @pl.when((t >= 1) & (t < SECTION))
        def _():
            feed_back(t - 1)

        @pl.when(t == SECTION - 1)
        def _():
            feed_back(t)

        @pl.when(t == SECTION)
        def _():
            for slot in range(2):
                scores_copy(slot, slot).start()
            loop(4, 128, norm_one_back)
            loop(3, 256, mix_back)

        @pl.when((t >= begin) & (t < begin + SECTION))
        def _():
            for index in range(units):
                u = (t - begin) * units + index
                at = lax.rem(u, 2)
                scores_copy(u, at).wait()
                attend_pair_back(u, at)

                @pl.when(u < 10)
                def _():
                    scores_copy(u + 2, at).start()

        done = begin + SECTION

        @pl.when((t >= done) & (t < done + 3))
        def _():
            input_back(pl.multiple_of((t - done) * 256, 256))

        @pl.when(t == done + 3)
        def _():
            acc_save.start()
            close_sums()
            small_copy(0).start()

        @pl.when(t == done + 4)
        def _():
            small_copy(0).wait()
            small_out[...] += sin[0]
            small_copy(1).start()

        @pl.when(t == done + 5)
        def _():
            small_copy(1).wait()
            small_out[...] += sin[1]
            small_copy(2).start()

        @pl.when(t == done + 6)
        def _():
            small_copy(2).wait()
            small_out[...] += sin[2]
            for step in (3, 4, 5):
                small_copy(step).start()

        @pl.when(t == done + 7)
        def _():
            for step in (3, 4, 5):
                small_copy(step).wait()
            small_out[...] = small_out[...] + sin[3] + sin[4] + sin[5]

        return carry

    lax.fori_loop(0, CHUNKS + 5, tick, 0)
    fin_save(WIDE, HALF).wait()
    fin_save(last, HALF).wait()
    for copy in (out_save, acc_save, kept_save):
        copy.wait()


def layer(*args):
    vm = pl.BlockSpec(memory_space=pltpu.VMEM)
    sm = pl.BlockSpec(memory_space=pltpu.SMEM)
    sds = jax.ShapeDtypeStruct
    dma = pltpu.SemaphoreType.DMA
    return pl.pallas_call(
        layer_kernel,
        out_shape=(
            sds((ROWS, D), bf16),
            sds((ROWS, D), f32),
            sds((3, 2, 2, 24, FF), f32),
            sds((72, D), jnp.int32),
            sds((16, D), f32),
        ),
        in_specs=[sm] * 3 + [vm] * 6 + [pl.BlockSpec(memory_space=pl.ANY)] * 7,
        out_specs=(pl.BlockSpec(memory_space=pl.ANY),) * 4 + (vm,),
        scratch_shapes=[
            pltpu.VMEM((ROWS, D), bf16),
            pltpu.VMEM((ROWS, D), f32),
            pltpu.VMEM((3, 2, 2, 24, FF), f32),
            pltpu.VMEM((72, D), jnp.int32),
            pltpu.VMEM((ROWS, D), bf16),
            pltpu.VMEM((8, 72, D), jnp.int32),
            pltpu.VMEM((8, 32, 128), f32),
            pltpu.VMEM((8, BLOCK, 128), f32),
            pltpu.VMEM((128, 128), f32),
            pltpu.VMEM((D, 3 * D), bf16),
            pltpu.VMEM((D, D), bf16),
            pltpu.VMEM((D, FF), bf16),
            pltpu.VMEM((FF, D), bf16),
            pltpu.VMEM((16, D), f32),
            pltpu.VMEM((8, 3 * D), f32),
            pltpu.VMEM((8, FF), f32),
            pltpu.VMEM((ROWS, 3 * D), bf16),
            pltpu.VMEM((ROWS, D), bf16),
            pltpu.VMEM((ROWS, D), f32),
            pltpu.VMEM((ROWS, D), f32),
            pltpu.VMEM((ROWS, 128), f32),
            pltpu.VMEM((ROWS, FF), f32),
            pltpu.VMEM((ROWS, FF), bf16),
            pltpu.VMEM((ROWS, FF), bf16),
            pltpu.VMEM((ROWS, D), f32),
            pltpu.VMEM((ROWS, D), bf16),
            pltpu.VMEM((2, 256, 256), bf16),
            pltpu.VMEM((2, 256, 256), bf16),
            pltpu.VMEM((D, ROWS), bf16),
            pltpu.VMEM((D, ROWS), bf16),
            pltpu.VMEM((D, ROWS), bf16),
            pltpu.VMEM((D, ROWS), bf16),
            pltpu.VMEM((24, D), f32),
            pltpu.VMEM((2, 2, 256, 256), bf16),
            pltpu.VMEM((SLOTS, 4, 2, 2, 2, 24, CHUNK), f32),
            pltpu.VMEM((2, 4, 2, 2, 24, CHUNK), f32),
            pltpu.VMEM((2, 2, 4, 2, 24, HALF), f32),
            pltpu.VMEM((2, 2, 3, 2, 24, HALF), f32),
            pltpu.VMEM((SLOTS, 2, 2, 2, 24, HALF), f32),
            pltpu.VMEM((3, 2, 2, 24, HALF), f32),
            pltpu.VMEM((3, 2, 2, 24, HALF), f32),
            pltpu.VMEM((3, 2, 2, 24, HALF // 2), f32),
            pltpu.VMEM((6, 16, D), f32),
        ]
        + [dma((SLOTS,))] * 2
        + [dma((SLOTS, 2))] * 4
        + [dma((SLOTS, 3, 2)), dma((SLOTS, 2, 2))]
        + [dma((SLOTS, 2))] * 4
        + [dma((6,))] * 2
        + [dma((2,)), dma((2, 4)), dma((4, 3)), dma((4, 3)), dma((4, 4)), dma((4, 4)), dma((5,)), dma((SLOTS,)), dma((3, 2)), dma((3, 2))],
        compiler_params=pltpu.CompilerParams(collective_id=0, has_side_effects=True, vmem_limit_bytes=LAYER_CAP),
        name="layer",
    )(*args)


def finish_kernel(
    count, small, kept, fin, out_in, grad_in, out, grad, tg, mg, wg, ng, tb, mb, wb, nb, gain, shift, clips, loss,
    fbuf, turned, tout, mout, wout, nout, obuf, gbuf, fsem, osem, psem,
):
    fcopies = [pltpu.make_async_copy(fin.at[i], fbuf.at[i], fsem.at[i]) for i in range(3)]
    ocopies = []
    for half in range(2):
        for index, (src, dst) in enumerate(((nout, ng), (wout, wg), (mout, mg), (tout, tg))):
            at = index * 2 + half
            ocopies.append(pltpu.make_async_copy(src.at[half], dst.at[half], osem.at[at]))
    for index in (1, 2, 0):
        fcopies[index].start()
    arrive = [
        pltpu.make_async_copy(out_in, obuf, psem.at[0]),
        pltpu.make_async_copy(grad_in, gbuf, psem.at[1]),
    ]
    depart = [
        pltpu.make_async_copy(obuf, out, psem.at[2]),
        pltpu.make_async_copy(gbuf, grad, psem.at[3]),
    ]
    for copy in arrive:
        copy.start()
    me = lax.axis_index("fsdp")
    z = lax.div(me, 2)
    core = lax.rem(me, 2)
    own = pltpu.roll(small[...], lax.rem(8 - me, 8) * BLOCK, 1)
    tb[...] = own[0:3, 0:BLOCK]
    mb[...] = own[3:4, 0:BLOCK]
    nb[...] = own[4:5, 0:BLOCK]
    gain[...] = own[5:7, 0:BLOCK]
    shift[...] = own[7:9, 0:BLOCK]
    wide = pltpu.roll(small[...], core * (4 * BLOCK), 1)
    row = lax.broadcasted_iota(jnp.int32, (16, D), 0)
    picked = jnp.sum(jnp.where(row == 9 + z, wide, 0.0), axis=0, keepdims=True)
    wb[...] = picked[:, 0 : 4 * BLOCK]
    line = small[13:14, :]
    lane = lax.broadcasted_iota(jnp.int32, (1, D), 1)
    for spot in range(4):
        clips[spot] = jnp.sum(jnp.where(lane == spot, line, 0.0))
    loss[...] = jnp.sum(jnp.where(lane == 4, line, 0.0)) * count[0]

    def keep(block, half, group, total, fan):
        word, bit = plane_of(block, half, group)
        bits = kept[word * 8 : (word + 1) * 8, :] & jnp.int32(bit)
        return jnp.where(bits != 0, total * (1.0 / math.sqrt(fan)), 0.0)

    def spread_out(blocks, half, dst, src, at):
        for index, block in enumerate(blocks):
            cols = slice(index * D, (index + 1) * D)
            for group in range(12):
                rows = slice(group * 8, (group + 1) * 8)
                total = src[rows, at + index * D : at + (index + 1) * D]
                dst[half, rows, cols] = keep(block, half, group, total, D)

    def leave(index, half):
        ocopies[index + 4 * half].start()

    fcopies[1].wait()
    for half in range(2):
        spread_out(range(4, 8), half, wout, fbuf.at[1], 0)
        leave(1, half)
    fcopies[2].wait()
    for half in range(2):
        spread_out(range(3), half, tout, fbuf.at[2], D)
        leave(3, half)
    for half in range(2):
        spread_out(range(3, 4), half, mout, fbuf.at[2], 0)
        leave(2, half)
    for index in range(2):
        arrive[index].wait()
        depart[index].start()
    fcopies[0].wait()
    for j in range(3):
        for i in range(2):
            tiles = range((j * 2 + i) * 4, (j * 2 + i) * 4 + 4)
            parts = [fbuf[0, :, tile * 128 : (tile + 1) * 128] for tile in tiles]
            total = jnp.concatenate(parts, axis=0).T
            turned[j * 128 : (j + 1) * 128, i * 384 : (i + 1) * 384] = total
    for half in range(2):
        for block in range(8, 12):
            for group in range(12):
                rows = slice((block - 8) * BLOCK + group * 8, (block - 8) * BLOCK + group * 8 + 8)
                nout[half, rows, :] = keep(block, half, group, turned[rows, :], FF)
        leave(0, half)
    for copy in depart + ocopies:
        copy.wait()


def finish(count, small, kept, fin, out, grad):
    vm = pl.BlockSpec(memory_space=pltpu.VMEM)
    sm = pl.BlockSpec(memory_space=pltpu.SMEM)
    hbm = pl.BlockSpec(memory_space=pl.ANY)
    sds = jax.ShapeDtypeStruct
    shapes = [(2, BLOCK, 3 * D), (2, BLOCK, D), (2, BLOCK, FF), (2, 4 * BLOCK, D)]
    dma = pltpu.SemaphoreType.DMA
    return pl.pallas_call(
        finish_kernel,
        out_shape=[sds((ROWS, D), bf16), sds((ROWS, D), f32)]
        + [sds(v, f32) for v in shapes]
        + [
            sds((3, BLOCK), f32), sds((1, BLOCK), f32), sds((1, 4 * BLOCK), f32),
            sds((1, BLOCK), f32), sds((2, BLOCK), f32), sds((2, BLOCK), f32),
            sds((4,), f32), sds((), f32),
        ],
        in_specs=[sm, vm, vm, hbm, hbm, hbm],
        out_specs=[hbm] * 6 + [vm] * 6 + [sm] * 2,
        scratch_shapes=[pltpu.VMEM((3, BLOCK, FF), f32), pltpu.VMEM((4 * BLOCK, D), f32)]
        + [pltpu.VMEM(v, f32) for v in shapes]
        + [pltpu.VMEM((ROWS, D), bf16), pltpu.VMEM((ROWS, D), f32)]
        + [dma((3,)), dma((8,)), dma((4,))],
        compiler_params=pltpu.CompilerParams(vmem_limit_bytes=VMEM_CAP),
        name="finish",
    )(count, small, kept, fin, out, grad)


def on_device_fast(
    hidden_in, teacher_hidden, teacher_scores, seq_lengths, live_counts, triple_latent,
    mixing_latent, widen_latent, narrow_latent, triple_bias, mixing_bias, widen_bias, narrow_bias,
    norm_gain, norm_shift, clip_level,
):
    out, input_grad, fin, kept, small_sum = layer(
        seq_lengths, live_counts, clip_level, triple_bias, mixing_bias[None], widen_bias,
        narrow_bias[None], norm_gain, norm_shift, hidden_in, teacher_hidden,
        jnp.transpose(teacher_scores, (1, 0, 2)), triple_latent, mixing_latent, widen_latent,
        narrow_latent,
    )
    fin = fin.reshape(3, BLOCK, FF)
    tokens = hidden_in.shape[0] * lax.axis_size("dp") * lax.axis_size("fsdp")
    count = jnp.full((1,), 1.0 / (tokens * D), f32)
    out, input_grad, tg, mg, wg, ng, tb, mb, wb, nb, gain, shift, clips, loss = finish(
        count, small_sum, kept, fin, out, input_grad
    )
    return (
        out, loss, input_grad, tg, mg, wg, ng, tb, mb.reshape(BLOCK),
        wb.reshape(4 * BLOCK), nb.reshape(BLOCK), gain, shift, clips,
    )


def solution(mesh):
    in_specs = (
        P(("dp", "fsdp"), None),
        P(("dp", "fsdp"), None),
        P(("dp", "fsdp"), None, None),
        P(("dp", "fsdp"), None),
        P(("dp", "fsdp"), None),
        P(None, "fsdp", None),
        P(None, "fsdp", None),
        P(None, "fsdp", None),
        P(None, "fsdp", None),
        P(None, "fsdp"),
        P("fsdp"),
        P("fsdp"),
        P("fsdp"),
        P(None, "fsdp"),
        P(None, "fsdp"),
        P(),
    )
    out_specs = (
        P(("dp", "fsdp"), None),
        P(),
        P(("dp", "fsdp"), None),
        P(None, "fsdp", None),
        P(None, "fsdp", None),
        P(None, "fsdp", None),
        P(None, "fsdp", None),
        P(None, "fsdp"),
        P("fsdp"),
        P("fsdp"),
        P("fsdp"),
        P(None, "fsdp"),
        P(None, "fsdp"),
        P(),
    )
    fits = mesh.shape["dp"] == 4 and mesh.shape["fsdp"] == 8
    return jax.shard_map(
        on_device_fast if fits else on_device, mesh=mesh, in_specs=in_specs, out_specs=out_specs, check_vma=False
    )
```

```python
import math

import jax
import jax.numpy as jnp
from jax import lax
from jax.experimental import pallas as pl
from jax.experimental.pallas import tpu as pltpu
from jax.sharding import PartitionSpec as P

D = 768
HEADS = 12
HEAD_DIM = 64
FF = 3072
LONG_LEN = 256
MID_LEN = 128
SHORT_LEN = 64
LONG_SLOTS = 1
MID_SLOTS = 1
SHORT_SLOTS = 2


bit_count = 32
norm_epsilon = 1e-12
masked_fill = -1e30


def soft_clip(values, clip_at):
    return clip_at * jnp.tanh(values / clip_at)


def layer_norm(values, gain_row, shift_row):
    center = values - jnp.mean(values, axis=-1, keepdims=True)
    variance = jnp.mean(center * center, axis=-1, keepdims=True)
    return center * lax.rsqrt(variance + norm_epsilon) * gain_row + shift_row


def gelu_exact(values):
    return 0.5 * values * (1.0 + lax.erf(values * (1.0 / math.sqrt(2.0))))


def pack_signs(latent):
    halves, row_count, columns = latent.shape
    sign_bits = (
        (latent > 0).astype(jnp.int32).reshape(halves, row_count, columns // bit_count, bit_count)
    )
    places = jnp.arange(bit_count, dtype=jnp.int32)
    return jnp.sum(jnp.left_shift(sign_bits, places), axis=-1, dtype=jnp.int32)


def unpack_weight(sign_words, scales):
    halves, row_count, word_count = sign_words.shape
    places = jnp.arange(bit_count, dtype=jnp.int32)
    sign_bits = jnp.bitwise_and(jnp.right_shift(sign_words[..., None], places), 1)
    sign_values = (
        (2 * sign_bits - 1).astype(jnp.float32).reshape(halves, row_count, word_count * bit_count)
    )
    return (scales[0][:, None] * sign_values[0] + scales[1][:, None] * sign_values[1]).astype(
        jnp.bfloat16
    )


def bucket_shapes():
    return ((LONG_SLOTS, LONG_LEN), (MID_SLOTS, MID_LEN), (SHORT_SLOTS, SHORT_LEN))


def bucket_masks(lengths, live_count, slot_count, bucket_len):
    places = jnp.arange(bucket_len, dtype=jnp.int32)
    key_ok = places[None, :] < lengths[:, None]
    query_ok = jnp.logical_and(
        key_ok, jnp.arange(slot_count, dtype=jnp.int32)[:, None] < live_count
    )
    return (key_ok, query_ok)


def split_heads(block, slot_count, bucket_len):
    return block.reshape(slot_count, bucket_len, HEADS, HEAD_DIM)


def bucket_scores(qkv_rows, teacher_rows, key_ok, query_ok, slot_count, bucket_len):
    queries = split_heads(qkv_rows[:, :D], slot_count, bucket_len)
    keys_part = split_heads(qkv_rows[:, D : 2 * D], slot_count, bucket_len)
    scores = jnp.einsum(
        "sqhd,skhd->shqk", queries, keys_part, preferred_element_type=jnp.float32
    ) * HEAD_DIM ** (-0.5)
    masked = jnp.where(key_ok[:, None, None, :], scores, masked_fill)
    teacher = jnp.transpose(
        teacher_rows.reshape(slot_count, bucket_len, HEADS, LONG_LEN)[..., :bucket_len],
        (0, 2, 1, 3),
    ).astype(jnp.float32)
    pair_ok = jnp.logical_and(query_ok[:, None, :, None], key_ok[:, None, None, :])
    score_gap = jnp.where(pair_ok, scores - teacher, 0.0)
    return (queries, keys_part, masked, score_gap)


def attend(qkv_rows, teacher_rows, key_ok, query_ok, slot_count, bucket_len):
    queries, keys_part, masked, score_gap = bucket_scores(
        qkv_rows, teacher_rows, key_ok, query_ok, slot_count, bucket_len
    )
    values_part = split_heads(qkv_rows[:, 2 * D :], slot_count, bucket_len)
    row_top = jnp.max(masked, axis=-1, keepdims=True)
    exponent = jnp.exp(masked - row_top)
    exp_total = jnp.sum(exponent, axis=-1, keepdims=True)
    attention = exponent / exp_total
    context = jnp.einsum(
        "shqk,skhd->sqhd",
        attention.astype(jnp.bfloat16),
        values_part,
        preferred_element_type=jnp.float32,
    )
    distill = 0.5 / LONG_LEN * jnp.sum(score_gap * score_gap)
    return (context.reshape(slot_count * bucket_len, D), row_top + jnp.log(exp_total), distill)


def attend_back(
    qkv_rows, teacher_rows, key_ok, query_ok, slot_count, bucket_len, log_total, context_grad
):
    queries, keys_part, masked, score_gap = bucket_scores(
        qkv_rows, teacher_rows, key_ok, query_ok, slot_count, bucket_len
    )
    values_part = split_heads(qkv_rows[:, 2 * D :], slot_count, bucket_len)
    attention = jnp.exp(masked - log_total)
    grad_heads = split_heads(context_grad, slot_count, bucket_len)
    values_grad = jnp.einsum(
        "shqk,sqhd->skhd",
        attention.astype(jnp.bfloat16),
        grad_heads,
        preferred_element_type=jnp.float32,
    )
    weight_grad = jnp.einsum(
        "sqhd,skhd->shqk", grad_heads, values_part, preferred_element_type=jnp.float32
    )
    score_grad = attention * (
        weight_grad - jnp.sum(weight_grad * attention, axis=-1, keepdims=True)
    ) + score_gap * (1.0 / LONG_LEN)
    score_low = score_grad.astype(jnp.bfloat16)
    score_scale = HEAD_DIM ** (-0.5)
    queries_grad = (
        jnp.einsum("shqk,skhd->sqhd", score_low, keys_part, preferred_element_type=jnp.float32)
        * score_scale
    )
    keys_grad = (
        jnp.einsum("shqk,sqhd->skhd", score_low, queries, preferred_element_type=jnp.float32)
        * score_scale
    )
    row_count = slot_count * bucket_len
    return jnp.concatenate(
        [
            queries_grad.reshape(row_count, D),
            keys_grad.reshape(row_count, D),
            values_grad.reshape(row_count, D),
        ],
        axis=-1,
    )


def on_device(
    hidden_in,
    teacher_hidden,
    teacher_scores,
    seq_lengths,
    live_counts,
    triple_latent,
    mixing_latent,
    widen_latent,
    narrow_latent,
    triple_bias,
    mixing_bias,
    widen_bias,
    narrow_bias,
    norm_gain,
    norm_shift,
    clip_level,
):
    latents = (triple_latent, mixing_latent, widen_latent, narrow_latent)
    fan_ins = (D, D, D, FF)
    own_scales = tuple(
        (
            jnp.mean(jnp.abs(latent), axis=-1) / math.sqrt(fan_in)
            for latent, fan_in in zip(latents, fan_ins)
        )
    )
    packed = tuple((pack_signs(latent) for latent in latents))
    gathered = (
        lax.all_gather(packed[0], "fsdp", axis=1, tiled=True),
        lax.all_gather(packed[1], "fsdp", axis=1, tiled=True),
        lax.all_gather(packed[2], "fsdp", axis=1, tiled=True),
        lax.all_gather(packed[3], "fsdp", axis=1, tiled=True),
    )
    factors = (
        lax.all_gather(own_scales[0], "fsdp", axis=1, tiled=True),
        lax.all_gather(own_scales[1], "fsdp", axis=1, tiled=True),
        lax.all_gather(own_scales[2], "fsdp", axis=1, tiled=True),
        lax.all_gather(own_scales[3], "fsdp", axis=1, tiled=True),
        lax.all_gather(triple_bias, "fsdp", axis=1, tiled=True),
        lax.all_gather(mixing_bias, "fsdp", axis=0, tiled=True),
        lax.all_gather(widen_bias, "fsdp", axis=0, tiled=True),
        lax.all_gather(narrow_bias, "fsdp", axis=0, tiled=True),
        lax.all_gather(norm_gain, "fsdp", axis=1, tiled=True),
        lax.all_gather(norm_shift, "fsdp", axis=1, tiled=True),
    )
    scales = factors[:4]
    triple_rows, full_mixing_bias, full_widen_bias, full_narrow_bias, gains, shifts = factors[4:]
    full_triple_bias = triple_rows.reshape(3 * D)
    weights = tuple(
        (unpack_weight(words_part, scale_part) for words_part, scale_part in zip(gathered, scales))
    )
    inputs = hidden_in.astype(jnp.float32)
    inputs_low = soft_clip(inputs, clip_level[0]).astype(jnp.bfloat16)
    qkv_all = (
        jnp.dot(inputs_low, weights[0], preferred_element_type=jnp.float32) + full_triple_bias
    ).astype(jnp.bfloat16)
    lengths = seq_lengths[0]
    counts = live_counts[0]
    plans = []
    row_start = 0
    slot_start = 0
    for bucket, shape_pair in enumerate(bucket_shapes()):
        slot_count, bucket_len = shape_pair
        key_ok, query_ok = bucket_masks(
            lengths[slot_start : slot_start + slot_count], counts[bucket], slot_count, bucket_len
        )
        plans.append(
            (
                row_start,
                row_start + slot_count * bucket_len,
                slot_count,
                bucket_len,
                key_ok,
                query_ok,
            )
        )
        row_start = row_start + slot_count * bucket_len
        slot_start = slot_start + slot_count
    contexts = []
    log_totals = []
    distill_sum = 0.0
    for plan in plans:
        row_begin, row_end, slot_count, bucket_len, key_ok, query_ok = plan
        context, log_total, distill = attend(
            qkv_all[row_begin:row_end],
            teacher_scores[row_begin:row_end],
            key_ok,
            query_ok,
            slot_count,
            bucket_len,
        )
        contexts.append(context)
        log_totals.append(log_total)
        distill_sum = distill_sum + distill
    context = jnp.concatenate(contexts, axis=0)
    token_ok = jnp.concatenate([plan[5].reshape(-1) for plan in plans])
    context_low = soft_clip(context, clip_level[1]).astype(jnp.bfloat16)
    mixed = jnp.dot(context_low, weights[1], preferred_element_type=jnp.float32) + full_mixing_bias
    first_sum = inputs + mixed
    first_norm = layer_norm(first_sum, gains[0], shifts[0])
    widen_low = soft_clip(first_norm, clip_level[2]).astype(jnp.bfloat16)
    widened = jnp.dot(widen_low, weights[2], preferred_element_type=jnp.float32) + full_widen_bias
    activated = gelu_exact(widened)
    activated_low = soft_clip(activated, clip_level[3]).astype(jnp.bfloat16)
    narrowed = (
        jnp.dot(activated_low, weights[3], preferred_element_type=jnp.float32) + full_narrow_bias
    )
    second_sum = first_norm + narrowed
    out_full = layer_norm(second_sum, gains[1], shifts[1])
    out_gap = jnp.where(token_ok[:, None], out_full - teacher_hidden.astype(jnp.float32), 0.0)
    loss_local = 0.5 * jnp.sum(out_gap * out_gap) + distill_sum
    regathered = (
        lax.all_gather(packed[0], "fsdp", axis=1, tiled=True),
        lax.all_gather(packed[1], "fsdp", axis=1, tiled=True),
        lax.all_gather(packed[2], "fsdp", axis=1, tiled=True),
        lax.all_gather(packed[3], "fsdp", axis=1, tiled=True),
    )
    back_weights = tuple(
        (
            unpack_weight(words_part, scale_part)
            for words_part, scale_part in zip(regathered, scales)
        )
    )
    _, second_back = jax.vjp(layer_norm, second_sum, gains[1], shifts[1])
    second_grad, gain_two, shift_two = second_back(out_gap)
    narrow_low = second_grad.astype(jnp.bfloat16)
    narrow_weight_grad = jnp.einsum(
        "rf,rd->fd", activated_low, narrow_low, preferred_element_type=jnp.float32
    )
    act_low_grad = jnp.einsum(
        "rd,fd->rf", narrow_low, back_weights[3], preferred_element_type=jnp.float32
    )
    _, clip_three_back = jax.vjp(soft_clip, activated, clip_level[3])
    act_grad, clip_three = clip_three_back(act_low_grad)
    _, gelu_back = jax.vjp(gelu_exact, widened)
    (widened_grad,) = gelu_back(act_grad)
    widen_grad_low = widened_grad.astype(jnp.bfloat16)
    widen_weight_grad = jnp.einsum(
        "rd,rf->df", widen_low, widen_grad_low, preferred_element_type=jnp.float32
    )
    norm_low_grad = jnp.einsum(
        "rf,df->rd", widen_grad_low, back_weights[2], preferred_element_type=jnp.float32
    )
    _, clip_two_back = jax.vjp(soft_clip, first_norm, clip_level[2])
    norm_grad, clip_two = clip_two_back(norm_low_grad)
    norm_grad = norm_grad + second_grad
    _, first_back = jax.vjp(layer_norm, first_sum, gains[0], shifts[0])
    first_grad, gain_one, shift_one = first_back(norm_grad)
    mixed_low = first_grad.astype(jnp.bfloat16)
    mixing_weight_grad = jnp.einsum(
        "rc,rd->cd", context_low, mixed_low, preferred_element_type=jnp.float32
    )
    context_low_grad = jnp.einsum(
        "rd,cd->rc", mixed_low, back_weights[1], preferred_element_type=jnp.float32
    )
    _, clip_one_back = jax.vjp(soft_clip, context, clip_level[1])
    context_grad, clip_one = clip_one_back(context_low_grad)
    context_grad_low = context_grad.astype(jnp.bfloat16)
    qkv_grads = []
    for plan, log_total in zip(plans, log_totals):
        row_begin, row_end, slot_count, bucket_len, key_ok, query_ok = plan
        qkv_grads.append(
            attend_back(
                qkv_all[row_begin:row_end],
                teacher_scores[row_begin:row_end],
                key_ok,
                query_ok,
                slot_count,
                bucket_len,
                log_total,
                context_grad_low[row_begin:row_end],
            )
        )
    qkv_grad_low = jnp.concatenate(qkv_grads, axis=0).astype(jnp.bfloat16)
    triple_weight_grad = jnp.einsum(
        "rd,re->de", inputs_low, qkv_grad_low, preferred_element_type=jnp.float32
    )
    input_low_grad = jnp.einsum(
        "re,de->rd", qkv_grad_low, back_weights[0], preferred_element_type=jnp.float32
    )
    _, clip_zero_back = jax.vjp(soft_clip, inputs, clip_level[0])
    input_side, clip_zero = clip_zero_back(input_low_grad)
    input_grad = input_side + first_grad
    bias_sums = (
        jnp.sum(qkv_grad_low, axis=0, dtype=jnp.float32).reshape(3, D),
        jnp.sum(mixed_low, axis=0, dtype=jnp.float32),
        jnp.sum(widen_grad_low, axis=0, dtype=jnp.float32),
        jnp.sum(narrow_low, axis=0, dtype=jnp.float32),
    )
    row_shares = (
        lax.psum_scatter(triple_weight_grad, "fsdp", scatter_dimension=0, tiled=True),
        lax.psum_scatter(mixing_weight_grad, "fsdp", scatter_dimension=0, tiled=True),
        lax.psum_scatter(widen_weight_grad, "fsdp", scatter_dimension=0, tiled=True),
        lax.psum_scatter(narrow_weight_grad, "fsdp", scatter_dimension=0, tiled=True),
    )
    totals = lax.psum((row_shares[0], row_shares[1], row_shares[2], row_shares[3]), "dp")
    small_sums = lax.psum(
        (
            bias_sums[0],
            bias_sums[1],
            bias_sums[2],
            bias_sums[3],
            jnp.stack([gain_one, gain_two]),
            jnp.stack([shift_one, shift_two]),
            jnp.stack([clip_zero, clip_one, clip_two, clip_three]),
            loss_local,
        ),
        ("dp", "fsdp"),
    )
    shard_index = lax.axis_index("fsdp")
    shard_parts = lax.axis_size("fsdp")

    def own_part(vector, along):
        share_width = vector.shape[along] // shard_parts
        return lax.dynamic_slice_in_dim(vector, shard_index * share_width, share_width, along)

    latent_grads = tuple(
        (
            jnp.where(jnp.abs(latent) <= 1.0, (total / math.sqrt(fan_in))[None], 0.0)
            for latent, total, fan_in in zip(latents, totals, fan_ins)
        )
    )
    loss = small_sums[7] / (hidden_in.shape[0] * D * lax.axis_size("dp") * shard_parts)
    return (
        out_full.astype(jnp.bfloat16),
        loss,
        input_grad,
        latent_grads[0],
        latent_grads[1],
        latent_grads[2],
        latent_grads[3],
        own_part(small_sums[0], 1),
        own_part(small_sums[1], 0),
        own_part(small_sums[2], 0),
        own_part(small_sums[3], 0),
        own_part(small_sums[4], 1),
        own_part(small_sums[5], 1),
        small_sums[6],
    )


bf16 = jnp.bfloat16
f32 = jnp.float32
MESH = pl.DeviceIdType.MESH
VMEM_CAP = 60 * 1024 * 1024
LAYER_CAP = 63 * 1024 * 1024
ROWS = LONG_SLOTS * LONG_LEN + MID_SLOTS * MID_LEN + SHORT_SLOTS * SHORT_LEN
BLOCK = 96
CHUNK = 512
HALF = CHUNK // 2
SECTION = FF // CHUNK
WIDE = 3 * SECTION - 1
CHUNKS = WIDE + 2
SLOTS = 4


def dot_nn(a, b):
    return lax.dot_general(a, b, (((1,), (0,)), ((), ())), preferred_element_type=f32)


def dot_nt(a, b):
    return lax.dot_general(a, b, (((1,), (1,)), ((), ())), preferred_element_type=f32)


def dot_tn(a, b):
    return lax.dot_general(a, b, (((0,), (0,)), ((), ())), preferred_element_type=f32)


def loop(count, step, body):
    def run(i, carry):
        body(pl.multiple_of(i * step, step))
        return carry

    lax.fori_loop(0, count, run, 0)


def plane_of(block, half, group):
    place = block * 24 + half * 12 + group
    bit = place % 32
    return place // 32, (1 << bit) if bit < 31 else -(1 << 31)


def unpack_blocks(words, scl, blocks, dst):
    def one(owner, carry):
        for block in blocks:
            unpack_owner(words, scl, block, dst, owner)
        return carry

    lax.fori_loop(0, 8, one, 0)


def unpack_owner(words, scl, block, dst, owner):
    index = 0 if block < 3 else 1 if block == 3 else 2 if block < 8 else block - 5

    for pair in range(6):
        parts = []
        for group in (2 * pair, 2 * pair + 1):
            total = None
            for half in range(2):
                word, bit = plane_of(block, half, group)
                bits = words[owner, word * 8 : (word + 1) * 8, :] & jnp.int32(bit)
                column = index * 2 + half
                scale = jnp.broadcast_to(
                    scl[owner, group * 8 : (group + 1) * 8, column : column + 1], (8, D)
                )
                value = jnp.where(bits != 0, scale, -scale)
                total = value if total is None else total + value
            parts.append(total)
        tile = jnp.concatenate(parts, axis=0).astype(bf16)
        if block < 8:
            start = owner * BLOCK + pair * 16
        else:
            start = owner * (4 * BLOCK) + (block - 8) * BLOCK + pair * 16
        rows = pl.ds(pl.multiple_of(start, 16), 16)
        if block < 3:
            dst[rows, block * D : (block + 1) * D] = tile
        elif block < 8 and block > 3:
            dst[rows, (block - 4) * D : (block - 3) * D] = tile
        else:
            dst[rows, :] = tile


def clip_back(grad, value, level, inverse):
    u = value * inverse
    t = jnp.tanh(u)
    slope = 1.0 - t * t
    return grad * slope, jnp.sum(grad * (t - u * slope), axis=0, keepdims=True)


def norm_rows(v):
    center = v - jnp.mean(v, axis=1, keepdims=True)
    variance = jnp.mean(center * center, axis=1, keepdims=True)
    rstd = lax.rsqrt(variance + norm_epsilon)
    return center * rstd, rstd


def norm_rows_back(grad, hat, rstd, gain_row):
    g = grad * gain_row
    return rstd * (
        g - jnp.mean(g, axis=1, keepdims=True) - hat * jnp.mean(g * hat, axis=1, keepdims=True)
    )


def colsum(v):
    return jnp.sum(v, axis=0, keepdims=True)


HALF_ROOT = 1.0 / math.sqrt(2.0)
DENSITY = 1.0 / math.sqrt(2.0 * math.pi)


def layer_kernel(
    seq, live, level, tb, mb, wb, nb, gain, shift, hid_in, teach, teach_scores, tl, ml, wl, nl,
    out_to, acc_to, fin_to, kept_to, small_out,
    out, acc, fin, kept, hid, words, small, scl, spread,
    wt, wm, ww, wn, prm, bias, wbias, qkv, low, ctx, hat1, rstd1, widened, act, wg, sgrad,
    cgrad, valid, pair, xlT, clT, wlT, nlT, sums, tbuf, pt, rb, rx, rz, rf, held, ry, rd, sin,
    s1, r1, s2, r2, s3, r3, s4, r4, s5, r5, s6, r6, sms, smr, tsem, lsem, zs, zr, cs_, cr_, hsem, fsem, s7, r7,
):
    dp = lax.axis_index("dp")
    me = lax.axis_index("fsdp")
    x = lax.rem(dp, 2)
    y = lax.div(dp, 2)
    z = lax.div(me, 2)
    core = lax.rem(me, 2)
    over_x = (dp + 1 - 2 * x, me)
    over_y = (dp + 2 - 4 * y, me)
    over_core = (dp, z * 2 + 1 - core)

    def remote(src, dst, send, recv, to):
        return pltpu.make_async_remote_copy(
            src_ref=src, dst_ref=dst, send_sem=send, recv_sem=recv, device_id=to,
            device_id_type=MESH,
        )

    greet = pltpu.get_barrier_semaphore()
    for to in (over_core, over_x, over_y) + tuple(
        (dp, lax.rem(z + hop, 4) * 2 + core) for hop in (1, 2, 3)
    ):
        pl.semaphore_signal(greet, inc=1, device_id=to, device_id_type=MESH)

    teach_load = pltpu.make_async_copy(teach, cgrad, hsem.at[0])
    hid_load = pltpu.make_async_copy(hid_in, hid, hsem.at[1])
    out_save = pltpu.make_async_copy(out, out_to, hsem.at[2])
    acc_save = pltpu.make_async_copy(acc, acc_to, hsem.at[3])
    kept_save = pltpu.make_async_copy(kept, kept_to, hsem.at[4])

    loads = []
    for half in range(2):
        band = slice(192 + half * BLOCK, 192 + (half + 1) * BLOCK)
        loads.append([
            pltpu.make_async_copy(tl.at[half], widened.at[band, 0 : 3 * D], lsem.at[half, 0]),
            pltpu.make_async_copy(ml.at[half], widened.at[band, 3 * D : FF], lsem.at[half, 1]),
            pltpu.make_async_copy(
                wl.at[half], widened.at[half * BLOCK : (half + 1) * BLOCK, :], lsem.at[half, 2]
            ),
            pltpu.make_async_copy(
                nl.at[half], (ctx if half == 0 else sgrad).at[0 : 4 * BLOCK, :], lsem.at[half, 3]
            ),
        ])
    for index in range(4):
        for half in range(2):
            loads[half][index].start()
    hid_load.start()
    teach_load.start()

    def latent_piece(block, half, group):
        if block < 4:
            rows = pl.ds(192 + half * BLOCK + group * 8, 8)
            return widened[rows, block * D : (block + 1) * D]
        if block < 8:
            return widened[pl.ds(half * BLOCK + group * 8, 8), (block - 4) * D : (block - 3) * D]
        rows = pl.ds((block - 8) * BLOCK + group * 8, 8)
        return (ctx if half == 0 else sgrad)[rows, :]

    planes = [[] for _ in range(9)]
    for block in range(12):
        for half in range(2):
            for group in range(12):
                word, bit = plane_of(block, half, group)
                planes[word].append((block, half, group, bit))

    def pack(word):
        total = jnp.zeros((8, D), jnp.int32)
        for block, half, group, bit in planes[word]:
            piece = latent_piece(block, half, group)
            total = total | jnp.where(piece > 0, jnp.int32(bit), jnp.int32(0))
        words[me, word * 8 : (word + 1) * 8, :] = total

    def pack_kept(word):
        total = jnp.zeros((8, D), jnp.int32)
        for block, half, group, bit in planes[word]:
            piece = jnp.abs(latent_piece(block, half, group))
            total = total | jnp.where(piece <= 1.0, jnp.int32(bit), jnp.int32(0))
        kept[word * 8 : (word + 1) * 8, :] = total

    def part_of(owner, index):
        return small.at[owner] if index == 3 else words.at[owner, index * 24 : (index + 1) * 24]

    def z_send(index, hop):
        ref = part_of(me, index)
        peer = lax.rem(z + hop, 4) * 2 + core
        return remote(ref, ref, zs.at[index, hop - 1], zr.at[index, hop - 1], (dp, peer))

    def core_send(index, hop):
        ref = part_of(lax.rem(z + 4 - hop, 4) * 2 + core, index)
        return remote(ref, ref, cs_.at[index, hop], cr_.at[index, hop], over_core)

    def send_out(index):
        for hop in (2, 1, 3):
            z_send(index, hop).start()
        core_send(index, 0).start()

    def pass_on(index):
        for hop in (1, 3, 2):
            z_send(index, hop).wait()
            core_send(index, hop).start()

    def all_here(index):
        for hop in range(4):
            core_send(index, hop).wait()

    for half in range(2):
        loads[half][0].wait()
        loads[half][1].wait()
    for word in range(3):
        pack(word)
    pl.semaphore_wait(greet, 6)
    send_out(0)
    for half in range(2):
        loads[half][2].wait()
        loads[half][3].wait()
    slot_lane = lax.broadcasted_iota(jnp.int32, (8, 128), 1)

    def scale_rows(pair):
        for part in range(2):
            scale_group(pl.multiple_of(pair + part * 8, 8))

    def scale_group(group):
        tile = jnp.zeros((8, 128), f32)
        for half in range(2):
            rows = pl.ds(pl.multiple_of(192 + half * BLOCK + group, 8), 8)
            for index in range(7):
                if index == 0:
                    part = widened[rows, 0 : 3 * D]
                elif index == 1:
                    part = widened[rows, 3 * D : FF]
                elif index == 2:
                    part = widened[pl.ds(pl.multiple_of(half * BLOCK + group, 8), 8), :]
                else:
                    at = pl.ds(pl.multiple_of((index - 3) * BLOCK + group, 8), 8)
                    part = (ctx if half == 0 else sgrad)[at, :]
                fan = FF if index >= 3 else D
                mean = jnp.sum(jnp.abs(part), axis=1, keepdims=True) * (1.0 / part.shape[1])
                tile = jnp.where(slot_lane == index * 2 + half, mean / math.sqrt(fan), tile)
        spread[pl.ds(group, 8), :] = tile

    loop(6, 16, scale_rows)
    spread[BLOCK:128, :] = jnp.zeros((128 - BLOCK, 128), f32)
    small[me, 0:16, :] = spread[...].T[0:16, :]
    small[me, 16:32, :] = jnp.zeros((16, 128), f32)
    small[me, 16:19, 0:BLOCK] = tb[...]
    small[me, 19:20, 0:BLOCK] = mb[...]
    small[me, 20:21, 0:BLOCK] = nb[...]
    small[me, 21:23, 0:BLOCK] = gain[...]
    small[me, 23:25, 0:BLOCK] = shift[...]
    for part in range(3):
        small[me, 25 + part : 26 + part, :] = wb[part * 128 : (part + 1) * 128].reshape(1, 128)
    send_out(3)
    for word in range(3, 9):
        pack(word)
    for word in range(9):
        pack_kept(word)
    kept_save.start()
    c0, c1, c2, c3 = level[0], level[1], level[2], level[3]
    i0, i1, i2, i3 = 1.0 / c0, 1.0 / c1, 1.0 / c2, 1.0 / c3
    sums[...] = jnp.zeros_like(sums)
    row = lax.broadcasted_iota(jnp.int32, (256, 256), 0)
    col = lax.broadcasted_iota(jnp.int32, (256, 256), 1)
    key_ok = col < seq[0, 0]
    query_ok = row < seq[0, 0] * live[0, 0]
    valid[0] = jnp.where(key_ok, 1.0, 0.0).astype(bf16)
    pair[0] = jnp.where(key_ok & query_ok, 1.0, 0.0).astype(bf16)

    def in_slots(at):
        mid = (at < 128) & (at < seq[0, 1])
        one = (at >= 128) & (at < 192) & (at - 128 < seq[0, 2])
        two = (at >= 192) & (at - 192 < seq[0, 3])
        return mid, one, two

    km, ko, kt = in_slots(col)
    qm, qo, qt = in_slots(row)
    key_ok = (km & (row < 128)) | (ko & (row >= 128) & (row < 192)) | (kt & (row >= 192))
    live_mid = row * 0 + live[0, 1] > 0
    live_one = row * 0 + live[0, 2] > 0
    live_two = row * 0 + live[0, 2] > 1
    query_ok = (qm & live_mid) | (qo & live_one) | (qt & live_two)
    valid[1] = jnp.where(key_ok, 1.0, 0.0).astype(bf16)
    pair[1] = jnp.where(key_ok & query_ok, 1.0, 0.0).astype(bf16)
    ones = jnp.where(query_ok, 1.0, 0.0)

    def clip_in(r):
        x = hid[pl.ds(r, 128), :].astype(f32)
        lo = (c0 * jnp.tanh(x * i0)).astype(bf16)
        low[pl.ds(r, 128), :] = lo

    hid_load.wait()
    for r in range(0, ROWS, 128):
        clip_in(r)
    pass_on(3)
    all_here(3)
    total = jnp.zeros((16, D), f32)
    param_lane = lax.broadcasted_iota(jnp.int32, (16, 128), 1)
    for owner in range(8):
        turned = jnp.concatenate([small[owner, 0:16, :], jnp.zeros((112, 128), f32)], axis=0).T
        scl[owner] = turned[0:BLOCK, :]
        piece = jnp.where(param_lane < BLOCK, small[owner, 16:32, :], 0.0)
        wide = jnp.concatenate([piece, jnp.zeros((16, D - 128), f32)], axis=1)
        total = total + (pltpu.roll(wide, owner * BLOCK, 1) if owner else wide)
        for part in range(3):
            at = owner * 4 * BLOCK + part * 128
            wbias[0:1, at : at + 128] = small[owner, 25 + part : 26 + part, :]
    prm[...] = total
    for part in range(3):
        bias[0:1, part * D : (part + 1) * D] = prm[part : part + 1, :]
    def same_core(hop, carry):
        @pl.when(hop > 0)
        def _():
            z_send(0, hop).wait()
            core_send(0, hop).start()

        for block in range(3):
            unpack_owner(words, scl, block, wt, lax.rem(z + 4 - hop, 4) * 2 + core)
        return carry

    def other_core(hop, carry):
        core_send(0, hop).wait()
        for block in range(3):
            unpack_owner(words, scl, block, wt, lax.rem(z + 4 - hop, 4) * 2 + 1 - core)
        return carry

    lax.fori_loop(0, 4, same_core, 0)
    send_out(1)
    lax.fori_loop(0, 4, other_core, 0)

    for part in range(9):
        cs = slice(part * 256, (part + 1) * 256)
        qkv[:, cs] = (dot_nn(low[...], wt[:, cs]) + bias[0:1, cs]).astype(bf16)
    send_out(2)
    lane = lax.broadcasted_iota(jnp.int32, (256, 128), 1)
    first = lane < 64

    def pick(v, j):
        return jnp.where(first, v, jnp.zeros_like(v)) if j == 0 else jnp.where(first, jnp.zeros_like(v), v)

    def softmax(q, k, ok, j):
        s = dot_nt(pick(q, j), k) * (HEAD_DIM**-0.5)
        masked = jnp.where(ok, s, masked_fill)
        e = jnp.exp(masked - jnp.max(masked, axis=1, keepdims=True))
        return s, e / jnp.sum(e, axis=1, keepdims=True)

    for g in range(2):
        for c in range(0, D, 128):
            rs = slice(g * 256, (g + 1) * 256)
            q, k, v = (qkv[rs, at + c : at + c + 128] for at in (0, D, 2 * D))
            ok = valid[g].astype(f32) > 0.5
            parts = []
            for j in range(2):
                s, p = softmax(q, k, ok, j)
                parts.append(dot_nn(p.astype(bf16), v))
            ctx[rs, c : c + 128] = jnp.where(first, parts[0], parts[1])
    pass_on(1)
    unpack_blocks(words, scl, (3,), wm)

    def clip_ctx(r):
        lo = (c1 * jnp.tanh(ctx[pl.ds(r, 128), :] * i1)).astype(bf16)
        low[pl.ds(r, 128), :] = lo

    for r in range(0, ROWS, 128):
        clip_ctx(r)

    for part in range(3):
        cs = slice(part * 256, (part + 1) * 256)
        acc[:, cs] = dot_nn(low[...], wm[:, cs]) + prm[3:4, cs] + hid[:, cs].astype(f32)

    def norm_one(r):
        rs = pl.ds(r, 128)
        hat, rstd = norm_rows(acc[rs, :])
        hat1[rs, :] = hat
        rstd1[rs, :] = jnp.broadcast_to(rstd, (128, 128))
        normed = hat * prm[5:6, :] + prm[7:8, :]
        lo = (c2 * jnp.tanh(normed * i2)).astype(bf16)
        low[rs, :] = lo
        acc[rs, :] = normed + prm[4:5, :]

    loop(4, 128, norm_one)
    all_here(1)
    pass_on(2)
    unpack_blocks(words, scl, range(4, 8), ww)
    all_here(2)

    for t in range(8):
        for owner in ((0, 1), (2,), (3,), (4,), (5,), (6,), (7,), ())[t]:
            for block in range(8, 12):
                unpack_owner(words, scl, block, wn, owner)
        if t < 6:
            cs = slice(t * 512, (t + 1) * 512)
            widened[:, cs] = dot_nn(low[...], ww[:, cs]) + wbias[0:1, cs]
        if 1 <= t <= 6:
            cs = slice((t - 1) * 512, t * 512)
            for r in range(0, ROWS, 64):
                w = widened[r : r + 64, cs]
                a = 0.5 * w * (1.0 + lax.erf(w * HALF_ROOT))
                act[r : r + 64, cs] = (c3 * jnp.tanh(a * i3)).astype(bf16)
        if t >= 2:
            cs = slice((t - 2) * 512, (t - 1) * 512)
            acc[...] += dot_nn(act[:, cs], wn[cs, :])

    teach_load.wait()

    def norm_two(r):
        rs = pl.ds(r, 128)
        hat, rstd = norm_rows(acc[rs, :])
        full = hat * prm[6:7, :] + prm[8:9, :]
        out[rs, :] = full.astype(bf16)
        at = lax.broadcasted_iota(jnp.int32, (128, D), 0) + r
        l0, l1, l2, l3 = seq[0, 0] * live[0, 0], seq[0, 1], seq[0, 2], seq[0, 3]
        l1 = jnp.where(live[0, 1] > 0, l1, 0)
        l2 = jnp.where(live[0, 2] > 0, l2, 0)
        l3 = jnp.where(live[0, 2] > 1, l3, 0)
        ok = (at < l0) | ((at >= 256) & (at < 256 + l1)) | ((at >= 384) & (at < 384 + l2))
        ok = ok | ((at >= 448) & (at < 448 + l3))
        gap = jnp.where(ok, full - cgrad[rs, :].astype(f32), 0.0)
        sums[15:16, :] += colsum(gap * gap) * 0.5
        sums[6:7, :] += colsum(gap * hat)
        sums[8:9, :] += colsum(gap)
        grad = norm_rows_back(gap, hat, rstd, prm[6:7, :])
        sgrad[rs, :] = grad
        acc[rs, :] = jnp.zeros((128, D), f32)
        lo = grad.astype(bf16)
        low[rs, :] = lo
        nlT[:, rs] = lo.T
        sums[4:5, :] += colsum(lo.astype(f32))

    loop(4, 128, norm_two)
    out_save.start()

    def feed_back(t):
        cs = pl.ds(pl.multiple_of(t * CHUNK, CHUNK), CHUNK)
        wbias[1:2, cs] = jnp.zeros((1, CHUNK), f32)

        def feed_back_rows(r):
            rs = pl.ds(r, 256)
            g = dot_nt(low[rs, :], wn[cs, :])
            w = widened[rs, cs]
            e = 0.5 * (1.0 + lax.erf(w * HALF_ROOT))
            a = w * e
            u = a * i3
            th = jnp.tanh(u)
            slope = 1.0 - th * th
            sums[14:15, 0:CHUNK] += colsum(g * (th - u * slope))
            back = g * slope * (e + w * (DENSITY * jnp.exp(-0.5 * w * w)))
            lo = back.astype(bf16)
            wg[rs, cs] = lo
            wbias[1:2, cs] += colsum(lo.astype(f32))
            acc[rs, :] += dot_nt(lo, ww[:, cs])

        loop(2, 256, feed_back_rows)

    def turn_widen(r):
        rs = pl.ds(r, 128)
        normed = hat1[rs, :] * prm[5:6, :] + prm[7:8, :]
        wlT[:, rs] = (c2 * jnp.tanh(normed * i2)).astype(bf16).T

    def turn_context(r):
        clT[:, pl.ds(r, 128)] = (c1 * jnp.tanh(ctx[pl.ds(r, 128), :] * i1)).astype(bf16).T

    def turn_inputs(r):
        v = hid[pl.ds(r, 128), :].astype(f32)
        xlT[:, pl.ds(r, 128)] = (c0 * jnp.tanh(v * i0)).astype(bf16).T

    def norm_one_back(r):
        rs = pl.ds(r, 128)
        hat = hat1[rs, :]
        normed = hat * prm[5:6, :] + prm[7:8, :]
        grad, clip_sum = clip_back(acc[rs, :], normed, c2, i2)
        sums[18:19, :] += clip_sum
        grad = grad + sgrad[rs, :]
        sums[5:6, :] += colsum(grad * hat)
        sums[7:8, :] += colsum(grad)
        grad = norm_rows_back(grad, hat, rstd1[rs, 0:1], prm[5:6, :])
        acc[rs, :] = grad
        lo = grad.astype(bf16)
        low[rs, :] = lo
        sums[3:4, :] += colsum(lo.astype(f32))

    def mix_back(c):
        cs = pl.ds(c, 256)
        g = dot_nt(low[...], wm[cs, :])
        grad, clip_sum = clip_back(g, ctx[:, cs], c1, i1)
        sums[17:18, cs] += clip_sum
        cgrad[:, cs] = grad.astype(bf16)

    def scores_copy(u, slot):
        g = lax.div(u, 6)
        hp = lax.rem(u, 6)
        rs = pl.ds(pl.multiple_of(g * 256, 256), 256)
        return pltpu.make_async_copy(
            teach_scores.at[pl.ds(2 * hp, 2), rs], tbuf.at[slot], tsem.at[slot]
        )

    def attend_pair_back(u, slot):
        g = lax.div(u, 6)
        hp = lax.rem(u, 6)
        rs = pl.ds(pl.multiple_of(g * 256, 256), 256)
        q0 = pl.multiple_of(hp * 128, 128)
        k0 = pl.multiple_of(D + q0, 128)
        v0 = pl.multiple_of(2 * D + q0, 128)
        q = qkv[rs, pl.ds(q0, 128)]
        k = qkv[rs, pl.ds(k0, 128)]
        v = qkv[rs, pl.ds(v0, 128)]
        cg = cgrad[rs, pl.ds(q0, 128)]
        ok = valid[g].astype(f32) > 0.5
        pairs = pair[g].astype(f32) > 0.5
        dq, dk, dv = [], [], []
        for j in range(2):
            s, p = softmax(q, k, ok, j)
            ts = tbuf[slot, j].astype(f32)
            second = pltpu.roll(ts[128:192], 128, 1)
            third = pltpu.roll(ts[192:256], 192, 1)
            moved = jnp.concatenate([ts[0:128], second, third], axis=0)
            ts = jnp.where(g > 0, moved, ts)
            gap = jnp.where(pairs, s - ts, 0.0)
            sums[16:17, 0:256] += colsum(gap * gap) * (0.5 / LONG_LEN)
            pg = dot_nt(pick(cg, j), v)
            sg = p * (pg - jnp.sum(pg * p, axis=1, keepdims=True)) + gap * (1.0 / LONG_LEN)
            sg = sg.astype(bf16)
            dv.append(dot_tn(p.astype(bf16), cg))
            dq.append(dot_nn(sg, k))
            dk.append(dot_tn(sg, q))
        scale = HEAD_DIM**-0.5
        dq = (jnp.where(first, dq[0], dq[1]) * scale).astype(bf16)
        dk = (jnp.where(first, dk[0], dk[1]) * scale).astype(bf16)
        dv = jnp.where(first, dv[0], dv[1]).astype(bf16)
        for index, (grad, at) in enumerate(((dq, q0), (dk, k0), (dv, v0))):
            qkv[rs, pl.ds(at, 128)] = grad
            sums[index : index + 1, pl.ds(q0, 128)] += colsum(grad.astype(f32))

    def input_back(c):
        cs = pl.ds(c, 256)
        g = dot_nt(qkv[...], wt[cs, :])
        grad, clip_sum = clip_back(g, hid[:, cs].astype(f32), c0, i0)
        sums[19:20, cs] += clip_sum
        acc[:, cs] += grad

    def close_sums():
        for part in range(4):
            sums[9 + part : 10 + part, :] = wbias[1:2, part * D : (part + 1) * D]
        at = lax.broadcasted_iota(jnp.int32, (1, D), 1)
        line = jnp.zeros((1, D), f32)
        for spot, value in enumerate(
            (
                sums[19:20, :], sums[17:18, :], sums[18:19, :], sums[14:15, :],
                sums[15:16, :] + sums[16:17, :],
            )
        ):
            line = jnp.where(at == spot, jnp.sum(value), line)
        sums[13:14, :] = line
        small_out[...] = sums[0:16, :]

    firsts = (over_x, over_y)
    seconds = (over_y, over_x)
    outer = (z == 0) | (z == 3)
    inner = (z == 1) | (z == 2)
    near = z + 1 - 2 * lax.rem(z, 2)
    beyond = 1 - lax.div(z, 2)

    def on_z(to):
        return (dp, to * 2 + core)

    def lanes(p, w):
        return pl.ds(p * (w // 2), w // 2)

    def core_copy(k, w):
        slot, duo = lax.rem(k, SLOTS), lax.rem(k, 2)
        cs = pl.ds(0, w)
        return remote(
            pt.at[slot, :, 1 - core, :, :, :, cs], rb.at[duo, :, :, :, :, cs], s1.at[slot],
            r1.at[slot], over_core,
        )

    def own_rows(slot, blocks, p, w, mine):
        i = (x if p == 0 else y) if mine else (1 - x if p == 0 else 1 - y)
        if p == 0:
            return pt.at[slot, blocks, core, i, :, :, lanes(p, w)]
        return pt.at[slot, blocks, core, :, i, :, lanes(p, w)]

    def first_copy(k, w, p):
        slot, duo = lax.rem(k, SLOTS), lax.rem(k, 2)
        src = own_rows(slot, pl.ds(0, 4), p, w, False)
        dst = rx.at[duo, p, :, :, :, lanes(0, w)]
        return remote(src, dst, s2.at[slot, p], r2.at[slot, p], firsts[p])

    def in_copy(k, w, p):
        slot, duo = lax.rem(k, SLOTS), lax.rem(k, 2)
        src = own_rows(slot, pl.ds(beyond, 3), p, w, True)
        dst = rz.at[duo, p, :, :, :, lanes(0, w)]
        return remote(src, dst, s3.at[slot, p], r3.at[slot, p], on_z(near))

    def out_copy(k, w, p, kind):
        slot = lax.rem(k, SLOTS)
        to = (near, 3 - z, lax.rem(z + 2, 4))[kind]
        return remote(
            own_rows(slot, to, p, w, True), rf.at[slot, min(kind, 1), p, :, :, lanes(0, w)],
            s4.at[slot, kind, p], r4.at[slot, min(kind, 1), p], on_z(to),
        )

    def direct_copy(p, hop):
        to = lax.rem(z + hop, 4)
        return remote(
            own_rows((CHUNKS - 1) % SLOTS, to, p, HALF, True), rd.at[hop - 1, p],
            s7.at[hop - 1, p], r7.at[hop - 1, p], on_z(to),
        )

    def room_of(k):
        return 2 if isinstance(k, int) else lax.rem(k, 2)

    def second_copy(k, w, p):
        slot, duo = lax.rem(k, SLOTS), room_of(k)
        cs = lanes(0, w)
        return remote(
            held.at[duo, p, :, :, cs], ry.at[duo, p, :, :, cs], s5.at[slot, p], r5.at[slot, p],
            seconds[p],
        )

    def fin_at(k, w, p, rows):
        if w == CHUNK:
            flat = k * CHUNK
        else:
            flat = WIDE * CHUNK + (k - WIDE) * w
        cs = pl.ds(pl.multiple_of(lax.rem(flat, FF) + p * (w // 2), 128), w // 2)
        return (lax.div(flat, FF), *((x, rows) if p == 0 else (rows, y)), slice(None), cs)

    def back_first(k, w, p):
        slot = lax.rem(k, SLOTS)
        ref = fin.at[fin_at(k, w, p, slice(None))]
        return remote(ref, ref, s6.at[slot, p], r6.at[slot, p], firsts[p])

    def small_copy(step):
        to = (
            over_core, over_x, over_y, on_z(lax.rem(z + 1, 4)), on_z(lax.rem(z + 2, 4)),
            on_z(lax.rem(z + 3, 4)),
        )[step]
        return remote(small_out, sin.at[step], sms.at[step], smr.at[step], to)

    def finish_first(k, w):
        for p in range(2):
            back_first(k, w, p).wait()
        fin_save(k, w).start()

    def fin_save(k, w):
        if w == CHUNK:
            flat = k * CHUNK
        else:
            flat = WIDE * CHUNK + (k - WIDE) * w
        cs = pl.ds(pl.multiple_of(lax.rem(flat, FF), 128), w)
        at = (lax.div(flat, FF), slice(None), slice(None), slice(None), cs)
        return pltpu.make_async_copy(fin.at[at], fin_to.at[at], fsem.at[lax.rem(k, SLOTS)])

    def finish_save(k, w):
        fin_save(k, w).wait()

    def finish_second(k, w):
        duo = room_of(k)
        for p in range(2):
            second_copy(k, w, p).wait()
            for i in range(2):
                cs = lanes(0, w)
                fin[fin_at(k, w, p, i)] = held[duo, p, i, :, cs] + ry[duo, p, i, :, cs]
            back_first(k, w, p).start()

    def finish_out(k, w):
        slot, duo = lax.rem(k, SLOTS), lax.rem(k, 2)
        cs = lanes(0, w)

        @pl.when(outer)
        def _():
            for p in range(2):
                out_copy(k, w, p, 0).wait_recv()
                out_copy(k, w, p, 2).wait_recv()
                for i in range(2):
                    at = (x, i) if p == 0 else (i, y)
                    own = pt[(slot, z, core, *at, slice(None), lanes(p, w))]
                    held[duo, p, i, :, cs] = (
                        own + rf[slot, 0, p, i, :, cs] + rf[slot, 1, p, i, :, cs]
                    )

        @pl.when(inner)
        def _():
            for p in range(2):
                out_copy(k, w, p, 1).wait()
                out_copy(k, w, p, 0).wait_send()
                out_copy(k, w, p, 2).wait_send()
                for i in range(2):
                    at = (x, i) if p == 0 else (i, y)
                    own = pt[(slot, z, core, *at, slice(None), lanes(p, w))]
                    held[duo, p, i, :, cs] = own + rf[slot, 1, p, i, :, cs]

        for p in range(2):
            second_copy(k, w, p).start()

    def finish_in(k, w):
        slot, duo = lax.rem(k, SLOTS), lax.rem(k, 2)

        @pl.when(outer)
        def _():
            for p in range(2):
                in_copy(k, w, p).wait_send()

        @pl.when(inner)
        def _():
            for p in range(2):
                in_copy(k, w, p).wait_recv()
                for q in range(3):
                    for i in range(2):
                        at = (x, i) if p == 0 else (i, y)
                        at = (slot, beyond + q, core, *at, slice(None), lanes(p, w))
                        pt[at] += rz[duo, p, q, i, :, lanes(0, w)]
                for kind in (2, 1, 0):
                    out_copy(k, w, p, kind).start()

    def add_first(k, w, p):
        slot, duo = lax.rem(k, SLOTS), lax.rem(k, 2)
        first_copy(k, w, p).wait()
        for q in range(4):
            for i in range(2):
                at = (x, i) if p == 0 else (i, y)
                at = (slot, q, core, *at, slice(None), lanes(p, w))
                pt[at] += rx[duo, p, q, i, :, lanes(0, w)]

    def finish_one(k, w):
        for p in range(2):
            add_first(k, w, p)

            @pl.when(outer)
            def _():
                in_copy(k, w, p).start()

    def last_one():
        for p in range(2):
            add_first(CHUNKS - 1, HALF, p)
            for hop in (2, 1, 3):
                direct_copy(p, hop).start()

    def last_direct():
        slot = (CHUNKS - 1) % SLOTS
        for p in range(2):
            for hop in (1, 3, 2):
                direct_copy(p, hop).wait()
            for i in range(2):
                at = (x, i) if p == 0 else (i, y)
                own = pt[(slot, z, core, *at, slice(None), lanes(p, HALF))]
                held[2, p, i, :, lanes(0, HALF)] = own + rd[0, p, i] + rd[1, p, i] + rd[2, p, i]
            second_copy(CHUNKS - 1, HALF, p).start()

    def finish_core(k, w):
        slot, duo = lax.rem(k, SLOTS), lax.rem(k, 2)
        core_copy(k, w).wait()
        cs = pl.ds(0, w)
        for q in range(4):
            pt[slot, q, core, :, :, :, cs] += rb[duo, q, :, :, :, cs]
        for p in range(2):
            first_copy(k, w, p).start()

    stages = (
        (7, finish_save), (6, finish_first), (5, finish_second), (4, finish_out), (3, finish_in),
        (2, finish_one), (1, finish_core),
    )
    last = CHUNKS - 1
    last_stages = {
        5: lambda: finish_second(last, HALF), 4: last_direct, 2: last_one,
        6: lambda: finish_first(last, HALF), 1: lambda: finish_core(last, HALF),
    }

    def tick(t, carry):
        for lag, step in stages:

            @pl.when((t >= lag) & (t < lag + WIDE))
            def _():
                step(t - lag, CHUNK)

            @pl.when(t == lag + WIDE)
            def _():
                step(t - lag, HALF)

            if lag in last_stages:

                @pl.when(t == last + lag - (1 if lag > 2 else 0))
                def _():
                    last_stages[lag]()

        slot = lax.rem(t, SLOTS)

        def put(owner, cs, block):
            for i in range(2):
                for j in range(2):
                    at = (i * 2 + j) * 24
                    pt[slot, owner // 2, owner % 2, i, j, :, cs] = block[at : at + 24, :]

        pieces = CHUNK // 128
        turns = 8 // pieces

        @pl.when(t < SECTION)
        def _():
            j = lax.div(t, turns)
            count = pieces * BLOCK
            left = nlT[pl.ds(pl.multiple_of(lax.rem(t, turns) * count, count), count), :]
            for owner in range(8):
                cs = pl.ds(pl.multiple_of(owner * 384 + j * 128, 128), 128)
                got = dot_nn(left, act[:, cs])
                for part in range(pieces):
                    put(owner, pl.ds(part * 128, 128), got[part * BLOCK : (part + 1) * BLOCK, :])

        def whole(left, right, half):
            got = dot_nn(left, right)
            for owner in range(8):
                put(owner, pl.ds(half * 256, 256), got[owner * BLOCK : (owner + 1) * BLOCK, :])

        for half in range(2):

            @pl.when((t >= SECTION) & (t < 2 * SECTION))
            def _():
                cs = pl.ds(pl.multiple_of((t - SECTION) * CHUNK + half * 256, 256), 256)
                whole(wlT[...], wg[:, cs], half)

            part = (t - 2 * SECTION) * 2 + half

            @pl.when((part >= 0) & (part < 3))
            def _():
                whole(clT[...], low[:, pl.ds(pl.multiple_of(part * 256, 256), 256)], half)

            @pl.when((part >= 3) & (part < 10))
            def _():
                whole(xlT[...], qkv[:, pl.ds(pl.multiple_of((part - 3) * 256, 256), 256)], half)

        @pl.when(t < WIDE)
        def _():
            core_copy(t, CHUNK).start()

        @pl.when((t >= WIDE) & (t < CHUNKS))
        def _():
            cs = pl.ds(pl.multiple_of((t - WIDE + 7) * 256, 256), 256)
            whole(xlT[...], qkv[:, cs], 0)
            core_copy(t, HALF).start()

        for when, turn in ((2, turn_inputs), (3, turn_context), (4, turn_widen)):

            @pl.when(t == when)
            def _():
                loop(4, 128, turn)

        units = 12 // SECTION
        begin = SECTION + 1

        @pl.when((t >= 1) & (t < SECTION))
        def _():
            feed_back(t - 1)

        @pl.when(t == SECTION - 1)
        def _():
            feed_back(t)

        @pl.when(t == SECTION)
        def _():
            for slot in range(2):
                scores_copy(slot, slot).start()
            loop(4, 128, norm_one_back)
            loop(3, 256, mix_back)

        @pl.when((t >= begin) & (t < begin + SECTION))
        def _():
            for index in range(units):
                u = (t - begin) * units + index
                at = lax.rem(u, 2)
                scores_copy(u, at).wait()
                attend_pair_back(u, at)

                @pl.when(u < 10)
                def _():
                    scores_copy(u + 2, at).start()

        done = begin + SECTION

        @pl.when((t >= done) & (t < done + 3))
        def _():
            input_back(pl.multiple_of((t - done) * 256, 256))

        @pl.when(t == done + 3)
        def _():
            acc_save.start()
            close_sums()
            small_copy(0).start()

        @pl.when(t == done + 4)
        def _():
            small_copy(0).wait()
            small_out[...] += sin[0]
            small_copy(1).start()

        @pl.when(t == done + 5)
        def _():
            small_copy(1).wait()
            small_out[...] += sin[1]
            small_copy(2).start()

        @pl.when(t == done + 6)
        def _():
            small_copy(2).wait()
            small_out[...] += sin[2]
            for step in (3, 4, 5):
                small_copy(step).start()

        @pl.when(t == done + 7)
        def _():
            for step in (3, 4, 5):
                small_copy(step).wait()
            small_out[...] = small_out[...] + sin[3] + sin[4] + sin[5]

        return carry

    lax.fori_loop(0, CHUNKS + 5, tick, 0)
    fin_save(WIDE, HALF).wait()
    fin_save(last, HALF).wait()
    for copy in (out_save, acc_save, kept_save):
        copy.wait()


def layer(*args):
    vm = pl.BlockSpec(memory_space=pltpu.VMEM)
    sm = pl.BlockSpec(memory_space=pltpu.SMEM)
    sds = jax.ShapeDtypeStruct
    dma = pltpu.SemaphoreType.DMA
    return pl.pallas_call(
        layer_kernel,
        out_shape=(
            sds((ROWS, D), bf16),
            sds((ROWS, D), f32),
            sds((3, 2, 2, 24, FF), f32),
            sds((72, D), jnp.int32),
            sds((16, D), f32),
        ),
        in_specs=[sm] * 3 + [vm] * 6 + [pl.BlockSpec(memory_space=pl.ANY)] * 7,
        out_specs=(pl.BlockSpec(memory_space=pl.ANY),) * 4 + (vm,),
        scratch_shapes=[
            pltpu.VMEM((ROWS, D), bf16),
            pltpu.VMEM((ROWS, D), f32),
            pltpu.VMEM((3, 2, 2, 24, FF), f32),
            pltpu.VMEM((72, D), jnp.int32),
            pltpu.VMEM((ROWS, D), bf16),
            pltpu.VMEM((8, 72, D), jnp.int32),
            pltpu.VMEM((8, 32, 128), f32),
            pltpu.VMEM((8, BLOCK, 128), f32),
            pltpu.VMEM((128, 128), f32),
            pltpu.VMEM((D, 3 * D), bf16),
            pltpu.VMEM((D, D), bf16),
            pltpu.VMEM((D, FF), bf16),
            pltpu.VMEM((FF, D), bf16),
            pltpu.VMEM((16, D), f32),
            pltpu.VMEM((8, 3 * D), f32),
            pltpu.VMEM((8, FF), f32),
            pltpu.VMEM((ROWS, 3 * D), bf16),
            pltpu.VMEM((ROWS, D), bf16),
            pltpu.VMEM((ROWS, D), f32),
            pltpu.VMEM((ROWS, D), f32),
            pltpu.VMEM((ROWS, 128), f32),
            pltpu.VMEM((ROWS, FF), f32),
            pltpu.VMEM((ROWS, FF), bf16),
            pltpu.VMEM((ROWS, FF), bf16),
            pltpu.VMEM((ROWS, D), f32),
            pltpu.VMEM((ROWS, D), bf16),
            pltpu.VMEM((2, 256, 256), bf16),
            pltpu.VMEM((2, 256, 256), bf16),
            pltpu.VMEM((D, ROWS), bf16),
            pltpu.VMEM((D, ROWS), bf16),
            pltpu.VMEM((D, ROWS), bf16),
            pltpu.VMEM((D, ROWS), bf16),
            pltpu.VMEM((24, D), f32),
            pltpu.VMEM((2, 2, 256, 256), bf16),
            pltpu.VMEM((SLOTS, 4, 2, 2, 2, 24, CHUNK), f32),
            pltpu.VMEM((2, 4, 2, 2, 24, CHUNK), f32),
            pltpu.VMEM((2, 2, 4, 2, 24, HALF), f32),
            pltpu.VMEM((2, 2, 3, 2, 24, HALF), f32),
            pltpu.VMEM((SLOTS, 2, 2, 2, 24, HALF), f32),
            pltpu.VMEM((3, 2, 2, 24, HALF), f32),
            pltpu.VMEM((3, 2, 2, 24, HALF), f32),
            pltpu.VMEM((3, 2, 2, 24, HALF // 2), f32),
            pltpu.VMEM((6, 16, D), f32),
        ]
        + [dma((SLOTS,))] * 2
        + [dma((SLOTS, 2))] * 4
        + [dma((SLOTS, 3, 2)), dma((SLOTS, 2, 2))]
        + [dma((SLOTS, 2))] * 4
        + [dma((6,))] * 2
        + [dma((2,)), dma((2, 4)), dma((4, 3)), dma((4, 3)), dma((4, 4)), dma((4, 4)), dma((5,)), dma((SLOTS,)), dma((3, 2)), dma((3, 2))],
        compiler_params=pltpu.CompilerParams(collective_id=0, has_side_effects=True, vmem_limit_bytes=LAYER_CAP),
        name="layer",
    )(*args)


def finish_kernel(
    count, small, kept, fin, out_in, grad_in, out, grad, tg, mg, wg, ng, tb, mb, wb, nb, gain, shift, clips, loss,
    fbuf, turned, tout, mout, wout, nout, obuf, gbuf, fsem, osem, psem,
):
    fcopies = [pltpu.make_async_copy(fin.at[i], fbuf.at[i], fsem.at[i]) for i in range(3)]
    ocopies = []
    for half in range(2):
        for index, (src, dst) in enumerate(((nout, ng), (wout, wg), (mout, mg), (tout, tg))):
            at = index * 2 + half
            ocopies.append(pltpu.make_async_copy(src.at[half], dst.at[half], osem.at[at]))
    for index in (1, 2, 0):
        fcopies[index].start()
    arrive = [
        pltpu.make_async_copy(out_in, obuf, psem.at[0]),
        pltpu.make_async_copy(grad_in, gbuf, psem.at[1]),
    ]
    depart = [
        pltpu.make_async_copy(obuf, out, psem.at[2]),
        pltpu.make_async_copy(gbuf, grad, psem.at[3]),
    ]
    me = lax.axis_index("fsdp")
    z = lax.div(me, 2)
    core = lax.rem(me, 2)
    own = pltpu.roll(small[...], lax.rem(8 - me, 8) * BLOCK, 1)
    tb[...] = own[0:3, 0:BLOCK]
    mb[...] = own[3:4, 0:BLOCK]
    nb[...] = own[4:5, 0:BLOCK]
    gain[...] = own[5:7, 0:BLOCK]
    shift[...] = own[7:9, 0:BLOCK]
    wide = pltpu.roll(small[...], core * (4 * BLOCK), 1)
    row = lax.broadcasted_iota(jnp.int32, (16, D), 0)
    picked = jnp.sum(jnp.where(row == 9 + z, wide, 0.0), axis=0, keepdims=True)
    wb[...] = picked[:, 0 : 4 * BLOCK]
    line = small[13:14, :]
    lane = lax.broadcasted_iota(jnp.int32, (1, D), 1)
    for spot in range(4):
        clips[spot] = jnp.sum(jnp.where(lane == spot, line, 0.0))
    loss[...] = jnp.sum(jnp.where(lane == 4, line, 0.0)) * count[0]

    def keep(block, half, group, total, fan):
        word, bit = plane_of(block, half, group)
        bits = kept[word * 8 : (word + 1) * 8, :] & jnp.int32(bit)
        return jnp.where(bits != 0, total * (1.0 / math.sqrt(fan)), 0.0)

    def spread_out(blocks, half, dst, src, at):
        for index, block in enumerate(blocks):
            cols = slice(index * D, (index + 1) * D)
            for group in range(12):
                rows = slice(group * 8, (group + 1) * 8)
                total = src[rows, at + index * D : at + (index + 1) * D]
                dst[half, rows, cols] = keep(block, half, group, total, D)

    def leave(index, half):
        ocopies[index + 4 * half].start()

    fcopies[1].wait()
    for copy in arrive:
        copy.start()
    for half in range(2):
        spread_out(range(4, 8), half, wout, fbuf.at[1], 0)
        leave(1, half)
    fcopies[2].wait()
    for half in range(2):
        spread_out(range(3), half, tout, fbuf.at[2], D)
        leave(3, half)
    for half in range(2):
        spread_out(range(3, 4), half, mout, fbuf.at[2], 0)
        leave(2, half)
    for index in range(2):
        arrive[index].wait()
        depart[index].start()
    fcopies[0].wait()
    for j in range(3):
        for i in range(2):
            tiles = range((j * 2 + i) * 4, (j * 2 + i) * 4 + 4)
            parts = [fbuf[0, :, tile * 128 : (tile + 1) * 128] for tile in tiles]
            total = jnp.concatenate(parts, axis=0).T
            turned[j * 128 : (j + 1) * 128, i * 384 : (i + 1) * 384] = total
    for half in range(2):
        for block in range(8, 12):
            for group in range(12):
                rows = slice((block - 8) * BLOCK + group * 8, (block - 8) * BLOCK + group * 8 + 8)
                nout[half, rows, :] = keep(block, half, group, turned[rows, :], FF)
        leave(0, half)
    for copy in depart + ocopies:
        copy.wait()


def finish(count, small, kept, fin, out, grad):
    vm = pl.BlockSpec(memory_space=pltpu.VMEM)
    sm = pl.BlockSpec(memory_space=pltpu.SMEM)
    hbm = pl.BlockSpec(memory_space=pl.ANY)
    sds = jax.ShapeDtypeStruct
    shapes = [(2, BLOCK, 3 * D), (2, BLOCK, D), (2, BLOCK, FF), (2, 4 * BLOCK, D)]
    dma = pltpu.SemaphoreType.DMA
    return pl.pallas_call(
        finish_kernel,
        out_shape=[sds((ROWS, D), bf16), sds((ROWS, D), f32)]
        + [sds(v, f32) for v in shapes]
        + [
            sds((3, BLOCK), f32), sds((1, BLOCK), f32), sds((1, 4 * BLOCK), f32),
            sds((1, BLOCK), f32), sds((2, BLOCK), f32), sds((2, BLOCK), f32),
            sds((4,), f32), sds((), f32),
        ],
        in_specs=[sm, vm, vm, hbm, hbm, hbm],
        out_specs=[hbm] * 6 + [vm] * 6 + [sm] * 2,
        scratch_shapes=[pltpu.VMEM((3, BLOCK, FF), f32), pltpu.VMEM((4 * BLOCK, D), f32)]
        + [pltpu.VMEM(v, f32) for v in shapes]
        + [pltpu.VMEM((ROWS, D), bf16), pltpu.VMEM((ROWS, D), f32)]
        + [dma((3,)), dma((8,)), dma((4,))],
        compiler_params=pltpu.CompilerParams(vmem_limit_bytes=VMEM_CAP),
        name="finish",
    )(count, small, kept, fin, out, grad)


def on_device_fast(
    hidden_in, teacher_hidden, teacher_scores, seq_lengths, live_counts, triple_latent,
    mixing_latent, widen_latent, narrow_latent, triple_bias, mixing_bias, widen_bias, narrow_bias,
    norm_gain, norm_shift, clip_level,
):
    out, input_grad, fin, kept, small_sum = layer(
        seq_lengths, live_counts, clip_level, triple_bias, mixing_bias[None], widen_bias,
        narrow_bias[None], norm_gain, norm_shift, hidden_in, teacher_hidden,
        jnp.transpose(teacher_scores, (1, 0, 2)), triple_latent, mixing_latent, widen_latent,
        narrow_latent,
    )
    fin = fin.reshape(3, BLOCK, FF)
    tokens = hidden_in.shape[0] * lax.axis_size("dp") * lax.axis_size("fsdp")
    count = jnp.full((1,), 1.0 / (tokens * D), f32)
    out, input_grad, tg, mg, wg, ng, tb, mb, wb, nb, gain, shift, clips, loss = finish(
        count, small_sum, kept, fin, out, input_grad
    )
    return (
        out, loss, input_grad, tg, mg, wg, ng, tb, mb.reshape(BLOCK),
        wb.reshape(4 * BLOCK), nb.reshape(BLOCK), gain, shift, clips,
    )


def solution(mesh):
    in_specs = (
        P(("dp", "fsdp"), None),
        P(("dp", "fsdp"), None),
        P(("dp", "fsdp"), None, None),
        P(("dp", "fsdp"), None),
        P(("dp", "fsdp"), None),
        P(None, "fsdp", None),
        P(None, "fsdp", None),
        P(None, "fsdp", None),
        P(None, "fsdp", None),
        P(None, "fsdp"),
        P("fsdp"),
        P("fsdp"),
        P("fsdp"),
        P(None, "fsdp"),
        P(None, "fsdp"),
        P(),
    )
    out_specs = (
        P(("dp", "fsdp"), None),
        P(),
        P(("dp", "fsdp"), None),
        P(None, "fsdp", None),
        P(None, "fsdp", None),
        P(None, "fsdp", None),
        P(None, "fsdp", None),
        P(None, "fsdp"),
        P("fsdp"),
        P("fsdp"),
        P("fsdp"),
        P(None, "fsdp"),
        P(None, "fsdp"),
        P(),
    )
    fits = mesh.shape["dp"] == 4 and mesh.shape["fsdp"] == 8
    return jax.shard_map(
        on_device_fast if fits else on_device, mesh=mesh, in_specs=in_specs, out_specs=out_specs, check_vma=False
    )
```
